32 devices in a mesh: depth: 4 (over y, x), tile: 8 (over z, core).
Axes of the slice: x: 2, y: 2, z: 4, core: 2. Of those that a mesh axis runs over, the one named last changes fastest.
Arguments:
- source: bfloat16 [16, 2, 128, 256], P('tile'), may hold values from -6 to 6
- anchors: int32 [16], P('tile'), may hold values from -256 to 1792, as said below
- counts: int32 [4], P('depth'), may hold values from 1 to 3, 8 in all
- reflect: bfloat16 [4, 3, 128, 2048], P('depth', None, None, 'tile'), may hold values from -0.3984375 to 0.3984375
- lateral_x: bfloat16 [4, 3, 2, 128, 128], P('depth'), may hold values from -0.375 to 0.375
- lateral_y: bfloat16 [4, 3, 2, 256, 256], P('depth'), may hold values from -0.25 to 0.25
Outputs:
- image: float32 [4, 3, 128, 2048], P('depth', None, None, 'tile')
The draws below stay inside these ranges and needn't reach their ends.
Inputs may be any that keep to these rules, and one draw needn't show every extreme that they name: `anchors`: the shots held by tile index t start their aperture between (t - 1) * 256 and t * 256. The counts sum to 8; slots at or past a section's count are unused.
All inputs are finite; a program needn't handle non-finite values. No bound on the sum of `counts` on one device may be relied on, other than what follows from the above.
Results may differ from the reference program's by a relative error of at most 0.023.
Values may be sent and summed in bfloat16 or wider, within the bound.
No kernel may reach another device: no remote copies, remote signals or barrier semaphores. Data moves between devices by JAX's collectives and lax.ppermute only.
A program may use at most 64 MiB of HBM per device.

```python
import math
import jax
import jax.numpy as jnp
import numpy as np
from jax import lax

AX = 128
AY = 256
TY = 256
LVL_MAX = 3
LEVELS = 8
SHOT_DEV = 2
SECTIONS = 4
SHOTS = 16
GY = 2048


def draw_anchors(key, part):
    owner = jnp.arange(SHOTS, dtype=jnp.int32) // SHOT_DEV
    jitter = jax.random.randint(key, (SHOTS,), 0, TY + 1, dtype=jnp.int32)
    jitter = jitter.at[0].set(0).at[SHOTS - 1].set(TY)
    return ((owner - 1) * TY + jitter).astype(jnp.int32)


def shard_levels(key, extent, split, smallest, high):
    def one(position, parts):
        draws = jax.random.uniform(jax.random.fold_in(jax.random.fold_in(key, 6), position), (parts,), jnp.float32, smallest / len(split), high / len(split))
        return jnp.repeat(jnp.exp(draws), extent[position] // parts).reshape((-1,) + (1,) * (len(extent) - position - 1))

    loudness = one(*split[0])
    for cut in split[1:]:
        loudness = loudness * one(*cut)
    return loudness


def profile(number_of, total, reach, lean):
    weights = [(1 << 20) // math.isqrt(standing ** lean) + 1 for standing in range(2, number_of + 1)]
    rest, holding = total - reach - (number_of - 1), [1] * (number_of - 1)
    while rest > 0:
        candidates = [i for i in range(number_of - 1) if holding[i] < reach]
        mass, remaining = sum([weights[i] for i in candidates]), rest
        for i in candidates:
            addition = min(reach - holding[i], max(1, remaining * weights[i] // mass), rest)
            holding[i] = holding[i] + addition
            rest = rest - addition
    return np.array([reach] + holding)


def ragged_sizes(stream_key, count, total, reach, slope):
    if count == 2:
        one = jax.random.randint(stream_key, (), max(1, total - reach), min(reach, total - 1) + 1)
        return jnp.stack([one, total - one])
    sizes = jnp.asarray(profile(count, total, reach, slope), jnp.int32)
    twos = (count - 1) // 2
    source_of, receiver = sizes[1:1 + 2 * twos:2], sizes[2:2 + 2 * twos:2]
    room = jnp.minimum(source_of - 1, reach - receiver)
    moved = jax.random.randint(jax.random.fold_in(stream_key, 1), (twos,), 0, 1 << 20) % (room + 1)
    sizes = sizes.at[1:1 + 2 * twos:2].set(source_of - moved).at[2:2 + 2 * twos:2].set(receiver + moved)
    return sizes[jax.random.permutation(jax.random.fold_in(stream_key, 2), count)]


def gaussian(own_key, extent, scale, bound, split=(), kind=jnp.bfloat16):
    factor_of = shard_levels(own_key, extent, split, -0.22, 0.18) if split else 1.0
    values = jax.random.normal(own_key, extent, jnp.float32) * scale * factor_of
    return jnp.minimum(jnp.maximum(values, -bound), bound).astype(kind)


def setup_inputs(seed: int = 0) -> dict:
    keys = jax.random.split(jax.random.key(seed), 7)
    return {
        "source": gaussian(keys[0], (SHOTS, 2, AX, AY), 1.0, 6.0, ((0, 8),)),
        "anchors": draw_anchors(jax.random.fold_in(keys[6], 71), 0),
        "counts": ragged_sizes(keys[2], SECTIONS, LEVELS, LVL_MAX, 0).astype(jnp.int32),
        "reflect": jnp.clip(jax.random.uniform(keys[3], (SECTIONS, LVL_MAX, AX, GY), jnp.float32, -0.3984375, 0.3984375) * shard_levels(keys[3], (SECTIONS, LVL_MAX, AX, GY), ((0, 4), (3, 8)), -0.4, 0.0), -0.3984375, 0.3984375).astype(jnp.bfloat16),
        "lateral_x": gaussian(keys[4], (SECTIONS, LVL_MAX, 2, AX, AX), (2 * AX) ** -0.5, 0.375, ((0, 4),)),
        "lateral_y": gaussian(keys[5], (SECTIONS, LVL_MAX, 2, AY, AY), (2 * AY) ** -0.5, 0.25, ((0, 4),)),
    }


def pair_product(einsum_form, first_pair, second_pair):
    real_part = jnp.einsum(einsum_form, first_pair[0], second_pair[0]) - jnp.einsum(einsum_form, first_pair[1], second_pair[1])
    imag_part = jnp.einsum(einsum_form, first_pair[0], second_pair[1]) + jnp.einsum(einsum_form, first_pair[1], second_pair[0])
    return jnp.stack([real_part, imag_part])


def settle(values):
    return lax.optimization_barrier(values.astype(jnp.bfloat16)).astype(jnp.float32)


def one_shot(source_shot, anchor, padded, lateral_x, lateral_y, counts):
    windows = lax.dynamic_slice_in_dim(padded, (anchor + TY).astype(jnp.int32), AY, 3).astype(jnp.float32)
    op_first = lateral_x.astype(jnp.float32)
    op_second = lateral_y.astype(jnp.float32)
    wavefield = source_shot
    stored = []
    for section in range(SECTIONS):
        for level_slot in range(LVL_MAX):
            stored.append(wavefield)
            current = wavefield.astype(jnp.float32)
            scaled = settle((1.0 + windows[section, level_slot]) * current)
            middle = settle(pair_product("ab,by->ay", op_first[section, level_slot], scaled))
            moved = pair_product("xb,ab->xa", middle, op_second[section, level_slot]).astype(jnp.bfloat16)
            wavefield = jnp.where(level_slot < counts[section], moved, wavefield)
    upgoing = jnp.zeros((2, AX, AY), jnp.bfloat16)
    per_level = [None] * (SECTIONS * LVL_MAX)
    for section in reversed(range(SECTIONS)):
        for level_slot in reversed(range(LVL_MAX)):
            flat_index = section * LVL_MAX + level_slot
            downgoing = stored[flat_index].astype(jnp.float32)
            back_wave = settle(pair_product("ba,by->ay", op_first[section, level_slot], upgoing.astype(jnp.float32)))
            spread = pair_product("xb,ba->xa", back_wave, op_second[section, level_slot])
            fresh = (windows[section, level_slot] * downgoing + spread).astype(jnp.bfloat16)
            is_live = level_slot < counts[section]
            upgoing = jnp.where(is_live, fresh, upgoing)
            product_pair = downgoing * upgoing.astype(jnp.float32)
            per_level[flat_index] = jnp.where(is_live, product_pair[0] + product_pair[1], jnp.float32(0.0))
    return jnp.stack(per_level).reshape(SECTIONS, LVL_MAX, AX, AY)


def reference(source, anchors, counts, reflect, lateral_x, lateral_y):
    padded = jnp.pad(reflect, ((0, 0), (0, 0), (0, 0), (TY, TY)))

    def absorb(canvas, inputs):
        source_shot, anchor = inputs
        contribution = one_shot(source_shot, anchor, padded, lateral_x, lateral_y, counts)
        offset = (anchor + TY).astype(jnp.int32)
        placed = lax.dynamic_slice_in_dim(canvas, offset, AY, 3) + contribution
        return lax.dynamic_update_slice_in_dim(canvas, placed, offset, 3), None

    canvas = jnp.zeros((SECTIONS, LVL_MAX, AX, GY + 2 * TY), jnp.float32)
    canvas, unused = lax.scan(absorb, canvas, (source, anchors))
    return canvas[:, :, :, TY:TY + GY]
```

```python
import functools

import jax
import jax.numpy as jnp
from jax import lax
from jax.experimental import pallas as pl
from jax.experimental.pallas import tpu as pltpu
from jax.sharding import PartitionSpec as P

BOTH = ("depth", "tile")
VMEM_BYTES = 48 * 1024 * 1024
TAIL = 16


class Plan:
    def __init__(self, shots):
        self.sections = lax.axis_size("depth")
        self.tiles = lax.axis_size("tile")
        self.shots = shots
        self.group = self.sections // shots
        assert self.sections == 4 and self.group * shots == self.sections
        assert self.tiles % self.group == 0

    def device(self, depth, tile):
        return depth * self.tiles + tile

    def bases(self):
        return range(0, self.tiles, self.group)

    def worker(self, base, w):
        return self.device(w, base + w // self.shots)

    def between_workers(self, r):
        return [
            (self.worker(base, w), self.worker(base, w ^ r))
            for base in self.bases()
            for w in range(self.sections)
        ]

    def to_workers(self, r):
        return [
            (self.device(w ^ r, base + w // self.shots), self.worker(base, w))
            for base in self.bases()
            for w in range(self.sections)
        ]

    def from_workers(self, r):
        return [(b, a) for a, b in self.to_workers(r)]


def window_kernel(shots, sizes, scalars, left_ref, right_ref, *out_refs):
    section, count = scalars[0], scalars[1]
    slots, rows, columns = sizes
    both = jnp.concatenate(
        [left_ref[...].astype(jnp.float32), right_ref[...].astype(jnp.float32)], axis=1
    )
    tail = jnp.full((TAIL, columns), count.astype(jnp.float32), jnp.float32)
    for q, out in enumerate(out_refs):
        offset = scalars[2 + lax.rem(section, shots)] if q == 0 else scalars[2 + (lax.rem(section, shots) ^ q)]
        back = lax.rem(2 * columns - offset, 2 * columns)
        turned = pltpu.roll(both, back, 1)
        out[: slots * rows] = turned[:, :columns].astype(out.dtype)
        out[slots * rows :] = tail.astype(out.dtype)


def sweep_kernel(sections, sizes, scalars, source_ref, *refs):
    slots, rows, columns = sizes
    halves = refs[: 2 * sections]
    windows = refs[2 * sections : 3 * sections]
    outs = refs[3 * sections : 4 * sections]
    ops, win, waves, wave_up, corr, counts, op_sem, win_sem, src_sem, out_sem = refs[4 * sections :]
    here, is_worker, shot = scalars[0], scalars[1], scalars[2]
    part = columns + rows // 2

    def op_copy(r, half):
        return pltpu.make_async_copy(halves[2 * r + half], ops.at[r, half], op_sem.at[r, half])

    def win_copy(r):
        return pltpu.make_async_copy(windows[r], win.at[r], win_sem.at[r])

    def out_copy(r):
        return pltpu.make_async_copy(corr.at[r], outs[r], out_sem.at[r])

    @pl.when(is_worker == 0)
    def _():
        corr[0] = jnp.zeros(corr.shape[1:], corr.dtype)
        out_copy(0).start()
        out_copy(0).wait()

    @pl.when(is_worker != 0)
    def _():
        src_copy = pltpu.make_async_copy(source_ref.at[shot], waves.at[0], src_sem)
        src_copy.start()
        for r in range(sections):
            win_copy(r).start()
        for r in range(sections):
            for half in range(2):
                op_copy(r, half).start()
        corr[...] = jnp.zeros(corr.shape, corr.dtype)
        for r in range(sections):
            win_copy(r).wait()
        for r in range(sections):
            value = jnp.max(win[r, slots * rows :, :].astype(jnp.float32))
            counts[r] = value.astype(jnp.int32)
        src_copy.wait()
        for r in range(sections):
            for half in range(2):
                op_copy(r, half).wait()

        def level(r, slot):
            first = pl.multiple_of(slot * part, part)
            op_y = [ops[r, half, pl.ds(first, columns), :] for half in range(2)]
            tail = pl.multiple_of(slot * part + columns, rows // 2)
            op_x = jnp.concatenate(
                [ops[r, half, pl.ds(tail, rows // 2), :] for half in range(2)], axis=0
            )
            spot = pl.multiple_of(slot * rows, rows)
            window = win[r, pl.ds(spot, rows), :].astype(jnp.float32)
            return window, op_x[:, :rows], op_x[:, rows:], op_y[0], op_y[1], spot

        def complex_sum(left, right):
            return left[:rows] - right[rows:], right[:rows] + left[rows:]

        def dot(a, b, dims):
            return lax.dot_general(a, b, (dims, ((), ())), preferred_element_type=jnp.float32)

        def down_section(section, place):
            r = section ^ here

            def down_level(slot, place):
                window, x_re, x_im, y_re, y_im, _ = level(r, slot)
                wave = waves[place].astype(jnp.float32)
                gain = 1.0 + window
                scaled = jnp.concatenate([gain * wave[:rows], gain * wave[rows:]], axis=0)
                op_first = jnp.concatenate(
                    [
                        jnp.concatenate([x_re, -x_im], axis=1),
                        jnp.concatenate([x_im, x_re], axis=1),
                    ],
                    axis=0,
                )
                middle = dot(op_first, scaled.astype(jnp.bfloat16), ((1,), (0,)))
                middle = middle.astype(jnp.bfloat16)
                moved_re, moved_im = complex_sum(
                    dot(middle, y_re, ((1,), (1,))), dot(middle, y_im, ((1,), (1,)))
                )
                waves[place + 1] = jnp.concatenate([moved_re, moved_im], axis=0).astype(
                    jnp.bfloat16
                )
                return place + 1

            return lax.fori_loop(0, counts[r], down_level, place)

        last = lax.fori_loop(0, sections, down_section, 0)
        wave_up[...] = jnp.zeros(wave_up.shape, wave_up.dtype)

        def up_section(step, place):
            r = (sections - 1 - step) ^ here
            count = counts[r]

            def up_level(inner, place):
                window, x_re, x_im, y_re, y_im, spot = level(r, count - 1 - inner)
                wave = waves[place - 1].astype(jnp.float32)
                op_first = jnp.concatenate(
                    [
                        jnp.concatenate([x_re, x_im], axis=1),
                        jnp.concatenate([-x_im, x_re], axis=1),
                    ],
                    axis=0,
                )
                back = dot(op_first, wave_up[...], ((0,), (0,))).astype(jnp.bfloat16)
                spread_re, spread_im = complex_sum(
                    dot(back, y_re, ((1,), (0,))), dot(back, y_im, ((1,), (0,)))
                )
                up_re = (window * wave[:rows] + spread_re).astype(jnp.bfloat16)
                up_im = (window * wave[rows:] + spread_im).astype(jnp.bfloat16)
                wave_up[:rows] = up_re
                wave_up[rows:] = up_im
                product = wave[:rows] * up_re.astype(jnp.float32)
                product += wave[rows:] * up_im.astype(jnp.float32)
                corr[r, pl.ds(spot, rows), :] = product.astype(corr.dtype)
                return place - 1

            return lax.fori_loop(0, count, up_level, place)

        lax.fori_loop(0, sections, up_section, last)
        for r in range(sections):
            out_copy(r).start()
        for r in range(sections):
            out_copy(r).wait()


def place_kernel(shots, scalars, *refs):
    arrived, (left_out, own_out) = refs[:-2], refs[-2:]
    section = scalars[0]
    columns = left_out.shape[1]
    canvas = None
    for q in range(shots):
        offset = scalars[2 + (lax.rem(section, shots) ^ q)]
        total = None
        for r in range(q, len(arrived), shots):
            value = arrived[r][...].astype(jnp.float32)
            total = value if total is None else total + value
        wide = jnp.concatenate([total, jnp.zeros_like(total)], axis=1)
        turned = pltpu.roll(wide, offset, 1)
        canvas = turned if canvas is None else canvas + turned
    left_out[...] = canvas[:, :columns].astype(left_out.dtype)
    own_out[...] = canvas[:, columns:]


def on_device(source, anchors, counts, reflect, lateral_x, lateral_y):
    shots, _, rows, columns = source.shape
    slots = reflect.shape[1]
    sizes = (slots, rows, columns)
    plan = Plan(shots)
    sections = plan.sections
    section = lax.axis_index("depth").astype(jnp.int32)
    tile = lax.axis_index("tile").astype(jnp.int32)
    bf16 = jnp.bfloat16
    smem = pl.BlockSpec(memory_space=pltpu.SMEM)
    vmem = pl.BlockSpec(memory_space=pltpu.VMEM)
    anywhere = pl.BlockSpec(memory_space=pl.ANY)
    params = pltpu.CompilerParams(vmem_limit_bytes=VMEM_BYTES)

    beside = jnp.concatenate([lateral_x[0, :, 0], lateral_x[0, :, 1]], axis=2)
    halves = [
        jnp.concatenate(
            [lateral_y[0, :, half], beside[:, half * (rows // 2) : (half + 1) * (rows // 2)]], axis=1
        ).reshape(slots * (columns + rows // 2), columns)
        for half in range(2)
    ]
    near, far = 1, 2
    near_pairs, far_pairs = plan.between_workers(near), plan.between_workers(far)

    halo = lax.ppermute(
        reflect[0].reshape(slots * rows, columns),
        "tile",
        [(i, i + 1) for i in range(plan.tiles - 1)],
    )
    near_0 = lax.ppermute(halves[0], BOTH, near_pairs)
    far_1 = lax.ppermute(halves[1], BOTH, far_pairs)
    near_1 = lax.ppermute(halves[1], BOTH, near_pairs)
    far_0 = lax.ppermute(halves[0], BOTH, far_pairs)
    cross_0 = lax.ppermute(near_0, BOTH, far_pairs)
    cross_1 = lax.ppermute(far_1, BOTH, near_pairs)

    offsets = anchors - (tile - 1) * columns
    scalars = jnp.concatenate([section[None], counts, offsets])
    message = jax.ShapeDtypeStruct((slots * rows + TAIL, columns), bf16)
    parts = pl.pallas_call(
        functools.partial(window_kernel, shots, sizes),
        out_shape=[message] * shots,
        in_specs=[smem, vmem, vmem],
        out_specs=[vmem] * shots,
        compiler_params=params,
        name="windows",
    )(scalars, halo, reflect[0].reshape(slots * rows, columns))
    windows = [parts[0]] + [
        lax.ppermute(parts[r % shots], BOTH, plan.to_workers(r)) for r in range(1, sections)
    ]

    is_worker = (section // shots == lax.rem(tile, plan.group)).astype(jnp.int32)
    roles = jnp.stack([section, is_worker, lax.rem(section, shots)])
    corr_shape = jax.ShapeDtypeStruct((slots * rows, columns), bf16)
    part = slots * (columns + rows // 2)
    correlations = pl.pallas_call(
        functools.partial(sweep_kernel, sections, sizes),
        out_shape=[corr_shape] * sections,
        in_specs=[smem] + [anywhere] * (1 + 3 * sections),
        out_specs=[anywhere] * sections,
        scratch_shapes=[
            pltpu.VMEM((sections, 2, part, columns), bf16),
            pltpu.VMEM((sections, slots * rows + TAIL, columns), bf16),
            pltpu.VMEM((sections * slots + 1, 2 * rows, columns), bf16),
            pltpu.VMEM((2 * rows, columns), bf16),
            pltpu.VMEM((sections, slots * rows, columns), bf16),
            pltpu.SMEM((sections,), jnp.int32),
            pltpu.SemaphoreType.DMA((sections, 2)),
            pltpu.SemaphoreType.DMA((sections,)),
            pltpu.SemaphoreType.DMA,
            pltpu.SemaphoreType.DMA((sections,)),
        ],
        compiler_params=params,
        name="sweep",
    )(
        roles,
        source.reshape(shots, 2 * rows, columns),
        halves[0], halves[1], near_0, near_1, far_0, far_1, cross_0, cross_1,
        *windows,
    )

    arrived = [correlations[0]] + [
        lax.ppermute(correlations[r], BOTH, plan.from_workers(r)) for r in range(1, sections)
    ]
    left, own = pl.pallas_call(
        functools.partial(place_kernel, shots),
        out_shape=[corr_shape, jax.ShapeDtypeStruct((slots * rows, columns), jnp.float32)],
        in_specs=[smem] + [vmem] * sections,
        out_specs=[vmem, vmem],
        compiler_params=params,
        name="place",
    )(scalars, *arrived)
    from_right = lax.ppermute(left, "tile", [(i + 1, i) for i in range(plan.tiles - 1)])
    image = own + from_right.astype(jnp.float32)
    return image.reshape(1, slots, rows, columns)


def solution(mesh):
    return jax.shard_map(
        on_device,
        mesh=mesh,
        in_specs=(
            P("tile", None, None, None),
            P("tile"),
            P("depth"),
            P("depth", None, None, "tile"),
            P("depth", None, None, None, None),
            P("depth", None, None, None, None),
        ),
        out_specs=P("depth", None, None, "tile"),
        check_vma=False,
    )
```

```python
import functools

import jax
import jax.numpy as jnp
from jax import lax
from jax.experimental import pallas as pl
from jax.experimental.pallas import tpu as pltpu
from jax.sharding import PartitionSpec as P

BOTH = ("depth", "tile")
MIB = 1024 * 1024
TAIL = 16


class Plan:
    def __init__(self, shots):
        self.sections = lax.axis_size("depth")
        self.tiles = lax.axis_size("tile")
        self.shots = shots
        self.group = self.sections // shots
        assert self.sections == 4 and self.group * shots == self.sections
        assert self.tiles % self.group == 0

    def device(self, depth, tile):
        return depth * self.tiles + tile

    def bases(self):
        return range(0, self.tiles, self.group)

    def worker(self, base, w):
        return self.device(w, base + w // self.shots)

    def beside_workers(self, by):
        return [
            (self.device(w, base + (w // self.shots + by) % self.group), self.worker(base, w))
            for base in self.bases()
            for w in range(self.sections)
        ]

    def to_workers(self, r):
        return [
            (self.device(w ^ r, base + w // self.shots), self.worker(base, w))
            for base in self.bases()
            for w in range(self.sections)
        ]

    def from_workers(self, r):
        return [(b, a) for a, b in self.to_workers(r)]


def pack_kernel(sizes, group, scalars, x_ref, y_ref, out_ref, sem):
    slots, rows, columns = sizes
    share = scalars[0]
    part, piece = columns + rows // group, rows // group
    copies = []
    for slot in range(slots):
        copies.append((y_ref.at[slot, share], out_ref.at[pl.ds(slot * part, columns), :]))
        for i in range(2):
            spot = pl.multiple_of(share * piece, piece)
            copies.append(
                (
                    x_ref.at[slot, i, pl.ds(spot, piece), :],
                    out_ref.at[pl.ds(slot * part + columns, piece), pl.ds(i * rows, rows)],
                )
            )
    copies = [pltpu.make_async_copy(a, b, sem.at[n]) for n, (a, b) in enumerate(copies)]
    for copy in copies:
        copy.start()
    for copy in copies:
        copy.wait()


def window_kernel(shots, sizes, scalars, left_ref, right_ref, *out_refs):
    section, count = scalars[0], scalars[1]
    slots, rows, columns = sizes
    both = jnp.concatenate(
        [left_ref[...].astype(jnp.float32), right_ref[...].astype(jnp.float32)], axis=1
    )
    tail = jnp.full((TAIL, columns), count.astype(jnp.float32), jnp.float32)
    for q, out in enumerate(out_refs):
        offset = scalars[2 + lax.rem(section, shots)] if q == 0 else scalars[2 + (lax.rem(section, shots) ^ q)]
        back = lax.rem(2 * columns - offset, 2 * columns)
        turned = pltpu.roll(both, back, 1)
        out[: slots * rows] = turned[:, :columns].astype(out.dtype)
        out[slots * rows :] = tail.astype(out.dtype)


def sweep_kernel(sections, sizes, group, scalars, source_ref, *refs):
    slots, rows, columns = sizes
    shares, refs = refs[:group], refs[group:]
    windows, refs = refs[:sections], refs[sections:]
    outs, refs = refs[:sections], refs[sections:]
    ops, win, waves, wave_up, corr, counts, op_sem, win_sem, src_sem, out_sem = refs
    here, is_worker, shot, mine = scalars[0], scalars[1], scalars[2], scalars[3]
    piece = rows // group
    part = columns + piece

    def op_copy(section, by):
        share = lax.rem(mine + by, group)
        return pltpu.make_async_copy(
            shares[by].at[section], ops.at[section, share], op_sem.at[section, by]
        )

    def win_copy(r):
        return pltpu.make_async_copy(windows[r], win.at[r], win_sem.at[r])

    def out_copy(r):
        return pltpu.make_async_copy(corr.at[r], outs[r], out_sem.at[r])

    @pl.when(is_worker == 0)
    def _():
        corr[0] = jnp.zeros(corr.shape[1:], corr.dtype)
        out_copy(0).start()
        out_copy(0).wait()

    @pl.when(is_worker != 0)
    def _():
        src_copy = pltpu.make_async_copy(source_ref.at[shot], waves.at[0], src_sem)
        src_copy.start()
        for r in range(sections):
            win_copy(r).start()
        for section in range(sections):
            for by in range(group):
                op_copy(section, by).start()
        corr[...] = jnp.zeros(corr.shape, corr.dtype)
        for r in range(sections):
            win_copy(r).wait()
        for r in range(sections):
            value = jnp.max(win[r, slots * rows :, :].astype(jnp.float32))
            counts[r] = value.astype(jnp.int32)
        src_copy.wait()

        def level(section, r, slot):
            first = pl.multiple_of(slot * part, part)
            op_y = [ops[section, share, pl.ds(first, columns), :] for share in range(2)]
            tail = pl.multiple_of(slot * part + columns, piece)
            op_x = jnp.concatenate(
                [ops[section, share, pl.ds(tail, piece), :] for share in range(group)], axis=0
            )
            spot = pl.multiple_of(slot * rows, rows)
            window = win[r, pl.ds(spot, rows), :].astype(jnp.float32)
            return window, op_x[:, :rows], op_x[:, rows:], op_y[0], op_y[1], spot

        def complex_sum(left, right):
            return left[:rows] - right[rows:], right[:rows] + left[rows:]

        def dot(a, b, dims):
            return lax.dot_general(a, b, (dims, ((), ())), preferred_element_type=jnp.float32)

        def down_section(section, place):
            r = section ^ here
            for by in range(group):
                op_copy(section, by).wait()

            def down_level(slot, place):
                window, x_re, x_im, y_re, y_im, _ = level(section, r, slot)
                wave = waves[place].astype(jnp.float32)
                gain = 1.0 + window
                scaled = jnp.concatenate([gain * wave[:rows], gain * wave[rows:]], axis=0)
                op_first = jnp.concatenate(
                    [
                        jnp.concatenate([x_re, -x_im], axis=1),
                        jnp.concatenate([x_im, x_re], axis=1),
                    ],
                    axis=0,
                )
                middle = dot(op_first, scaled.astype(jnp.bfloat16), ((1,), (0,)))
                middle = middle.astype(jnp.bfloat16)
                moved_re, moved_im = complex_sum(
                    dot(middle, y_re, ((1,), (1,))), dot(middle, y_im, ((1,), (1,)))
                )
                waves[place + 1] = jnp.concatenate([moved_re, moved_im], axis=0).astype(
                    jnp.bfloat16
                )
                return place + 1

            return lax.fori_loop(0, counts[r], down_level, place)

        last = lax.fori_loop(0, sections, down_section, 0)
        wave_up[...] = jnp.zeros(wave_up.shape, wave_up.dtype)

        def up_section(step, place):
            section = sections - 1 - step
            r = section ^ here
            count = counts[r]

            def up_level(inner, place):
                window, x_re, x_im, y_re, y_im, spot = level(section, r, count - 1 - inner)
                wave = waves[place - 1].astype(jnp.float32)
                op_first = jnp.concatenate(
                    [
                        jnp.concatenate([x_re, x_im], axis=1),
                        jnp.concatenate([-x_im, x_re], axis=1),
                    ],
                    axis=0,
                )
                back = dot(op_first, wave_up[...], ((0,), (0,))).astype(jnp.bfloat16)
                spread_re, spread_im = complex_sum(
                    dot(back, y_re, ((1,), (0,))), dot(back, y_im, ((1,), (0,)))
                )
                up_re = (window * wave[:rows] + spread_re).astype(jnp.bfloat16)
                up_im = (window * wave[rows:] + spread_im).astype(jnp.bfloat16)
                wave_up[:rows] = up_re
                wave_up[rows:] = up_im
                product = wave[:rows] * up_re.astype(jnp.float32)
                product += wave[rows:] * up_im.astype(jnp.float32)
                corr[r, pl.ds(spot, rows), :] = product.astype(corr.dtype)
                return place - 1

            return lax.fori_loop(0, count, up_level, place)

        lax.fori_loop(0, sections, up_section, last)
        for r in range(sections):
            out_copy(r).start()
        for r in range(sections):
            out_copy(r).wait()


def place_kernel(shots, scalars, *refs):
    arrived, (left_out, own_out) = refs[:-2], refs[-2:]
    section = scalars[0]
    columns = left_out.shape[1]
    canvas = None
    for q in range(shots):
        offset = scalars[2 + (lax.rem(section, shots) ^ q)]
        total = None
        for r in range(q, len(arrived), shots):
            value = arrived[r][...].astype(jnp.float32)
            total = value if total is None else total + value
        wide = jnp.concatenate([total, jnp.zeros_like(total)], axis=1)
        turned = pltpu.roll(wide, offset, 1)
        canvas = turned if canvas is None else canvas + turned
    left_out[...] = canvas[:, :columns].astype(left_out.dtype)
    own_out[...] = canvas[:, columns:]


def on_device(source, anchors, counts, reflect, lateral_x, lateral_y):
    shots, _, rows, columns = source.shape
    slots = reflect.shape[1]
    sizes = (slots, rows, columns)
    plan = Plan(shots)
    sections = plan.sections
    section = lax.axis_index("depth").astype(jnp.int32)
    tile = lax.axis_index("tile").astype(jnp.int32)
    bf16 = jnp.bfloat16
    smem = pl.BlockSpec(memory_space=pltpu.SMEM)
    vmem = pl.BlockSpec(memory_space=pltpu.VMEM)
    anywhere = pl.BlockSpec(memory_space=pl.ANY)

    def params(mib):
        return pltpu.CompilerParams(vmem_limit_bytes=mib * MIB)

    group = plan.group
    assert group == 2
    mine = lax.rem(tile, group)
    part = slots * (columns + rows // group)
    share = pl.pallas_call(
        functools.partial(pack_kernel, sizes, group),
        out_shape=jax.ShapeDtypeStruct((part, columns), bf16),
        in_specs=[smem, anywhere, anywhere],
        out_specs=anywhere,
        scratch_shapes=[pltpu.SemaphoreType.DMA((3 * slots,))],
        name="pack",
    )(mine[None], lateral_x[0], lateral_y[0])
    gathered = lax.all_gather(share, "depth")
    shares = [gathered] + [
        lax.ppermute(gathered, BOTH, plan.beside_workers(by)) for by in range(1, group)
    ]

    halo = lax.ppermute(
        reflect[0].reshape(slots * rows, columns),
        "tile",
        [(i, i + 1) for i in range(plan.tiles - 1)],
    )

    offsets = anchors - (tile - 1) * columns
    scalars = jnp.concatenate([section[None], counts, offsets])
    message = jax.ShapeDtypeStruct((slots * rows + TAIL, columns), bf16)
    parts = pl.pallas_call(
        functools.partial(window_kernel, shots, sizes),
        out_shape=[message] * shots,
        in_specs=[smem, vmem, vmem],
        out_specs=[vmem] * shots,
        compiler_params=params(8),
        name="windows",
    )(scalars, halo, reflect[0].reshape(slots * rows, columns))
    windows = [parts[0]] + [
        lax.ppermute(parts[r % shots], BOTH, plan.to_workers(r)) for r in range(1, sections)
    ]

    is_worker = (section // shots == lax.rem(tile, plan.group)).astype(jnp.int32)
    roles = jnp.stack([section, is_worker, lax.rem(section, shots), mine])
    corr_shape = jax.ShapeDtypeStruct((slots * rows, columns), bf16)
    correlations = pl.pallas_call(
        functools.partial(sweep_kernel, sections, sizes, group),
        out_shape=[corr_shape] * sections,
        in_specs=[smem] + [anywhere] * (1 + group + sections),
        out_specs=[anywhere] * sections,
        scratch_shapes=[
            pltpu.VMEM((sections, group, part, columns), bf16),
            pltpu.VMEM((sections, slots * rows + TAIL, columns), bf16),
            pltpu.VMEM((sections * slots + 1, 2 * rows, columns), bf16),
            pltpu.VMEM((2 * rows, columns), bf16),
            pltpu.VMEM((sections, slots * rows, columns), bf16),
            pltpu.SMEM((sections,), jnp.int32),
            pltpu.SemaphoreType.DMA((sections, group)),
            pltpu.SemaphoreType.DMA((sections,)),
            pltpu.SemaphoreType.DMA,
            pltpu.SemaphoreType.DMA((sections,)),
        ],
        compiler_params=params(14),
        name="sweep",
    )(
        roles,
        source.reshape(shots, 2 * rows, columns),
        *shares,
        *windows,
    )

    arrived = [correlations[0]] + [
        lax.ppermute(correlations[r], BOTH, plan.from_workers(r)) for r in range(1, sections)
    ]
    left, own = pl.pallas_call(
        functools.partial(place_kernel, shots),
        out_shape=[corr_shape, jax.ShapeDtypeStruct((slots * rows, columns), jnp.float32)],
        in_specs=[smem] + [vmem] * sections,
        out_specs=[vmem, vmem],
        compiler_params=params(8),
        name="place",
    )(scalars, *arrived)
    from_right = lax.ppermute(left, "tile", [(i + 1, i) for i in range(plan.tiles - 1)])
    image = own + from_right.astype(jnp.float32)
    return image.reshape(1, slots, rows, columns)


def solution(mesh):
    return jax.shard_map(
        on_device,
        mesh=mesh,
        in_specs=(
            P("tile", None, None, None),
            P("tile"),
            P("depth"),
            P("depth", None, None, "tile"),
            P("depth", None, None, None, None),
            P("depth", None, None, None, None),
        ),
        out_specs=P("depth", None, None, "tile"),
        check_vma=False,
    )
```

```python
import functools

import jax
import jax.numpy as jnp
from jax import lax
from jax.experimental import pallas as pl
from jax.experimental.pallas import tpu as pltpu
from jax.sharding import PartitionSpec as P

BOTH = ("depth", "tile")
MIB = 1024 * 1024
TAIL = 16


class Plan:
    def __init__(self, shots):
        self.sections = lax.axis_size("depth")
        self.tiles = lax.axis_size("tile")
        self.shots = shots
        self.group = self.sections // shots
        assert self.sections == 4 and self.group * shots == self.sections
        assert self.tiles % (2 * self.group) == 0

    def device(self, depth, tile):
        return depth * self.tiles + tile

    def bases(self):
        return range(0, self.tiles, self.group)

    def worker(self, base, w):
        return self.device(w, base + w // self.shots)

    def other(self, w, base):
        return self.device(w, base + (w // self.shots + 1) % self.group)

    def ops_to_workers(self, r):
        return [
            (self.other(w ^ r, base), self.worker(base, w))
            for base in self.bases()
            for w in range(self.sections)
        ]

    def swap_workers(self):
        return [
            (self.worker(base, w), self.worker((base // self.group ^ 1) * self.group, w))
            for base in self.bases()
            for w in range(self.sections)
        ]

    def to_workers(self, r):
        return [
            (self.device(w ^ r, base + w // self.shots), self.worker(base, w))
            for base in self.bases()
            for w in range(self.sections)
        ]

    def from_workers(self, r):
        return [(b, a) for a, b in self.to_workers(r)]


def pack_kernel(sizes, scalars, x_ref, y_ref, whole_ref, half_ref):
    slots, rows, columns = sizes
    piece = rows // 2
    part = columns + piece
    for half in range(2):
        for slot in range(slots):
            whole_ref[half, slot * part : slot * part + columns, :] = y_ref[slot, half]
            whole_ref[half, slot * part + columns : (slot + 1) * part, :] = jnp.concatenate(
                [x_ref[slot, i, half * piece : (half + 1) * piece, :] for i in range(2)], axis=1
            )
    half_ref[...] = whole_ref[scalars[0]]


def window_kernel(shots, sizes, scalars, left_ref, right_ref, *out_refs):
    section, count = scalars[0], scalars[1]
    slots, rows, columns = sizes
    both = jnp.concatenate(
        [left_ref[...].astype(jnp.float32), right_ref[...].astype(jnp.float32)], axis=1
    )
    tail = jnp.full((TAIL, columns), count.astype(jnp.float32), jnp.float32)
    for q, out in enumerate(out_refs):
        offset = scalars[2 + lax.rem(section, shots)] if q == 0 else scalars[2 + (lax.rem(section, shots) ^ q)]
        back = lax.rem(2 * columns - offset, 2 * columns)
        turned = pltpu.roll(both, back, 1)
        out[: slots * rows] = turned[:, :columns].astype(out.dtype)
        out[slots * rows :] = tail.astype(out.dtype)


def sweep_kernel(sections, sizes, scalars, source_ref, *refs):
    slots, rows, columns = sizes
    wholes, halves, refs = refs[: sections - 1], refs[sections - 1 : sections + 1], refs[sections + 1 :]
    windows, refs = refs[:sections], refs[sections:]
    outs, refs = refs[:sections], refs[sections:]
    ops, win, waves, turned_x, wave_up, corr, counts, op_sem, win_sem, src_sem, out_sem = refs
    here, is_worker, shot, plane = scalars[0], scalars[1], scalars[2], scalars[3]
    piece = rows // 2
    part = columns + piece

    def op_copy(r, half):
        if r < sections - 1:
            return pltpu.make_async_copy(wholes[r].at[half], ops.at[r, half], op_sem.at[r, half])
        place = plane if half == 0 else 1 - plane
        return pltpu.make_async_copy(halves[half], ops.at[r, place], op_sem.at[r, half])

    def op_wait(r):
        for half in range(2):
            pltpu.make_async_copy(halves[half], ops.at[r, half], op_sem.at[r, half]).wait()

    def win_copy(r):
        return pltpu.make_async_copy(windows[r], win.at[r], win_sem.at[r])

    def out_copy(r):
        return pltpu.make_async_copy(corr.at[r], outs[r], out_sem.at[r])

    @pl.when(is_worker == 0)
    def _():
        corr[0] = jnp.zeros(corr.shape[1:], corr.dtype)
        out_copy(0).start()
        out_copy(0).wait()

    @pl.when(is_worker != 0)
    def _():
        src_copy = pltpu.make_async_copy(source_ref.at[shot], waves.at[0], src_sem)
        src_copy.start()
        for r in range(sections):
            win_copy(r).start()
        for r in range(sections):
            for half in range(2):
                op_copy(r, half).start()
        corr[...] = jnp.zeros(corr.shape, corr.dtype)
        for r in range(sections):
            win_copy(r).wait()
        for r in range(sections):
            value = jnp.max(win[r, slots * rows :, :].astype(jnp.float32))
            counts[r] = value.astype(jnp.int32)
        src_copy.wait()

        def level(r, slot):
            first = pl.multiple_of(slot * part, part)
            op_y = [ops[r, half, pl.ds(first, columns), :] for half in range(2)]
            spot = pl.multiple_of(slot * rows, rows)
            window = win[r, pl.ds(spot, rows), :].astype(jnp.float32)
            return window, op_y[0], op_y[1], spot

        def level_x(r, slot):
            tail = pl.multiple_of(slot * part + columns, piece)
            op_x = jnp.concatenate(
                [ops[r, half, pl.ds(tail, piece), :] for half in range(2)], axis=0
            )
            return op_x[:, :rows], op_x[:, rows:]

        def blocks(re, im):
            upper = jnp.concatenate([re, -im], axis=1)
            return jnp.concatenate([upper, jnp.concatenate([im, re], axis=1)], axis=0)

        def complex_sum(left, right):
            return left[:rows] - right[rows:], right[:rows] + left[rows:]

        def dot(a, b, dims):
            return lax.dot_general(a, b, (dims, ((), ())), preferred_element_type=jnp.float32)

        def down_section(section, place):
            r = section ^ here
            op_wait(r)

            def down_level(slot, place):
                window, y_re, y_im, _ = level(r, slot)
                x_re, x_im = level_x(r, slot)
                wave = waves[place].astype(jnp.float32)
                gain = 1.0 + window
                scaled = jnp.concatenate([gain * wave[:rows], gain * wave[rows:]], axis=0)
                op_first = blocks(x_re, x_im)
                turned_x[place] = blocks(x_re.T, x_im.T)
                middle = dot(op_first, scaled.astype(jnp.bfloat16), ((1,), (0,)))
                middle = middle.astype(jnp.bfloat16)
                moved_re, moved_im = complex_sum(
                    dot(middle, y_re, ((1,), (1,))), dot(middle, y_im, ((1,), (1,)))
                )
                waves[place + 1] = jnp.concatenate([moved_re, moved_im], axis=0).astype(
                    jnp.bfloat16
                )
                return place + 1

            return lax.fori_loop(0, counts[r], down_level, place)

        last = lax.fori_loop(0, sections, down_section, 0)
        wave_up[...] = jnp.zeros(wave_up.shape, wave_up.dtype)

        def up_section(step, place):
            r = (sections - 1 - step) ^ here
            count = counts[r]

            def up_level(inner, place):
                window, y_re, y_im, spot = level(r, count - 1 - inner)
                wave = waves[place - 1].astype(jnp.float32)
                back = dot(turned_x[place - 1], wave_up[...], ((1,), (0,))).astype(jnp.bfloat16)
                spread_re, spread_im = complex_sum(
                    dot(back, y_re, ((1,), (0,))), dot(back, y_im, ((1,), (0,)))
                )
                up_re = (window * wave[:rows] + spread_re).astype(jnp.bfloat16)
                up_im = (window * wave[rows:] + spread_im).astype(jnp.bfloat16)
                wave_up[:rows] = up_re
                wave_up[rows:] = up_im
                product = wave[:rows] * up_re.astype(jnp.float32)
                product += wave[rows:] * up_im.astype(jnp.float32)
                corr[r, pl.ds(spot, rows), :] = product.astype(corr.dtype)
                return place - 1

            return lax.fori_loop(0, count, up_level, place)

        lax.fori_loop(0, sections, up_section, last)
        for r in range(sections):
            out_copy(r).start()
        for r in range(sections):
            out_copy(r).wait()


def place_kernel(shots, scalars, *refs):
    arrived, (left_out, own_out) = refs[:-2], refs[-2:]
    section = scalars[0]
    columns = left_out.shape[1]
    canvas = None
    for q in range(shots):
        offset = scalars[2 + (lax.rem(section, shots) ^ q)]
        total = None
        for r in range(q, len(arrived), shots):
            value = arrived[r][...].astype(jnp.float32)
            total = value if total is None else total + value
        wide = jnp.concatenate([total, jnp.zeros_like(total)], axis=1)
        turned = pltpu.roll(wide, offset, 1)
        canvas = turned if canvas is None else canvas + turned
    left_out[...] = canvas[:, :columns].astype(left_out.dtype)
    own_out[...] = canvas[:, columns:]


def on_device(source, anchors, counts, reflect, lateral_x, lateral_y):
    shots, _, rows, columns = source.shape
    slots = reflect.shape[1]
    sizes = (slots, rows, columns)
    plan = Plan(shots)
    sections = plan.sections
    section = lax.axis_index("depth").astype(jnp.int32)
    tile = lax.axis_index("tile").astype(jnp.int32)
    bf16 = jnp.bfloat16
    smem = pl.BlockSpec(memory_space=pltpu.SMEM)
    vmem = pl.BlockSpec(memory_space=pltpu.VMEM)
    hbm = pl.BlockSpec(memory_space=pltpu.HBM)
    anywhere = pl.BlockSpec(memory_space=pl.ANY)

    def params(mib):
        return pltpu.CompilerParams(vmem_limit_bytes=mib * MIB)

    plane = lax.rem(tile // plan.group, 2)
    half_shape = (slots * (columns + rows // 2), columns)
    whole, half = pl.pallas_call(
        functools.partial(pack_kernel, sizes),
        out_shape=[
            jax.ShapeDtypeStruct((2,) + half_shape, bf16),
            jax.ShapeDtypeStruct(half_shape, bf16),
        ],
        in_specs=[smem, vmem, vmem],
        out_specs=[vmem, vmem],
        compiler_params=params(6),
        name="pack",
    )(plane[None], lateral_x[0], lateral_y[0])
    far_half = lax.ppermute(half, BOTH, plan.ops_to_workers(sections - 1))
    wholes = [whole] + [
        lax.ppermute(whole, BOTH, plan.ops_to_workers(r)) for r in range(1, sections - 1)
    ]

    halo = lax.ppermute(
        reflect[0].reshape(slots * rows, columns),
        "tile",
        [(i, i + 1) for i in range(plan.tiles - 1)],
    )

    offsets = anchors - (tile - 1) * columns
    scalars = jnp.concatenate([section[None], counts, offsets])
    message = jax.ShapeDtypeStruct((slots * rows + TAIL, columns), bf16)
    parts = pl.pallas_call(
        functools.partial(window_kernel, shots, sizes),
        out_shape=[message] * shots,
        in_specs=[smem, vmem, vmem],
        out_specs=[vmem] * shots,
        compiler_params=params(8),
        name="windows",
    )(scalars, halo, reflect[0].reshape(slots * rows, columns))
    other_half = lax.ppermute(far_half, BOTH, plan.swap_workers())
    windows = [parts[0]] + [
        lax.ppermute(parts[r % shots], BOTH, plan.to_workers(r)) for r in range(1, sections)
    ]

    is_worker = (section // shots == lax.rem(tile, plan.group)).astype(jnp.int32)
    roles = jnp.stack([section, is_worker, lax.rem(section, shots), plane])
    corr_shape = jax.ShapeDtypeStruct((slots * rows, columns), bf16)
    correlations = pl.pallas_call(
        functools.partial(sweep_kernel, sections, sizes),
        out_shape=[corr_shape] * sections,
        in_specs=[smem] + [hbm] + [anywhere] * (sections + 1 + sections),
        out_specs=[anywhere] * sections,
        scratch_shapes=[
            pltpu.VMEM((sections, 2) + half_shape, bf16),
            pltpu.VMEM((sections, slots * rows + TAIL, columns), bf16),
            pltpu.VMEM((sections * slots + 1, 2 * rows, columns), bf16),
            pltpu.VMEM((sections * slots, 2 * rows, 2 * rows), bf16),
            pltpu.VMEM((2 * rows, columns), bf16),
            pltpu.VMEM((sections, slots * rows, columns), bf16),
            pltpu.SMEM((sections,), jnp.int32),
            pltpu.SemaphoreType.DMA((sections, 2)),
            pltpu.SemaphoreType.DMA((sections,)),
            pltpu.SemaphoreType.DMA,
            pltpu.SemaphoreType.DMA((sections,)),
        ],
        compiler_params=params(14),
        name="sweep",
    )(
        roles,
        source.reshape(shots, 2 * rows, columns),
        *wholes, far_half, other_half,
        *windows,
    )

    arrived = [correlations[0]] + [
        lax.ppermute(correlations[r], BOTH, plan.from_workers(r)) for r in range(1, sections)
    ]
    left, own = pl.pallas_call(
        functools.partial(place_kernel, shots),
        out_shape=[corr_shape, jax.ShapeDtypeStruct((slots * rows, columns), jnp.float32)],
        in_specs=[smem] + [vmem] * sections,
        out_specs=[vmem, vmem],
        compiler_params=params(8),
        name="place",
    )(scalars, *arrived)
    from_right = lax.ppermute(left, "tile", [(i + 1, i) for i in range(plan.tiles - 1)])
    image = own + from_right.astype(jnp.float32)
    return image.reshape(1, slots, rows, columns)


def solution(mesh):
    return jax.shard_map(
        on_device,
        mesh=mesh,
        in_specs=(
            P("tile", None, None, None),
            P("tile"),
            P("depth"),
            P("depth", None, None, "tile"),
            P("depth", None, None, None, None),
            P("depth", None, None, None, None),
        ),
        out_specs=P("depth", None, None, "tile"),
        check_vma=False,
    )
```

```python
import functools

import jax
import jax.numpy as jnp
from jax import lax
from jax.experimental import pallas as pl
from jax.experimental.pallas import tpu as pltpu
from jax.sharding import PartitionSpec as P

BOTH = ("depth", "tile")
MIB = 1024 * 1024
TAIL = 16


class Plan:
    def __init__(self, shots):
        self.sections = lax.axis_size("depth")
        self.tiles = lax.axis_size("tile")
        self.shots = shots
        self.group = self.sections // shots
        assert self.sections == 4 and self.group * shots == self.sections
        assert self.tiles % (2 * self.group) == 0

    def device(self, depth, tile):
        return depth * self.tiles + tile

    def bases(self):
        return range(0, self.tiles, self.group)

    def worker(self, base, w):
        return self.device(w, base + w // self.shots)

    def swap_workers(self):
        return [
            (self.worker(base, w), self.worker((base // self.group ^ 1) * self.group, w))
            for base in self.bases()
            for w in range(self.sections)
        ]

    def to_workers(self, r):
        return [
            (self.device(w ^ r, base + w // self.shots), self.worker(base, w))
            for base in self.bases()
            for w in range(self.sections)
        ]

    def from_workers(self, r):
        return [(b, a) for a, b in self.to_workers(r)]


def pack_kernel(group, sizes, x_hbm, y_hbm, *refs):
    slots, rows, columns = sizes
    outs, (x_ref, y_ref, sem) = refs[:-3], refs[-3:]
    loads = [
        pltpu.make_async_copy(x_hbm, x_ref, sem.at[0]),
        pltpu.make_async_copy(y_hbm, y_ref, sem.at[1]),
    ]
    for load in loads:
        load.start()
    for load in loads:
        load.wait()
    piece = rows // 2
    part = columns + piece
    half_rows = slots * part
    for half in range(2):
        for slot in range(slots):
            spot = half * half_rows + slot * part
            op_x = jnp.concatenate(
                [x_ref[slot, i, half * piece : (half + 1) * piece, :] for i in range(2)], axis=1
            )
            for out in outs[:-1]:
                out[spot : spot + columns, :] = y_ref[slot, half]
                out[spot + columns : spot + part, :] = op_x
    plane = lax.rem(lax.axis_index("tile") // group, 2)
    first = pl.multiple_of(plane * half_rows, half_rows)
    outs[-1][:half_rows] = outs[0][pl.ds(first, half_rows), :]


def window_kernel(shots, sizes, anchors_hbm, counts, left_ref, right_hbm, *refs):
    slots, rows, columns = sizes
    messages, refs = refs[shots : 2 * shots], refs[2 * shots :]
    alone, anchors, right_ref, held, sem = refs
    loads = [
        pltpu.make_async_copy(anchors_hbm, anchors, sem.at[shots]),
        pltpu.make_async_copy(right_hbm, right_ref, sem.at[shots + 1]),
    ]
    for load in loads:
        load.start()
    for load in loads:
        load.wait()
    section, tile = lax.axis_index("depth"), lax.axis_index("tile")
    both = jnp.concatenate(
        [left_ref[...].astype(jnp.float32), right_ref[...].astype(jnp.float32)], axis=1
    )
    tail = jnp.full((TAIL, columns), counts[0].astype(jnp.float32), jnp.float32)
    copies = []
    for q, message in enumerate(messages):
        offset = anchors[lax.rem(section, shots) ^ q] - (tile - 1) * columns
        back = lax.rem(2 * columns - offset, 2 * columns)
        held[q, : slots * rows] = pltpu.roll(both, back, 1)[:, :columns].astype(held.dtype)
        held[q, slots * rows :] = tail.astype(held.dtype)
        ahead = message.shape[0] - held.shape[1]
        place = message.at[pl.ds(ahead, held.shape[1]), :]
        copies.append(pltpu.make_async_copy(held.at[q], place, sem.at[q]))
        copies[-1].start()
    alone[...] = held[shots - 1]
    for copy in copies:
        copy.wait()


def sweep_kernel(sections, shots, group, sizes, source_ref, *refs):
    slots, rows, columns = sizes
    messages, refs = refs[: sections + 2], refs[sections + 2 :]
    outs, refs = refs[:sections], refs[sections:]
    ops, win, waves, turned_x, wave_up, corr, counts, op_sem, win_sem, src_sem, out_sem = refs
    here, tile = lax.axis_index("depth"), lax.axis_index("tile")
    shot = lax.rem(here, shots)
    is_worker = (here // shots == lax.rem(tile, group)).astype(jnp.int32)
    plane = lax.rem(tile // group, 2)
    piece = rows // 2
    part = columns + piece
    half_rows = slots * part
    win_rows = slots * rows + TAIL

    def op_copy(r, half):
        if r < sections - 1:
            place, message, first = half, messages[r], half * half_rows
        else:
            place, message, first = (plane, 1 - plane)[half], messages[r + half], 0
        source = message.at[pl.ds(first, half_rows), :]
        return pltpu.make_async_copy(source, ops.at[r, place], op_sem.at[r, half])

    def op_wait(r):
        for half in range(2):
            pltpu.make_async_copy(
                messages[0].at[pl.ds(0, half_rows), :], ops.at[r, half], op_sem.at[r, half]
            ).wait()

    def win_copy(r):
        message = messages[r] if r < sections - 1 else messages[-1]
        first = message.shape[0] - win_rows
        return pltpu.make_async_copy(
            message.at[pl.ds(first, win_rows), :], win.at[r], win_sem.at[r]
        )

    def out_copy(r):
        return pltpu.make_async_copy(corr.at[r], outs[r], out_sem.at[r])

    @pl.when(is_worker == 0)
    def _():
        corr[0] = jnp.zeros(corr.shape[1:], corr.dtype)
        out_copy(0).start()
        out_copy(0).wait()

    @pl.when(is_worker != 0)
    def _():
        src_copy = pltpu.make_async_copy(source_ref.at[shot], waves.at[0], src_sem)
        src_copy.start()
        for r in range(sections):
            win_copy(r).start()
        for r in range(sections):
            for half in range(2):
                op_copy(r, half).start()
        corr[...] = jnp.zeros(corr.shape, corr.dtype)
        for r in range(sections):
            win_copy(r).wait()
        for r in range(sections):
            value = jnp.max(win[r, slots * rows :, :].astype(jnp.float32))
            counts[r] = value.astype(jnp.int32)
        src_copy.wait()

        def level(r, slot):
            first = pl.multiple_of(slot * part, part)
            op_y = [ops[r, half, pl.ds(first, columns), :] for half in range(2)]
            spot = pl.multiple_of(slot * rows, rows)
            window = win[r, pl.ds(spot, rows), :].astype(jnp.float32)
            return window, op_y[0], op_y[1], spot

        def level_x(r, slot):
            tail = pl.multiple_of(slot * part + columns, piece)
            op_x = jnp.concatenate(
                [ops[r, half, pl.ds(tail, piece), :] for half in range(2)], axis=0
            )
            return op_x[:, :rows], op_x[:, rows:]

        def blocks(re, im):
            upper = jnp.concatenate([re, -im], axis=1)
            return jnp.concatenate([upper, jnp.concatenate([im, re], axis=1)], axis=0)

        def complex_sum(left, right):
            return left[:rows] - right[rows:], right[:rows] + left[rows:]

        def dot(a, b, dims):
            return lax.dot_general(a, b, (dims, ((), ())), preferred_element_type=jnp.float32)

        def down_section(section, place):
            r = section ^ here
            op_wait(r)

            def down_level(slot, place):
                window, y_re, y_im, _ = level(r, slot)
                x_re, x_im = level_x(r, slot)
                wave = waves[place].astype(jnp.float32)
                gain = 1.0 + window
                scaled = jnp.concatenate([gain * wave[:rows], gain * wave[rows:]], axis=0)
                op_first = blocks(x_re, x_im)
                turned_x[place] = blocks(x_re.T, x_im.T)
                middle = dot(op_first, scaled.astype(jnp.bfloat16), ((1,), (0,)))
                middle = middle.astype(jnp.bfloat16)
                moved_re, moved_im = complex_sum(
                    dot(middle, y_re, ((1,), (1,))), dot(middle, y_im, ((1,), (1,)))
                )
                waves[place + 1] = jnp.concatenate([moved_re, moved_im], axis=0).astype(
                    jnp.bfloat16
                )
                return place + 1

            return lax.fori_loop(0, counts[r], down_level, place)

        last = lax.fori_loop(0, sections, down_section, 0)
        wave_up[...] = jnp.zeros(wave_up.shape, wave_up.dtype)

        def up_section(step, place):
            r = (sections - 1 - step) ^ here
            count = counts[r]

            def up_level(inner, place):
                window, y_re, y_im, spot = level(r, count - 1 - inner)
                wave = waves[place - 1].astype(jnp.float32)
                back = dot(turned_x[place - 1], wave_up[...], ((1,), (0,))).astype(jnp.bfloat16)
                spread_re, spread_im = complex_sum(
                    dot(back, y_re, ((1,), (0,))), dot(back, y_im, ((1,), (0,)))
                )
                up_re = (window * wave[:rows] + spread_re).astype(jnp.bfloat16)
                up_im = (window * wave[rows:] + spread_im).astype(jnp.bfloat16)
                wave_up[:rows] = up_re
                wave_up[rows:] = up_im
                product = wave[:rows] * up_re.astype(jnp.float32)
                product += wave[rows:] * up_im.astype(jnp.float32)
                corr[r, pl.ds(spot, rows), :] = product.astype(corr.dtype)
                return place - 1

            return lax.fori_loop(0, count, up_level, place)

        lax.fori_loop(0, sections, up_section, last)
        for r in range(sections):
            out_copy(r).start()
        for r in range(sections):
            out_copy(r).wait()


def place_kernel(shots, anchors_hbm, *refs):
    arrived, (left_out, own_out, anchors, sem) = refs[:-4], refs[-4:]
    load = pltpu.make_async_copy(anchors_hbm, anchors, sem)
    load.start()
    load.wait()
    section, tile = lax.axis_index("depth"), lax.axis_index("tile")
    columns = left_out.shape[1]
    canvas = None
    for q in range(shots):
        offset = anchors[lax.rem(section, shots) ^ q] - (tile - 1) * columns
        total = None
        for r in range(q, len(arrived), shots):
            value = arrived[r][...].astype(jnp.float32)
            total = value if total is None else total + value
        wide = jnp.concatenate([total, jnp.zeros_like(total)], axis=1)
        turned = pltpu.roll(wide, offset, 1)
        canvas = turned if canvas is None else canvas + turned
    left_out[...] = canvas[:, :columns].astype(left_out.dtype)
    own_out[...] = canvas[:, columns:]


def kept(array):
    return pltpu.with_memory_space_constraint(array, pltpu.HBM)


def on_device(source, anchors, counts, reflect, lateral_x, lateral_y):
    shots, _, rows, columns = source.shape
    slots = reflect.shape[1]
    sizes = (slots, rows, columns)
    plan = Plan(shots)
    sections, group = plan.sections, plan.group
    assert shots == 2
    bf16 = jnp.bfloat16
    smem = pl.BlockSpec(memory_space=pltpu.SMEM)
    vmem = pl.BlockSpec(memory_space=pltpu.VMEM)
    hbm = pl.BlockSpec(memory_space=pltpu.HBM)
    anywhere = pl.BlockSpec(memory_space=pl.ANY)

    def params(mib):
        return pltpu.CompilerParams(vmem_limit_bytes=mib * MIB)

    tile_reflect = reflect[0].reshape(slots * rows, columns)
    halo = lax.ppermute(tile_reflect, "tile", [(i, i + 1) for i in range(plan.tiles - 1)])
    half_rows, win_rows = slots * (columns + rows // 2), slots * rows + TAIL
    whole = jax.ShapeDtypeStruct((2 * half_rows + win_rows, columns), bf16)
    half = jax.ShapeDtypeStruct((half_rows + columns, columns), bf16)
    alone = jax.ShapeDtypeStruct((win_rows, columns), bf16)
    *wholes, far_half = pl.pallas_call(
        functools.partial(pack_kernel, group, sizes),
        out_shape=[whole] * shots + [half],
        in_specs=[hbm, hbm],
        out_specs=[vmem] * (shots + 1),
        scratch_shapes=[
            pltpu.VMEM(lateral_x.shape[1:], bf16),
            pltpu.VMEM(lateral_y.shape[1:], bf16),
            pltpu.SemaphoreType.DMA((2,)),
        ],
        compiler_params=params(12),
        name="pack",
    )(kept(lateral_x[0]), kept(lateral_y[0]))
    last = sections - 1
    far_half = lax.ppermute(far_half, BOTH, plan.to_workers(last))
    *wholes, far_window = pl.pallas_call(
        functools.partial(window_kernel, shots, sizes),
        out_shape=[whole] * shots + [alone],
        in_specs=[hbm, smem, vmem, hbm] + [anywhere] * shots,
        out_specs=[anywhere] * shots + [vmem],
        scratch_shapes=[
            pltpu.SMEM((shots,), jnp.int32),
            pltpu.VMEM((slots * rows, columns), bf16),
            pltpu.VMEM((shots, win_rows, columns), bf16),
            pltpu.SemaphoreType.DMA((shots + 2,)),
        ],
        input_output_aliases={4 + q: q for q in range(shots)},
        compiler_params=params(8),
        name="windows",
    )(kept(anchors), counts, halo, kept(tile_reflect), *wholes)
    messages = [wholes[0]] + [
        lax.ppermute(wholes[r % shots], BOTH, plan.to_workers(r)) for r in range(1, last)
    ]
    far_window = lax.ppermute(far_window, BOTH, plan.to_workers(last))
    other_half = lax.ppermute(far_half, BOTH, plan.swap_workers())

    corr_shape = jax.ShapeDtypeStruct((slots * rows, columns), bf16)
    correlations = pl.pallas_call(
        functools.partial(sweep_kernel, sections, shots, group, sizes),
        out_shape=[corr_shape] * sections,
        in_specs=[hbm] + [anywhere] * (sections + 2),
        out_specs=[anywhere] * sections,
        scratch_shapes=[
            pltpu.VMEM((sections, 2, half_rows, columns), bf16),
            pltpu.VMEM((sections, win_rows, columns), bf16),
            pltpu.VMEM((sections * slots + 1, 2 * rows, columns), bf16),
            pltpu.VMEM((sections * slots, 2 * rows, 2 * rows), bf16),
            pltpu.VMEM((2 * rows, columns), bf16),
            pltpu.VMEM((sections, slots * rows, columns), bf16),
            pltpu.SMEM((sections,), jnp.int32),
            pltpu.SemaphoreType.DMA((sections, 2)),
            pltpu.SemaphoreType.DMA((sections,)),
            pltpu.SemaphoreType.DMA,
            pltpu.SemaphoreType.DMA((sections,)),
        ],
        compiler_params=params(14),
        name="sweep",
    )(
        kept(source.reshape(shots, 2 * rows, columns)), *messages, far_half, other_half, far_window
    )

    arrived = [correlations[0]] + [
        lax.ppermute(correlations[r], BOTH, plan.from_workers(r)) for r in range(1, sections)
    ]
    left, own = pl.pallas_call(
        functools.partial(place_kernel, shots),
        out_shape=[corr_shape, jax.ShapeDtypeStruct((slots * rows, columns), jnp.float32)],
        in_specs=[hbm] + [vmem] * sections,
        out_specs=[vmem, vmem],
        scratch_shapes=[pltpu.SMEM((shots,), jnp.int32), pltpu.SemaphoreType.DMA],
        compiler_params=params(8),
        name="place",
    )(kept(anchors), *arrived)
    from_right = lax.ppermute(left, "tile", [(i + 1, i) for i in range(plan.tiles - 1)])
    image = own + from_right.astype(jnp.float32)
    return image.reshape(1, slots, rows, columns)


def solution(mesh):
    return jax.shard_map(
        on_device,
        mesh=mesh,
        in_specs=(
            P("tile", None, None, None),
            P("tile"),
            P("depth"),
            P("depth", None, None, "tile"),
            P("depth", None, None, None, None),
            P("depth", None, None, None, None),
        ),
        out_specs=P("depth", None, None, "tile"),
        check_vma=False,
    )
```

```python
import functools

import jax
import jax.numpy as jnp
from jax import lax
from jax.experimental import pallas as pl
from jax.experimental.pallas import tpu as pltpu
from jax.sharding import PartitionSpec as P

BOTH = ("depth", "tile")
MIB = 1024 * 1024
TAIL = 16


class Plan:
    def __init__(self, shots):
        self.sections = lax.axis_size("depth")
        self.tiles = lax.axis_size("tile")
        self.shots = shots
        self.group = self.sections // shots
        assert self.sections == 4 and self.group * shots == self.sections
        assert self.tiles % (2 * self.group) == 0

    def device(self, depth, tile):
        return depth * self.tiles + tile

    def bases(self):
        return range(0, self.tiles, self.group)

    def worker(self, base, w):
        return self.device(w, base + w // self.shots)

    def swap_workers(self):
        return [
            (self.worker(base, w), self.worker((base // self.group ^ 1) * self.group, w))
            for base in self.bases()
            for w in range(self.sections)
        ]

    def to_workers(self, r):
        return [
            (self.device(w ^ r, base + w // self.shots), self.worker(base, w))
            for base in self.bases()
            for w in range(self.sections)
        ]

    def from_workers(self, r):
        return [(b, a) for a, b in self.to_workers(r)]


def pack_kernel(group, sizes, x_hbm, y_hbm, *refs):
    slots, rows, columns = sizes
    outs, (x_ref, y_ref, sem) = refs[:-3], refs[-3:]
    loads = [
        pltpu.make_async_copy(x_hbm, x_ref, sem.at[0]),
        pltpu.make_async_copy(y_hbm, y_ref, sem.at[1]),
    ]
    for load in loads:
        load.start()
    for load in loads:
        load.wait()
    piece = rows // 2
    part = columns + piece
    half_rows = slots * part
    for half in range(2):
        for slot in range(slots):
            spot = half * half_rows + slot * part
            op_x = jnp.concatenate(
                [x_ref[slot, i, half * piece : (half + 1) * piece, :] for i in range(2)], axis=1
            )
            for out in outs[:-1]:
                out[spot : spot + columns, :] = y_ref[slot, half]
                out[spot + columns : spot + part, :] = op_x
    plane = lax.rem(lax.axis_index("tile") // group, 2)
    first = pl.multiple_of(plane * half_rows, half_rows)
    outs[-1][:half_rows] = outs[0][pl.ds(first, half_rows), :]


def window_kernel(shots, sizes, anchors_hbm, counts, left_ref, right_hbm, *refs):
    slots, rows, columns = sizes
    message, alone, (anchors, right_ref, sem) = refs[1], refs[2 : 2 + shots], refs[2 + shots :]
    loads = [
        pltpu.make_async_copy(anchors_hbm, anchors, sem.at[0]),
        pltpu.make_async_copy(right_hbm, right_ref, sem.at[1]),
    ]
    for load in loads:
        load.start()
    for load in loads:
        load.wait()
    section, tile = lax.axis_index("depth"), lax.axis_index("tile")
    both = jnp.concatenate(
        [left_ref[...].astype(jnp.float32), right_ref[...].astype(jnp.float32)], axis=1
    )
    tail = jnp.full((TAIL, columns), counts[0].astype(jnp.float32), jnp.float32)
    for q in reversed(range(shots)):
        offset = anchors[lax.rem(section, shots) ^ q] - (tile - 1) * columns
        back = lax.rem(2 * columns - offset, 2 * columns)
        window = pltpu.roll(both, back, 1)[:, :columns]
        alone[q][: slots * rows] = window.astype(alone[q].dtype)
        alone[q][slots * rows :] = tail.astype(alone[q].dtype)
        if q == shots - 1:
            win_rows = alone[q].shape[0]
            place = message.at[pl.ds(message.shape[0] - win_rows, win_rows), :]
            copy = pltpu.make_async_copy(alone[q], place, sem.at[2])
            copy.start()
    copy.wait()


def sweep_kernel(sections, shots, group, sizes, source_ref, *refs):
    slots, rows, columns = sizes
    operators, refs = refs[: sections + 1], refs[sections + 1 :]
    windows, refs = refs[: sections - 1], refs[sections - 1 :]
    outs, refs = refs[:sections], refs[sections:]
    ops, win, waves, turned_x, wave_up, corr, counts, op_sem, win_sem, src_sem, out_sem = refs
    here, tile = lax.axis_index("depth"), lax.axis_index("tile")
    shot = lax.rem(here, shots)
    is_worker = (here // shots == lax.rem(tile, group)).astype(jnp.int32)
    plane = lax.rem(tile // group, 2)
    piece = rows // 2
    part = columns + piece
    half_rows = slots * part
    win_rows = slots * rows + TAIL

    def op_copy(r, half):
        if r < sections - 1:
            place, message, first = half, operators[r], half * half_rows
        else:
            place, message, first = (plane, 1 - plane)[half], operators[r + half], 0
        source = message.at[pl.ds(first, half_rows), :]
        return pltpu.make_async_copy(source, ops.at[r, place], op_sem.at[r, half])

    def op_wait(r):
        for half in range(2):
            pltpu.make_async_copy(
                operators[0].at[pl.ds(0, half_rows), :], ops.at[r, half], op_sem.at[r, half]
            ).wait()

    def win_copy(r):
        message = operators[1] if r == 1 else windows[max(r - 1, 0)]
        first = message.shape[0] - win_rows
        return pltpu.make_async_copy(
            message.at[pl.ds(first, win_rows), :], win.at[r], win_sem.at[r]
        )

    def out_copy(r):
        return pltpu.make_async_copy(corr.at[r], outs[r], out_sem.at[r])

    @pl.when(is_worker == 0)
    def _():
        corr[0] = jnp.zeros(corr.shape[1:], corr.dtype)
        out_copy(0).start()
        out_copy(0).wait()

    @pl.when(is_worker != 0)
    def _():
        src_copy = pltpu.make_async_copy(source_ref.at[shot], waves.at[0], src_sem)
        src_copy.start()
        for r in range(sections):
            win_copy(r).start()
        for r in range(sections):
            for half in range(2):
                op_copy(r, half).start()
        corr[...] = jnp.zeros(corr.shape, corr.dtype)
        for r in range(sections):
            win_copy(r).wait()
        for r in range(sections):
            value = jnp.max(win[r, slots * rows :, :].astype(jnp.float32))
            counts[r] = value.astype(jnp.int32)
        src_copy.wait()

        def level(r, slot):
            first = pl.multiple_of(slot * part, part)
            op_y = [ops[r, half, pl.ds(first, columns), :] for half in range(2)]
            spot = pl.multiple_of(slot * rows, rows)
            window = win[r, pl.ds(spot, rows), :].astype(jnp.float32)
            return window, op_y[0], op_y[1], spot

        def level_x(r, slot):
            tail = pl.multiple_of(slot * part + columns, piece)
            op_x = jnp.concatenate(
                [ops[r, half, pl.ds(tail, piece), :] for half in range(2)], axis=0
            )
            return op_x[:, :rows], op_x[:, rows:]

        def blocks(re, im):
            upper = jnp.concatenate([re, -im], axis=1)
            return jnp.concatenate([upper, jnp.concatenate([im, re], axis=1)], axis=0)

        def complex_sum(left, right):
            return left[:rows] - right[rows:], right[:rows] + left[rows:]

        def dot(a, b, dims):
            return lax.dot_general(a, b, (dims, ((), ())), preferred_element_type=jnp.float32)

        def down_section(section, place):
            r = section ^ here
            op_wait(r)

            def down_level(slot, place):
                window, y_re, y_im, _ = level(r, slot)
                x_re, x_im = level_x(r, slot)
                wave = waves[place].astype(jnp.float32)
                gain = 1.0 + window
                scaled = jnp.concatenate([gain * wave[:rows], gain * wave[rows:]], axis=0)
                op_first = blocks(x_re, x_im)
                turned_x[place] = blocks(x_re.T, x_im.T)
                middle = dot(op_first, scaled.astype(jnp.bfloat16), ((1,), (0,)))
                middle = middle.astype(jnp.bfloat16)
                moved_re, moved_im = complex_sum(
                    dot(middle, y_re, ((1,), (1,))), dot(middle, y_im, ((1,), (1,)))
                )
                waves[place + 1] = jnp.concatenate([moved_re, moved_im], axis=0).astype(
                    jnp.bfloat16
                )
                return place + 1

            return lax.fori_loop(0, counts[r], down_level, place)

        last = lax.fori_loop(0, sections, down_section, 0)
        wave_up[...] = jnp.zeros(wave_up.shape, wave_up.dtype)

        def up_section(step, place):
            r = (sections - 1 - step) ^ here
            count = counts[r]

            def up_level(inner, place):
                window, y_re, y_im, spot = level(r, count - 1 - inner)
                wave = waves[place - 1].astype(jnp.float32)
                back = dot(turned_x[place - 1], wave_up[...], ((1,), (0,))).astype(jnp.bfloat16)
                spread_re, spread_im = complex_sum(
                    dot(back, y_re, ((1,), (0,))), dot(back, y_im, ((1,), (0,)))
                )
                up_re = (window * wave[:rows] + spread_re).astype(jnp.bfloat16)
                up_im = (window * wave[rows:] + spread_im).astype(jnp.bfloat16)
                wave_up[:rows] = up_re
                wave_up[rows:] = up_im
                product = wave[:rows] * up_re.astype(jnp.float32)
                product += wave[rows:] * up_im.astype(jnp.float32)
                corr[r, pl.ds(spot, rows), :] = product.astype(corr.dtype)
                return place - 1

            return lax.fori_loop(0, count, up_level, place)

        lax.fori_loop(0, sections, up_section, last)
        for r in range(sections):
            out_copy(r).start()
        for r in range(sections):
            out_copy(r).wait()


def place_kernel(shots, anchors_hbm, *refs):
    arrived, (left_out, own_out, anchors, sem) = refs[:-4], refs[-4:]
    load = pltpu.make_async_copy(anchors_hbm, anchors, sem)
    load.start()
    load.wait()
    section, tile = lax.axis_index("depth"), lax.axis_index("tile")
    columns = left_out.shape[1]
    canvas = None
    for q in range(shots):
        offset = anchors[lax.rem(section, shots) ^ q] - (tile - 1) * columns
        total = None
        for r in range(q, len(arrived), shots):
            value = arrived[r][...].astype(jnp.float32)
            total = value if total is None else total + value
        wide = jnp.concatenate([total, jnp.zeros_like(total)], axis=1)
        turned = pltpu.roll(wide, offset, 1)
        canvas = turned if canvas is None else canvas + turned
    left_out[...] = canvas[:, :columns].astype(left_out.dtype)
    own_out[...] = canvas[:, columns:]


def kept(array):
    return pltpu.with_memory_space_constraint(array, pltpu.HBM)


def on_device(source, anchors, counts, reflect, lateral_x, lateral_y):
    shots, _, rows, columns = source.shape
    slots = reflect.shape[1]
    sizes = (slots, rows, columns)
    plan = Plan(shots)
    sections, group = plan.sections, plan.group
    assert shots == 2
    bf16 = jnp.bfloat16
    smem = pl.BlockSpec(memory_space=pltpu.SMEM)
    vmem = pl.BlockSpec(memory_space=pltpu.VMEM)
    hbm = pl.BlockSpec(memory_space=pltpu.HBM)
    anywhere = pl.BlockSpec(memory_space=pl.ANY)

    def params(mib):
        return pltpu.CompilerParams(vmem_limit_bytes=mib * MIB)

    tile_reflect = reflect[0].reshape(slots * rows, columns)
    halo = lax.ppermute(tile_reflect, "tile", [(i, i + 1) for i in range(plan.tiles - 1)])
    half_rows, win_rows = slots * (columns + rows // 2), slots * rows + TAIL
    whole = jax.ShapeDtypeStruct((2 * half_rows + win_rows + TAIL, columns), bf16)
    longer = jax.ShapeDtypeStruct((2 * half_rows + win_rows, columns), bf16)
    half = jax.ShapeDtypeStruct((half_rows + columns, columns), bf16)
    alone = jax.ShapeDtypeStruct((win_rows, columns), bf16)
    whole, near, far_half = pl.pallas_call(
        functools.partial(pack_kernel, group, sizes),
        out_shape=[whole, longer, half],
        in_specs=[hbm, hbm],
        out_specs=[vmem] * 3,
        scratch_shapes=[
            pltpu.VMEM(lateral_x.shape[1:], bf16),
            pltpu.VMEM(lateral_y.shape[1:], bf16),
            pltpu.SemaphoreType.DMA((2,)),
        ],
        compiler_params=params(12),
        name="pack",
    )(kept(lateral_x[0]), kept(lateral_y[0]))
    last = sections - 1
    far_half = lax.ppermute(far_half, BOTH, plan.to_workers(last))
    far = lax.ppermute(whole, BOTH, plan.to_workers(2))
    near, own_window, other_window = pl.pallas_call(
        functools.partial(window_kernel, shots, sizes),
        out_shape=[longer] + [alone] * shots,
        in_specs=[hbm, smem, vmem, hbm, anywhere],
        out_specs=[anywhere] + [vmem] * shots,
        scratch_shapes=[
            pltpu.SMEM((shots,), jnp.int32),
            pltpu.VMEM((slots * rows, columns), bf16),
            pltpu.SemaphoreType.DMA((3,)),
        ],
        input_output_aliases={4: 0},
        compiler_params=params(8),
        name="windows",
    )(kept(anchors), counts, halo, kept(tile_reflect), near)
    near = lax.ppermute(near, BOTH, plan.to_workers(1))
    far_window = lax.ppermute(own_window, BOTH, plan.to_workers(2))
    cross_window = lax.ppermute(other_window, BOTH, plan.to_workers(last))
    other_half = lax.ppermute(far_half, BOTH, plan.swap_workers())

    corr_shape = jax.ShapeDtypeStruct((slots * rows, columns), bf16)
    correlations = pl.pallas_call(
        functools.partial(sweep_kernel, sections, shots, group, sizes),
        out_shape=[corr_shape] * sections,
        in_specs=[hbm] + [anywhere] * (2 * sections),
        out_specs=[anywhere] * sections,
        scratch_shapes=[
            pltpu.VMEM((sections, 2, half_rows, columns), bf16),
            pltpu.VMEM((sections, win_rows, columns), bf16),
            pltpu.VMEM((sections * slots + 1, 2 * rows, columns), bf16),
            pltpu.VMEM((sections * slots, 2 * rows, 2 * rows), bf16),
            pltpu.VMEM((2 * rows, columns), bf16),
            pltpu.VMEM((sections, slots * rows, columns), bf16),
            pltpu.SMEM((sections,), jnp.int32),
            pltpu.SemaphoreType.DMA((sections, 2)),
            pltpu.SemaphoreType.DMA((sections,)),
            pltpu.SemaphoreType.DMA,
            pltpu.SemaphoreType.DMA((sections,)),
        ],
        compiler_params=params(14),
        name="sweep",
    )(
        kept(source.reshape(shots, 2 * rows, columns)), whole, near, far, far_half, other_half,
        own_window, far_window, cross_window
    )

    arrived = [correlations[0]] + [
        lax.ppermute(correlations[r], BOTH, plan.from_workers(r)) for r in range(1, sections)
    ]
    left, own = pl.pallas_call(
        functools.partial(place_kernel, shots),
        out_shape=[corr_shape, jax.ShapeDtypeStruct((slots * rows, columns), jnp.float32)],
        in_specs=[hbm] + [vmem] * sections,
        out_specs=[vmem, vmem],
        scratch_shapes=[pltpu.SMEM((shots,), jnp.int32), pltpu.SemaphoreType.DMA],
        compiler_params=params(8),
        name="place",
    )(kept(anchors), *arrived)
    from_right = lax.ppermute(left, "tile", [(i + 1, i) for i in range(plan.tiles - 1)])
    image = own + from_right.astype(jnp.float32)
    return image.reshape(1, slots, rows, columns)


def solution(mesh):
    return jax.shard_map(
        on_device,
        mesh=mesh,
        in_specs=(
            P("tile", None, None, None),
            P("tile"),
            P("depth"),
            P("depth", None, None, "tile"),
            P("depth", None, None, None, None),
            P("depth", None, None, None, None),
        ),
        out_specs=P("depth", None, None, "tile"),
        check_vma=False,
    )
```

```python
import functools

import jax
import jax.numpy as jnp
from jax import lax
from jax.experimental import pallas as pl
from jax.experimental.pallas import tpu as pltpu
from jax.sharding import PartitionSpec as P

BOTH = ("depth", "tile")
MIB = 1024 * 1024
TAIL = 16


class Plan:
    def __init__(self, shots):
        self.sections = lax.axis_size("depth")
        self.tiles = lax.axis_size("tile")
        self.shots = shots
        self.group = self.sections // shots
        assert self.sections == 4 and self.group * shots == self.sections
        assert self.tiles % (2 * self.group) == 0

    def device(self, depth, tile):
        return depth * self.tiles + tile

    def bases(self):
        return range(0, self.tiles, self.group)

    def worker(self, base, w):
        return self.device(w, base + w // self.shots)

    def other(self, w, base):
        return self.device(w, base + (w // self.shots + 1) % self.group)

    def ops_to_workers(self, r):
        return [
            (self.other(w ^ r, base), self.worker(base, w))
            for base in self.bases()
            for w in range(self.sections)
        ]

    def swap_workers(self):
        return [
            (self.worker(base, w), self.worker((base // self.group ^ 1) * self.group, w))
            for base in self.bases()
            for w in range(self.sections)
        ]

    def to_workers(self, r):
        return [
            (self.device(w ^ r, base + w // self.shots), self.worker(base, w))
            for base in self.bases()
            for w in range(self.sections)
        ]

    def from_workers(self, r):
        return [(b, a) for a, b in self.to_workers(r)]


def pack_kernel(group, sizes, x_hbm, y_hbm, out, half_out, x_ref, y_ref, sem):
    slots, rows, columns = sizes
    loads = [
        pltpu.make_async_copy(x_hbm, x_ref, sem.at[0]),
        pltpu.make_async_copy(y_hbm, y_ref, sem.at[1]),
    ]
    for load in loads:
        load.start()
    for load in loads:
        load.wait()
    piece = rows // 2
    part = columns + piece
    for half in range(2):
        for slot in range(slots):
            spot = slot * part
            out[half, spot : spot + columns, :] = y_ref[slot, half]
            out[half, spot + columns : spot + part, :] = jnp.concatenate(
                [x_ref[slot, i, half * piece : (half + 1) * piece, :] for i in range(2)], axis=1
            )
    half_out[...] = out[lax.rem(lax.axis_index("tile") // group, 2)]


def window_kernel(shots, sizes, anchors_hbm, counts, left_ref, right_hbm, *refs):
    slots, rows, columns = sizes
    outs, (anchors, right_ref, sem) = refs[:shots], refs[shots:]
    loads = [
        pltpu.make_async_copy(anchors_hbm, anchors, sem.at[0]),
        pltpu.make_async_copy(right_hbm, right_ref, sem.at[1]),
    ]
    for load in loads:
        load.start()
    for load in loads:
        load.wait()
    section, tile = lax.axis_index("depth"), lax.axis_index("tile")
    both = jnp.concatenate(
        [left_ref[...].astype(jnp.float32), right_ref[...].astype(jnp.float32)], axis=1
    )
    tail = jnp.full((TAIL, columns), counts[0].astype(jnp.float32), jnp.float32)
    for q, out in enumerate(outs):
        offset = anchors[lax.rem(section, shots) ^ q] - (tile - 1) * columns
        back = lax.rem(2 * columns - offset, 2 * columns)
        out[: slots * rows] = pltpu.roll(both, back, 1)[:, :columns].astype(out.dtype)
        out[slots * rows :] = tail.astype(out.dtype)


def sweep_kernel(sections, shots, group, sizes, source_ref, *refs):
    slots, rows, columns = sizes
    operators, refs = refs[: sections + 1], refs[sections + 1 :]
    windows, refs = refs[:sections], refs[sections:]
    outs, refs = refs[:sections], refs[sections:]
    ops, win, waves, turned_x, wave_up, corr, counts, op_sem, win_sem, src_sem, out_sem = refs
    here, tile = lax.axis_index("depth"), lax.axis_index("tile")
    shot = lax.rem(here, shots)
    is_worker = (here // shots == lax.rem(tile, group)).astype(jnp.int32)
    plane = lax.rem(tile // group, 2)
    piece = rows // 2
    part = columns + piece

    def op_copy(r, half):
        if r < sections - 1:
            place, source = half, operators[r].at[half]
        else:
            place, source = (plane, 1 - plane)[half], operators[r + half]
        return pltpu.make_async_copy(source, ops.at[r, place], op_sem.at[r, half])

    def op_wait(r):
        for half in range(2):
            pltpu.make_async_copy(operators[-1], ops.at[r, half], op_sem.at[r, half]).wait()

    def win_copy(r):
        return pltpu.make_async_copy(windows[r], win.at[r], win_sem.at[r])

    def out_copy(r):
        return pltpu.make_async_copy(corr.at[r], outs[r], out_sem.at[r])

    @pl.when(is_worker == 0)
    def _():
        corr[0] = jnp.zeros(corr.shape[1:], corr.dtype)
        out_copy(0).start()
        out_copy(0).wait()

    @pl.when(is_worker != 0)
    def _():
        src_copy = pltpu.make_async_copy(source_ref.at[shot], waves.at[0], src_sem)
        src_copy.start()
        for r in range(sections):
            win_copy(r).start()
        for r in range(sections):
            for half in range(2):
                op_copy(r, half).start()
        corr[...] = jnp.zeros(corr.shape, corr.dtype)
        for r in range(sections):
            win_copy(r).wait()
        for r in range(sections):
            value = jnp.max(win[r, slots * rows :, :].astype(jnp.float32))
            counts[r] = value.astype(jnp.int32)
        src_copy.wait()

        def level(r, slot):
            first = pl.multiple_of(slot * part, part)
            op_y = [ops[r, half, pl.ds(first, columns), :] for half in range(2)]
            spot = pl.multiple_of(slot * rows, rows)
            window = win[r, pl.ds(spot, rows), :].astype(jnp.float32)
            return window, op_y[0], op_y[1], spot

        def level_x(r, slot):
            tail = pl.multiple_of(slot * part + columns, piece)
            op_x = jnp.concatenate(
                [ops[r, half, pl.ds(tail, piece), :] for half in range(2)], axis=0
            )
            return op_x[:, :rows], op_x[:, rows:]

        def blocks(re, im):
            upper = jnp.concatenate([re, -im], axis=1)
            return jnp.concatenate([upper, jnp.concatenate([im, re], axis=1)], axis=0)

        def complex_sum(left, right):
            return left[:rows] - right[rows:], right[:rows] + left[rows:]

        def dot(a, b, dims):
            return lax.dot_general(a, b, (dims, ((), ())), preferred_element_type=jnp.float32)

        def down_section(section, place):
            r = section ^ here
            op_wait(r)

            def down_level(slot, place):
                window, y_re, y_im, _ = level(r, slot)
                x_re, x_im = level_x(r, slot)
                wave = waves[place].astype(jnp.float32)
                gain = 1.0 + window
                scaled = jnp.concatenate([gain * wave[:rows], gain * wave[rows:]], axis=0)
                op_first = blocks(x_re, x_im)
                turned_x[place] = blocks(x_re.T, x_im.T)
                middle = dot(op_first, scaled.astype(jnp.bfloat16), ((1,), (0,)))
                middle = middle.astype(jnp.bfloat16)
                moved_re, moved_im = complex_sum(
                    dot(middle, y_re, ((1,), (1,))), dot(middle, y_im, ((1,), (1,)))
                )
                waves[place + 1] = jnp.concatenate([moved_re, moved_im], axis=0).astype(
                    jnp.bfloat16
                )
                return place + 1

            return lax.fori_loop(0, counts[r], down_level, place)

        last = lax.fori_loop(0, sections, down_section, 0)
        wave_up[...] = jnp.zeros(wave_up.shape, wave_up.dtype)

        def up_section(step, place):
            r = (sections - 1 - step) ^ here
            count = counts[r]

            def up_level(inner, place):
                window, y_re, y_im, spot = level(r, count - 1 - inner)
                wave = waves[place - 1].astype(jnp.float32)
                back = dot(turned_x[place - 1], wave_up[...], ((1,), (0,))).astype(jnp.bfloat16)
                spread_re, spread_im = complex_sum(
                    dot(back, y_re, ((1,), (0,))), dot(back, y_im, ((1,), (0,)))
                )
                up_re = (window * wave[:rows] + spread_re).astype(jnp.bfloat16)
                up_im = (window * wave[rows:] + spread_im).astype(jnp.bfloat16)
                wave_up[:rows] = up_re
                wave_up[rows:] = up_im
                product = wave[:rows] * up_re.astype(jnp.float32)
                product += wave[rows:] * up_im.astype(jnp.float32)
                corr[r, pl.ds(spot, rows), :] = product.astype(corr.dtype)
                return place - 1

            return lax.fori_loop(0, count, up_level, place)

        lax.fori_loop(0, sections, up_section, last)
        for r in range(sections):
            out_copy(r).start()
        for r in range(sections):
            out_copy(r).wait()


def place_kernel(shots, anchors_hbm, *refs):
    arrived, (left_out, own_out, anchors, sem) = refs[:-4], refs[-4:]
    load = pltpu.make_async_copy(anchors_hbm, anchors, sem)
    load.start()
    load.wait()
    section, tile = lax.axis_index("depth"), lax.axis_index("tile")
    columns = left_out.shape[1]
    canvas = None
    for q in range(shots):
        offset = anchors[lax.rem(section, shots) ^ q] - (tile - 1) * columns
        total = None
        for r in range(q, len(arrived), shots):
            value = arrived[r][...].astype(jnp.float32)
            total = value if total is None else total + value
        wide = jnp.concatenate([total, jnp.zeros_like(total)], axis=1)
        turned = pltpu.roll(wide, offset, 1)
        canvas = turned if canvas is None else canvas + turned
    left_out[...] = canvas[:, :columns].astype(left_out.dtype)
    own_out[...] = canvas[:, columns:]


def kept(array):
    return pltpu.with_memory_space_constraint(array, pltpu.HBM)


def on_device(source, anchors, counts, reflect, lateral_x, lateral_y):
    shots, _, rows, columns = source.shape
    slots = reflect.shape[1]
    sizes = (slots, rows, columns)
    plan = Plan(shots)
    sections, group = plan.sections, plan.group
    assert shots == 2
    bf16 = jnp.bfloat16
    smem = pl.BlockSpec(memory_space=pltpu.SMEM)
    vmem = pl.BlockSpec(memory_space=pltpu.VMEM)
    hbm = pl.BlockSpec(memory_space=pltpu.HBM)
    anywhere = pl.BlockSpec(memory_space=pl.ANY)

    def params(mib):
        return pltpu.CompilerParams(vmem_limit_bytes=mib * MIB)

    tile_reflect = reflect[0].reshape(slots * rows, columns)
    halo = lax.ppermute(tile_reflect, "tile", [(i, i + 1) for i in range(plan.tiles - 1)])
    half_rows, win_rows = slots * (columns + rows // 2), slots * rows + TAIL
    whole, half = pl.pallas_call(
        functools.partial(pack_kernel, group, sizes),
        out_shape=[
            jax.ShapeDtypeStruct((2, half_rows, columns), bf16),
            jax.ShapeDtypeStruct((half_rows, columns), bf16),
        ],
        in_specs=[hbm, hbm],
        out_specs=[vmem, vmem],
        scratch_shapes=[
            pltpu.VMEM(lateral_x.shape[1:], bf16),
            pltpu.VMEM(lateral_y.shape[1:], bf16),
            pltpu.SemaphoreType.DMA((2,)),
        ],
        compiler_params=params(8),
        name="pack",
    )(kept(lateral_x[0]), kept(lateral_y[0]))
    near = lax.ppermute(whole, BOTH, plan.ops_to_workers(1))
    far = lax.ppermute(whole, BOTH, plan.ops_to_workers(2))
    cross = lax.ppermute(half, BOTH, plan.ops_to_workers(sections - 1))
    other = lax.ppermute(cross, BOTH, plan.swap_workers())
    parts = pl.pallas_call(
        functools.partial(window_kernel, shots, sizes),
        out_shape=[jax.ShapeDtypeStruct((win_rows, columns), bf16)] * shots,
        in_specs=[hbm, smem, vmem, hbm],
        out_specs=[vmem] * shots,
        scratch_shapes=[
            pltpu.SMEM((shots,), jnp.int32),
            pltpu.VMEM((slots * rows, columns), bf16),
            pltpu.SemaphoreType.DMA((2,)),
        ],
        compiler_params=params(8),
        cost_estimate=pl.CostEstimate(flops=10**10, bytes_accessed=4 * MIB, transcendentals=0),
        name="windows",
    )(kept(anchors), counts, halo, kept(tile_reflect))
    windows = [parts[0]] + [
        lax.ppermute(parts[r % shots], BOTH, plan.to_workers(r)) for r in range(1, sections)
    ]

    corr_shape = jax.ShapeDtypeStruct((slots * rows, columns), bf16)
    correlations = pl.pallas_call(
        functools.partial(sweep_kernel, sections, shots, group, sizes),
        out_shape=[corr_shape] * sections,
        in_specs=[hbm] + [anywhere] * (2 * sections + 1),
        out_specs=[anywhere] * sections,
        scratch_shapes=[
            pltpu.VMEM((sections, 2, half_rows, columns), bf16),
            pltpu.VMEM((sections, win_rows, columns), bf16),
            pltpu.VMEM((sections * slots + 1, 2 * rows, columns), bf16),
            pltpu.VMEM((sections * slots, 2 * rows, 2 * rows), bf16),
            pltpu.VMEM((2 * rows, columns), bf16),
            pltpu.VMEM((sections, slots * rows, columns), bf16),
            pltpu.SMEM((sections,), jnp.int32),
            pltpu.SemaphoreType.DMA((sections, 2)),
            pltpu.SemaphoreType.DMA((sections,)),
            pltpu.SemaphoreType.DMA,
            pltpu.SemaphoreType.DMA((sections,)),
        ],
        compiler_params=params(14),
        name="sweep",
    )(
        kept(source.reshape(shots, 2 * rows, columns)), whole, near, far, cross, other, *windows
    )

    arrived = [correlations[0]] + [
        lax.ppermute(correlations[r], BOTH, plan.from_workers(r)) for r in range(1, sections)
    ]
    left, own = pl.pallas_call(
        functools.partial(place_kernel, shots),
        out_shape=[corr_shape, jax.ShapeDtypeStruct((slots * rows, columns), jnp.float32)],
        in_specs=[hbm] + [vmem] * sections,
        out_specs=[vmem, vmem],
        scratch_shapes=[pltpu.SMEM((shots,), jnp.int32), pltpu.SemaphoreType.DMA],
        compiler_params=params(8),
        name="place",
    )(kept(anchors), *arrived)
    from_right = lax.ppermute(left, "tile", [(i + 1, i) for i in range(plan.tiles - 1)])
    image = own + from_right.astype(jnp.float32)
    return image.reshape(1, slots, rows, columns)


def solution(mesh):
    return jax.shard_map(
        on_device,
        mesh=mesh,
        in_specs=(
            P("tile", None, None, None),
            P("tile"),
            P("depth"),
            P("depth", None, None, "tile"),
            P("depth", None, None, None, None),
            P("depth", None, None, None, None),
        ),
        out_specs=P("depth", None, None, "tile"),
        check_vma=False,
    )
```

```python
import functools

import jax
import jax.numpy as jnp
from jax import lax
from jax.experimental import pallas as pl
from jax.experimental.pallas import tpu as pltpu
from jax.sharding import PartitionSpec as P

BOTH = ("depth", "tile")
MIB = 1024 * 1024
TAIL = 16


class Plan:
    def __init__(self, shots):
        self.sections = lax.axis_size("depth")
        self.tiles = lax.axis_size("tile")
        self.shots = shots
        self.group = self.sections // shots
        assert self.sections == 4 and self.group * shots == self.sections
        assert self.tiles % (2 * self.group) == 0

    def device(self, depth, tile):
        return depth * self.tiles + tile

    def bases(self):
        return range(0, self.tiles, self.group)

    def worker(self, base, w):
        return self.device(w, base + w // self.shots)

    def other(self, w, base):
        return self.device(w, base + (w // self.shots + 1) % self.group)

    def ops_to_workers(self, r):
        return [
            (self.other(w ^ r, base), self.worker(base, w))
            for base in self.bases()
            for w in range(self.sections)
        ]

    def swap_workers(self):
        return [
            (self.worker(base, w), self.worker((base // self.group ^ 1) * self.group, w))
            for base in self.bases()
            for w in range(self.sections)
        ]

    def to_workers(self, r):
        return [
            (self.device(w ^ r, base + w // self.shots), self.worker(base, w))
            for base in self.bases()
            for w in range(self.sections)
        ]

    def from_workers(self, r):
        return [(b, a) for a, b in self.to_workers(r)]


def pack_kernel(group, sizes, x_hbm, y_hbm, out, half_out, x_ref, y_ref, sem):
    slots, rows, columns = sizes
    loads = [
        pltpu.make_async_copy(x_hbm, x_ref, sem.at[0]),
        pltpu.make_async_copy(y_hbm, y_ref, sem.at[1]),
    ]
    for load in loads:
        load.start()
    for load in loads:
        load.wait()
    piece = rows // 2
    part = columns + piece
    for half in range(2):
        for slot in range(slots):
            spot = slot * part
            out[half, spot : spot + columns, :] = y_ref[slot, half]
            out[half, spot + columns : spot + part, :] = jnp.concatenate(
                [x_ref[slot, i, half * piece : (half + 1) * piece, :] for i in range(2)], axis=1
            )
    half_out[...] = out[lax.rem(lax.axis_index("tile") // group, 2)]


def window_kernel(shots, sizes, anchors_hbm, counts, left_ref, right_hbm, *refs):
    slots, rows, columns = sizes
    out, anchors, right_ref, sem = refs
    loads = [
        pltpu.make_async_copy(anchors_hbm, anchors, sem.at[0]),
        pltpu.make_async_copy(right_hbm, right_ref, sem.at[1]),
    ]
    for load in loads:
        load.start()
    for load in loads:
        load.wait()
    section, tile = lax.axis_index("depth"), lax.axis_index("tile")
    both = jnp.concatenate(
        [left_ref[...].astype(jnp.float32), right_ref[...].astype(jnp.float32)], axis=1
    )
    tail = jnp.full((TAIL, columns), counts[0].astype(jnp.float32), jnp.float32)
    for q in range(shots):
        offset = anchors[lax.rem(section, shots) ^ q] - (tile - 1) * columns
        back = lax.rem(2 * columns - offset, 2 * columns)
        out[q, : slots * rows] = pltpu.roll(both, back, 1)[:, :columns].astype(out.dtype)
        out[q, slots * rows :] = tail.astype(out.dtype)


def sweep_kernel(sections, shots, group, sizes, source_ref, *refs):
    slots, rows, columns = sizes
    operators, refs = refs[: sections + 1], refs[sections + 1 :]
    (own_win, far_win, near_win), refs = refs[:3], refs[3:]
    windows = [own_win.at[0], near_win.at[0], far_win.at[0], near_win.at[1]]
    outs, refs = refs[:sections], refs[sections:]
    ops, win, waves, turned_x, wave_up, corr, counts, op_sem, win_sem, src_sem, out_sem = refs
    here, tile = lax.axis_index("depth"), lax.axis_index("tile")
    shot = lax.rem(here, shots)
    is_worker = (here // shots == lax.rem(tile, group)).astype(jnp.int32)
    plane = lax.rem(tile // group, 2)
    piece = rows // 2
    part = columns + piece

    def op_copy(r, half):
        if r < sections - 1:
            place, source = half, operators[r].at[half]
        else:
            place, source = (plane, 1 - plane)[half], operators[r + half]
        return pltpu.make_async_copy(source, ops.at[r, place], op_sem.at[r, half])

    def op_wait(r):
        for half in range(2):
            pltpu.make_async_copy(operators[-1], ops.at[r, half], op_sem.at[r, half]).wait()

    def win_copy(r):
        return pltpu.make_async_copy(windows[r], win.at[r], win_sem.at[r])

    def out_copy(r):
        return pltpu.make_async_copy(corr.at[r], outs[r], out_sem.at[r])

    @pl.when(is_worker == 0)
    def _():
        corr[0] = jnp.zeros(corr.shape[1:], corr.dtype)
        out_copy(0).start()
        out_copy(0).wait()

    @pl.when(is_worker != 0)
    def _():
        src_copy = pltpu.make_async_copy(source_ref.at[shot], waves.at[0], src_sem)
        src_copy.start()
        for r in range(sections):
            win_copy(r).start()
        for r in range(sections):
            for half in range(2):
                op_copy(r, half).start()
        corr[...] = jnp.zeros(corr.shape, corr.dtype)
        for r in range(sections):
            win_copy(r).wait()
        for r in range(sections):
            value = jnp.max(win[r, slots * rows :, :].astype(jnp.float32))
            counts[r] = value.astype(jnp.int32)
        src_copy.wait()

        def level(r, slot):
            first = pl.multiple_of(slot * part, part)
            op_y = [ops[r, half, pl.ds(first, columns), :] for half in range(2)]
            spot = pl.multiple_of(slot * rows, rows)
            window = win[r, pl.ds(spot, rows), :].astype(jnp.float32)
            return window, op_y[0], op_y[1], spot

        def level_x(r, slot):
            tail = pl.multiple_of(slot * part + columns, piece)
            op_x = jnp.concatenate(
                [ops[r, half, pl.ds(tail, piece), :] for half in range(2)], axis=0
            )
            return op_x[:, :rows], op_x[:, rows:]

        def blocks(re, im):
            upper = jnp.concatenate([re, -im], axis=1)
            return jnp.concatenate([upper, jnp.concatenate([im, re], axis=1)], axis=0)

        def complex_sum(left, right):
            return left[:rows] - right[rows:], right[:rows] + left[rows:]

        def dot(a, b, dims):
            return lax.dot_general(a, b, (dims, ((), ())), preferred_element_type=jnp.float32)

        def down_section(section, place):
            r = section ^ here
            op_wait(r)

            def down_level(slot, place):
                window, y_re, y_im, _ = level(r, slot)
                x_re, x_im = level_x(r, slot)
                wave = waves[place].astype(jnp.float32)
                gain = 1.0 + window
                scaled = jnp.concatenate([gain * wave[:rows], gain * wave[rows:]], axis=0)
                op_first = blocks(x_re, x_im)
                turned_x[place] = blocks(x_re.T, x_im.T)
                middle = dot(op_first, scaled.astype(jnp.bfloat16), ((1,), (0,)))
                middle = middle.astype(jnp.bfloat16)
                moved_re, moved_im = complex_sum(
                    dot(middle, y_re, ((1,), (1,))), dot(middle, y_im, ((1,), (1,)))
                )
                waves[place + 1] = jnp.concatenate([moved_re, moved_im], axis=0).astype(
                    jnp.bfloat16
                )
                return place + 1

            return lax.fori_loop(0, counts[r], down_level, place)

        last = lax.fori_loop(0, sections, down_section, 0)
        wave_up[...] = jnp.zeros(wave_up.shape, wave_up.dtype)

        def up_section(step, place):
            r = (sections - 1 - step) ^ here
            count = counts[r]

            def up_level(inner, place):
                window, y_re, y_im, spot = level(r, count - 1 - inner)
                wave = waves[place - 1].astype(jnp.float32)
                back = dot(turned_x[place - 1], wave_up[...], ((1,), (0,))).astype(jnp.bfloat16)
                spread_re, spread_im = complex_sum(
                    dot(back, y_re, ((1,), (0,))), dot(back, y_im, ((1,), (0,)))
                )
                up_re = (window * wave[:rows] + spread_re).astype(jnp.bfloat16)
                up_im = (window * wave[rows:] + spread_im).astype(jnp.bfloat16)
                wave_up[:rows] = up_re
                wave_up[rows:] = up_im
                product = wave[:rows] * up_re.astype(jnp.float32)
                product += wave[rows:] * up_im.astype(jnp.float32)
                corr[r, pl.ds(spot, rows), :] = product.astype(corr.dtype)
                return place - 1

            return lax.fori_loop(0, count, up_level, place)

        lax.fori_loop(0, sections, up_section, last)
        for r in range(sections):
            out_copy(r).start()
        for r in range(sections):
            out_copy(r).wait()


def place_kernel(shots, anchors_hbm, *refs):
    arrived, (left_out, own_out, anchors, sem) = refs[:-4], refs[-4:]
    load = pltpu.make_async_copy(anchors_hbm, anchors, sem)
    load.start()
    load.wait()
    section, tile = lax.axis_index("depth"), lax.axis_index("tile")
    columns = left_out.shape[1]
    canvas = None
    for q in range(shots):
        offset = anchors[lax.rem(section, shots) ^ q] - (tile - 1) * columns
        total = None
        for r in range(q, len(arrived), shots):
            value = arrived[r][...].astype(jnp.float32)
            total = value if total is None else total + value
        wide = jnp.concatenate([total, jnp.zeros_like(total)], axis=1)
        turned = pltpu.roll(wide, offset, 1)
        canvas = turned if canvas is None else canvas + turned
    left_out[...] = canvas[:, :columns].astype(left_out.dtype)
    own_out[...] = canvas[:, columns:]


def kept(array):
    return pltpu.with_memory_space_constraint(array, pltpu.HBM)


def on_device(source, anchors, counts, reflect, lateral_x, lateral_y):
    shots, _, rows, columns = source.shape
    slots = reflect.shape[1]
    sizes = (slots, rows, columns)
    plan = Plan(shots)
    sections, group = plan.sections, plan.group
    assert shots == 2
    bf16 = jnp.bfloat16
    smem = pl.BlockSpec(memory_space=pltpu.SMEM)
    vmem = pl.BlockSpec(memory_space=pltpu.VMEM)
    hbm = pl.BlockSpec(memory_space=pltpu.HBM)
    anywhere = pl.BlockSpec(memory_space=pl.ANY)

    def params(mib):
        return pltpu.CompilerParams(vmem_limit_bytes=mib * MIB)

    tile_reflect = reflect[0].reshape(slots * rows, columns)
    halo = lax.ppermute(tile_reflect, "tile", [(i, i + 1) for i in range(plan.tiles - 1)])
    half_rows, win_rows = slots * (columns + rows // 2), slots * rows + TAIL
    whole, half = pl.pallas_call(
        functools.partial(pack_kernel, group, sizes),
        out_shape=[
            jax.ShapeDtypeStruct((2, half_rows, columns), bf16),
            jax.ShapeDtypeStruct((half_rows, columns), bf16),
        ],
        in_specs=[hbm, hbm],
        out_specs=[vmem, vmem],
        scratch_shapes=[
            pltpu.VMEM(lateral_x.shape[1:], bf16),
            pltpu.VMEM(lateral_y.shape[1:], bf16),
            pltpu.SemaphoreType.DMA((2,)),
        ],
        compiler_params=params(8),
        name="pack",
    )(kept(lateral_x[0]), kept(lateral_y[0]))
    near = lax.ppermute(whole, BOTH, plan.ops_to_workers(1))
    far = lax.ppermute(whole, BOTH, plan.ops_to_workers(2))
    cross = lax.ppermute(half, BOTH, plan.ops_to_workers(sections - 1))
    other = lax.ppermute(cross, BOTH, plan.swap_workers())
    own_window = pl.pallas_call(
        functools.partial(window_kernel, shots, sizes),
        out_shape=jax.ShapeDtypeStruct((shots, win_rows, columns), bf16),
        in_specs=[hbm, smem, vmem, hbm],
        out_specs=vmem,
        scratch_shapes=[
            pltpu.SMEM((shots,), jnp.int32),
            pltpu.VMEM((slots * rows, columns), bf16),
            pltpu.SemaphoreType.DMA((2,)),
        ],
        compiler_params=params(8),
        name="windows",
    )(kept(anchors), counts, halo, kept(tile_reflect))
    far_window = lax.ppermute(own_window, BOTH, plan.to_workers(2))
    near_window = lax.ppermute(
        jnp.stack([own_window[1], far_window[1]]), BOTH, plan.to_workers(1)
    )

    corr_shape = jax.ShapeDtypeStruct((slots * rows, columns), bf16)
    correlations = pl.pallas_call(
        functools.partial(sweep_kernel, sections, shots, group, sizes),
        out_shape=[corr_shape] * sections,
        in_specs=[hbm] + [anywhere] * (sections + 4),
        out_specs=[anywhere] * sections,
        scratch_shapes=[
            pltpu.VMEM((sections, 2, half_rows, columns), bf16),
            pltpu.VMEM((sections, win_rows, columns), bf16),
            pltpu.VMEM((sections * slots + 1, 2 * rows, columns), bf16),
            pltpu.VMEM((sections * slots, 2 * rows, 2 * rows), bf16),
            pltpu.VMEM((2 * rows, columns), bf16),
            pltpu.VMEM((sections, slots * rows, columns), bf16),
            pltpu.SMEM((sections,), jnp.int32),
            pltpu.SemaphoreType.DMA((sections, 2)),
            pltpu.SemaphoreType.DMA((sections,)),
            pltpu.SemaphoreType.DMA,
            pltpu.SemaphoreType.DMA((sections,)),
        ],
        compiler_params=params(14),
        name="sweep",
    )(
        kept(source.reshape(shots, 2 * rows, columns)), whole, near, far, cross, other,
        own_window, far_window, near_window
    )

    arrived = [correlations[0]] + [
        lax.ppermute(correlations[r], BOTH, plan.from_workers(r)) for r in range(1, sections)
    ]
    left, own = pl.pallas_call(
        functools.partial(place_kernel, shots),
        out_shape=[corr_shape, jax.ShapeDtypeStruct((slots * rows, columns), jnp.float32)],
        in_specs=[hbm] + [vmem] * sections,
        out_specs=[vmem, vmem],
        scratch_shapes=[pltpu.SMEM((shots,), jnp.int32), pltpu.SemaphoreType.DMA],
        compiler_params=params(8),
        name="place",
    )(kept(anchors), *arrived)
    from_right = lax.ppermute(left, "tile", [(i + 1, i) for i in range(plan.tiles - 1)])
    image = own + from_right.astype(jnp.float32)
    return image.reshape(1, slots, rows, columns)


def solution(mesh):
    return jax.shard_map(
        on_device,
        mesh=mesh,
        in_specs=(
            P("tile", None, None, None),
            P("tile"),
            P("depth"),
            P("depth", None, None, "tile"),
            P("depth", None, None, None, None),
            P("depth", None, None, None, None),
        ),
        out_specs=P("depth", None, None, "tile"),
        check_vma=False,
    )
```

```python
import functools

import jax
import jax.numpy as jnp
from jax import lax
from jax.experimental import pallas as pl
from jax.experimental.pallas import tpu as pltpu
from jax.sharding import PartitionSpec as P

BOTH = ("depth", "tile")
MIB = 1024 * 1024
TAIL = 16


class Plan:
    def __init__(self, shots):
        self.sections = lax.axis_size("depth")
        self.tiles = lax.axis_size("tile")
        self.shots = shots
        self.group = self.sections // shots
        assert self.sections == 4 and self.group * shots == self.sections
        assert self.tiles % (2 * self.group) == 0

    def device(self, depth, tile):
        return depth * self.tiles + tile

    def bases(self):
        return range(0, self.tiles, self.group)

    def worker(self, base, w):
        return self.device(w, base + w // self.shots)

    def swap_workers(self):
        return [
            (self.worker(base, w), self.worker((base // self.group ^ 1) * self.group, w))
            for base in self.bases()
            for w in range(self.sections)
        ]

    def to_workers(self, r):
        return [
            (self.device(w ^ r, base + w // self.shots), self.worker(base, w))
            for base in self.bases()
            for w in range(self.sections)
        ]

    def from_workers(self, r):
        return [(b, a) for a, b in self.to_workers(r)]


def pack_kernel(group, sizes, x_hbm, y_hbm, *refs):
    slots, rows, columns = sizes
    outs, (x_ref, y_ref, sem) = refs[:-3], refs[-3:]
    loads = [
        pltpu.make_async_copy(x_hbm, x_ref, sem.at[0]),
        pltpu.make_async_copy(y_hbm, y_ref, sem.at[1]),
    ]
    for load in loads:
        load.start()
    for load in loads:
        load.wait()
    piece = rows // 2
    part = columns + piece
    half_rows = slots * part
    for half in range(2):
        for slot in range(slots):
            spot = half * half_rows + slot * part
            op_x = jnp.concatenate(
                [x_ref[slot, i, half * piece : (half + 1) * piece, :] for i in range(2)], axis=1
            )
            for out in outs[:-1]:
                out[spot : spot + columns, :] = y_ref[slot, half]
                out[spot + columns : spot + part, :] = op_x
    plane = lax.rem(lax.axis_index("tile") // group, 2)
    first = pl.multiple_of(plane * half_rows, half_rows)
    outs[-1][:half_rows] = outs[0][pl.ds(first, half_rows), :]


def window_kernel(shots, sizes, anchors_hbm, counts, left_ref, right_hbm, *refs):
    slots, rows, columns = sizes
    messages, refs = refs[shots : 2 * shots], refs[2 * shots :]
    alone, anchors, right_ref, held, sem = refs
    loads = [
        pltpu.make_async_copy(anchors_hbm, anchors, sem.at[shots]),
        pltpu.make_async_copy(right_hbm, right_ref, sem.at[shots + 1]),
    ]
    for load in loads:
        load.start()
    for load in loads:
        load.wait()
    section, tile = lax.axis_index("depth"), lax.axis_index("tile")
    both = jnp.concatenate(
        [left_ref[...].astype(jnp.float32), right_ref[...].astype(jnp.float32)], axis=1
    )
    tail = jnp.full((TAIL, columns), counts[0].astype(jnp.float32), jnp.float32)
    copies = []
    for q, message in enumerate(messages):
        offset = anchors[lax.rem(section, shots) ^ q] - (tile - 1) * columns
        back = lax.rem(2 * columns - offset, 2 * columns)
        held[q, : slots * rows] = pltpu.roll(both, back, 1)[:, :columns].astype(held.dtype)
        held[q, slots * rows :] = tail.astype(held.dtype)
        ahead = message.shape[0] - held.shape[1]
        place = message.at[pl.ds(ahead, held.shape[1]), :]
        copies.append(pltpu.make_async_copy(held.at[q], place, sem.at[q]))
        copies[-1].start()
    alone[...] = held[shots - 1]
    for copy in copies:
        copy.wait()


def sweep_kernel(sections, shots, group, sizes, source_ref, *refs):
    slots, rows, columns = sizes
    messages, refs = refs[: sections + 1], refs[sections + 1 :]
    outs, refs = refs[:sections], refs[sections:]
    ops, win, waves, turned_x, wave_up, corr, counts, op_sem, win_sem, src_sem, out_sem = refs
    here, tile = lax.axis_index("depth"), lax.axis_index("tile")
    shot = lax.rem(here, shots)
    is_worker = (here // shots == lax.rem(tile, group)).astype(jnp.int32)
    piece = rows // 2
    part = columns + piece
    half_rows = slots * part
    win_rows = slots * rows + TAIL

    def op_copy(r, half):
        message = messages[r]
        if r < sections - 1:
            message = message.at[pl.ds(half * half_rows, half_rows), :]
        else:
            message = message.at[half]
        return pltpu.make_async_copy(message, ops.at[r, half], op_sem.at[r, half])

    def op_wait(r):
        for half in range(2):
            pltpu.make_async_copy(
                messages[0].at[pl.ds(0, half_rows), :], ops.at[r, half], op_sem.at[r, half]
            ).wait()

    def win_copy(r):
        message = messages[r] if r < sections - 1 else messages[-1]
        first = message.shape[0] - win_rows
        return pltpu.make_async_copy(
            message.at[pl.ds(first, win_rows), :], win.at[r], win_sem.at[r]
        )

    def out_copy(r):
        return pltpu.make_async_copy(corr.at[r], outs[r], out_sem.at[r])

    @pl.when(is_worker == 0)
    def _():
        corr[0] = jnp.zeros(corr.shape[1:], corr.dtype)
        out_copy(0).start()
        out_copy(0).wait()

    @pl.when(is_worker != 0)
    def _():
        src_copy = pltpu.make_async_copy(source_ref.at[shot], waves.at[0], src_sem)
        src_copy.start()
        for r in range(sections):
            win_copy(r).start()
        for section in range(sections):
            for r in range(sections):

                @pl.when((section ^ here) == r)
                def _():
                    for half in range(2):
                        op_copy(r, half).start()

        corr[...] = jnp.zeros(corr.shape, corr.dtype)
        for r in range(sections):
            win_copy(r).wait()
        for r in range(sections):
            value = jnp.max(win[r, slots * rows :, :].astype(jnp.float32))
            counts[r] = value.astype(jnp.int32)
        src_copy.wait()

        def level(r, slot):
            first = pl.multiple_of(slot * part, part)
            op_y = [ops[r, half, pl.ds(first, columns), :] for half in range(2)]
            spot = pl.multiple_of(slot * rows, rows)
            window = win[r, pl.ds(spot, rows), :].astype(jnp.float32)
            return window, op_y[0], op_y[1], spot

        def level_x(r, slot):
            tail = pl.multiple_of(slot * part + columns, piece)
            op_x = jnp.concatenate(
                [ops[r, half, pl.ds(tail, piece), :] for half in range(2)], axis=0
            )
            return op_x[:, :rows], op_x[:, rows:]

        def blocks(re, im):
            upper = jnp.concatenate([re, -im], axis=1)
            return jnp.concatenate([upper, jnp.concatenate([im, re], axis=1)], axis=0)

        def complex_sum(left, right):
            return left[:rows] - right[rows:], right[:rows] + left[rows:]

        def dot(a, b, dims):
            return lax.dot_general(a, b, (dims, ((), ())), preferred_element_type=jnp.float32)

        def down_section(section, place):
            r = section ^ here
            op_wait(r)

            def down_level(slot, place):
                window, y_re, y_im, _ = level(r, slot)
                x_re, x_im = level_x(r, slot)
                wave = waves[place].astype(jnp.float32)
                gain = 1.0 + window
                scaled = jnp.concatenate([gain * wave[:rows], gain * wave[rows:]], axis=0)
                op_first = blocks(x_re, x_im)
                turned_x[place] = blocks(x_re.T, x_im.T)
                middle = dot(op_first, scaled.astype(jnp.bfloat16), ((1,), (0,)))
                middle = middle.astype(jnp.bfloat16)
                moved_re, moved_im = complex_sum(
                    dot(middle, y_re, ((1,), (1,))), dot(middle, y_im, ((1,), (1,)))
                )
                waves[place + 1] = jnp.concatenate([moved_re, moved_im], axis=0).astype(
                    jnp.bfloat16
                )
                return place + 1

            return lax.fori_loop(0, counts[r], down_level, place)

        last = lax.fori_loop(0, sections, down_section, 0)
        wave_up[...] = jnp.zeros(wave_up.shape, wave_up.dtype)

        def up_section(step, place):
            r = (sections - 1 - step) ^ here
            count = counts[r]

            def up_level(inner, place):
                window, y_re, y_im, spot = level(r, count - 1 - inner)
                wave = waves[place - 1].astype(jnp.float32)
                back = dot(turned_x[place - 1], wave_up[...], ((1,), (0,))).astype(jnp.bfloat16)
                spread_re, spread_im = complex_sum(
                    dot(back, y_re, ((1,), (0,))), dot(back, y_im, ((1,), (0,)))
                )
                up_re = (window * wave[:rows] + spread_re).astype(jnp.bfloat16)
                up_im = (window * wave[rows:] + spread_im).astype(jnp.bfloat16)
                wave_up[:rows] = up_re
                wave_up[rows:] = up_im
                product = wave[:rows] * up_re.astype(jnp.float32)
                product += wave[rows:] * up_im.astype(jnp.float32)
                corr[r, pl.ds(spot, rows), :] = product.astype(corr.dtype)
                return place - 1

            place = lax.fori_loop(0, count, up_level, place)
            for out in range(sections):

                @pl.when(r == out)
                def _():
                    out_copy(out).start()

            return place

        lax.fori_loop(0, sections, up_section, last)
        for r in range(sections):
            out_copy(r).wait()


def join_kernel(group, first_ref, second_ref, out_ref, sem):
    plane = lax.rem(lax.axis_index("tile") // group, 2)
    copies = [
        pltpu.make_async_copy(first_ref, out_ref.at[plane], sem.at[0]),
        pltpu.make_async_copy(second_ref, out_ref.at[1 - plane], sem.at[1]),
    ]
    for copy in copies:
        copy.start()
    for copy in copies:
        copy.wait()


def place_kernel(shots, anchors_hbm, *refs):
    arrived, (left_out, own_out, anchors, sem) = refs[:-4], refs[-4:]
    load = pltpu.make_async_copy(anchors_hbm, anchors, sem)
    load.start()
    load.wait()
    section, tile = lax.axis_index("depth"), lax.axis_index("tile")
    columns = left_out.shape[1]
    canvas = None
    for q in range(shots):
        offset = anchors[lax.rem(section, shots) ^ q] - (tile - 1) * columns
        total = None
        for r in range(q, len(arrived), shots):
            value = arrived[r][...].astype(jnp.float32)
            total = value if total is None else total + value
        wide = jnp.concatenate([total, jnp.zeros_like(total)], axis=1)
        turned = pltpu.roll(wide, offset, 1)
        canvas = turned if canvas is None else canvas + turned
    left_out[...] = canvas[:, :columns].astype(left_out.dtype)
    own_out[...] = canvas[:, columns:]


def kept(array):
    return pltpu.with_memory_space_constraint(array, pltpu.HBM)


def on_device(source, anchors, counts, reflect, lateral_x, lateral_y):
    shots, _, rows, columns = source.shape
    slots = reflect.shape[1]
    sizes = (slots, rows, columns)
    plan = Plan(shots)
    sections, group = plan.sections, plan.group
    assert shots == 2
    bf16 = jnp.bfloat16
    smem = pl.BlockSpec(memory_space=pltpu.SMEM)
    vmem = pl.BlockSpec(memory_space=pltpu.VMEM)
    hbm = pl.BlockSpec(memory_space=pltpu.HBM)
    anywhere = pl.BlockSpec(memory_space=pl.ANY)

    def params(mib):
        return pltpu.CompilerParams(vmem_limit_bytes=mib * MIB)

    tile_reflect = reflect[0].reshape(slots * rows, columns)
    halo = lax.ppermute(tile_reflect, "tile", [(i, i + 1) for i in range(plan.tiles - 1)])
    half_rows, win_rows = slots * (columns + rows // 2), slots * rows + TAIL
    whole = jax.ShapeDtypeStruct((2 * half_rows + win_rows, columns), bf16)
    half = jax.ShapeDtypeStruct((half_rows, columns), bf16)
    alone = jax.ShapeDtypeStruct((win_rows, columns), bf16)
    *wholes, far_half = pl.pallas_call(
        functools.partial(pack_kernel, group, sizes),
        out_shape=[whole] * shots + [half],
        in_specs=[hbm, hbm],
        out_specs=[vmem] * (shots + 1),
        scratch_shapes=[
            pltpu.VMEM(lateral_x.shape[1:], bf16),
            pltpu.VMEM(lateral_y.shape[1:], bf16),
            pltpu.SemaphoreType.DMA((2,)),
        ],
        compiler_params=params(12),
        name="pack",
    )(kept(lateral_x[0]), kept(lateral_y[0]))
    last = sections - 1
    far_half = lax.ppermute(far_half, BOTH, plan.to_workers(last))
    *wholes, far_window = pl.pallas_call(
        functools.partial(window_kernel, shots, sizes),
        out_shape=[whole] * shots + [alone],
        in_specs=[hbm, smem, vmem, hbm] + [anywhere] * shots,
        out_specs=[anywhere] * shots + [vmem],
        scratch_shapes=[
            pltpu.SMEM((shots,), jnp.int32),
            pltpu.VMEM((slots * rows, columns), bf16),
            pltpu.VMEM((shots, win_rows, columns), bf16),
            pltpu.SemaphoreType.DMA((shots + 2,)),
        ],
        input_output_aliases={4 + q: q for q in range(shots)},
        compiler_params=params(8),
        name="windows",
    )(kept(anchors), counts, halo, kept(tile_reflect), *wholes)
    messages = [wholes[0]] + [
        lax.ppermute(wholes[r % shots], BOTH, plan.to_workers(r)) for r in range(1, last)
    ]
    far_window = lax.ppermute(far_window, BOTH, plan.to_workers(last))
    other_half = lax.ppermute(far_half, BOTH, plan.swap_workers())
    joined = pl.pallas_call(
        functools.partial(join_kernel, group),
        out_shape=jax.ShapeDtypeStruct((2, half_rows, columns), bf16),
        in_specs=[anywhere] * 2,
        out_specs=anywhere,
        scratch_shapes=[pltpu.SemaphoreType.DMA((2,))],
        compiler_params=params(2),
        cost_estimate=pl.CostEstimate(flops=4 * 10**9, bytes_accessed=4 * MIB, transcendentals=0),
        name="join",
    )(far_half, other_half)

    corr_shape = jax.ShapeDtypeStruct((slots * rows, columns), bf16)
    correlations = pl.pallas_call(
        functools.partial(sweep_kernel, sections, shots, group, sizes),
        out_shape=[corr_shape] * sections,
        in_specs=[hbm] + [anywhere] * (sections + 1),
        out_specs=[anywhere] * sections,
        scratch_shapes=[
            pltpu.VMEM((sections, 2, half_rows, columns), bf16),
            pltpu.VMEM((sections, win_rows, columns), bf16),
            pltpu.VMEM((sections * slots + 1, 2 * rows, columns), bf16),
            pltpu.VMEM((sections * slots, 2 * rows, 2 * rows), bf16),
            pltpu.VMEM((2 * rows, columns), bf16),
            pltpu.VMEM((sections, slots * rows, columns), bf16),
            pltpu.SMEM((sections,), jnp.int32),
            pltpu.SemaphoreType.DMA((sections, 2)),
            pltpu.SemaphoreType.DMA((sections,)),
            pltpu.SemaphoreType.DMA,
            pltpu.SemaphoreType.DMA((sections,)),
        ],
        compiler_params=params(14),
        name="sweep",
    )(
        kept(source.reshape(shots, 2 * rows, columns)), *messages, joined, far_window
    )

    arrived = [correlations[0]] + [
        lax.ppermute(correlations[r], BOTH, plan.from_workers(r)) for r in range(1, sections)
    ]
    left, own = pl.pallas_call(
        functools.partial(place_kernel, shots),
        out_shape=[corr_shape, jax.ShapeDtypeStruct((slots * rows, columns), jnp.float32)],
        in_specs=[hbm] + [vmem] * sections,
        out_specs=[vmem, vmem],
        scratch_shapes=[pltpu.SMEM((shots,), jnp.int32), pltpu.SemaphoreType.DMA],
        compiler_params=params(8),
        name="place",
    )(kept(anchors), *arrived)
    from_right = lax.ppermute(left, "tile", [(i + 1, i) for i in range(plan.tiles - 1)])
    image = own + from_right.astype(jnp.float32)
    return image.reshape(1, slots, rows, columns)


def solution(mesh):
    return jax.shard_map(
        on_device,
        mesh=mesh,
        in_specs=(
            P("tile", None, None, None),
            P("tile"),
            P("depth"),
            P("depth", None, None, "tile"),
            P("depth", None, None, None, None),
            P("depth", None, None, None, None),
        ),
        out_specs=P("depth", None, None, "tile"),
        check_vma=False,
    )
```

```python
import functools

import jax
import jax.numpy as jnp
from jax import lax
from jax.experimental import pallas as pl
from jax.experimental.pallas import tpu as pltpu
from jax.sharding import PartitionSpec as P

BOTH = ("depth", "tile")
MIB = 1024 * 1024
TAIL = 16


class Plan:
    def __init__(self, shots):
        self.sections = lax.axis_size("depth")
        self.tiles = lax.axis_size("tile")
        self.shots = shots
        self.group = self.sections // shots
        assert self.sections == 4 and self.group * shots == self.sections
        assert self.tiles % (2 * self.group) == 0

    def device(self, depth, tile):
        return depth * self.tiles + tile

    def bases(self):
        return range(0, self.tiles, self.group)

    def worker(self, base, w):
        return self.device(w, base + w // self.shots)

    def other(self, w, base):
        return self.device(w, base + (w // self.shots + 1) % self.group)

    def ops_to_workers(self, r):
        return [
            (self.other(w ^ r, base), self.worker(base, w))
            for base in self.bases()
            for w in range(self.sections)
        ]

    def swap_workers(self):
        return [
            (self.worker(base, w), self.worker((base // self.group ^ 1) * self.group, w))
            for base in self.bases()
            for w in range(self.sections)
        ]

    def to_workers(self, r):
        return [
            (self.device(w ^ r, base + w // self.shots), self.worker(base, w))
            for base in self.bases()
            for w in range(self.sections)
        ]

    def from_workers(self, r):
        return [(b, a) for a, b in self.to_workers(r)]


def pack_kernel(group, sizes, x_hbm, y_hbm, early, *refs):
    slots, rows, columns = sizes
    messages, (half_out, x_ref, y_ref, sem) = refs[:-4], refs[-4:]
    loads = [
        pltpu.make_async_copy(x_hbm, x_ref, sem.at[0]),
        pltpu.make_async_copy(y_hbm, y_ref, sem.at[1]),
    ]
    for load in loads:
        load.start()
    for load in loads:
        load.wait()
    piece = rows // 2
    part = columns + piece
    plane = lax.rem(lax.axis_index("tile") // group, 2)
    first = slots - 1
    for half in range(2):
        for slot in range(slots):
            op_x = jnp.concatenate(
                [x_ref[slot, i, half * piece : (half + 1) * piece, :] for i in range(2)], axis=1
            )
            op_y = y_ref[slot, half]
            if slot < first:
                early[half, slot * part : slot * part + columns, :] = op_y
                early[half, slot * part + columns : (slot + 1) * part, :] = op_x
            else:
                for out in messages:
                    out[half * part : half * part + columns, :] = op_y
                    out[half * part + columns : (half + 1) * part, :] = op_x
    half_out[: first * part, :] = early[plane]
    last = pl.multiple_of(plane * part, part)
    half_out[first * part :, :] = messages[0][pl.ds(last, part), :]


def window_kernel(shots, sizes, anchors_hbm, counts, left_ref, right_hbm, *refs):
    slots, rows, columns = sizes
    messages, (alone, anchors, right_ref, sem) = refs[shots : 2 * shots], refs[2 * shots :]
    loads = [
        pltpu.make_async_copy(anchors_hbm, anchors, sem.at[0]),
        pltpu.make_async_copy(right_hbm, right_ref, sem.at[1]),
    ]
    for load in loads:
        load.start()
    for load in loads:
        load.wait()
    section, tile = lax.axis_index("depth"), lax.axis_index("tile")
    both = jnp.concatenate(
        [left_ref[...].astype(jnp.float32), right_ref[...].astype(jnp.float32)], axis=1
    )
    tail = jnp.full((TAIL, columns), counts[0].astype(jnp.float32), jnp.float32)
    for q, message in enumerate(messages):
        offset = anchors[lax.rem(section, shots) ^ q] - (tile - 1) * columns
        back = lax.rem(2 * columns - offset, 2 * columns)
        window = pltpu.roll(both, back, 1)[:, :columns].astype(message.dtype)
        for out in [message] + ([alone] if q == shots - 1 else []):
            spot = out.shape[0] - TAIL - slots * rows
            out[spot : spot + slots * rows, :] = window
            out[spot + slots * rows :, :] = tail.astype(out.dtype)


def sweep_kernel(sections, shots, group, sizes, source_ref, *refs):
    slots, rows, columns = sizes
    earlies, refs = refs[: sections - 1], refs[sections - 1 :]
    lates, refs = refs[: sections - 1], refs[sections - 1 :]
    (far_half, other_half, far_window), refs = refs[:3], refs[3:]
    outs, refs = refs[:sections], refs[sections:]
    ops, win, waves, turned_x, wave_up, corr, counts, op_sem, win_sem, src_sem, out_sem = refs
    here, tile = lax.axis_index("depth"), lax.axis_index("tile")
    shot = lax.rem(here, shots)
    is_worker = (here // shots == lax.rem(tile, group)).astype(jnp.int32)
    plane = lax.rem(tile // group, 2)
    piece = rows // 2
    part = columns + piece
    half_rows = slots * part
    win_rows = slots * rows + TAIL

    def op_copies(r, half):
        place, sem = ops.at[r, half], op_sem.at[r, half]
        if r == sections - 1:
            place = ops.at[r, 1 - plane if half else plane]
            return [pltpu.make_async_copy(other_half if half else far_half, place, sem)]
        early, late = half_rows - part, lates[r].at[pl.ds(half * part, part), :]
        return [
            pltpu.make_async_copy(earlies[r].at[half], place.at[pl.ds(0, early), :], sem),
            pltpu.make_async_copy(late, place.at[pl.ds(early, part), :], sem),
        ]

    def op_wait(r):
        for half in range(2):
            pltpu.make_async_copy(far_half, ops.at[r, half], op_sem.at[r, half]).wait()

    def win_copy(r):
        message = lates[r] if r < sections - 1 else far_window
        first = message.shape[0] - win_rows
        return pltpu.make_async_copy(
            message.at[pl.ds(first, win_rows), :], win.at[r], win_sem.at[r]
        )

    def out_copy(r):
        return pltpu.make_async_copy(corr.at[r], outs[r], out_sem.at[r])

    @pl.when(is_worker == 0)
    def _():
        corr[0] = jnp.zeros(corr.shape[1:], corr.dtype)
        out_copy(0).start()
        out_copy(0).wait()

    @pl.when(is_worker != 0)
    def _():
        src_copy = pltpu.make_async_copy(source_ref.at[shot], waves.at[0], src_sem)
        src_copy.start()
        for r in range(sections):
            win_copy(r).start()
        for section in range(sections):
            for r in range(sections):

                @pl.when((section ^ here) == r)
                def _():
                    for half in range(2):
                        for copy in op_copies(r, half):
                            copy.start()

        corr[...] = jnp.zeros(corr.shape, corr.dtype)
        for r in range(sections):
            win_copy(r).wait()
        for r in range(sections):
            value = jnp.max(win[r, slots * rows :, :].astype(jnp.float32))
            counts[r] = value.astype(jnp.int32)
        src_copy.wait()

        def level(r, slot):
            first = pl.multiple_of(slot * part, part)
            op_y = [ops[r, half, pl.ds(first, columns), :] for half in range(2)]
            spot = pl.multiple_of(slot * rows, rows)
            window = win[r, pl.ds(spot, rows), :].astype(jnp.float32)
            return window, op_y[0], op_y[1], spot

        def level_x(r, slot):
            tail = pl.multiple_of(slot * part + columns, piece)
            op_x = jnp.concatenate(
                [ops[r, half, pl.ds(tail, piece), :] for half in range(2)], axis=0
            )
            return op_x[:, :rows], op_x[:, rows:]

        def blocks(re, im):
            upper = jnp.concatenate([re, -im], axis=1)
            return jnp.concatenate([upper, jnp.concatenate([im, re], axis=1)], axis=0)

        def complex_sum(left, right):
            return left[:rows] - right[rows:], right[:rows] + left[rows:]

        def dot(a, b, dims):
            return lax.dot_general(a, b, (dims, ((), ())), preferred_element_type=jnp.float32)

        def down_section(section, place):
            r = section ^ here
            op_wait(r)

            def down_level(slot, place):
                window, y_re, y_im, _ = level(r, slot)
                x_re, x_im = level_x(r, slot)
                wave = waves[place].astype(jnp.float32)
                gain = 1.0 + window
                scaled = jnp.concatenate([gain * wave[:rows], gain * wave[rows:]], axis=0)
                op_first = blocks(x_re, x_im)
                turned_x[place] = blocks(x_re.T, x_im.T)
                middle = dot(op_first, scaled.astype(jnp.bfloat16), ((1,), (0,)))
                middle = middle.astype(jnp.bfloat16)
                moved_re, moved_im = complex_sum(
                    dot(middle, y_re, ((1,), (1,))), dot(middle, y_im, ((1,), (1,)))
                )
                waves[place + 1] = jnp.concatenate([moved_re, moved_im], axis=0).astype(
                    jnp.bfloat16
                )
                return place + 1

            return lax.fori_loop(0, counts[r], down_level, place)

        last = lax.fori_loop(0, sections, down_section, 0)
        wave_up[...] = jnp.zeros(wave_up.shape, wave_up.dtype)

        def up_section(step, place):
            r = (sections - 1 - step) ^ here
            count = counts[r]

            def up_level(inner, place):
                window, y_re, y_im, spot = level(r, count - 1 - inner)
                wave = waves[place - 1].astype(jnp.float32)
                back = dot(turned_x[place - 1], wave_up[...], ((1,), (0,))).astype(jnp.bfloat16)
                spread_re, spread_im = complex_sum(
                    dot(back, y_re, ((1,), (0,))), dot(back, y_im, ((1,), (0,)))
                )
                up_re = (window * wave[:rows] + spread_re).astype(jnp.bfloat16)
                up_im = (window * wave[rows:] + spread_im).astype(jnp.bfloat16)
                wave_up[:rows] = up_re
                wave_up[rows:] = up_im
                product = wave[:rows] * up_re.astype(jnp.float32)
                product += wave[rows:] * up_im.astype(jnp.float32)
                corr[r, pl.ds(spot, rows), :] = product.astype(corr.dtype)
                return place - 1

            place = lax.fori_loop(0, count, up_level, place)
            for out in range(sections):

                @pl.when(r == out)
                def _():
                    out_copy(out).start()

            return place

        lax.fori_loop(0, sections, up_section, last)
        for r in range(sections):
            out_copy(r).wait()


def hold_kernel(*refs):
    pass


def place_kernel(shots, anchors_hbm, *refs):
    arrived, (left_out, own_out, anchors, sem) = refs[:-4], refs[-4:]
    load = pltpu.make_async_copy(anchors_hbm, anchors, sem)
    load.start()
    load.wait()
    section, tile = lax.axis_index("depth"), lax.axis_index("tile")
    columns = left_out.shape[1]
    canvas = None
    for q in range(shots):
        offset = anchors[lax.rem(section, shots) ^ q] - (tile - 1) * columns
        total = None
        for r in range(q, len(arrived), shots):
            value = arrived[r][...].astype(jnp.float32)
            total = value if total is None else total + value
        wide = jnp.concatenate([total, jnp.zeros_like(total)], axis=1)
        turned = pltpu.roll(wide, offset, 1)
        canvas = turned if canvas is None else canvas + turned
    left_out[...] = canvas[:, :columns].astype(left_out.dtype)
    own_out[...] = canvas[:, columns:]


def kept(array):
    return pltpu.with_memory_space_constraint(array, pltpu.HBM)


def on_device(source, anchors, counts, reflect, lateral_x, lateral_y):
    shots, _, rows, columns = source.shape
    slots = reflect.shape[1]
    sizes = (slots, rows, columns)
    plan = Plan(shots)
    sections, group = plan.sections, plan.group
    assert shots == 2
    bf16 = jnp.bfloat16
    smem = pl.BlockSpec(memory_space=pltpu.SMEM)
    vmem = pl.BlockSpec(memory_space=pltpu.VMEM)
    hbm = pl.BlockSpec(memory_space=pltpu.HBM)
    anywhere = pl.BlockSpec(memory_space=pl.ANY)

    def params(mib):
        return pltpu.CompilerParams(vmem_limit_bytes=mib * MIB)

    tile_reflect = reflect[0].reshape(slots * rows, columns)
    halo = lax.ppermute(tile_reflect, "tile", [(i, i + 1) for i in range(plan.tiles - 1)])
    part = columns + rows // 2
    half_rows, win_rows = slots * part, slots * rows + TAIL
    even = jax.ShapeDtypeStruct((2 * part + TAIL + win_rows, columns), bf16)
    odd = jax.ShapeDtypeStruct((2 * part + win_rows, columns), bf16)
    half = jax.ShapeDtypeStruct((half_rows, columns), bf16)
    alone = jax.ShapeDtypeStruct((win_rows, columns), bf16)
    early, even_late, odd_late, far_half = pl.pallas_call(
        functools.partial(pack_kernel, group, sizes),
        out_shape=[jax.ShapeDtypeStruct((2, half_rows - part, columns), bf16), even, odd, half],
        in_specs=[hbm, hbm],
        out_specs=[vmem] * 4,
        scratch_shapes=[
            pltpu.VMEM(lateral_x.shape[1:], bf16),
            pltpu.VMEM(lateral_y.shape[1:], bf16),
            pltpu.SemaphoreType.DMA((2,)),
        ],
        compiler_params=params(12),
        name="pack",
    )(kept(lateral_x[0]), kept(lateral_y[0]))
    last = sections - 1
    far_half = lax.ppermute(far_half, BOTH, plan.ops_to_workers(last))
    earlies = [early] + [
        lax.ppermute(early, BOTH, plan.ops_to_workers(r)) for r in range(1, last)
    ]
    even_late, odd_late, far_window = pl.pallas_call(
        functools.partial(window_kernel, shots, sizes),
        out_shape=[even, odd, alone],
        in_specs=[hbm, smem, vmem, hbm, vmem, vmem],
        out_specs=[vmem] * 3,
        scratch_shapes=[
            pltpu.SMEM((shots,), jnp.int32),
            pltpu.VMEM((slots * rows, columns), bf16),
            pltpu.SemaphoreType.DMA((2,)),
        ],
        input_output_aliases={4: 0, 5: 1},
        compiler_params=params(12),
        cost_estimate=pl.CostEstimate(flops=5 * 10**9, bytes_accessed=4 * MIB, transcendentals=0),
        name="windows",
    )(kept(anchors), counts, halo, kept(tile_reflect), even_late, odd_late)
    lates = [
        even_late,
        lax.ppermute(odd_late, BOTH, plan.to_workers(1)),
        lax.ppermute(even_late, BOTH, plan.to_workers(2)),
    ]
    far_window = lax.ppermute(far_window, BOTH, plan.to_workers(last))
    other_half = lax.ppermute(far_half, BOTH, plan.swap_workers())
    held = pl.pallas_call(
        hold_kernel,
        out_shape=[jax.ShapeDtypeStruct(early.shape, bf16)] * 2,
        in_specs=[anywhere] * 2,
        out_specs=[anywhere] * 2,
        input_output_aliases={0: 0, 1: 1},
        compiler_params=params(2),
        cost_estimate=pl.CostEstimate(flops=0, bytes_accessed=0, transcendentals=0),
        name="hold",
    )(*earlies[1:])
    earlies = [early, *held]
    corr_shape = jax.ShapeDtypeStruct((slots * rows, columns), bf16)
    correlations = pl.pallas_call(
        functools.partial(sweep_kernel, sections, shots, group, sizes),
        out_shape=[corr_shape] * sections,
        in_specs=[hbm] + [anywhere] * (2 * sections + 1),
        out_specs=[anywhere] * sections,
        scratch_shapes=[
            pltpu.VMEM((sections, 2, half_rows, columns), bf16),
            pltpu.VMEM((sections, win_rows, columns), bf16),
            pltpu.VMEM((sections * slots + 1, 2 * rows, columns), bf16),
            pltpu.VMEM((sections * slots, 2 * rows, 2 * rows), bf16),
            pltpu.VMEM((2 * rows, columns), bf16),
            pltpu.VMEM((sections, slots * rows, columns), bf16),
            pltpu.SMEM((sections,), jnp.int32),
            pltpu.SemaphoreType.DMA((sections, 2)),
            pltpu.SemaphoreType.DMA((sections,)),
            pltpu.SemaphoreType.DMA,
            pltpu.SemaphoreType.DMA((sections,)),
        ],
        compiler_params=params(14),
        name="sweep",
    )(
        kept(source.reshape(shots, 2 * rows, columns)), *earlies, *lates, far_half,
        other_half, far_window
    )

    arrived = [correlations[0]] + [
        lax.ppermute(correlations[r], BOTH, plan.from_workers(r)) for r in range(1, sections)
    ]
    left, own = pl.pallas_call(
        functools.partial(place_kernel, shots),
        out_shape=[corr_shape, jax.ShapeDtypeStruct((slots * rows, columns), jnp.float32)],
        in_specs=[hbm] + [vmem] * sections,
        out_specs=[vmem, vmem],
        scratch_shapes=[pltpu.SMEM((shots,), jnp.int32), pltpu.SemaphoreType.DMA],
        compiler_params=params(8),
        name="place",
    )(kept(anchors), *arrived)
    from_right = lax.ppermute(left, "tile", [(i + 1, i) for i in range(plan.tiles - 1)])
    image = own + from_right.astype(jnp.float32)
    return image.reshape(1, slots, rows, columns)


def solution(mesh):
    return jax.shard_map(
        on_device,
        mesh=mesh,
        in_specs=(
            P("tile", None, None, None),
            P("tile"),
            P("depth"),
            P("depth", None, None, "tile"),
            P("depth", None, None, None, None),
            P("depth", None, None, None, None),
        ),
        out_specs=P("depth", None, None, "tile"),
        check_vma=False,
    )
```

```python
import functools

import jax
import jax.numpy as jnp
from jax import lax
from jax.experimental import pallas as pl
from jax.experimental.pallas import tpu as pltpu
from jax.sharding import PartitionSpec as P

BOTH = ("depth", "tile")
MIB = 1024 * 1024
TAIL = 16


class Plan:
    def __init__(self, shots):
        self.sections = lax.axis_size("depth")
        self.tiles = lax.axis_size("tile")
        self.shots = shots
        self.group = self.sections // shots
        assert self.sections == 4 and self.group * shots == self.sections
        assert self.tiles % (2 * self.group) == 0

    def device(self, depth, tile):
        return depth * self.tiles + tile

    def bases(self):
        return range(0, self.tiles, self.group)

    def worker(self, base, w):
        return self.device(w, base + w // self.shots)

    def swap_workers(self):
        return [
            (self.worker(base, w), self.worker((base // self.group ^ 1) * self.group, w))
            for base in self.bases()
            for w in range(self.sections)
        ]

    def to_workers(self, r):
        return [
            (self.device(w ^ r, base + w // self.shots), self.worker(base, w))
            for base in self.bases()
            for w in range(self.sections)
        ]

    def from_workers(self, r, left):
        return [
            (self.worker(base, w), self.device(w ^ r, base + w // self.shots - left))
            for base in self.bases()
            for w in range(self.sections)
            if base + w // self.shots >= left
        ]


def pack_kernel(group, sizes, x_hbm, y_hbm, *refs):
    slots, rows, columns = sizes
    outs, (x_ref, y_ref, sem) = refs[:-3], refs[-3:]
    loads = [
        pltpu.make_async_copy(x_hbm, x_ref, sem.at[0]),
        pltpu.make_async_copy(y_hbm, y_ref, sem.at[1]),
    ]
    for load in loads:
        load.start()
    for load in loads:
        load.wait()
    piece = rows // 2
    part = columns + piece
    half_rows = slots * part
    for half in range(2):
        for slot in range(slots):
            spot = half * half_rows + slot * part
            op_x = jnp.concatenate(
                [x_ref[slot, i, half * piece : (half + 1) * piece, :] for i in range(2)], axis=1
            )
            for out in outs[:-1]:
                out[spot : spot + columns, :] = y_ref[slot, half]
                out[spot + columns : spot + part, :] = op_x
    plane = lax.rem(lax.axis_index("tile") // group, 2)
    first = pl.multiple_of(plane * half_rows, half_rows)
    outs[-1][:half_rows] = outs[0][pl.ds(first, half_rows), :]


def window_kernel(shots, sizes, anchors_hbm, counts, left_ref, right_hbm, *refs):
    slots, rows, columns = sizes
    messages, (alone, anchors, right_ref, sem) = refs[shots : 2 * shots], refs[2 * shots :]
    loads = [
        pltpu.make_async_copy(anchors_hbm, anchors, sem.at[0]),
        pltpu.make_async_copy(right_hbm, right_ref, sem.at[1]),
    ]
    for load in loads:
        load.start()
    for load in loads:
        load.wait()
    section, tile = lax.axis_index("depth"), lax.axis_index("tile")
    both = jnp.concatenate(
        [left_ref[...].astype(jnp.float32), right_ref[...].astype(jnp.float32)], axis=1
    )
    tail = jnp.full((TAIL, columns), counts[0].astype(jnp.float32), jnp.float32)
    for q, message in enumerate(messages):
        offset = anchors[lax.rem(section, shots) ^ q] - (tile - 1) * columns
        back = lax.rem(2 * columns - offset, 2 * columns)
        window = pltpu.roll(both, back, 1)[:, :columns].astype(message.dtype)
        for out in [message] + ([alone] if q == shots - 1 else []):
            spot = out.shape[0] - TAIL - slots * rows
            out[spot : spot + slots * rows, :] = window
            out[spot + slots * rows :, :] = tail.astype(out.dtype)


def sweep_kernel(sections, shots, group, sizes, source_ref, anchors_hbm, *refs):
    slots, rows, columns = sizes
    messages, refs = refs[: sections + 1], refs[sections + 1 :]
    outs, refs = refs[: 2 * sections], refs[2 * sections :]
    ops, win, waves, turned_x, wave_up, corr, counts, anchors, *sems = refs
    op_sem, win_sem, src_sem, anchor_sem, out_sem = sems
    here, tile = lax.axis_index("depth"), lax.axis_index("tile")
    shot = lax.rem(here, shots)
    is_worker = (here // shots == lax.rem(tile, group)).astype(jnp.int32)
    piece = rows // 2
    part = columns + piece
    half_rows = slots * part
    win_rows = slots * rows + TAIL

    def op_copy(r, half):
        message = messages[r]
        if r < sections - 1:
            message = message.at[pl.ds(half * half_rows, half_rows), :]
        else:
            message = message.at[half]
        return pltpu.make_async_copy(message, ops.at[r, half], op_sem.at[r, half])

    def op_wait(r):
        for half in range(2):
            pltpu.make_async_copy(
                messages[0].at[pl.ds(0, half_rows), :], ops.at[r, half], op_sem.at[r, half]
            ).wait()

    def win_copy(r):
        message = messages[r] if r < sections - 1 else messages[-1]
        first = message.shape[0] - win_rows
        return pltpu.make_async_copy(
            message.at[pl.ds(first, win_rows), :], win.at[r], win_sem.at[r]
        )

    def out_copy(r, left):
        return pltpu.make_async_copy(
            corr.at[r, left], outs[2 * r + left], out_sem.at[r, left]
        )

    @pl.when(is_worker == 0)
    def _():
        corr[0, 0] = jnp.zeros(corr.shape[2:], corr.dtype)
        out_copy(0, 0).start()
        out_copy(0, 0).wait()

    @pl.when(is_worker != 0)
    def _():
        src_copy = pltpu.make_async_copy(source_ref.at[shot], waves.at[0], src_sem)
        anchor_copy = pltpu.make_async_copy(anchors_hbm, anchors, anchor_sem)
        src_copy.start()
        anchor_copy.start()
        for r in range(sections):
            win_copy(r).start()
        for section in range(sections):
            for r in range(sections):

                @pl.when((section ^ here) == r)
                def _():
                    for half in range(2):
                        op_copy(r, half).start()

        corr[...] = jnp.zeros(corr.shape, corr.dtype)
        for r in range(sections):
            win_copy(r).wait()
        for r in range(sections):
            value = jnp.max(win[r, slots * rows :, :].astype(jnp.float32))
            counts[r] = value.astype(jnp.int32)
        src_copy.wait()
        anchor_copy.wait()
        offset = anchors[shot] - (tile - 1) * columns

        def level(r, slot):
            first = pl.multiple_of(slot * part, part)
            op_y = [ops[r, half, pl.ds(first, columns), :] for half in range(2)]
            spot = pl.multiple_of(slot * rows, rows)
            window = win[r, pl.ds(spot, rows), :].astype(jnp.float32)
            return window, op_y[0], op_y[1], spot

        def level_x(r, slot):
            tail = pl.multiple_of(slot * part + columns, piece)
            op_x = jnp.concatenate(
                [ops[r, half, pl.ds(tail, piece), :] for half in range(2)], axis=0
            )
            return op_x[:, :rows], op_x[:, rows:]

        def blocks(re, im):
            upper = jnp.concatenate([re, -im], axis=1)
            return jnp.concatenate([upper, jnp.concatenate([im, re], axis=1)], axis=0)

        def complex_sum(both):
            with_re, with_im = both[:, :columns], both[:, columns:]
            return with_re[:rows] - with_im[rows:], with_im[:rows] + with_re[rows:]

        def dot(a, b, dims):
            return lax.dot_general(a, b, (dims, ((), ())), preferred_element_type=jnp.float32)

        def down_section(section, place):
            r = section ^ here
            op_wait(r)

            def down_level(slot, place):
                window, y_re, y_im, _ = level(r, slot)
                x_re, x_im = level_x(r, slot)
                wave = waves[place].astype(jnp.float32)
                gain = 1.0 + window
                scaled = jnp.concatenate([gain * wave[:rows], gain * wave[rows:]], axis=0)
                op_first = blocks(x_re, x_im)
                turned_x[place] = blocks(x_re.T, x_im.T)
                middle = dot(op_first, scaled.astype(jnp.bfloat16), ((1,), (0,)))
                middle = middle.astype(jnp.bfloat16)
                both_y = jnp.concatenate([y_re, y_im], axis=0)
                moved_re, moved_im = complex_sum(dot(middle, both_y, ((1,), (1,))))
                waves[place + 1] = jnp.concatenate([moved_re, moved_im], axis=0).astype(
                    jnp.bfloat16
                )
                return place + 1

            return lax.fori_loop(0, counts[r], down_level, place)

        last = lax.fori_loop(0, sections, down_section, 0)
        wave_up[...] = jnp.zeros(wave_up.shape, wave_up.dtype)

        def up_section(step, place):
            r = (sections - 1 - step) ^ here
            count = counts[r]

            def up_level(inner, place):
                window, y_re, y_im, spot = level(r, count - 1 - inner)
                wave = waves[place - 1].astype(jnp.float32)
                back = dot(turned_x[place - 1], wave_up[...], ((1,), (0,))).astype(jnp.bfloat16)
                both_y = jnp.concatenate([y_re, y_im], axis=1)
                spread_re, spread_im = complex_sum(dot(back, both_y, ((1,), (0,))))
                up_re = (window * wave[:rows] + spread_re).astype(jnp.bfloat16)
                up_im = (window * wave[rows:] + spread_im).astype(jnp.bfloat16)
                wave_up[:rows] = up_re
                wave_up[rows:] = up_im
                product = wave[:rows] * up_re.astype(jnp.float32)
                product += wave[rows:] * up_im.astype(jnp.float32)
                wide = jnp.concatenate([product, jnp.zeros_like(product)], axis=1)
                placed = pltpu.roll(wide, offset, 1).astype(corr.dtype)
                corr[r, 0, pl.ds(spot, rows), :] = placed[:, columns:]
                corr[r, 1, pl.ds(spot, rows), :] = placed[:, :columns]
                return place - 1

            place = lax.fori_loop(0, count, up_level, place)
            for out in range(sections):

                @pl.when(r == out)
                def _():
                    for left in range(2):
                        out_copy(out, left).start()

            return place

        lax.fori_loop(0, sections, up_section, last)
        for r in range(sections):
            for left in range(2):
                out_copy(r, left).wait()


def join_kernel(group, first_ref, second_ref, out_ref, sem):
    plane = lax.rem(lax.axis_index("tile") // group, 2)
    copies = [
        pltpu.make_async_copy(first_ref, out_ref.at[plane], sem.at[0]),
        pltpu.make_async_copy(second_ref, out_ref.at[1 - plane], sem.at[1]),
    ]
    for copy in copies:
        copy.start()
    for copy in copies:
        copy.wait()


def kept(array):
    return pltpu.with_memory_space_constraint(array, pltpu.HBM)


def on_device(source, anchors, counts, reflect, lateral_x, lateral_y):
    shots, _, rows, columns = source.shape
    slots = reflect.shape[1]
    sizes = (slots, rows, columns)
    plan = Plan(shots)
    sections, group = plan.sections, plan.group
    assert shots == 2
    bf16 = jnp.bfloat16
    smem = pl.BlockSpec(memory_space=pltpu.SMEM)
    vmem = pl.BlockSpec(memory_space=pltpu.VMEM)
    hbm = pl.BlockSpec(memory_space=pltpu.HBM)
    anywhere = pl.BlockSpec(memory_space=pl.ANY)

    def params(mib):
        return pltpu.CompilerParams(vmem_limit_bytes=mib * MIB)

    tile_reflect = reflect[0].reshape(slots * rows, columns)
    halo = lax.ppermute(tile_reflect, "tile", [(i, i + 1) for i in range(plan.tiles - 1)])
    half_rows, win_rows = slots * (columns + rows // 2), slots * rows + TAIL
    even = jax.ShapeDtypeStruct((2 * half_rows + TAIL + win_rows, columns), bf16)
    odd = jax.ShapeDtypeStruct((2 * half_rows + win_rows, columns), bf16)
    half = jax.ShapeDtypeStruct((half_rows, columns), bf16)
    alone = jax.ShapeDtypeStruct((win_rows, columns), bf16)
    *wholes, far_half = pl.pallas_call(
        functools.partial(pack_kernel, group, sizes),
        out_shape=[even, odd, half],
        in_specs=[hbm, hbm],
        out_specs=[vmem] * (shots + 1),
        scratch_shapes=[
            pltpu.VMEM(lateral_x.shape[1:], bf16),
            pltpu.VMEM(lateral_y.shape[1:], bf16),
            pltpu.SemaphoreType.DMA((2,)),
        ],
        compiler_params=params(12),
        name="pack",
    )(kept(lateral_x[0]), kept(lateral_y[0]))
    last = sections - 1
    far_half = lax.ppermute(far_half, BOTH, plan.to_workers(last))
    *wholes, far_window = pl.pallas_call(
        functools.partial(window_kernel, shots, sizes),
        out_shape=[even, odd, alone],
        in_specs=[hbm, smem, vmem, hbm, vmem, vmem],
        out_specs=[vmem] * 3,
        scratch_shapes=[
            pltpu.SMEM((shots,), jnp.int32),
            pltpu.VMEM((slots * rows, columns), bf16),
            pltpu.SemaphoreType.DMA((2,)),
        ],
        input_output_aliases={4: 0, 5: 1},
        compiler_params=params(12),
        name="windows",
    )(kept(anchors), counts, halo, kept(tile_reflect), *wholes)
    messages = [wholes[0]] + [
        lax.ppermute(wholes[r % shots], BOTH, plan.to_workers(r)) for r in range(1, last)
    ]
    far_window = lax.ppermute(far_window, BOTH, plan.to_workers(last))
    other_half = lax.ppermute(far_half, BOTH, plan.swap_workers())
    joined = pl.pallas_call(
        functools.partial(join_kernel, group),
        out_shape=jax.ShapeDtypeStruct((2, half_rows, columns), bf16),
        in_specs=[anywhere] * 2,
        out_specs=anywhere,
        scratch_shapes=[pltpu.SemaphoreType.DMA((2,))],
        compiler_params=params(2),
        cost_estimate=pl.CostEstimate(flops=4 * 10**9, bytes_accessed=4 * MIB, transcendentals=0),
        name="join",
    )(far_half, other_half)

    corr_shape = jax.ShapeDtypeStruct((slots * rows, columns), bf16)
    correlations = pl.pallas_call(
        functools.partial(sweep_kernel, sections, shots, group, sizes),
        out_shape=[corr_shape] * (2 * sections),
        in_specs=[hbm, hbm] + [anywhere] * (sections + 1),
        out_specs=[anywhere] * (2 * sections),
        scratch_shapes=[
            pltpu.VMEM((sections, 2, half_rows, columns), bf16),
            pltpu.VMEM((sections, win_rows, columns), bf16),
            pltpu.VMEM((sections * slots + 1, 2 * rows, columns), bf16),
            pltpu.VMEM((sections * slots, 2 * rows, 2 * rows), bf16),
            pltpu.VMEM((2 * rows, columns), bf16),
            pltpu.VMEM((sections, 2, slots * rows, columns), bf16),
            pltpu.SMEM((sections,), jnp.int32),
            pltpu.SMEM((shots,), jnp.int32),
            pltpu.SemaphoreType.DMA((sections, 2)),
            pltpu.SemaphoreType.DMA((sections,)),
            pltpu.SemaphoreType.DMA,
            pltpu.SemaphoreType.DMA,
            pltpu.SemaphoreType.DMA((sections, 2)),
        ],
        compiler_params=params(16),
        name="sweep",
    )(
        kept(source.reshape(shots, 2 * rows, columns)), kept(anchors), *messages, joined, far_window
    )

    image = correlations[0].astype(jnp.float32)
    for r in range(sections):
        for left in range(2):
            if r or left:
                part = lax.ppermute(
                    correlations[2 * r + left], BOTH, plan.from_workers(r, left)
                )
                image = image + part.astype(jnp.float32)
    return image.reshape(1, slots, rows, columns)


def solution(mesh):
    return jax.shard_map(
        on_device,
        mesh=mesh,
        in_specs=(
            P("tile", None, None, None),
            P("tile"),
            P("depth"),
            P("depth", None, None, "tile"),
            P("depth", None, None, None, None),
            P("depth", None, None, None, None),
        ),
        out_specs=P("depth", None, None, "tile"),
        check_vma=False,
    )
```

```python
import functools

import jax
import jax.numpy as jnp
from jax import lax
from jax.experimental import pallas as pl
from jax.experimental.pallas import tpu as pltpu
from jax.sharding import PartitionSpec as P

BOTH = ("depth", "tile")
MIB = 1024 * 1024
TAIL = 16


class Plan:
    def __init__(self, shots):
        self.sections = lax.axis_size("depth")
        self.tiles = lax.axis_size("tile")
        self.shots = shots
        self.group = self.sections // shots
        assert self.sections == 4 and self.group * shots == self.sections
        assert self.tiles % (2 * self.group) == 0

    def device(self, depth, tile):
        return depth * self.tiles + tile

    def bases(self):
        return range(0, self.tiles, self.group)

    def worker(self, base, w):
        return self.device(w, base + w // self.shots)

    def swap_workers(self):
        return [
            (self.worker(base, w), self.worker((base // self.group ^ 1) * self.group, w))
            for base in self.bases()
            for w in range(self.sections)
        ]

    def to_workers(self, r):
        return [
            (self.device(w ^ r, base + w // self.shots), self.worker(base, w))
            for base in self.bases()
            for w in range(self.sections)
        ]

    def from_workers(self, r):
        return [(b, a) for a, b in self.to_workers(r)]


def pack_kernel(group, sizes, x_hbm, y_hbm, *refs):
    slots, rows, columns = sizes
    outs, (x_ref, y_ref, sem) = refs[:-3], refs[-3:]
    loads = [
        pltpu.make_async_copy(x_hbm, x_ref, sem.at[0]),
        pltpu.make_async_copy(y_hbm, y_ref, sem.at[1]),
    ]
    for load in loads:
        load.start()
    for load in loads:
        load.wait()
    piece = rows // 2
    part = columns + piece
    half_rows = slots * part
    for half in range(2):
        for slot in range(slots):
            spot = half * half_rows + slot * part
            op_x = jnp.concatenate(
                [x_ref[slot, i, half * piece : (half + 1) * piece, :] for i in range(2)], axis=1
            )
            for out in outs[:-1]:
                out[spot : spot + columns, :] = y_ref[slot, half]
                out[spot + columns : spot + part, :] = op_x
    plane = lax.rem(lax.axis_index("tile") // group, 2)
    first = pl.multiple_of(plane * half_rows, half_rows)
    outs[-1][:half_rows] = outs[0][pl.ds(first, half_rows), :]


def window_kernel(shots, sizes, anchors_hbm, counts, left_ref, right_hbm, *refs):
    slots, rows, columns = sizes
    messages, (alone, anchors, right_ref, sem) = refs[shots : 2 * shots], refs[2 * shots :]
    loads = [
        pltpu.make_async_copy(anchors_hbm, anchors, sem.at[0]),
        pltpu.make_async_copy(right_hbm, right_ref, sem.at[1]),
    ]
    for load in loads:
        load.start()
    for load in loads:
        load.wait()
    section, tile = lax.axis_index("depth"), lax.axis_index("tile")
    both = jnp.concatenate(
        [left_ref[...].astype(jnp.float32), right_ref[...].astype(jnp.float32)], axis=1
    )
    tail = jnp.full((TAIL, columns), counts[0].astype(jnp.float32), jnp.float32)
    for q, message in enumerate(messages):
        offset = anchors[lax.rem(section, shots) ^ q] - (tile - 1) * columns
        back = lax.rem(2 * columns - offset, 2 * columns)
        window = pltpu.roll(both, back, 1)[:, :columns].astype(message.dtype)
        for out in [message] + ([alone] if q == shots - 1 else []):
            spot = out.shape[0] - TAIL - slots * rows
            out[spot : spot + slots * rows, :] = window
            out[spot + slots * rows :, :] = tail.astype(out.dtype)


def sweep_kernel(sections, shots, group, sizes, source_ref, *refs):
    slots, rows, columns = sizes
    messages, refs = refs[: sections + 1], refs[sections + 1 :]
    outs, refs = refs[:sections], refs[sections:]
    ops, win, waves, turned_x, wave_up, corr, counts, op_sem, win_sem, src_sem, out_sem = refs
    here, tile = lax.axis_index("depth"), lax.axis_index("tile")
    shot = lax.rem(here, shots)
    is_worker = (here // shots == lax.rem(tile, group)).astype(jnp.int32)
    piece = rows // 2
    part = columns + piece
    half_rows = slots * part
    win_rows = slots * rows + TAIL

    def op_copy(r, half):
        message = messages[r]
        if r < sections - 1:
            message = message.at[pl.ds(half * half_rows, half_rows), :]
        else:
            message = message.at[half]
        return pltpu.make_async_copy(message, ops.at[r, half], op_sem.at[r, half])

    def op_wait(r):
        for half in range(2):
            pltpu.make_async_copy(
                messages[0].at[pl.ds(0, half_rows), :], ops.at[r, half], op_sem.at[r, half]
            ).wait()

    def win_copy(r):
        message = messages[r] if r < sections - 1 else messages[-1]
        first = message.shape[0] - win_rows
        return pltpu.make_async_copy(
            message.at[pl.ds(first, win_rows), :], win.at[r], win_sem.at[r]
        )

    def out_copy(r):
        place = outs[r].at[pl.ds(0, slots * rows), :]
        return pltpu.make_async_copy(corr.at[r], place, out_sem.at[r])

    @pl.when(is_worker == 0)
    def _():
        corr[0] = jnp.zeros(corr.shape[1:], corr.dtype)
        out_copy(0).start()
        out_copy(0).wait()

    @pl.when(is_worker != 0)
    def _():
        src_copy = pltpu.make_async_copy(source_ref.at[shot], waves.at[0], src_sem)
        src_copy.start()
        for r in range(sections):
            win_copy(r).start()
        for section in range(sections):
            for r in range(sections):

                @pl.when((section ^ here) == r)
                def _():
                    for half in range(2):
                        op_copy(r, half).start()

        corr[...] = jnp.zeros(corr.shape, corr.dtype)
        for r in range(sections):
            win_copy(r).wait()
        for r in range(sections):
            value = jnp.max(win[r, slots * rows :, :].astype(jnp.float32))
            counts[r] = value.astype(jnp.int32)
        src_copy.wait()

        def level(r, slot):
            first = pl.multiple_of(slot * part, part)
            op_y = [ops[r, half, pl.ds(first, columns), :] for half in range(2)]
            spot = pl.multiple_of(slot * rows, rows)
            window = win[r, pl.ds(spot, rows), :].astype(jnp.float32)
            return window, op_y[0], op_y[1], spot

        def level_x(r, slot):
            tail = pl.multiple_of(slot * part + columns, piece)
            op_x = jnp.concatenate(
                [ops[r, half, pl.ds(tail, piece), :] for half in range(2)], axis=0
            )
            return op_x[:, :rows], op_x[:, rows:]

        def blocks(re, im):
            upper = jnp.concatenate([re, -im], axis=1)
            return jnp.concatenate([upper, jnp.concatenate([im, re], axis=1)], axis=0)

        def complex_sum(both):
            with_re, with_im = both[:, :columns], both[:, columns:]
            return with_re[:rows] - with_im[rows:], with_im[:rows] + with_re[rows:]

        def dot(a, b, dims):
            return lax.dot_general(a, b, (dims, ((), ())), preferred_element_type=jnp.float32)

        def down_section(section, place):
            r = section ^ here
            op_wait(r)

            def down_level(slot, place):
                window, y_re, y_im, _ = level(r, slot)
                x_re, x_im = level_x(r, slot)
                wave = waves[place].astype(jnp.float32)
                gain = 1.0 + window
                scaled = jnp.concatenate([gain * wave[:rows], gain * wave[rows:]], axis=0)
                op_first = blocks(x_re, x_im)
                turned_x[place] = blocks(x_re.T, x_im.T)
                middle = dot(op_first, scaled.astype(jnp.bfloat16), ((1,), (0,)))
                middle = middle.astype(jnp.bfloat16)
                both_y = jnp.concatenate([y_re, y_im], axis=0)
                moved_re, moved_im = complex_sum(dot(middle, both_y, ((1,), (1,))))
                waves[place + 1] = jnp.concatenate([moved_re, moved_im], axis=0).astype(
                    jnp.bfloat16
                )
                return place + 1

            return lax.fori_loop(0, counts[r], down_level, place)

        last = lax.fori_loop(0, sections, down_section, 0)
        wave_up[...] = jnp.zeros(wave_up.shape, wave_up.dtype)

        def up_section(step, place):
            r = (sections - 1 - step) ^ here
            count = counts[r]

            def up_level(inner, place):
                window, y_re, y_im, spot = level(r, count - 1 - inner)
                wave = waves[place - 1].astype(jnp.float32)
                back = dot(turned_x[place - 1], wave_up[...], ((1,), (0,))).astype(jnp.bfloat16)
                both_y = jnp.concatenate([y_re, y_im], axis=1)
                spread_re, spread_im = complex_sum(dot(back, both_y, ((1,), (0,))))
                up_re = (window * wave[:rows] + spread_re).astype(jnp.bfloat16)
                up_im = (window * wave[rows:] + spread_im).astype(jnp.bfloat16)
                wave_up[:rows] = up_re
                wave_up[rows:] = up_im
                product = wave[:rows] * up_re.astype(jnp.float32)
                product += wave[rows:] * up_im.astype(jnp.float32)
                corr[r, pl.ds(spot, rows), :] = product.astype(corr.dtype)
                return place - 1

            place = lax.fori_loop(0, count, up_level, place)
            for out in range(sections):

                @pl.when(r == out)
                def _():
                    out_copy(out).start()

            return place

        lax.fori_loop(0, sections, up_section, last)
        for r in range(sections):
            out_copy(r).wait()


def join_kernel(group, first_ref, second_ref, out_ref, sem):
    plane = lax.rem(lax.axis_index("tile") // group, 2)
    copies = [
        pltpu.make_async_copy(first_ref, out_ref.at[plane], sem.at[0]),
        pltpu.make_async_copy(second_ref, out_ref.at[1 - plane], sem.at[1]),
    ]
    for copy in copies:
        copy.start()
    for copy in copies:
        copy.wait()


def place_kernel(shots, anchors, *refs):
    arrived, (left_out, own_out) = refs[:-2], refs[-2:]
    section, tile = lax.axis_index("depth"), lax.axis_index("tile")
    places, columns = left_out.shape
    canvas = None
    for q in range(shots):
        offset = anchors[lax.rem(section, shots) ^ q] - (tile - 1) * columns
        total = None
        for r in range(q, len(arrived), shots):
            value = arrived[r][:places, :].astype(jnp.float32)
            total = value if total is None else total + value
        wide = jnp.concatenate([total, jnp.zeros_like(total)], axis=1)
        turned = pltpu.roll(wide, offset, 1)
        canvas = turned if canvas is None else canvas + turned
    left_out[...] = canvas[:, :columns].astype(left_out.dtype)
    own_out[...] = canvas[:, columns:]


def kept(array):
    return pltpu.with_memory_space_constraint(array, pltpu.HBM)


def on_device(source, anchors, counts, reflect, lateral_x, lateral_y):
    shots, _, rows, columns = source.shape
    slots = reflect.shape[1]
    sizes = (slots, rows, columns)
    plan = Plan(shots)
    sections, group = plan.sections, plan.group
    assert shots == 2
    bf16 = jnp.bfloat16
    smem = pl.BlockSpec(memory_space=pltpu.SMEM)
    vmem = pl.BlockSpec(memory_space=pltpu.VMEM)
    hbm = pl.BlockSpec(memory_space=pltpu.HBM)
    anywhere = pl.BlockSpec(memory_space=pl.ANY)

    def params(mib):
        return pltpu.CompilerParams(vmem_limit_bytes=mib * MIB)

    tile_reflect = reflect[0].reshape(slots * rows, columns)
    halo = lax.ppermute(tile_reflect, "tile", [(i, i + 1) for i in range(plan.tiles - 1)])
    half_rows, win_rows = slots * (columns + rows // 2), slots * rows + TAIL
    even = jax.ShapeDtypeStruct((2 * half_rows + TAIL + win_rows, columns), bf16)
    odd = jax.ShapeDtypeStruct((2 * half_rows + win_rows, columns), bf16)
    half = jax.ShapeDtypeStruct((half_rows, columns), bf16)
    alone = jax.ShapeDtypeStruct((win_rows, columns), bf16)
    *wholes, far_half = pl.pallas_call(
        functools.partial(pack_kernel, group, sizes),
        out_shape=[even, odd, half],
        in_specs=[hbm, hbm],
        out_specs=[vmem] * (shots + 1),
        scratch_shapes=[
            pltpu.VMEM(lateral_x.shape[1:], bf16),
            pltpu.VMEM(lateral_y.shape[1:], bf16),
            pltpu.SemaphoreType.DMA((2,)),
        ],
        compiler_params=params(12),
        name="pack",
    )(kept(lateral_x[0]), kept(lateral_y[0]))
    last = sections - 1
    far_half = lax.ppermute(far_half, BOTH, plan.to_workers(last))
    *wholes, far_window = pl.pallas_call(
        functools.partial(window_kernel, shots, sizes),
        out_shape=[even, odd, alone],
        in_specs=[hbm, smem, vmem, hbm, vmem, vmem],
        out_specs=[vmem] * 3,
        scratch_shapes=[
            pltpu.SMEM((shots,), jnp.int32),
            pltpu.VMEM((slots * rows, columns), bf16),
            pltpu.SemaphoreType.DMA((2,)),
        ],
        input_output_aliases={4: 0, 5: 1},
        compiler_params=params(12),
        name="windows",
    )(kept(anchors), counts, halo, kept(tile_reflect), *wholes)
    messages = [wholes[0]] + [
        lax.ppermute(wholes[r % shots], BOTH, plan.to_workers(r)) for r in range(1, last)
    ]
    far_window = lax.ppermute(far_window, BOTH, plan.to_workers(last))
    other_half = lax.ppermute(far_half, BOTH, plan.swap_workers())
    joined = pl.pallas_call(
        functools.partial(join_kernel, group),
        out_shape=jax.ShapeDtypeStruct((2, half_rows, columns), bf16),
        in_specs=[anywhere] * 2,
        out_specs=anywhere,
        scratch_shapes=[pltpu.SemaphoreType.DMA((2,))],
        compiler_params=params(2),
        cost_estimate=pl.CostEstimate(flops=4 * 10**9, bytes_accessed=4 * MIB, transcendentals=0),
        name="join",
    )(far_half, other_half)

    corr_shape = jax.ShapeDtypeStruct((slots * rows, columns), bf16)
    correlations = pl.pallas_call(
        functools.partial(sweep_kernel, sections, shots, group, sizes),
        out_shape=[
            jax.ShapeDtypeStruct((slots * rows + TAIL * r, columns), bf16) for r in range(sections)
        ],
        in_specs=[hbm] + [anywhere] * (sections + 1),
        out_specs=[anywhere] * sections,
        scratch_shapes=[
            pltpu.VMEM((sections, 2, half_rows, columns), bf16),
            pltpu.VMEM((sections, win_rows, columns), bf16),
            pltpu.VMEM((sections * slots + 1, 2 * rows, columns), bf16),
            pltpu.VMEM((sections * slots, 2 * rows, 2 * rows), bf16),
            pltpu.VMEM((2 * rows, columns), bf16),
            pltpu.VMEM((sections, slots * rows, columns), bf16),
            pltpu.SMEM((sections,), jnp.int32),
            pltpu.SemaphoreType.DMA((sections, 2)),
            pltpu.SemaphoreType.DMA((sections,)),
            pltpu.SemaphoreType.DMA,
            pltpu.SemaphoreType.DMA((sections,)),
        ],
        compiler_params=params(16),
        name="sweep",
    )(
        kept(source.reshape(shots, 2 * rows, columns)), *messages, joined, far_window
    )

    arrived = [correlations[0]] + [
        lax.ppermute(correlations[r], BOTH, plan.from_workers(r)) for r in range(1, sections)
    ]
    left, own = pl.pallas_call(
        functools.partial(place_kernel, shots),
        out_shape=[corr_shape, jax.ShapeDtypeStruct((slots * rows, columns), jnp.float32)],
        in_specs=[smem] + [vmem] * sections,
        out_specs=[vmem, vmem],
        compiler_params=params(8),
        name="place",
    )(anchors, *arrived)
    from_right = lax.ppermute(left, "tile", [(i + 1, i) for i in range(plan.tiles - 1)])
    image = own + from_right.astype(jnp.float32)
    return image.reshape(1, slots, rows, columns)


def solution(mesh):
    return jax.shard_map(
        on_device,
        mesh=mesh,
        in_specs=(
            P("tile", None, None, None),
            P("tile"),
            P("depth"),
            P("depth", None, None, "tile"),
            P("depth", None, None, None, None),
            P("depth", None, None, None, None),
        ),
        out_specs=P("depth", None, None, "tile"),
        check_vma=False,
    )
```

```python
import functools

import jax
import jax.numpy as jnp
from jax import lax
from jax.experimental import pallas as pl
from jax.experimental.pallas import tpu as pltpu
from jax.sharding import PartitionSpec as P

BOTH = ("depth", "tile")
MIB = 1024 * 1024
TAIL = 16


class Plan:
    def __init__(self, shots):
        self.sections = lax.axis_size("depth")
        self.tiles = lax.axis_size("tile")
        self.shots = shots
        self.group = self.sections // shots
        assert self.sections == 4 and self.group * shots == self.sections
        assert self.tiles % (2 * self.group) == 0

    def device(self, depth, tile):
        return depth * self.tiles + tile

    def bases(self):
        return range(0, self.tiles, self.group)

    def worker(self, base, w):
        return self.device(w, base + w // self.shots)

    def other(self, w, base):
        return self.device(w, base + (w // self.shots + 1) % self.group)

    def ops_to_workers(self, r):
        return [
            (self.other(w ^ r, base), self.worker(base, w))
            for base in self.bases()
            for w in range(self.sections)
        ]

    def swap_workers(self):
        return [
            (self.worker(base, w), self.worker((base // self.group ^ 1) * self.group, w))
            for base in self.bases()
            for w in range(self.sections)
        ]

    def to_workers(self, r):
        return [
            (self.device(w ^ r, base + w // self.shots), self.worker(base, w))
            for base in self.bases()
            for w in range(self.sections)
        ]

    def from_workers(self, r):
        return [(b, a) for a, b in self.to_workers(r)]


def pack_kernel(group, sizes, x_hbm, y_hbm, even, odd, late, half_out, x_ref, y_ref, sem):
    slots, rows, columns = sizes
    loads = [
        pltpu.make_async_copy(x_hbm, x_ref, sem.at[0]),
        pltpu.make_async_copy(y_hbm, y_ref, sem.at[1]),
    ]
    for load in loads:
        load.start()
    for load in loads:
        load.wait()
    piece = rows // 2
    part = columns + piece
    first = (slots - 1) * part
    for half in range(2):
        for slot in range(slots):
            op_x = jnp.concatenate(
                [x_ref[slot, i, half * piece : (half + 1) * piece, :] for i in range(2)], axis=1
            )
            op_y = y_ref[slot, half]
            if slot < slots - 1:
                places = [(out, half * first + slot * part) for out in (even, odd)]
            else:
                places = [(late, half * part)]
            for out, spot in places:
                out[spot : spot + columns, :] = op_y
                out[spot + columns : spot + part, :] = op_x
    plane = lax.rem(lax.axis_index("tile") // group, 2)
    half_out[:first, :] = even[pl.ds(pl.multiple_of(plane * first, first), first), :]
    half_out[first:, :] = late[pl.ds(pl.multiple_of(plane * part, part), part), :]


def window_kernel(shots, sizes, anchors_hbm, counts, left_ref, right_hbm, *refs):
    slots, rows, columns = sizes
    messages, (alone, anchors, right_ref, sem) = refs[shots : 2 * shots], refs[2 * shots :]
    loads = [
        pltpu.make_async_copy(anchors_hbm, anchors, sem.at[0]),
        pltpu.make_async_copy(right_hbm, right_ref, sem.at[1]),
    ]
    for load in loads:
        load.start()
    for load in loads:
        load.wait()
    section, tile = lax.axis_index("depth"), lax.axis_index("tile")
    both = jnp.concatenate(
        [left_ref[...].astype(jnp.float32), right_ref[...].astype(jnp.float32)], axis=1
    )
    tail = jnp.full((TAIL, columns), counts[0].astype(jnp.float32), jnp.float32)
    for q, message in enumerate(messages):
        offset = anchors[lax.rem(section, shots) ^ q] - (tile - 1) * columns
        back = lax.rem(2 * columns - offset, 2 * columns)
        window = pltpu.roll(both, back, 1)[:, :columns].astype(message.dtype)
        for out in [message] + ([alone] if q == shots - 1 else []):
            spot = out.shape[0] - TAIL - slots * rows
            out[spot : spot + slots * rows, :] = window
            out[spot + slots * rows :, :] = tail.astype(out.dtype)


class Sweep:
    def __init__(self, shots, group, sizes, ops, win, waves, turned_x):
        self.sizes = sizes
        self.ops, self.win, self.waves, self.turned_x = ops, win, waves, turned_x
        slots, rows, columns = sizes
        self.piece = rows // 2
        self.part = columns + self.piece
        self.first = (slots - 1) * self.part
        self.here, tile = lax.axis_index("depth"), lax.axis_index("tile")
        self.shot = lax.rem(self.here, shots)
        self.is_worker = (self.here // shots == lax.rem(tile, group)).astype(jnp.int32)

    def level(self, r, slot):
        _, rows, columns = self.sizes
        start = pl.multiple_of(slot * self.part, self.part)
        op_y = [self.ops[r, half, pl.ds(start, columns), :] for half in range(2)]
        spot = pl.multiple_of(slot * rows, rows)
        window = self.win[r, pl.ds(spot, rows), :].astype(jnp.float32)
        return window, op_y[0], op_y[1], spot

    def level_x(self, r, slot):
        rows, columns = self.sizes[1:]
        tail = pl.multiple_of(slot * self.part + columns, self.piece)
        op_x = jnp.concatenate(
            [self.ops[r, half, pl.ds(tail, self.piece), :] for half in range(2)], axis=0
        )
        return op_x[:, :rows], op_x[:, rows:]

    def blocks(self, re, im):
        upper = jnp.concatenate([re, -im], axis=1)
        return jnp.concatenate([upper, jnp.concatenate([im, re], axis=1)], axis=0)

    def complex_sum(self, both):
        _, rows, columns = self.sizes
        with_re, with_im = both[:, :columns], both[:, columns:]
        return with_re[:rows] - with_im[rows:], with_im[:rows] + with_re[rows:]

    def dot(self, a, b, dims):
        return lax.dot_general(a, b, (dims, ((), ())), preferred_element_type=jnp.float32)

    def down(self, r, slot, place):
        rows = self.sizes[1]
        window, y_re, y_im, _ = self.level(r, slot)
        x_re, x_im = self.level_x(r, slot)
        wave = self.waves[place].astype(jnp.float32)
        gain = 1.0 + window
        scaled = jnp.concatenate([gain * wave[:rows], gain * wave[rows:]], axis=0)
        self.turned_x[place] = self.blocks(x_re.T, x_im.T)
        middle = self.dot(self.blocks(x_re, x_im), scaled.astype(jnp.bfloat16), ((1,), (0,)))
        middle = middle.astype(jnp.bfloat16)
        both_y = jnp.concatenate([y_re, y_im], axis=0)
        moved_re, moved_im = self.complex_sum(self.dot(middle, both_y, ((1,), (1,))))
        moved = jnp.concatenate([moved_re, moved_im], axis=0)
        self.waves[place + 1] = moved.astype(jnp.bfloat16)
        return place + 1

    def up(self, r, slot, place, wave_up, corr):
        rows = self.sizes[1]
        window, y_re, y_im, spot = self.level(r, slot)
        wave = self.waves[place - 1].astype(jnp.float32)
        back = self.dot(self.turned_x[place - 1], wave_up[...], ((1,), (0,)))
        both_y = jnp.concatenate([y_re, y_im], axis=1)
        spread_re, spread_im = self.complex_sum(
            self.dot(back.astype(jnp.bfloat16), both_y, ((1,), (0,)))
        )
        up_re = (window * wave[:rows] + spread_re).astype(jnp.bfloat16)
        up_im = (window * wave[rows:] + spread_im).astype(jnp.bfloat16)
        wave_up[:rows] = up_re
        wave_up[rows:] = up_im
        product = wave[:rows] * up_re.astype(jnp.float32)
        product += wave[rows:] * up_im.astype(jnp.float32)
        corr[r, pl.ds(spot, rows), :] = product.astype(corr.dtype)
        return place - 1


def down_kernel(sections, shots, group, sizes, source_ref, *refs):
    slots, rows, columns = sizes
    messages, (own_late, joined, far_window) = refs[: sections - 1], refs[sections - 1 : sections + 2]
    ops, win, waves, turned_x, state, op_sem, win_sem, src_sem = refs[sections + 2 :]
    it = Sweep(shots, group, sizes, ops, win, waves, turned_x)
    first, part = it.first, it.part
    half_rows, win_rows = first + part, slots * rows + TAIL

    def op_copies(r, half):
        place, sem = ops.at[r, half], op_sem.at[r, half]
        if r == sections - 1:
            return [pltpu.make_async_copy(joined.at[half], place, sem)]
        message = messages[r].at[pl.ds(half * first, first), :]
        copies = [pltpu.make_async_copy(message, place.at[pl.ds(0, first), :], sem)]
        if r == 0:
            last = own_late.at[pl.ds(half * part, part), :]
            copies.append(pltpu.make_async_copy(last, place.at[pl.ds(first, part), :], sem))
        return copies

    def op_wait(r, partial):
        count = first if partial else half_rows
        for half in range(2):
            place = ops.at[r, half, pl.ds(0, count), :]
            source = joined.at[half, pl.ds(0, count), :]
            pltpu.make_async_copy(source, place, op_sem.at[r, half]).wait()

    def win_copy(r):
        message = messages[r] if r < sections - 1 else far_window
        start = message.shape[0] - win_rows
        return pltpu.make_async_copy(
            message.at[pl.ds(start, win_rows), :], win.at[r], win_sem.at[r]
        )

    @pl.when(it.is_worker == 0)
    def _():
        for i in range(3 + sections):
            state[i] = 0

    @pl.when(it.is_worker != 0)
    def _():
        src_copy = pltpu.make_async_copy(source_ref.at[it.shot], waves.at[0], src_sem)
        src_copy.start()
        for r in range(sections):
            win_copy(r).start()
        for section in range(sections):
            for r in range(sections):

                @pl.when((section ^ it.here) == r)
                def _():
                    for half in range(2):
                        for copy in op_copies(r, half):
                            copy.start()

        for r in range(sections):
            win_copy(r).wait()
        for r in range(sections):
            value = jnp.max(win[r, slots * rows :, :].astype(jnp.float32))
            state[3 + r] = value.astype(jnp.int32)
        src_copy.wait()

        def section_down(section, carry):
            place, going, next_section, next_slot = carry
            r = section ^ it.here
            partial = (r != 0) & (r != sections - 1)

            @pl.when(partial)
            def _():
                op_wait(r, True)

            @pl.when(jnp.logical_not(partial))
            def _():
                op_wait(r, False)

            count = state[3 + r]
            ready = jnp.where(partial, jnp.minimum(count, slots - 1), count)
            place = lax.fori_loop(
                0, jnp.where(going, ready, 0), lambda slot, place: it.down(r, slot, place), place
            )
            whole = ready == count
            next_section = jnp.where(going, jnp.where(whole, section + 1, section), next_section)
            next_slot = jnp.where(going, jnp.where(whole, 0, ready), next_slot)
            return place, going & whole, next_section, next_slot

        zero = jnp.int32(0)
        carry = (zero, jnp.bool_(True), zero, zero)
        place, _, next_section, next_slot = lax.fori_loop(0, sections, section_down, carry)
        state[0] = next_section
        state[1] = next_slot
        state[2] = place


def up_kernel(sections, shots, group, sizes, state, *refs):
    slots, rows, columns = sizes
    near_late, far_late, win = refs[:3]
    outs, refs = refs[6 : 6 + sections], refs[6 + sections :]
    ops, waves, turned_x, wave_up, corr, op_sem, out_sem = refs
    it = Sweep(shots, group, sizes, ops, win, waves, turned_x)
    first, part = it.first, it.part

    def late_copies():
        return [
            pltpu.make_async_copy(
                late.at[pl.ds(half * part, part), :],
                ops.at[r, half, pl.ds(first, part), :],
                op_sem.at[r, half],
            )
            for r, late in ((1, near_late), (2, far_late))
            for half in range(2)
        ]

    def out_copy(r):
        place = outs[r].at[pl.ds(0, slots * rows), :]
        return pltpu.make_async_copy(corr.at[r], place, out_sem.at[r])

    @pl.when(it.is_worker == 0)
    def _():
        corr[0] = jnp.zeros(corr.shape[1:], corr.dtype)
        out_copy(0).start()
        out_copy(0).wait()

    @pl.when(it.is_worker != 0)
    def _():
        for copy in late_copies():
            copy.start()
        corr[...] = jnp.zeros(corr.shape, corr.dtype)
        wave_up[...] = jnp.zeros(wave_up.shape, wave_up.dtype)
        next_section, next_slot = state[0], state[1]
        for copy in late_copies():
            copy.wait()

        def section_down(section, place):
            r = section ^ it.here
            begin = jnp.where(section == next_section, next_slot, 0)
            return lax.fori_loop(
                begin, state[3 + r], lambda slot, place: it.down(r, slot, place), place
            )

        last = lax.fori_loop(next_section, sections, section_down, state[2])

        def section_up(step, place):
            r = (sections - 1 - step) ^ it.here
            count = state[3 + r]
            place = lax.fori_loop(
                0,
                count,
                lambda inner, place: it.up(r, count - 1 - inner, place, wave_up, corr),
                place,
            )
            for out in range(sections):

                @pl.when(r == out)
                def _():
                    out_copy(out).start()

            return place

        lax.fori_loop(0, sections, section_up, last)
        for r in range(sections):
            out_copy(r).wait()


def join_kernel(group, first_ref, second_ref, out_ref, sem):
    plane = lax.rem(lax.axis_index("tile") // group, 2)
    copies = [
        pltpu.make_async_copy(first_ref, out_ref.at[plane], sem.at[0]),
        pltpu.make_async_copy(second_ref, out_ref.at[1 - plane], sem.at[1]),
    ]
    for copy in copies:
        copy.start()
    for copy in copies:
        copy.wait()


def hold_kernel(array_ref, after_ref, out_ref):
    pass


def place_kernel(shots, anchors, *refs):
    arrived, (left_out, own_out) = refs[:-2], refs[-2:]
    section, tile = lax.axis_index("depth"), lax.axis_index("tile")
    places, columns = left_out.shape
    canvas = None
    for q in range(shots):
        offset = anchors[lax.rem(section, shots) ^ q] - (tile - 1) * columns
        total = None
        for r in range(q, len(arrived), shots):
            value = arrived[r][:places, :].astype(jnp.float32)
            total = value if total is None else total + value
        wide = jnp.concatenate([total, jnp.zeros_like(total)], axis=1)
        turned = pltpu.roll(wide, offset, 1)
        canvas = turned if canvas is None else canvas + turned
    left_out[...] = canvas[:, :columns].astype(left_out.dtype)
    own_out[...] = canvas[:, columns:]


def kept(array):
    return pltpu.with_memory_space_constraint(array, pltpu.HBM)


def held(array):
    return pltpu.with_memory_space_constraint(array, pltpu.VMEM)


def on_device(source, anchors, counts, reflect, lateral_x, lateral_y):
    shots, _, rows, columns = source.shape
    slots = reflect.shape[1]
    sizes = (slots, rows, columns)
    plan = Plan(shots)
    sections, group = plan.sections, plan.group
    assert shots == 2
    bf16 = jnp.bfloat16
    smem = pl.BlockSpec(memory_space=pltpu.SMEM)
    vmem = pl.BlockSpec(memory_space=pltpu.VMEM)
    hbm = pl.BlockSpec(memory_space=pltpu.HBM)
    anywhere = pl.BlockSpec(memory_space=pl.ANY)

    def params(mib):
        return pltpu.CompilerParams(vmem_limit_bytes=mib * MIB)

    tile_reflect = reflect[0].reshape(slots * rows, columns)
    halo = lax.ppermute(tile_reflect, "tile", [(i, i + 1) for i in range(plan.tiles - 1)])
    part = columns + rows // 2
    half_rows, win_rows = slots * part, slots * rows + TAIL
    early_rows = 2 * (half_rows - part) + win_rows
    even = pltpu.VMEM((early_rows + TAIL, columns), bf16)
    odd = pltpu.VMEM((early_rows, columns), bf16)
    even_early, odd_early, late, far_half = pl.pallas_call(
        functools.partial(pack_kernel, group, sizes),
        out_shape=[
            even,
            odd,
            jax.ShapeDtypeStruct((2 * part, columns), bf16),
            jax.ShapeDtypeStruct((half_rows, columns), bf16),
        ],
        in_specs=[hbm, hbm],
        out_specs=[vmem] * 4,
        scratch_shapes=[
            pltpu.VMEM(lateral_x.shape[1:], bf16),
            pltpu.VMEM(lateral_y.shape[1:], bf16),
            pltpu.SemaphoreType.DMA((2,)),
        ],
        compiler_params=params(12),
        name="pack",
    )(kept(lateral_x[0]), kept(lateral_y[0]))
    last = sections - 1
    far_half = lax.ppermute(far_half, BOTH, plan.to_workers(last))
    even_early, odd_early, far_window = pl.pallas_call(
        functools.partial(window_kernel, shots, sizes),
        out_shape=[even, odd, jax.ShapeDtypeStruct((win_rows, columns), bf16)],
        in_specs=[hbm, smem, vmem, hbm, vmem, vmem],
        out_specs=[vmem] * 3,
        scratch_shapes=[
            pltpu.SMEM((shots,), jnp.int32),
            pltpu.VMEM((slots * rows, columns), bf16),
            pltpu.SemaphoreType.DMA((2,)),
        ],
        input_output_aliases={4: 0, 5: 1},
        compiler_params=params(12),
        cost_estimate=pl.CostEstimate(flops=0, bytes_accessed=4 * MIB, transcendentals=0),
        name="windows",
    )(kept(anchors), counts, halo, kept(tile_reflect), held(even_early), held(odd_early))
    messages = [
        even_early,
        lax.ppermute(odd_early, BOTH, plan.to_workers(1)),
        lax.ppermute(even_early, BOTH, plan.to_workers(2)),
    ]
    far_window = lax.ppermute(far_window, BOTH, plan.to_workers(last))
    other_half = lax.ppermute(far_half, BOTH, plan.swap_workers())
    late = pl.pallas_call(
        hold_kernel,
        out_shape=jax.ShapeDtypeStruct(late.shape, bf16),
        in_specs=[anywhere] * 2,
        out_specs=anywhere,
        input_output_aliases={0: 0},
        compiler_params=params(2),
        name="hold",
    )(late, far_window)
    lates = [lax.ppermute(late, BOTH, plan.ops_to_workers(r)) for r in (1, 2)]
    joined = pl.pallas_call(
        functools.partial(join_kernel, group),
        out_shape=jax.ShapeDtypeStruct((2, half_rows, columns), bf16),
        in_specs=[anywhere] * 2,
        out_specs=anywhere,
        scratch_shapes=[pltpu.SemaphoreType.DMA((2,))],
        compiler_params=params(2),
        cost_estimate=pl.CostEstimate(flops=0, bytes_accessed=4 * MIB, transcendentals=0),
        name="join",
    )(far_half, other_half)

    ops = pltpu.VMEM((sections, 2, half_rows, columns), bf16)
    win = pltpu.VMEM((sections, win_rows, columns), bf16)
    waves = pltpu.VMEM((sections * slots + 1, 2 * rows, columns), bf16)
    turned_x = pltpu.VMEM((sections * slots, 2 * rows, 2 * rows), bf16)
    buffers = pl.pallas_call(
        functools.partial(down_kernel, sections, shots, group, sizes),
        out_shape=[ops, win, waves, turned_x, jax.ShapeDtypeStruct((3 + sections,), jnp.int32)],
        in_specs=[hbm] + [anywhere] * (sections + 2),
        out_specs=[vmem] * 4 + [smem],
        scratch_shapes=[
            pltpu.SemaphoreType.DMA((sections, 2)),
            pltpu.SemaphoreType.DMA((sections,)),
            pltpu.SemaphoreType.DMA,
        ],
        compiler_params=params(16),
        cost_estimate=pl.CostEstimate(flops=0, bytes_accessed=4 * MIB, transcendentals=0),
        name="down",
    )(
        kept(source.reshape(shots, 2 * rows, columns)), *messages, late, joined, far_window
    )
    ops_done, win_done, waves_done, turned_done = [held(buffer) for buffer in buffers[:4]]
    corr_shape = jax.ShapeDtypeStruct((slots * rows, columns), bf16)
    correlations = pl.pallas_call(
        functools.partial(up_kernel, sections, shots, group, sizes),
        out_shape=[
            jax.ShapeDtypeStruct((slots * rows + TAIL * r, columns), bf16) for r in range(sections)
        ]
        + [ops, waves, turned_x],
        in_specs=[smem] + [anywhere] * 2 + [vmem] * 4,
        out_specs=[anywhere] * sections + [vmem] * 3,
        scratch_shapes=[
            pltpu.VMEM((2 * rows, columns), bf16),
            pltpu.VMEM((sections, slots * rows, columns), bf16),
            pltpu.SemaphoreType.DMA((sections, 2)),
            pltpu.SemaphoreType.DMA((sections,)),
        ],
        input_output_aliases={4: sections, 5: sections + 1, 6: sections + 2},
        compiler_params=params(16),
        name="up",
    )(buffers[4], *lates, win_done, ops_done, waves_done, turned_done)

    arrived = [correlations[0]] + [
        lax.ppermute(correlations[r], BOTH, plan.from_workers(r)) for r in range(1, sections)
    ]
    left, own = pl.pallas_call(
        functools.partial(place_kernel, shots),
        out_shape=[corr_shape, jax.ShapeDtypeStruct((slots * rows, columns), jnp.float32)],
        in_specs=[smem] + [vmem] * sections,
        out_specs=[vmem, vmem],
        compiler_params=params(8),
        name="place",
    )(anchors, *arrived)
    from_right = lax.ppermute(left, "tile", [(i + 1, i) for i in range(plan.tiles - 1)])
    image = own + from_right.astype(jnp.float32)
    return image.reshape(1, slots, rows, columns)


def solution(mesh):
    return jax.shard_map(
        on_device,
        mesh=mesh,
        in_specs=(
            P("tile", None, None, None),
            P("tile"),
            P("depth"),
            P("depth", None, None, "tile"),
            P("depth", None, None, None, None),
            P("depth", None, None, None, None),
        ),
        out_specs=P("depth", None, None, "tile"),
        check_vma=False,
    )
```

```python
import functools

import jax
import jax.numpy as jnp
from jax import lax
from jax.experimental import pallas as pl
from jax.experimental.pallas import tpu as pltpu
from jax.sharding import PartitionSpec as P

BOTH = ("depth", "tile")
MIB = 1024 * 1024
TAIL = 16


class Plan:
    def __init__(self, shots):
        self.sections = lax.axis_size("depth")
        self.tiles = lax.axis_size("tile")
        self.shots = shots
        self.group = self.sections // shots
        assert self.sections == 4 and self.group * shots == self.sections
        assert self.tiles % (2 * self.group) == 0

    def device(self, depth, tile):
        return depth * self.tiles + tile

    def bases(self):
        return range(0, self.tiles, self.group)

    def worker(self, base, w):
        return self.device(w, base + w // self.shots)

    def other(self, w, base):
        return self.device(w, base + (w // self.shots + 1) % self.group)

    def ops_to_workers(self, r):
        return [
            (self.other(w ^ r, base), self.worker(base, w))
            for base in self.bases()
            for w in range(self.sections)
        ]

    def swap_workers(self):
        return [
            (self.worker(base, w), self.worker((base // self.group ^ 1) * self.group, w))
            for base in self.bases()
            for w in range(self.sections)
        ]

    def to_workers(self, r):
        return [
            (self.device(w ^ r, base + w // self.shots), self.worker(base, w))
            for base in self.bases()
            for w in range(self.sections)
        ]

    def from_workers(self, r):
        return [(b, a) for a, b in self.to_workers(r)]


def pack_kernel(group, sizes, x_hbm, y_hbm, even, odd, late, half_out, x_ref, y_ref, sem):
    slots, rows, columns = sizes
    loads = [
        pltpu.make_async_copy(x_hbm, x_ref, sem.at[0]),
        pltpu.make_async_copy(y_hbm, y_ref, sem.at[1]),
    ]
    for load in loads:
        load.start()
    for load in loads:
        load.wait()
    piece = rows // 2
    part = columns + piece
    first = (slots - 1) * part
    for half in range(2):
        for slot in range(slots):
            op_x = jnp.concatenate(
                [x_ref[slot, i, half * piece : (half + 1) * piece, :] for i in range(2)], axis=1
            )
            op_y = y_ref[slot, half]
            if slot < slots - 1:
                places = [(out, half * first + slot * part) for out in (even, odd)]
            else:
                places = [(late, half * part)]
            for out, spot in places:
                out[spot : spot + columns, :] = op_y
                out[spot + columns : spot + part, :] = op_x
    plane = lax.rem(lax.axis_index("tile") // group, 2)
    half_out[:first, :] = even[pl.ds(pl.multiple_of(plane * first, first), first), :]
    half_out[first:, :] = late[pl.ds(pl.multiple_of(plane * part, part), part), :]


def window_kernel(shots, sizes, anchors_hbm, counts, left_ref, right_hbm, *refs):
    slots, rows, columns = sizes
    messages, (alone, anchors, right_ref, sem) = refs[shots : 2 * shots], refs[2 * shots :]
    loads = [
        pltpu.make_async_copy(anchors_hbm, anchors, sem.at[0]),
        pltpu.make_async_copy(right_hbm, right_ref, sem.at[1]),
    ]
    for load in loads:
        load.start()
    for load in loads:
        load.wait()
    section, tile = lax.axis_index("depth"), lax.axis_index("tile")
    both = jnp.concatenate(
        [left_ref[...].astype(jnp.float32), right_ref[...].astype(jnp.float32)], axis=1
    )
    tail = jnp.full((TAIL, columns), counts[0].astype(jnp.float32), jnp.float32)
    for q, message in enumerate(messages):
        offset = anchors[lax.rem(section, shots) ^ q] - (tile - 1) * columns
        back = lax.rem(2 * columns - offset, 2 * columns)
        window = pltpu.roll(both, back, 1)[:, :columns].astype(message.dtype)
        for out in [message] + ([alone] if q == shots - 1 else []):
            spot = out.shape[0] - TAIL - slots * rows
            out[spot : spot + slots * rows, :] = window
            out[spot + slots * rows :, :] = tail.astype(out.dtype)


class Sweep:
    def __init__(self, shots, group, sizes, ops, win, waves, turned_x):
        self.sizes = sizes
        self.ops, self.win, self.waves, self.turned_x = ops, win, waves, turned_x
        slots, rows, columns = sizes
        self.piece = rows // 2
        self.part = columns + self.piece
        self.first = (slots - 1) * self.part
        self.here, tile = lax.axis_index("depth"), lax.axis_index("tile")
        self.shot = lax.rem(self.here, shots)
        self.is_worker = (self.here // shots == lax.rem(tile, group)).astype(jnp.int32)

    def level(self, r, slot):
        _, rows, columns = self.sizes
        start = pl.multiple_of(slot * self.part, self.part)
        op_y = [self.ops[r, half, pl.ds(start, columns), :] for half in range(2)]
        spot = pl.multiple_of(slot * rows, rows)
        window = self.win[r, pl.ds(spot, rows), :].astype(jnp.float32)
        return window, op_y[0], op_y[1], spot

    def level_x(self, r, slot):
        rows, columns = self.sizes[1:]
        tail = pl.multiple_of(slot * self.part + columns, self.piece)
        op_x = jnp.concatenate(
            [self.ops[r, half, pl.ds(tail, self.piece), :] for half in range(2)], axis=0
        )
        return op_x[:, :rows], op_x[:, rows:]

    def blocks(self, re, im):
        upper = jnp.concatenate([re, -im], axis=1)
        return jnp.concatenate([upper, jnp.concatenate([im, re], axis=1)], axis=0)

    def complex_sum(self, both):
        _, rows, columns = self.sizes
        with_re, with_im = both[:, :columns], both[:, columns:]
        return with_re[:rows] - with_im[rows:], with_im[:rows] + with_re[rows:]

    def dot(self, a, b, dims):
        return lax.dot_general(a, b, (dims, ((), ())), preferred_element_type=jnp.float32)

    def down(self, r, slot, place):
        rows = self.sizes[1]
        window, y_re, y_im, _ = self.level(r, slot)
        x_re, x_im = self.level_x(r, slot)
        wave = self.waves[place].astype(jnp.float32)
        gain = 1.0 + window
        scaled = jnp.concatenate([gain * wave[:rows], gain * wave[rows:]], axis=0)
        self.turned_x[place] = self.blocks(x_re.T, x_im.T)
        middle = self.dot(self.blocks(x_re, x_im), scaled.astype(jnp.bfloat16), ((1,), (0,)))
        middle = middle.astype(jnp.bfloat16)
        both_y = jnp.concatenate([y_re, y_im], axis=0)
        moved_re, moved_im = self.complex_sum(self.dot(middle, both_y, ((1,), (1,))))
        moved = jnp.concatenate([moved_re, moved_im], axis=0)
        self.waves[place + 1] = moved.astype(jnp.bfloat16)
        return place + 1

    def up(self, r, slot, place, wave_up, corr):
        rows = self.sizes[1]
        window, y_re, y_im, spot = self.level(r, slot)
        wave = self.waves[place - 1].astype(jnp.float32)
        back = self.dot(self.turned_x[place - 1], wave_up[...], ((1,), (0,)))
        both_y = jnp.concatenate([y_re, y_im], axis=1)
        spread_re, spread_im = self.complex_sum(
            self.dot(back.astype(jnp.bfloat16), both_y, ((1,), (0,)))
        )
        up_re = (window * wave[:rows] + spread_re).astype(jnp.bfloat16)
        up_im = (window * wave[rows:] + spread_im).astype(jnp.bfloat16)
        wave_up[:rows] = up_re
        wave_up[rows:] = up_im
        product = wave[:rows] * up_re.astype(jnp.float32)
        product += wave[rows:] * up_im.astype(jnp.float32)
        corr[r, pl.ds(spot, rows), :] = product.astype(corr.dtype)
        return place - 1


def down_kernel(sections, shots, group, sizes, source_ref, *refs):
    slots, rows, columns = sizes
    messages, refs = refs[: sections - 1], refs[sections - 1 :]
    own_late, far_half, other_half, far_window, *refs = refs
    ops, win, waves, turned_x, state, op_sem, win_sem, src_sem = refs
    plane = lax.rem(lax.axis_index("tile") // group, 2)
    it = Sweep(shots, group, sizes, ops, win, waves, turned_x)
    first, part = it.first, it.part
    half_rows, win_rows = first + part, slots * rows + TAIL

    def op_copies(r, half):
        place, sem = ops.at[r, half], op_sem.at[r, half]
        if r == sections - 1:
            place = ops.at[r, 1 - plane if half else plane]
            return [pltpu.make_async_copy(other_half if half else far_half, place, sem)]
        message = messages[r].at[pl.ds(half * first, first), :]
        copies = [pltpu.make_async_copy(message, place.at[pl.ds(0, first), :], sem)]
        if r == 0:
            last = own_late.at[pl.ds(half * part, part), :]
            copies.append(pltpu.make_async_copy(last, place.at[pl.ds(first, part), :], sem))
        return copies

    def op_wait(r, partial):
        count = first if partial else half_rows
        for half in range(2):
            place = ops.at[r, half, pl.ds(0, count), :]
            source = far_half.at[pl.ds(0, count), :]
            pltpu.make_async_copy(source, place, op_sem.at[r, half]).wait()

    def win_copy(r):
        message = messages[r] if r < sections - 1 else far_window
        start = message.shape[0] - win_rows
        return pltpu.make_async_copy(
            message.at[pl.ds(start, win_rows), :], win.at[r], win_sem.at[r]
        )

    @pl.when(it.is_worker == 0)
    def _():
        for i in range(3 + sections):
            state[i] = 0

    @pl.when(it.is_worker != 0)
    def _():
        src_copy = pltpu.make_async_copy(source_ref.at[it.shot], waves.at[0], src_sem)
        src_copy.start()
        for r in range(sections):
            win_copy(r).start()
        for section in range(sections):
            for r in range(sections):

                @pl.when((section ^ it.here) == r)
                def _():
                    for half in range(2):
                        for copy in op_copies(r, half):
                            copy.start()

        for r in range(sections):
            win_copy(r).wait()
        for r in range(sections):
            value = jnp.max(win[r, slots * rows :, :].astype(jnp.float32))
            state[3 + r] = value.astype(jnp.int32)
        src_copy.wait()

        def section_down(section, carry):
            place, going, next_section, next_slot = carry
            r = section ^ it.here
            partial = (r != 0) & (r != sections - 1)

            @pl.when(partial)
            def _():
                op_wait(r, True)

            @pl.when(jnp.logical_not(partial))
            def _():
                op_wait(r, False)

            count = state[3 + r]
            ready = jnp.where(partial, jnp.minimum(count, slots - 1), count)
            place = lax.fori_loop(
                0, jnp.where(going, ready, 0), lambda slot, place: it.down(r, slot, place), place
            )
            whole = ready == count
            next_section = jnp.where(going, jnp.where(whole, section + 1, section), next_section)
            next_slot = jnp.where(going, jnp.where(whole, 0, ready), next_slot)
            return place, going & whole, next_section, next_slot

        zero = jnp.int32(0)
        carry = (zero, jnp.bool_(True), zero, zero)
        place, _, next_section, next_slot = lax.fori_loop(0, sections, section_down, carry)
        state[0] = next_section
        state[1] = next_slot
        state[2] = place


def up_kernel(sections, shots, group, sizes, state, *refs):
    slots, rows, columns = sizes
    near_late, far_late, win = refs[:3]
    outs, refs = refs[6 : 6 + sections], refs[6 + sections :]
    ops, waves, turned_x, wave_up, corr, op_sem, out_sem = refs
    it = Sweep(shots, group, sizes, ops, win, waves, turned_x)
    first, part = it.first, it.part

    def late_copies():
        return [
            pltpu.make_async_copy(
                late.at[pl.ds(half * part, part), :],
                ops.at[r, half, pl.ds(first, part), :],
                op_sem.at[r, half],
            )
            for r, late in ((1, near_late), (2, far_late))
            for half in range(2)
        ]

    def out_copy(r):
        place = outs[r].at[pl.ds(0, slots * rows), :]
        return pltpu.make_async_copy(corr.at[r], place, out_sem.at[r])

    @pl.when(it.is_worker == 0)
    def _():
        corr[0] = jnp.zeros(corr.shape[1:], corr.dtype)
        out_copy(0).start()
        out_copy(0).wait()

    @pl.when(it.is_worker != 0)
    def _():
        for copy in late_copies():
            copy.start()
        corr[...] = jnp.zeros(corr.shape, corr.dtype)
        wave_up[...] = jnp.zeros(wave_up.shape, wave_up.dtype)
        next_section, next_slot = state[0], state[1]
        for copy in late_copies():
            copy.wait()

        def section_down(section, place):
            r = section ^ it.here
            begin = jnp.where(section == next_section, next_slot, 0)
            return lax.fori_loop(
                begin, state[3 + r], lambda slot, place: it.down(r, slot, place), place
            )

        last = lax.fori_loop(next_section, sections, section_down, state[2])

        def section_up(step, place):
            r = (sections - 1 - step) ^ it.here
            count = state[3 + r]
            place = lax.fori_loop(
                0,
                count,
                lambda inner, place: it.up(r, count - 1 - inner, place, wave_up, corr),
                place,
            )
            for out in range(sections):

                @pl.when(r == out)
                def _():
                    out_copy(out).start()

            return place

        lax.fori_loop(0, sections, section_up, last)
        for r in range(sections):
            out_copy(r).wait()


def hold_kernel(array_ref, after_ref, out_ref):
    pass


def place_kernel(shots, anchors, *refs):
    arrived, (left_out, own_out) = refs[:-2], refs[-2:]
    section, tile = lax.axis_index("depth"), lax.axis_index("tile")
    places, columns = left_out.shape
    canvas = None
    for q in range(shots):
        offset = anchors[lax.rem(section, shots) ^ q] - (tile - 1) * columns
        total = None
        for r in range(q, len(arrived), shots):
            value = arrived[r][:places, :].astype(jnp.float32)
            total = value if total is None else total + value
        wide = jnp.concatenate([total, jnp.zeros_like(total)], axis=1)
        turned = pltpu.roll(wide, offset, 1)
        canvas = turned if canvas is None else canvas + turned
    left_out[...] = canvas[:, :columns].astype(left_out.dtype)
    own_out[...] = canvas[:, columns:]


def kept(array):
    return pltpu.with_memory_space_constraint(array, pltpu.HBM)


def held(array):
    return pltpu.with_memory_space_constraint(array, pltpu.VMEM)


def on_device(source, anchors, counts, reflect, lateral_x, lateral_y):
    shots, _, rows, columns = source.shape
    slots = reflect.shape[1]
    sizes = (slots, rows, columns)
    plan = Plan(shots)
    sections, group = plan.sections, plan.group
    assert shots == 2
    bf16 = jnp.bfloat16
    smem = pl.BlockSpec(memory_space=pltpu.SMEM)
    vmem = pl.BlockSpec(memory_space=pltpu.VMEM)
    hbm = pl.BlockSpec(memory_space=pltpu.HBM)
    anywhere = pl.BlockSpec(memory_space=pl.ANY)

    def params(mib):
        return pltpu.CompilerParams(vmem_limit_bytes=mib * MIB)

    tile_reflect = reflect[0].reshape(slots * rows, columns)
    halo = lax.ppermute(tile_reflect, "tile", [(i, i + 1) for i in range(plan.tiles - 1)])
    part = columns + rows // 2
    half_rows, win_rows = slots * part, slots * rows + TAIL
    early_rows = 2 * (half_rows - part) + win_rows
    even = pltpu.VMEM((early_rows + 5 * TAIL, columns), bf16)
    odd = pltpu.VMEM((early_rows, columns), bf16)
    even_early, odd_early, late, far_half = pl.pallas_call(
        functools.partial(pack_kernel, group, sizes),
        out_shape=[
            even,
            odd,
            jax.ShapeDtypeStruct((2 * part, columns), bf16),
            jax.ShapeDtypeStruct((half_rows, columns), bf16),
        ],
        in_specs=[hbm, hbm],
        out_specs=[vmem] * 4,
        scratch_shapes=[
            pltpu.VMEM(lateral_x.shape[1:], bf16),
            pltpu.VMEM(lateral_y.shape[1:], bf16),
            pltpu.SemaphoreType.DMA((2,)),
        ],
        compiler_params=params(12),
        name="pack",
    )(kept(lateral_x[0]), kept(lateral_y[0]))
    last = sections - 1
    far_half = lax.ppermute(far_half, BOTH, plan.to_workers(last))
    even_early, odd_early, far_window = pl.pallas_call(
        functools.partial(window_kernel, shots, sizes),
        out_shape=[even, odd, jax.ShapeDtypeStruct((win_rows, columns), bf16)],
        in_specs=[hbm, smem, vmem, hbm, vmem, vmem],
        out_specs=[vmem] * 3,
        scratch_shapes=[
            pltpu.SMEM((shots,), jnp.int32),
            pltpu.VMEM((slots * rows, columns), bf16),
            pltpu.SemaphoreType.DMA((2,)),
        ],
        input_output_aliases={4: 0, 5: 1},
        compiler_params=params(12),
        cost_estimate=pl.CostEstimate(flops=3 * 10**9, bytes_accessed=4 * MIB, transcendentals=0),
        name="windows",
    )(kept(anchors), counts, halo, kept(tile_reflect), held(even_early), held(odd_early))
    messages = [
        even_early,
        lax.ppermute(odd_early, BOTH, plan.to_workers(1)),
        lax.ppermute(even_early, BOTH, plan.to_workers(2)),
    ]
    far_window = lax.ppermute(far_window, BOTH, plan.to_workers(last))
    other_half = lax.ppermute(far_half, BOTH, plan.swap_workers())
    late = pl.pallas_call(
        hold_kernel,
        out_shape=jax.ShapeDtypeStruct(late.shape, bf16),
        in_specs=[anywhere] * 2,
        out_specs=anywhere,
        input_output_aliases={0: 0},
        compiler_params=params(2),
        cost_estimate=pl.CostEstimate(flops=36 * 10**8, bytes_accessed=0, transcendentals=0),
        name="hold",
    )(late, far_window)
    lates = [lax.ppermute(late, BOTH, plan.ops_to_workers(r)) for r in (1, 2)]
    ops = pltpu.VMEM((sections, 2, half_rows, columns), bf16)
    win = pltpu.VMEM((sections, win_rows, columns), bf16)
    waves = pltpu.VMEM((sections * slots + 1, 2 * rows, columns), bf16)
    turned_x = pltpu.VMEM((sections * slots, 2 * rows, 2 * rows), bf16)
    buffers = pl.pallas_call(
        functools.partial(down_kernel, sections, shots, group, sizes),
        out_shape=[ops, win, waves, turned_x, jax.ShapeDtypeStruct((3 + sections,), jnp.int32)],
        in_specs=[hbm] + [anywhere] * (sections + 3),
        out_specs=[vmem] * 4 + [smem],
        scratch_shapes=[
            pltpu.SemaphoreType.DMA((sections, 2)),
            pltpu.SemaphoreType.DMA((sections,)),
            pltpu.SemaphoreType.DMA,
        ],
        compiler_params=params(16),
        cost_estimate=pl.CostEstimate(flops=0, bytes_accessed=4 * MIB, transcendentals=0),
        name="down",
    )(
        kept(source.reshape(shots, 2 * rows, columns)), *messages, late, far_half, other_half,
        far_window
    )
    ops_done, win_done, waves_done, turned_done = [held(buffer) for buffer in buffers[:4]]
    corr_shape = jax.ShapeDtypeStruct((slots * rows, columns), bf16)
    correlations = pl.pallas_call(
        functools.partial(up_kernel, sections, shots, group, sizes),
        out_shape=[
            jax.ShapeDtypeStruct((slots * rows + TAIL * r, columns), bf16) for r in range(sections)
        ]
        + [ops, waves, turned_x],
        in_specs=[smem] + [anywhere] * 2 + [vmem] * 4,
        out_specs=[anywhere] * sections + [vmem] * 3,
        scratch_shapes=[
            pltpu.VMEM((2 * rows, columns), bf16),
            pltpu.VMEM((sections, slots * rows, columns), bf16),
            pltpu.SemaphoreType.DMA((sections, 2)),
            pltpu.SemaphoreType.DMA((sections,)),
        ],
        input_output_aliases={4: sections, 5: sections + 1, 6: sections + 2},
        compiler_params=params(16),
        name="up",
    )(buffers[4], *lates, win_done, ops_done, waves_done, turned_done)

    arrived = [correlations[0]] + [
        lax.ppermute(correlations[r], BOTH, plan.from_workers(r)) for r in range(1, sections)
    ]
    left, own = pl.pallas_call(
        functools.partial(place_kernel, shots),
        out_shape=[corr_shape, jax.ShapeDtypeStruct((slots * rows, columns), jnp.float32)],
        in_specs=[smem] + [vmem] * sections,
        out_specs=[vmem, vmem],
        compiler_params=params(8),
        name="place",
    )(anchors, *arrived)
    from_right = lax.ppermute(left, "tile", [(i + 1, i) for i in range(plan.tiles - 1)])
    image = own + from_right.astype(jnp.float32)
    return image.reshape(1, slots, rows, columns)


def solution(mesh):
    return jax.shard_map(
        on_device,
        mesh=mesh,
        in_specs=(
            P("tile", None, None, None),
            P("tile"),
            P("depth"),
            P("depth", None, None, "tile"),
            P("depth", None, None, None, None),
            P("depth", None, None, None, None),
        ),
        out_specs=P("depth", None, None, "tile"),
        check_vma=False,
    )
```

```python
import functools

import jax
import jax.numpy as jnp
from jax import lax
from jax.experimental import pallas as pl
from jax.experimental.pallas import tpu as pltpu
from jax.sharding import PartitionSpec as P

BOTH = ("depth", "tile")
MIB = 1024 * 1024
TAIL = 16


class Plan:
    def __init__(self, shots):
        self.sections = lax.axis_size("depth")
        self.tiles = lax.axis_size("tile")
        self.shots = shots
        self.group = self.sections // shots
        assert self.sections == 4 and self.group * shots == self.sections
        assert self.tiles % (2 * self.group) == 0

    def device(self, depth, tile):
        return depth * self.tiles + tile

    def bases(self):
        return range(0, self.tiles, self.group)

    def worker(self, base, w):
        return self.device(w, base + w // self.shots)

    def other(self, w, base):
        return self.device(w, base + (w // self.shots + 1) % self.group)

    def ops_to_workers(self, r):
        return [
            (self.other(w ^ r, base), self.worker(base, w))
            for base in self.bases()
            for w in range(self.sections)
        ]

    def swap_workers(self):
        return [
            (self.worker(base, w), self.worker((base // self.group ^ 1) * self.group, w))
            for base in self.bases()
            for w in range(self.sections)
        ]

    def to_workers(self, r):
        return [
            (self.device(w ^ r, base + w // self.shots), self.worker(base, w))
            for base in self.bases()
            for w in range(self.sections)
        ]

    def from_workers(self, r):
        return [(b, a) for a, b in self.to_workers(r)]


def pack_kernel(group, sizes, x_hbm, y_hbm, even, odd, late, half_out, x_ref, y_ref, sem):
    slots, rows, columns = sizes
    loads = [
        pltpu.make_async_copy(x_hbm, x_ref, sem.at[0]),
        pltpu.make_async_copy(y_hbm, y_ref, sem.at[1]),
    ]
    for load in loads:
        load.start()
    for load in loads:
        load.wait()
    piece = rows // 2
    part = columns + piece
    first = (slots - 1) * part
    for half in range(2):
        for slot in range(slots):
            op_x = jnp.concatenate(
                [x_ref[slot, i, half * piece : (half + 1) * piece, :] for i in range(2)], axis=1
            )
            op_y = y_ref[slot, half]
            if slot < slots - 1:
                places = [(out, half * first + slot * part) for out in (even, odd)]
            else:
                places = [(late, half * part)]
            for out, spot in places:
                out[spot : spot + columns, :] = op_y
                out[spot + columns : spot + part, :] = op_x
    plane = lax.rem(lax.axis_index("tile") // group, 2)
    half_out[:first, :] = even[pl.ds(pl.multiple_of(plane * first, first), first), :]
    half_out[first:, :] = late[pl.ds(pl.multiple_of(plane * part, part), part), :]


def window_kernel(shots, sizes, anchors_hbm, counts, left_ref, right_hbm, *refs):
    slots, rows, columns = sizes
    messages, (alone, anchors, right_ref, sem) = refs[shots : 2 * shots], refs[2 * shots :]
    loads = [
        pltpu.make_async_copy(anchors_hbm, anchors, sem.at[0]),
        pltpu.make_async_copy(right_hbm, right_ref, sem.at[1]),
    ]
    for load in loads:
        load.start()
    for load in loads:
        load.wait()
    section, tile = lax.axis_index("depth"), lax.axis_index("tile")
    left, right = left_ref[...].astype(jnp.float32), right_ref[...].astype(jnp.float32)
    lanes = lax.broadcasted_iota(jnp.int32, left.shape, 1)
    tail = jnp.full((TAIL, columns), counts[0].astype(jnp.float32), jnp.float32)
    for q, message in enumerate(messages):
        offset = anchors[lax.rem(section, shots) ^ q] - (tile - 1) * columns
        merged = jnp.where(lanes >= offset, left, right)
        back = lax.rem(columns - lax.rem(offset, columns), columns)
        window = pltpu.roll(merged, back, 1).astype(message.dtype)
        for out in [message] + ([alone] if q == shots - 1 else []):
            spot = out.shape[0] - TAIL - slots * rows
            out[spot : spot + slots * rows, :] = window
            out[spot + slots * rows :, :] = tail.astype(out.dtype)


class Sweep:
    def __init__(self, shots, group, sizes, ops, win, waves, turned_x):
        self.sizes = sizes
        self.ops, self.win, self.waves, self.turned_x = ops, win, waves, turned_x
        slots, rows, columns = sizes
        self.piece = rows // 2
        self.part = columns + self.piece
        self.first = (slots - 1) * self.part
        self.here, tile = lax.axis_index("depth"), lax.axis_index("tile")
        self.shot = lax.rem(self.here, shots)
        self.is_worker = (self.here // shots == lax.rem(tile, group)).astype(jnp.int32)

    def level(self, r, slot):
        _, rows, columns = self.sizes
        start = pl.multiple_of(slot * self.part, self.part)
        op_y = [self.ops[r, half, pl.ds(start, columns), :] for half in range(2)]
        spot = pl.multiple_of(slot * rows, rows)
        window = self.win[r, pl.ds(spot, rows), :].astype(jnp.float32)
        return window, op_y[0], op_y[1], spot

    def level_x(self, r, slot):
        rows, columns = self.sizes[1:]
        tail = pl.multiple_of(slot * self.part + columns, self.piece)
        op_x = jnp.concatenate(
            [self.ops[r, half, pl.ds(tail, self.piece), :] for half in range(2)], axis=0
        )
        return op_x[:, :rows], op_x[:, rows:]

    def blocks(self, re, im):
        upper = jnp.concatenate([re, -im], axis=1)
        return jnp.concatenate([upper, jnp.concatenate([im, re], axis=1)], axis=0)

    def dot(self, a, b, dims):
        return lax.dot_general(a, b, (dims, ((), ())), preferred_element_type=jnp.float32)

    def both_products(self, op_first, wave, both_y, dims):
        _, rows, columns = self.sizes
        parts = []
        for i in range(2):
            middle = self.dot(op_first[i * rows : (i + 1) * rows], wave, ((1,), (0,)))
            parts.append(self.dot(middle.astype(jnp.bfloat16), both_y, dims))
        re, im = parts
        return re[:, :columns] - im[:, columns:], re[:, columns:] + im[:, :columns]

    def down(self, r, slot, place):
        rows = self.sizes[1]
        window, y_re, y_im, _ = self.level(r, slot)
        x_re, x_im = self.level_x(r, slot)
        wave = self.waves[place].astype(jnp.float32)
        gain = 1.0 + window
        scaled = jnp.concatenate([gain * wave[:rows], gain * wave[rows:]], axis=0)
        self.turned_x[place] = self.blocks(x_re.T, x_im.T)
        both_y = jnp.concatenate([y_re, y_im], axis=0)
        moved_re, moved_im = self.both_products(
            self.blocks(x_re, x_im), scaled.astype(jnp.bfloat16), both_y, ((1,), (1,))
        )
        moved = jnp.concatenate([moved_re, moved_im], axis=0)
        self.waves[place + 1] = moved.astype(jnp.bfloat16)
        return place + 1

    def up(self, r, slot, place, wave_up, corr):
        rows = self.sizes[1]
        window, y_re, y_im, spot = self.level(r, slot)
        wave = self.waves[place - 1].astype(jnp.float32)
        both_y = jnp.concatenate([y_re, y_im], axis=1)
        spread_re, spread_im = self.both_products(
            self.turned_x[place - 1], wave_up[...], both_y, ((1,), (0,))
        )
        up_re = (window * wave[:rows] + spread_re).astype(jnp.bfloat16)
        up_im = (window * wave[rows:] + spread_im).astype(jnp.bfloat16)
        wave_up[:rows] = up_re
        wave_up[rows:] = up_im
        product = wave[:rows] * up_re.astype(jnp.float32)
        product += wave[rows:] * up_im.astype(jnp.float32)
        corr[r, pl.ds(spot, rows), :] = product.astype(corr.dtype)
        return place - 1


def down_kernel(sections, shots, group, sizes, source_ref, *refs):
    slots, rows, columns = sizes
    messages, refs = refs[: sections - 1], refs[sections - 1 :]
    own_late, far_half, other_half, far_window, *refs = refs
    ops, win, waves, turned_x, state, op_sem, win_sem, src_sem = refs
    plane = lax.rem(lax.axis_index("tile") // group, 2)
    it = Sweep(shots, group, sizes, ops, win, waves, turned_x)
    first, part = it.first, it.part
    half_rows, win_rows = first + part, slots * rows + TAIL

    def op_copies(r, half):
        place, sem = ops.at[r, half], op_sem.at[r, half]
        if r == sections - 1:
            place = ops.at[r, 1 - plane if half else plane]
            return [pltpu.make_async_copy(other_half if half else far_half, place, sem)]
        message = messages[r].at[pl.ds(half * first, first), :]
        copies = [pltpu.make_async_copy(message, place.at[pl.ds(0, first), :], sem)]
        if r == 0:
            last = own_late.at[pl.ds(half * part, part), :]
            copies.append(pltpu.make_async_copy(last, place.at[pl.ds(first, part), :], sem))
        return copies

    def op_wait(r, partial):
        count = first if partial else half_rows
        for half in range(2):
            place = ops.at[r, half, pl.ds(0, count), :]
            source = far_half.at[pl.ds(0, count), :]
            pltpu.make_async_copy(source, place, op_sem.at[r, half]).wait()

    def win_copy(r):
        message = messages[r] if r < sections - 1 else far_window
        start = message.shape[0] - win_rows
        return pltpu.make_async_copy(
            message.at[pl.ds(start, win_rows), :], win.at[r], win_sem.at[r]
        )

    @pl.when(it.is_worker == 0)
    def _():
        for i in range(3 + sections):
            state[i] = 0

    @pl.when(it.is_worker != 0)
    def _():
        src_copy = pltpu.make_async_copy(source_ref.at[it.shot], waves.at[0], src_sem)
        src_copy.start()
        for r in range(sections):
            win_copy(r).start()
        for section in range(sections):
            for r in range(sections):

                @pl.when((section ^ it.here) == r)
                def _():
                    for half in range(2):
                        for copy in op_copies(r, half):
                            copy.start()

        for r in range(sections):
            win_copy(r).wait()
        for r in range(sections):
            value = jnp.max(win[r, slots * rows :, :].astype(jnp.float32))
            state[3 + r] = value.astype(jnp.int32)
        src_copy.wait()

        def section_down(section, carry):
            place, going, next_section, next_slot = carry
            r = section ^ it.here
            partial = (r != 0) & (r != sections - 1)

            @pl.when(partial)
            def _():
                op_wait(r, True)

            @pl.when(jnp.logical_not(partial))
            def _():
                op_wait(r, False)

            count = state[3 + r]
            ready = jnp.where(partial, jnp.minimum(count, slots - 1), count)
            place = lax.fori_loop(
                0, jnp.where(going, ready, 0), lambda slot, place: it.down(r, slot, place), place
            )
            whole = ready == count
            next_section = jnp.where(going, jnp.where(whole, section + 1, section), next_section)
            next_slot = jnp.where(going, jnp.where(whole, 0, ready), next_slot)
            return place, going & whole, next_section, next_slot

        zero = jnp.int32(0)
        carry = (zero, jnp.bool_(True), zero, zero)
        place, _, next_section, next_slot = lax.fori_loop(0, sections, section_down, carry)
        state[0] = next_section
        state[1] = next_slot
        state[2] = place


def up_kernel(sections, shots, group, sizes, state, *refs):
    slots, rows, columns = sizes
    near_late, far_late, win = refs[:3]
    outs, refs = refs[6 : 6 + sections], refs[6 + sections :]
    ops, waves, turned_x, wave_up, corr, op_sem, out_sem = refs
    it = Sweep(shots, group, sizes, ops, win, waves, turned_x)
    first, part = it.first, it.part

    def late_copies():
        return [
            pltpu.make_async_copy(
                late.at[pl.ds(half * part, part), :],
                ops.at[r, half, pl.ds(first, part), :],
                op_sem.at[r, half],
            )
            for r, late in ((1, near_late), (2, far_late))
            for half in range(2)
        ]

    def out_copy(r):
        place = outs[r].at[pl.ds(0, slots * rows), :]
        return pltpu.make_async_copy(corr.at[r], place, out_sem.at[r])

    @pl.when(it.is_worker == 0)
    def _():
        corr[0] = jnp.zeros(corr.shape[1:], corr.dtype)
        out_copy(0).start()
        out_copy(0).wait()

    @pl.when(it.is_worker != 0)
    def _():
        for copy in late_copies():
            copy.start()
        corr[...] = jnp.zeros(corr.shape, corr.dtype)
        wave_up[...] = jnp.zeros(wave_up.shape, wave_up.dtype)
        next_section, next_slot = state[0], state[1]
        for copy in late_copies():
            copy.wait()

        def section_down(section, place):
            r = section ^ it.here
            begin = jnp.where(section == next_section, next_slot, 0)
            return lax.fori_loop(
                begin, state[3 + r], lambda slot, place: it.down(r, slot, place), place
            )

        last = lax.fori_loop(next_section, sections, section_down, state[2])

        def section_up(step, place):
            r = (sections - 1 - step) ^ it.here
            count = state[3 + r]
            place = lax.fori_loop(
                0,
                count,
                lambda inner, place: it.up(r, count - 1 - inner, place, wave_up, corr),
                place,
            )
            for out in range(sections):

                @pl.when(r == out)
                def _():
                    out_copy(out).start()

            return place

        lax.fori_loop(0, sections, section_up, last)
        for r in range(sections):
            out_copy(r).wait()


def hold_kernel(array_ref, after_ref, out_ref):
    pass


def place_kernel(shots, anchors, *refs):
    arrived, (left_out, own_out) = refs[:-2], refs[-2:]
    section, tile = lax.axis_index("depth"), lax.axis_index("tile")
    places, columns = left_out.shape
    left_sum, own_sum = None, None
    for q in range(shots):
        offset = anchors[lax.rem(section, shots) ^ q] - (tile - 1) * columns
        total = None
        for r in range(q, len(arrived), shots):
            value = arrived[r][:places, :].astype(jnp.float32)
            total = value if total is None else total + value
        turned = pltpu.roll(total, lax.rem(offset, columns), 1)
        lanes = lax.broadcasted_iota(jnp.int32, turned.shape, 1)
        left = jnp.where(lanes >= offset, turned, 0.0)
        own = jnp.where(lanes >= offset, 0.0, turned)
        left_sum = left if left_sum is None else left_sum + left
        own_sum = own if own_sum is None else own_sum + own
    left_out[...] = left_sum.astype(left_out.dtype)
    own_out[...] = own_sum


def kept(array):
    return pltpu.with_memory_space_constraint(array, pltpu.HBM)


def held(array):
    return pltpu.with_memory_space_constraint(array, pltpu.VMEM)


def on_device(source, anchors, counts, reflect, lateral_x, lateral_y):
    shots, _, rows, columns = source.shape
    slots = reflect.shape[1]
    sizes = (slots, rows, columns)
    plan = Plan(shots)
    sections, group = plan.sections, plan.group
    assert shots == 2
    bf16 = jnp.bfloat16
    smem = pl.BlockSpec(memory_space=pltpu.SMEM)
    vmem = pl.BlockSpec(memory_space=pltpu.VMEM)
    hbm = pl.BlockSpec(memory_space=pltpu.HBM)
    anywhere = pl.BlockSpec(memory_space=pl.ANY)

    def params(mib):
        return pltpu.CompilerParams(vmem_limit_bytes=mib * MIB)

    tile_reflect = reflect[0].reshape(slots * rows, columns)
    halo = lax.ppermute(tile_reflect, "tile", [(i, i + 1) for i in range(plan.tiles - 1)])
    part = columns + rows // 2
    half_rows, win_rows = slots * part, slots * rows + TAIL
    early_rows = 2 * (half_rows - part) + win_rows
    even = pltpu.VMEM((early_rows + 5 * TAIL, columns), bf16)
    odd = pltpu.VMEM((early_rows, columns), bf16)
    even_early, odd_early, late, far_half = pl.pallas_call(
        functools.partial(pack_kernel, group, sizes),
        out_shape=[
            even,
            odd,
            jax.ShapeDtypeStruct((2 * part, columns), bf16),
            jax.ShapeDtypeStruct((half_rows, columns), bf16),
        ],
        in_specs=[hbm, hbm],
        out_specs=[vmem] * 4,
        scratch_shapes=[
            pltpu.VMEM(lateral_x.shape[1:], bf16),
            pltpu.VMEM(lateral_y.shape[1:], bf16),
            pltpu.SemaphoreType.DMA((2,)),
        ],
        compiler_params=params(12),
        name="pack",
    )(kept(lateral_x[0]), kept(lateral_y[0]))
    last = sections - 1
    far_half = lax.ppermute(far_half, BOTH, plan.to_workers(last))
    even_early, odd_early, far_window = pl.pallas_call(
        functools.partial(window_kernel, shots, sizes),
        out_shape=[even, odd, jax.ShapeDtypeStruct((win_rows, columns), bf16)],
        in_specs=[hbm, smem, vmem, hbm, vmem, vmem],
        out_specs=[vmem] * 3,
        scratch_shapes=[
            pltpu.SMEM((shots,), jnp.int32),
            pltpu.VMEM((slots * rows, columns), bf16),
            pltpu.SemaphoreType.DMA((2,)),
        ],
        input_output_aliases={4: 0, 5: 1},
        compiler_params=params(12),
        cost_estimate=pl.CostEstimate(flops=3 * 10**9, bytes_accessed=4 * MIB, transcendentals=0),
        name="windows",
    )(kept(anchors), counts, halo, kept(tile_reflect), held(even_early), held(odd_early))
    messages = [
        even_early,
        lax.ppermute(odd_early, BOTH, plan.to_workers(1)),
        lax.ppermute(even_early, BOTH, plan.to_workers(2)),
    ]
    far_window = lax.ppermute(far_window, BOTH, plan.to_workers(last))
    other_half = lax.ppermute(far_half, BOTH, plan.swap_workers())
    late = pl.pallas_call(
        hold_kernel,
        out_shape=jax.ShapeDtypeStruct(late.shape, bf16),
        in_specs=[anywhere] * 2,
        out_specs=anywhere,
        input_output_aliases={0: 0},
        compiler_params=params(2),
        cost_estimate=pl.CostEstimate(flops=36 * 10**8, bytes_accessed=0, transcendentals=0),
        name="hold",
    )(late, far_window)
    lates = [lax.ppermute(late, BOTH, plan.ops_to_workers(r)) for r in (1, 2)]
    ops = pltpu.VMEM((sections, 2, half_rows, columns), bf16)
    win = pltpu.VMEM((sections, win_rows, columns), bf16)
    waves = pltpu.VMEM((sections * slots + 1, 2 * rows, columns), bf16)
    turned_x = pltpu.VMEM((sections * slots, 2 * rows, 2 * rows), bf16)
    buffers = pl.pallas_call(
        functools.partial(down_kernel, sections, shots, group, sizes),
        out_shape=[ops, win, waves, turned_x, jax.ShapeDtypeStruct((3 + sections,), jnp.int32)],
        in_specs=[hbm] + [anywhere] * (sections + 3),
        out_specs=[vmem] * 4 + [smem],
        scratch_shapes=[
            pltpu.SemaphoreType.DMA((sections, 2)),
            pltpu.SemaphoreType.DMA((sections,)),
            pltpu.SemaphoreType.DMA,
        ],
        compiler_params=params(16),
        cost_estimate=pl.CostEstimate(flops=0, bytes_accessed=4 * MIB, transcendentals=0),
        name="down",
    )(
        kept(source.reshape(shots, 2 * rows, columns)), *messages, late, far_half, other_half,
        far_window
    )
    ops_done, win_done, waves_done, turned_done = [held(buffer) for buffer in buffers[:4]]
    corr_shape = jax.ShapeDtypeStruct((slots * rows, columns), bf16)
    correlations = pl.pallas_call(
        functools.partial(up_kernel, sections, shots, group, sizes),
        out_shape=[
            jax.ShapeDtypeStruct((slots * rows + TAIL * r, columns), bf16) for r in range(sections)
        ]
        + [ops, waves, turned_x],
        in_specs=[smem] + [anywhere] * 2 + [vmem] * 4,
        out_specs=[anywhere] * sections + [vmem] * 3,
        scratch_shapes=[
            pltpu.VMEM((2 * rows, columns), bf16),
            pltpu.VMEM((sections, slots * rows, columns), bf16),
            pltpu.SemaphoreType.DMA((sections, 2)),
            pltpu.SemaphoreType.DMA((sections,)),
        ],
        input_output_aliases={4: sections, 5: sections + 1, 6: sections + 2},
        compiler_params=params(16),
        name="up",
    )(buffers[4], *lates, win_done, ops_done, waves_done, turned_done)

    arrived = [correlations[0]] + [
        lax.ppermute(correlations[r], BOTH, plan.from_workers(r)) for r in range(1, sections)
    ]
    left, own = pl.pallas_call(
        functools.partial(place_kernel, shots),
        out_shape=[corr_shape, jax.ShapeDtypeStruct((slots * rows, columns), jnp.float32)],
        in_specs=[smem] + [vmem] * sections,
        out_specs=[vmem, vmem],
        compiler_params=params(8),
        name="place",
    )(anchors, *arrived)
    from_right = lax.ppermute(left, "tile", [(i + 1, i) for i in range(plan.tiles - 1)])
    image = own + from_right.astype(jnp.float32)
    return image.reshape(1, slots, rows, columns)


def solution(mesh):
    return jax.shard_map(
        on_device,
        mesh=mesh,
        in_specs=(
            P("tile", None, None, None),
            P("tile"),
            P("depth"),
            P("depth", None, None, "tile"),
            P("depth", None, None, None, None),
            P("depth", None, None, None, None),
        ),
        out_specs=P("depth", None, None, "tile"),
        check_vma=False,
    )
```

```python
import functools

import jax
import jax.numpy as jnp
from jax import lax
from jax.experimental import pallas as pl
from jax.experimental.pallas import tpu as pltpu
from jax.sharding import PartitionSpec as P

BOTH = ("depth", "tile")
MIB = 1024 * 1024
TAIL = 16


class Plan:
    def __init__(self, shots):
        self.sections = lax.axis_size("depth")
        self.tiles = lax.axis_size("tile")
        self.shots = shots
        self.group = self.sections // shots
        assert self.sections == 4 and self.group * shots == self.sections
        assert self.tiles % (2 * self.group) == 0

    def device(self, depth, tile):
        return depth * self.tiles + tile

    def bases(self):
        return range(0, self.tiles, self.group)

    def worker(self, base, w):
        return self.device(w, base + w // self.shots)

    def other(self, w, base):
        return self.device(w, base + (w // self.shots + 1) % self.group)

    def ops_to_workers(self, r):
        return [
            (self.other(w ^ r, base), self.worker(base, w))
            for base in self.bases()
            for w in range(self.sections)
        ]

    def swap_workers(self):
        return [
            (self.worker(base, w), self.worker((base // self.group ^ 1) * self.group, w))
            for base in self.bases()
            for w in range(self.sections)
        ]

    def to_workers(self, r):
        return [
            (self.device(w ^ r, base + w // self.shots), self.worker(base, w))
            for base in self.bases()
            for w in range(self.sections)
        ]

    def from_workers(self, r):
        return [(b, a) for a, b in self.to_workers(r)]


def pack_kernel(group, sizes, x_hbm, y_hbm, even, odd, late, half_out, x_ref, y_ref, sem):
    slots, rows, columns = sizes
    loads = [
        pltpu.make_async_copy(x_hbm, x_ref, sem.at[0]),
        pltpu.make_async_copy(y_hbm, y_ref, sem.at[1]),
    ]
    for load in loads:
        load.start()
    for load in loads:
        load.wait()
    piece = rows // 2
    part = columns + piece
    first = (slots - 1) * part
    for half in range(2):
        for slot in range(slots):
            op_x = jnp.concatenate(
                [x_ref[slot, i, half * piece : (half + 1) * piece, :] for i in range(2)], axis=1
            )
            op_y = y_ref[slot, half]
            if slot < slots - 1:
                places = [(out, half * first + slot * part) for out in (even, odd)]
            else:
                places = [(late, half * part)]
            for out, spot in places:
                out[spot : spot + columns, :] = op_y
                out[spot + columns : spot + part, :] = op_x
    plane = lax.rem(lax.axis_index("tile") // group, 2)
    half_out[:first, :] = even[pl.ds(pl.multiple_of(plane * first, first), first), :]
    half_out[first:, :] = late[pl.ds(pl.multiple_of(plane * part, part), part), :]


def window_kernel(shots, sizes, anchors_hbm, counts, left_ref, right_hbm, *refs):
    slots, rows, columns = sizes
    messages, (alone, anchors, right_ref, sem) = refs[shots : 2 * shots], refs[2 * shots :]
    loads = [
        pltpu.make_async_copy(anchors_hbm, anchors, sem.at[0]),
        pltpu.make_async_copy(right_hbm, right_ref, sem.at[1]),
    ]
    for load in loads:
        load.start()
    for load in loads:
        load.wait()
    section, tile = lax.axis_index("depth"), lax.axis_index("tile")
    left, right = left_ref[...].astype(jnp.float32), right_ref[...].astype(jnp.float32)
    lanes = lax.broadcasted_iota(jnp.int32, left.shape, 1)
    tail = jnp.full((TAIL, columns), counts[0].astype(jnp.float32), jnp.float32)
    for q, message in enumerate(messages):
        offset = anchors[lax.rem(section, shots) ^ q] - (tile - 1) * columns
        merged = jnp.where(lanes >= offset, left, right)
        back = lax.rem(columns - lax.rem(offset, columns), columns)
        window = pltpu.roll(merged, back, 1).astype(message.dtype)
        for out in [message] + ([alone] if q == shots - 1 else []):
            spot = out.shape[0] - TAIL - slots * rows
            out[spot : spot + slots * rows, :] = window
            out[spot + slots * rows :, :] = tail.astype(out.dtype)


class Sweep:
    def __init__(self, shots, group, sizes, level_y, turned_x, level_w, waves, stage_x):
        self.sizes = sizes
        self.level_y, self.turned_x, self.level_w = level_y, turned_x, level_w
        self.waves, self.stage_x = waves, stage_x
        slots, rows, columns = sizes
        self.piece = rows // 2
        self.part = columns + self.piece
        self.first = (slots - 1) * self.part
        self.half_rows = self.first + self.part
        self.win_rows = slots * rows + TAIL
        self.here, tile = lax.axis_index("depth"), lax.axis_index("tile")
        self.shot = lax.rem(self.here, shots)
        self.is_worker = (self.here // shots == lax.rem(tile, group)).astype(jnp.int32)

    def window_start(self, window_ref):
        return window_ref.shape[0] - self.win_rows

    def fetch(self, r, slot, place, sources):
        slots, rows, columns = self.sizes
        for r_of, (early, late, window) in enumerate(sources):
            early_slots = slots if early.shape[0] == 2 * self.half_rows else slots - 1
            choices = [(early, early_slots * self.part, slot < early_slots, slot)]
            if late is not None:
                choices.append((late, self.part, slot == slots - 1, 0))
            for ref, stride, chosen, at in choices:

                @pl.when((r == r_of) & chosen)
                def _():
                    for half in range(2):
                        start = pl.multiple_of(half * stride + at * self.part, self.piece)
                        self.level_y[place, half * columns : (half + 1) * columns, :] = ref[
                            pl.ds(start, columns), :
                        ]
                        tail = pl.multiple_of(start + columns, self.piece)
                        self.stage_x[half * self.piece : (half + 1) * self.piece, :] = ref[
                            pl.ds(tail, self.piece), :
                        ]
                    spot = self.window_start(window) + slot * rows
                    self.level_w[place] = window[pl.ds(pl.multiple_of(spot, TAIL), rows), :]

    def blocks(self, re, im):
        upper = jnp.concatenate([re, -im], axis=1)
        return jnp.concatenate([upper, jnp.concatenate([im, re], axis=1)], axis=0)

    def complex_sum(self, both):
        _, rows, columns = self.sizes
        with_re, with_im = both[:, :columns], both[:, columns:]
        return with_re[:rows] - with_im[rows:], with_im[:rows] + with_re[rows:]

    def dot(self, a, b, dims):
        return lax.dot_general(a, b, (dims, ((), ())), preferred_element_type=jnp.float32)

    def down(self, place):
        rows = self.sizes[1]
        x_re, x_im = self.stage_x[:, :rows], self.stage_x[:, rows:]
        wave = self.waves[place].astype(jnp.float32)
        gain = 1.0 + self.level_w[place].astype(jnp.float32)
        scaled = jnp.concatenate([gain * wave[:rows], gain * wave[rows:]], axis=0)
        self.turned_x[place] = self.blocks(x_re.T, x_im.T)
        middle = self.dot(self.blocks(x_re, x_im), scaled.astype(jnp.bfloat16), ((1,), (0,)))
        both = self.dot(middle.astype(jnp.bfloat16), self.level_y[place], ((1,), (1,)))
        moved = jnp.concatenate(self.complex_sum(both), axis=0)
        self.waves[place + 1] = moved.astype(jnp.bfloat16)
        return place + 1

    def up(self, r, slot, place, wave_up, corr):
        _, rows, columns = self.sizes
        level = place - 1
        wave = self.waves[level].astype(jnp.float32)
        window = self.level_w[level].astype(jnp.float32)
        back = self.dot(self.turned_x[level], wave_up[...], ((1,), (0,)))
        both_y = jnp.concatenate(
            [self.level_y[level, :columns, :], self.level_y[level, columns:, :]], axis=1
        )
        both = self.dot(back.astype(jnp.bfloat16), both_y, ((1,), (0,)))
        spread_re, spread_im = self.complex_sum(both)
        up_re = (window * wave[:rows] + spread_re).astype(jnp.bfloat16)
        up_im = (window * wave[rows:] + spread_im).astype(jnp.bfloat16)
        wave_up[:rows] = up_re
        wave_up[rows:] = up_im
        product = wave[:rows] * up_re.astype(jnp.float32)
        product += wave[rows:] * up_im.astype(jnp.float32)
        spot = pl.multiple_of(slot * rows, rows)
        corr[r, pl.ds(spot, rows), :] = product.astype(corr.dtype)
        return level


def down_kernel(sections, shots, group, sizes, source_ref, *refs):
    slots, rows, _ = sizes
    (own, near, far), (own_late, joined, far_window) = refs[:3], refs[3:6]
    level_y, turned_x, level_w, waves, state, stage_x = refs[6:]
    it = Sweep(shots, group, sizes, level_y, turned_x, level_w, waves, stage_x)
    sources = [
        (own, own_late, own),
        (near, None, near),
        (far, None, far),
        (joined, None, far_window),
    ]

    @pl.when(it.is_worker == 0)
    def _():
        for i in range(3 + sections):
            state[i] = 0

    @pl.when(it.is_worker != 0)
    def _():
        waves[0] = source_ref[it.shot]
        for r, (_, _, window) in enumerate(sources):
            value = jnp.max(window[window.shape[0] - TAIL :, :].astype(jnp.float32))
            state[3 + r] = value.astype(jnp.int32)

        def section_down(section, carry):
            place, going, next_section, next_slot = carry
            r = section ^ it.here
            partial = (r != 0) & (r != sections - 1)
            count = state[3 + r]
            ready = jnp.where(partial, jnp.minimum(count, slots - 1), count)

            def level_down(slot, place):
                it.fetch(r, slot, place, sources)
                return it.down(place)

            place = lax.fori_loop(0, jnp.where(going, ready, 0), level_down, place)
            whole = ready == count
            next_section = jnp.where(going, jnp.where(whole, section + 1, section), next_section)
            next_slot = jnp.where(going, jnp.where(whole, 0, ready), next_slot)
            return place, going & whole, next_section, next_slot

        zero = jnp.int32(0)
        carry = (zero, jnp.bool_(True), zero, zero)
        place, _, next_section, next_slot = lax.fori_loop(0, sections, section_down, carry)
        state[0] = next_section
        state[1] = next_slot
        state[2] = place


def up_kernel(sections, shots, group, sizes, state, *refs):
    slots, rows, _ = sizes
    (own, near, far), (own_late, near_late, far_late, joined, far_window) = refs[:3], refs[3:8]
    outs, refs = refs[12 : 12 + sections], refs[12 + sections :]
    level_y, turned_x, level_w, waves, stage_x, wave_up, corr, out_sem = refs
    it = Sweep(shots, group, sizes, level_y, turned_x, level_w, waves, stage_x)
    sources = [
        (own, own_late, own),
        (near, near_late, near),
        (far, far_late, far),
        (joined, None, far_window),
    ]

    def out_copy(r):
        place = outs[r].at[pl.ds(0, slots * rows), :]
        return pltpu.make_async_copy(corr.at[r], place, out_sem.at[r])

    @pl.when(it.is_worker == 0)
    def _():
        corr[0] = jnp.zeros(corr.shape[1:], corr.dtype)
        out_copy(0).start()
        out_copy(0).wait()

    @pl.when(it.is_worker != 0)
    def _():
        corr[...] = jnp.zeros(corr.shape, corr.dtype)
        wave_up[...] = jnp.zeros(wave_up.shape, wave_up.dtype)
        next_section, next_slot = state[0], state[1]

        def section_down(section, place):
            r = section ^ it.here
            begin = jnp.where(section == next_section, next_slot, 0)

            def level_down(slot, place):
                it.fetch(r, slot, place, sources)
                return it.down(place)

            return lax.fori_loop(begin, state[3 + r], level_down, place)

        last = lax.fori_loop(next_section, sections, section_down, state[2])

        def section_up(step, place):
            r = (sections - 1 - step) ^ it.here
            count = state[3 + r]
            place = lax.fori_loop(
                0,
                count,
                lambda inner, place: it.up(r, count - 1 - inner, place, wave_up, corr),
                place,
            )
            for out in range(sections):

                @pl.when(r == out)
                def _():
                    out_copy(out).start()

            return place

        lax.fori_loop(0, sections, section_up, last)
        for r in range(sections):
            out_copy(r).wait()


def join_kernel(group, first_ref, second_ref, out_ref):
    plane = lax.rem(lax.axis_index("tile") // group, 2)
    half_rows = first_ref.shape[0]
    for i, ref in enumerate((first_ref, second_ref)):
        start = pl.multiple_of((plane if i == 0 else 1 - plane) * half_rows, half_rows)
        out_ref[pl.ds(start, half_rows), :] = ref[...]


def hold_kernel(array_ref, after_ref, out_ref):
    pass


def place_kernel(shots, anchors, *refs):
    arrived, (left_out, own_out) = refs[:-2], refs[-2:]
    section, tile = lax.axis_index("depth"), lax.axis_index("tile")
    places, columns = left_out.shape
    left_sum, own_sum = None, None
    for q in range(shots):
        offset = anchors[lax.rem(section, shots) ^ q] - (tile - 1) * columns
        total = None
        for r in range(q, len(arrived), shots):
            value = arrived[r][:places, :].astype(jnp.float32)
            total = value if total is None else total + value
        turned = pltpu.roll(total, lax.rem(offset, columns), 1)
        lanes = lax.broadcasted_iota(jnp.int32, turned.shape, 1)
        left = jnp.where(lanes >= offset, turned, 0.0)
        own = jnp.where(lanes >= offset, 0.0, turned)
        left_sum = left if left_sum is None else left_sum + left
        own_sum = own if own_sum is None else own_sum + own
    left_out[...] = left_sum.astype(left_out.dtype)
    own_out[...] = own_sum


def kept(array):
    return pltpu.with_memory_space_constraint(array, pltpu.HBM)


def held(array):
    return pltpu.with_memory_space_constraint(array, pltpu.VMEM)


def on_device(source, anchors, counts, reflect, lateral_x, lateral_y):
    shots, _, rows, columns = source.shape
    slots = reflect.shape[1]
    sizes = (slots, rows, columns)
    plan = Plan(shots)
    sections, group = plan.sections, plan.group
    assert shots == 2
    bf16 = jnp.bfloat16
    smem = pl.BlockSpec(memory_space=pltpu.SMEM)
    vmem = pl.BlockSpec(memory_space=pltpu.VMEM)
    hbm = pl.BlockSpec(memory_space=pltpu.HBM)
    anywhere = pl.BlockSpec(memory_space=pl.ANY)

    def params(mib):
        return pltpu.CompilerParams(vmem_limit_bytes=mib * MIB)

    tile_reflect = reflect[0].reshape(slots * rows, columns)
    halo = lax.ppermute(tile_reflect, "tile", [(i, i + 1) for i in range(plan.tiles - 1)])
    part = columns + rows // 2
    half_rows, win_rows = slots * part, slots * rows + TAIL
    early_rows = 2 * (half_rows - part) + win_rows
    even = pltpu.VMEM((early_rows + 5 * TAIL, columns), bf16)
    odd = pltpu.VMEM((early_rows, columns), bf16)
    even_early, odd_early, late, far_half = pl.pallas_call(
        functools.partial(pack_kernel, group, sizes),
        out_shape=[
            even,
            odd,
            jax.ShapeDtypeStruct((2 * part, columns), bf16),
            jax.ShapeDtypeStruct((half_rows, columns), bf16),
        ],
        in_specs=[hbm, hbm],
        out_specs=[vmem] * 4,
        scratch_shapes=[
            pltpu.VMEM(lateral_x.shape[1:], bf16),
            pltpu.VMEM(lateral_y.shape[1:], bf16),
            pltpu.SemaphoreType.DMA((2,)),
        ],
        compiler_params=params(12),
        name="pack",
    )(kept(lateral_x[0]), kept(lateral_y[0]))
    last = sections - 1
    far_half = lax.ppermute(far_half, BOTH, plan.to_workers(last))
    even_early, odd_early, far_window = pl.pallas_call(
        functools.partial(window_kernel, shots, sizes),
        out_shape=[even, odd, jax.ShapeDtypeStruct((win_rows, columns), bf16)],
        in_specs=[hbm, smem, vmem, hbm, vmem, vmem],
        out_specs=[vmem] * 3,
        scratch_shapes=[
            pltpu.SMEM((shots,), jnp.int32),
            pltpu.VMEM((slots * rows, columns), bf16),
            pltpu.SemaphoreType.DMA((2,)),
        ],
        input_output_aliases={4: 0, 5: 1},
        compiler_params=params(12),
        cost_estimate=pl.CostEstimate(flops=3 * 10**9, bytes_accessed=4 * MIB, transcendentals=0),
        name="windows",
    )(kept(anchors), counts, halo, kept(tile_reflect), held(even_early), held(odd_early))
    messages = [
        even_early,
        lax.ppermute(odd_early, BOTH, plan.to_workers(1)),
        lax.ppermute(even_early, BOTH, plan.to_workers(2)),
    ]
    far_window = lax.ppermute(far_window, BOTH, plan.to_workers(last))
    other_half = lax.ppermute(far_half, BOTH, plan.swap_workers())
    late = pl.pallas_call(
        hold_kernel,
        out_shape=jax.ShapeDtypeStruct(late.shape, bf16),
        in_specs=[anywhere] * 2,
        out_specs=anywhere,
        input_output_aliases={0: 0},
        compiler_params=params(2),
        cost_estimate=pl.CostEstimate(flops=36 * 10**8, bytes_accessed=0, transcendentals=0),
        name="hold",
    )(late, far_window)
    lates = [lax.ppermute(late, BOTH, plan.ops_to_workers(r)) for r in (1, 2)]
    joined = pl.pallas_call(
        functools.partial(join_kernel, group),
        out_shape=pltpu.VMEM((2 * half_rows, columns), bf16),
        in_specs=[vmem] * 2,
        out_specs=vmem,
        compiler_params=params(8),
        name="join",
    )(held(far_half), held(other_half))

    levels = sections * slots
    buffers = [
        pltpu.VMEM((levels, 2 * columns, columns), bf16),
        pltpu.VMEM((levels, 2 * rows, 2 * rows), bf16),
        pltpu.VMEM((levels, rows, columns), bf16),
        pltpu.VMEM((levels + 1, 2 * rows, columns), bf16),
    ]
    stage_x = pltpu.VMEM((rows, 2 * rows), bf16)
    messages = [held(message) for message in messages]
    late, joined, far_window = held(late), held(joined), held(far_window)
    *filled, state = pl.pallas_call(
        functools.partial(down_kernel, sections, shots, group, sizes),
        out_shape=buffers + [jax.ShapeDtypeStruct((3 + sections,), jnp.int32)],
        in_specs=[vmem] * 7,
        out_specs=[vmem] * 4 + [smem],
        scratch_shapes=[stage_x],
        compiler_params=params(24),
        name="down",
    )(held(source.reshape(shots, 2 * rows, columns)), *messages, late, joined, far_window)
    correlations = pl.pallas_call(
        functools.partial(up_kernel, sections, shots, group, sizes),
        out_shape=[
            jax.ShapeDtypeStruct((slots * rows + TAIL * r, columns), bf16) for r in range(sections)
        ]
        + buffers,
        in_specs=[smem] + [vmem] * 12,
        out_specs=[anywhere] * sections + [vmem] * 4,
        scratch_shapes=[
            stage_x,
            pltpu.VMEM((2 * rows, columns), bf16),
            pltpu.VMEM((sections, slots * rows, columns), bf16),
            pltpu.SemaphoreType.DMA((sections,)),
        ],
        input_output_aliases={9 + i: sections + i for i in range(4)},
        compiler_params=params(24),
        name="up",
    )(
        state, *messages, late, *[held(part) for part in lates], joined, far_window,
        *[held(buffer) for buffer in filled],
    )

    corr_shape = jax.ShapeDtypeStruct((slots * rows, columns), bf16)
    arrived = [correlations[0]] + [
        lax.ppermute(correlations[r], BOTH, plan.from_workers(r)) for r in range(1, sections)
    ]
    left, own = pl.pallas_call(
        functools.partial(place_kernel, shots),
        out_shape=[corr_shape, jax.ShapeDtypeStruct((slots * rows, columns), jnp.float32)],
        in_specs=[smem] + [vmem] * sections,
        out_specs=[vmem, vmem],
        compiler_params=params(8),
        name="place",
    )(anchors, *arrived)
    from_right = lax.ppermute(left, "tile", [(i + 1, i) for i in range(plan.tiles - 1)])
    image = own + from_right.astype(jnp.float32)
    return image.reshape(1, slots, rows, columns)


def solution(mesh):
    return jax.shard_map(
        on_device,
        mesh=mesh,
        in_specs=(
            P("tile", None, None, None),
            P("tile"),
            P("depth"),
            P("depth", None, None, "tile"),
            P("depth", None, None, None, None),
            P("depth", None, None, None, None),
        ),
        out_specs=P("depth", None, None, "tile"),
        check_vma=False,
    )
```

```python
import functools

import jax
import jax.numpy as jnp
from jax import lax
from jax.experimental import pallas as pl
from jax.experimental.pallas import tpu as pltpu
from jax.sharding import PartitionSpec as P

BOTH = ("depth", "tile")
MIB = 1024 * 1024
TAIL = 16


class Plan:
    def __init__(self, shots):
        self.sections = lax.axis_size("depth")
        self.tiles = lax.axis_size("tile")
        self.shots = shots
        self.group = self.sections // shots
        assert self.sections == 4 and self.group * shots == self.sections
        assert self.tiles % (2 * self.group) == 0

    def device(self, depth, tile):
        return depth * self.tiles + tile

    def bases(self):
        return range(0, self.tiles, self.group)

    def worker(self, base, w):
        return self.device(w, base + w // self.shots)

    def other(self, w, base):
        return self.device(w, base + (w // self.shots + 1) % self.group)

    def ops_to_workers(self, r):
        return [
            (self.other(w ^ r, base), self.worker(base, w))
            for base in self.bases()
            for w in range(self.sections)
        ]

    def swap_workers(self):
        return [
            (self.worker(base, w), self.worker((base // self.group ^ 1) * self.group, w))
            for base in self.bases()
            for w in range(self.sections)
        ]

    def to_workers(self, r):
        return [
            (self.device(w ^ r, base + w // self.shots), self.worker(base, w))
            for base in self.bases()
            for w in range(self.sections)
        ]

    def from_workers(self, r):
        return [(b, a) for a, b in self.to_workers(r)]


def pack_kernel(group, sizes, x_hbm, y_hbm, even, odd, late, half_out, x_ref, y_ref, sem):
    slots, rows, columns = sizes
    loads = [
        pltpu.make_async_copy(x_hbm, x_ref, sem.at[0]),
        pltpu.make_async_copy(y_hbm, y_ref, sem.at[1]),
    ]
    for load in loads:
        load.start()
    for load in loads:
        load.wait()
    piece = rows // 2
    part = columns + piece
    first = (slots - 1) * part
    for half in range(2):
        for slot in range(slots):
            op_x = jnp.concatenate(
                [x_ref[slot, i, half * piece : (half + 1) * piece, :] for i in range(2)], axis=1
            )
            op_y = y_ref[slot, half]
            if slot < slots - 1:
                places = [(out, half * first + slot * part) for out in (even, odd)]
            else:
                places = [(late, half * part)]
            for out, spot in places:
                out[spot : spot + columns, :] = op_y
                out[spot + columns : spot + part, :] = op_x
    plane = lax.rem(lax.axis_index("tile") // group, 2)
    half_out[:first, :] = even[pl.ds(pl.multiple_of(plane * first, first), first), :]
    half_out[first:, :] = late[pl.ds(pl.multiple_of(plane * part, part), part), :]


def window_kernel(shots, sizes, anchors_hbm, counts, left_ref, right_hbm, *refs):
    slots, rows, columns = sizes
    messages, (alone, anchors, right_ref, sem) = refs[shots : 2 * shots], refs[2 * shots :]
    loads = [
        pltpu.make_async_copy(anchors_hbm, anchors, sem.at[0]),
        pltpu.make_async_copy(right_hbm, right_ref, sem.at[1]),
    ]
    for load in loads:
        load.start()
    for load in loads:
        load.wait()
    section, tile = lax.axis_index("depth"), lax.axis_index("tile")
    left, right = left_ref[...].astype(jnp.float32), right_ref[...].astype(jnp.float32)
    lanes = lax.broadcasted_iota(jnp.int32, left.shape, 1)
    tail = jnp.full((TAIL, columns), counts[0].astype(jnp.float32), jnp.float32)
    for q, message in enumerate(messages):
        offset = anchors[lax.rem(section, shots) ^ q] - (tile - 1) * columns
        merged = jnp.where(lanes >= offset, left, right)
        back = lax.rem(columns - lax.rem(offset, columns), columns)
        window = pltpu.roll(merged, back, 1).astype(message.dtype)
        for out in [message] + ([alone] if q == shots - 1 else []):
            spot = out.shape[0] - TAIL - slots * rows
            out[spot : spot + slots * rows, :] = window
            out[spot + slots * rows :, :] = tail.astype(out.dtype)


class Sweep:
    def __init__(self, shots, group, sizes, level_y, turned_x, level_w, waves, stage_x):
        self.sizes = sizes
        self.level_y, self.turned_x, self.level_w = level_y, turned_x, level_w
        self.waves, self.stage_x = waves, stage_x
        slots, rows, columns = sizes
        self.piece = rows // 2
        self.part = columns + self.piece
        self.first = (slots - 1) * self.part
        self.half_rows = self.first + self.part
        self.win_rows = slots * rows + TAIL
        self.here, tile = lax.axis_index("depth"), lax.axis_index("tile")
        self.shot = lax.rem(self.here, shots)
        self.is_worker = (self.here // shots == lax.rem(tile, group)).astype(jnp.int32)

    def window_start(self, window_ref):
        return window_ref.shape[0] - self.win_rows

    def fetch(self, r, slot, place, sources):
        slots, rows, columns = self.sizes
        for r_of, (early, late, window) in enumerate(sources):
            early_slots = slots if early.shape[0] == 2 * self.half_rows else slots - 1
            choices = [(early, early_slots * self.part, slot < early_slots, slot)]
            if late is not None:
                choices.append((late, self.part, slot == slots - 1, 0))
            for ref, stride, chosen, at in choices:

                @pl.when((r == r_of) & chosen)
                def _():
                    for half in range(2):
                        start = pl.multiple_of(half * stride + at * self.part, self.piece)
                        self.level_y[place, half * columns : (half + 1) * columns, :] = ref[
                            pl.ds(start, columns), :
                        ]
                        tail = pl.multiple_of(start + columns, self.piece)
                        self.stage_x[half * self.piece : (half + 1) * self.piece, :] = ref[
                            pl.ds(tail, self.piece), :
                        ]
                    spot = self.window_start(window) + slot * rows
                    self.level_w[place] = window[pl.ds(pl.multiple_of(spot, TAIL), rows), :]

    def blocks(self, re, im):
        upper = jnp.concatenate([re, -im], axis=1)
        return jnp.concatenate([upper, jnp.concatenate([im, re], axis=1)], axis=0)

    def complex_sum(self, both):
        _, rows, columns = self.sizes
        with_re, with_im = both[:, :columns], both[:, columns:]
        return with_re[:rows] - with_im[rows:], with_im[:rows] + with_re[rows:]

    def dot(self, a, b, dims):
        return lax.dot_general(a, b, (dims, ((), ())), preferred_element_type=jnp.float32)

    def down(self, place):
        rows = self.sizes[1]
        x_re, x_im = self.stage_x[:, :rows], self.stage_x[:, rows:]
        wave = self.waves[place].astype(jnp.float32)
        gain = 1.0 + self.level_w[place].astype(jnp.float32)
        scaled = jnp.concatenate([gain * wave[:rows], gain * wave[rows:]], axis=0)
        self.turned_x[place] = self.blocks(x_re.T, x_im.T)
        middle = self.dot(self.blocks(x_re, x_im), scaled.astype(jnp.bfloat16), ((1,), (0,)))
        both = self.dot(middle.astype(jnp.bfloat16), self.level_y[place], ((1,), (1,)))
        moved = jnp.concatenate(self.complex_sum(both), axis=0)
        self.waves[place + 1] = moved.astype(jnp.bfloat16)
        return place + 1

    def up(self, r, slot, place, wave_up, outs):
        _, rows, columns = self.sizes
        level = place - 1
        wave = self.waves[level].astype(jnp.float32)
        window = self.level_w[level].astype(jnp.float32)
        back = self.dot(self.turned_x[level], wave_up[...], ((1,), (0,)))
        both_y = jnp.concatenate(
            [self.level_y[level, :columns, :], self.level_y[level, columns:, :]], axis=1
        )
        both = self.dot(back.astype(jnp.bfloat16), both_y, ((1,), (0,)))
        spread_re, spread_im = self.complex_sum(both)
        up_re = (window * wave[:rows] + spread_re).astype(jnp.bfloat16)
        up_im = (window * wave[rows:] + spread_im).astype(jnp.bfloat16)
        wave_up[:rows] = up_re
        wave_up[rows:] = up_im
        product = wave[:rows] * up_re.astype(jnp.float32)
        product += wave[rows:] * up_im.astype(jnp.float32)
        spot = pl.multiple_of(slot * rows, rows)
        for r_of, out in enumerate(outs):

            @pl.when(r == r_of)
            def _():
                out[pl.ds(spot, rows), :] = product.astype(out.dtype)

        return level


def down_kernel(sections, shots, group, sizes, source_ref, *refs):
    slots, rows, _ = sizes
    (own, near, far), (own_late, joined, far_window) = refs[:3], refs[3:6]
    level_y, turned_x, level_w, waves, state, stage_x = refs[6:]
    it = Sweep(shots, group, sizes, level_y, turned_x, level_w, waves, stage_x)
    sources = [
        (own, own_late, own),
        (near, None, near),
        (far, None, far),
        (joined, None, far_window),
    ]

    @pl.when(it.is_worker == 0)
    def _():
        for i in range(3 + sections):
            state[i] = 0

    @pl.when(it.is_worker != 0)
    def _():
        waves[0] = source_ref[it.shot]
        for r, (_, _, window) in enumerate(sources):
            value = jnp.max(window[window.shape[0] - TAIL :, :].astype(jnp.float32))
            state[3 + r] = value.astype(jnp.int32)

        def section_down(section, carry):
            place, going, next_section, next_slot = carry
            r = section ^ it.here
            partial = (r != 0) & (r != sections - 1)
            count = state[3 + r]
            ready = jnp.where(partial, jnp.minimum(count, slots - 1), count)

            def level_down(slot, place):
                it.fetch(r, slot, place, sources)
                return it.down(place)

            place = lax.fori_loop(0, jnp.where(going, ready, 0), level_down, place)
            whole = ready == count
            next_section = jnp.where(going, jnp.where(whole, section + 1, section), next_section)
            next_slot = jnp.where(going, jnp.where(whole, 0, ready), next_slot)
            return place, going & whole, next_section, next_slot

        zero = jnp.int32(0)
        carry = (zero, jnp.bool_(True), zero, zero)
        place, _, next_section, next_slot = lax.fori_loop(0, sections, section_down, carry)
        state[0] = next_section
        state[1] = next_slot
        state[2] = place


def up_kernel(sections, shots, group, sizes, state, *refs):
    slots, rows, _ = sizes
    (own, near, far), (own_late, near_late, far_late, joined, far_window) = refs[:3], refs[3:8]
    outs, refs = refs[12 : 12 + sections], refs[12 + sections :]
    level_y, turned_x, level_w, waves, stage_x, wave_up = refs
    it = Sweep(shots, group, sizes, level_y, turned_x, level_w, waves, stage_x)
    sources = [
        (own, own_late, own),
        (near, near_late, near),
        (far, far_late, far),
        (joined, None, far_window),
    ]

    @pl.when(it.is_worker == 0)
    def _():
        outs[0][...] = jnp.zeros(outs[0].shape, outs[0].dtype)

    @pl.when(it.is_worker != 0)
    def _():
        for out in outs:
            out[...] = jnp.zeros(out.shape, out.dtype)
        wave_up[...] = jnp.zeros(wave_up.shape, wave_up.dtype)
        next_section, next_slot = state[0], state[1]

        def section_down(section, place):
            r = section ^ it.here
            begin = jnp.where(section == next_section, next_slot, 0)

            def level_down(slot, place):
                it.fetch(r, slot, place, sources)
                return it.down(place)

            return lax.fori_loop(begin, state[3 + r], level_down, place)

        last = lax.fori_loop(next_section, sections, section_down, state[2])

        def section_up(step, place):
            r = (sections - 1 - step) ^ it.here
            count = state[3 + r]
            return lax.fori_loop(
                0,
                count,
                lambda inner, place: it.up(r, count - 1 - inner, place, wave_up, outs),
                place,
            )

        lax.fori_loop(0, sections, section_up, last)


def join_kernel(group, first_ref, second_ref, out_ref):
    plane = lax.rem(lax.axis_index("tile") // group, 2)
    half_rows = first_ref.shape[0]
    for i, ref in enumerate((first_ref, second_ref)):
        start = pl.multiple_of((plane if i == 0 else 1 - plane) * half_rows, half_rows)
        out_ref[pl.ds(start, half_rows), :] = ref[...]


def hold_kernel(array_ref, after_ref, out_ref):
    pass


def place_kernel(shots, anchors, *refs):
    arrived, (left_out, own_out) = refs[:-2], refs[-2:]
    section, tile = lax.axis_index("depth"), lax.axis_index("tile")
    places, columns = left_out.shape
    left_sum, own_sum = None, None
    for q in range(shots):
        offset = anchors[lax.rem(section, shots) ^ q] - (tile - 1) * columns
        total = None
        for r in range(q, len(arrived), shots):
            value = arrived[r][:places, :].astype(jnp.float32)
            total = value if total is None else total + value
        turned = pltpu.roll(total, lax.rem(offset, columns), 1)
        lanes = lax.broadcasted_iota(jnp.int32, turned.shape, 1)
        left = jnp.where(lanes >= offset, turned, 0.0)
        own = jnp.where(lanes >= offset, 0.0, turned)
        left_sum = left if left_sum is None else left_sum + left
        own_sum = own if own_sum is None else own_sum + own
    left_out[...] = left_sum.astype(left_out.dtype)
    own_out[...] = own_sum


def kept(array):
    return pltpu.with_memory_space_constraint(array, pltpu.HBM)


def held(array):
    return pltpu.with_memory_space_constraint(array, pltpu.VMEM)


def on_device(source, anchors, counts, reflect, lateral_x, lateral_y):
    shots, _, rows, columns = source.shape
    slots = reflect.shape[1]
    sizes = (slots, rows, columns)
    plan = Plan(shots)
    sections, group = plan.sections, plan.group
    assert shots == 2
    bf16 = jnp.bfloat16
    smem = pl.BlockSpec(memory_space=pltpu.SMEM)
    vmem = pl.BlockSpec(memory_space=pltpu.VMEM)
    hbm = pl.BlockSpec(memory_space=pltpu.HBM)
    anywhere = pl.BlockSpec(memory_space=pl.ANY)

    def params(mib):
        return pltpu.CompilerParams(vmem_limit_bytes=mib * MIB)

    tile_reflect = reflect[0].reshape(slots * rows, columns)
    halo = lax.ppermute(tile_reflect, "tile", [(i, i + 1) for i in range(plan.tiles - 1)])
    part = columns + rows // 2
    half_rows, win_rows = slots * part, slots * rows + TAIL
    early_rows = 2 * (half_rows - part) + win_rows
    even = pltpu.VMEM((early_rows + 5 * TAIL, columns), bf16)
    odd = pltpu.VMEM((early_rows, columns), bf16)
    even_early, odd_early, late, far_half = pl.pallas_call(
        functools.partial(pack_kernel, group, sizes),
        out_shape=[
            even,
            odd,
            jax.ShapeDtypeStruct((2 * part, columns), bf16),
            jax.ShapeDtypeStruct((half_rows, columns), bf16),
        ],
        in_specs=[hbm, hbm],
        out_specs=[vmem] * 4,
        scratch_shapes=[
            pltpu.VMEM(lateral_x.shape[1:], bf16),
            pltpu.VMEM(lateral_y.shape[1:], bf16),
            pltpu.SemaphoreType.DMA((2,)),
        ],
        compiler_params=params(12),
        name="pack",
    )(kept(lateral_x[0]), kept(lateral_y[0]))
    last = sections - 1
    far_half = lax.ppermute(far_half, BOTH, plan.to_workers(last))
    even_early, odd_early, far_window = pl.pallas_call(
        functools.partial(window_kernel, shots, sizes),
        out_shape=[even, odd, jax.ShapeDtypeStruct((win_rows, columns), bf16)],
        in_specs=[hbm, smem, vmem, hbm, vmem, vmem],
        out_specs=[vmem] * 3,
        scratch_shapes=[
            pltpu.SMEM((shots,), jnp.int32),
            pltpu.VMEM((slots * rows, columns), bf16),
            pltpu.SemaphoreType.DMA((2,)),
        ],
        input_output_aliases={4: 0, 5: 1},
        compiler_params=params(12),
        cost_estimate=pl.CostEstimate(flops=3 * 10**9, bytes_accessed=4 * MIB, transcendentals=0),
        name="windows",
    )(kept(anchors), counts, halo, kept(tile_reflect), held(even_early), held(odd_early))
    messages = [
        even_early,
        lax.ppermute(odd_early, BOTH, plan.to_workers(1)),
        lax.ppermute(even_early, BOTH, plan.to_workers(2)),
    ]
    far_window = lax.ppermute(far_window, BOTH, plan.to_workers(last))
    other_half = lax.ppermute(far_half, BOTH, plan.swap_workers())
    late = pl.pallas_call(
        hold_kernel,
        out_shape=jax.ShapeDtypeStruct(late.shape, bf16),
        in_specs=[anywhere] * 2,
        out_specs=anywhere,
        input_output_aliases={0: 0},
        compiler_params=params(2),
        cost_estimate=pl.CostEstimate(flops=36 * 10**8, bytes_accessed=0, transcendentals=0),
        name="hold",
    )(late, far_window)
    lates = [lax.ppermute(late, BOTH, plan.ops_to_workers(r)) for r in (1, 2)]
    joined = pl.pallas_call(
        functools.partial(join_kernel, group),
        out_shape=pltpu.VMEM((2 * half_rows, columns), bf16),
        in_specs=[vmem] * 2,
        out_specs=vmem,
        compiler_params=params(8),
        name="join",
    )(held(far_half), held(other_half))

    levels = sections * slots
    buffers = [
        pltpu.VMEM((levels, 2 * columns, columns), bf16),
        pltpu.VMEM((levels, 2 * rows, 2 * rows), bf16),
        pltpu.VMEM((levels, rows, columns), bf16),
        pltpu.VMEM((levels + 1, 2 * rows, columns), bf16),
    ]
    stage_x = pltpu.VMEM((rows, 2 * rows), bf16)
    messages = [held(message) for message in messages]
    late, joined, far_window = held(late), held(joined), held(far_window)
    *filled, state = pl.pallas_call(
        functools.partial(down_kernel, sections, shots, group, sizes),
        out_shape=buffers + [jax.ShapeDtypeStruct((3 + sections,), jnp.int32)],
        in_specs=[vmem] * 7,
        out_specs=[vmem] * 4 + [smem],
        scratch_shapes=[stage_x],
        compiler_params=params(24),
        name="down",
    )(held(source.reshape(shots, 2 * rows, columns)), *messages, late, joined, far_window)
    correlations = pl.pallas_call(
        functools.partial(up_kernel, sections, shots, group, sizes),
        out_shape=[
            jax.ShapeDtypeStruct((slots * rows + TAIL * more, columns), bf16)
            for more in (0, 1, 0, 2)
        ]
        + buffers,
        in_specs=[smem] + [vmem] * 12,
        out_specs=[vmem] * (sections + 4),
        scratch_shapes=[
            stage_x,
            pltpu.VMEM((2 * rows, columns), bf16),
        ],
        input_output_aliases={9 + i: sections + i for i in range(4)},
        compiler_params=params(24),
        name="up",
    )(
        state, *messages, late, *[held(part) for part in lates], joined, far_window,
        *[held(buffer) for buffer in filled],
    )

    corr_shape = jax.ShapeDtypeStruct((slots * rows, columns), bf16)
    arrived = [correlations[0]] + [
        lax.ppermute(correlations[r], BOTH, plan.from_workers(r)) for r in range(1, sections)
    ]
    left, own = pl.pallas_call(
        functools.partial(place_kernel, shots),
        out_shape=[corr_shape, jax.ShapeDtypeStruct((slots * rows, columns), jnp.float32)],
        in_specs=[smem] + [vmem] * sections,
        out_specs=[vmem, vmem],
        compiler_params=params(8),
        name="place",
    )(anchors, *arrived)
    from_right = lax.ppermute(left, "tile", [(i + 1, i) for i in range(plan.tiles - 1)])
    image = own + from_right.astype(jnp.float32)
    return image.reshape(1, slots, rows, columns)


def solution(mesh):
    return jax.shard_map(
        on_device,
        mesh=mesh,
        in_specs=(
            P("tile", None, None, None),
            P("tile"),
            P("depth"),
            P("depth", None, None, "tile"),
            P("depth", None, None, None, None),
            P("depth", None, None, None, None),
        ),
        out_specs=P("depth", None, None, "tile"),
        check_vma=False,
    )
```

```python
import functools

import jax
import jax.numpy as jnp
from jax import lax
from jax.experimental import pallas as pl
from jax.experimental.pallas import tpu as pltpu
from jax.sharding import PartitionSpec as P

BOTH = ("depth", "tile")
MIB = 1024 * 1024
TAIL = 16


class Plan:
    def __init__(self, shots):
        self.sections = lax.axis_size("depth")
        self.tiles = lax.axis_size("tile")
        self.shots = shots
        self.group = self.sections // shots
        assert self.sections == 4 and self.group * shots == self.sections
        assert self.tiles % (2 * self.group) == 0

    def device(self, depth, tile):
        return depth * self.tiles + tile

    def bases(self):
        return range(0, self.tiles, self.group)

    def worker(self, base, w):
        return self.device(w, base + w // self.shots)

    def other(self, w, base):
        return self.device(w, base + (w // self.shots + 1) % self.group)

    def ops_to_workers(self, r):
        return [
            (self.other(w ^ r, base), self.worker(base, w))
            for base in self.bases()
            for w in range(self.sections)
        ]

    def swap_workers(self):
        return [
            (self.worker(base, w), self.worker((base // self.group ^ 1) * self.group, w))
            for base in self.bases()
            for w in range(self.sections)
        ]

    def to_workers(self, r):
        return [
            (self.device(w ^ r, base + w // self.shots), self.worker(base, w))
            for base in self.bases()
            for w in range(self.sections)
        ]

    def from_workers(self, r):
        return [(b, a) for a, b in self.to_workers(r)]


def pack_kernel(group, sizes, x_hbm, y_hbm, even, odd, late, half_out, x_ref, y_ref, sem):
    slots, rows, columns = sizes
    loads = [
        pltpu.make_async_copy(x_hbm, x_ref, sem.at[0]),
        pltpu.make_async_copy(y_hbm, y_ref, sem.at[1]),
    ]
    for load in loads:
        load.start()
    for load in loads:
        load.wait()
    piece = rows // 2
    part = columns + piece
    first = (slots - 1) * part
    for half in range(2):
        for slot in range(slots):
            op_x = jnp.concatenate(
                [x_ref[slot, i, half * piece : (half + 1) * piece, :] for i in range(2)], axis=1
            )
            op_y = y_ref[slot, half]
            if slot < slots - 1:
                places = [(out, half * first + slot * part) for out in (even, odd)]
            else:
                places = [(late, half * part)]
            for out, spot in places:
                out[spot : spot + columns, :] = op_y
                out[spot + columns : spot + part, :] = op_x
    plane = lax.rem(lax.axis_index("tile") // group, 2)
    half_out[:first, :] = even[pl.ds(pl.multiple_of(plane * first, first), first), :]
    half_out[first:, :] = late[pl.ds(pl.multiple_of(plane * part, part), part), :]


def window_kernel(shots, sizes, anchors_hbm, counts, left_ref, right_hbm, *refs):
    slots, rows, columns = sizes
    messages, (alone, anchors, right_ref, sem) = refs[shots : 2 * shots], refs[2 * shots :]
    loads = [
        pltpu.make_async_copy(anchors_hbm, anchors, sem.at[0]),
        pltpu.make_async_copy(right_hbm, right_ref, sem.at[1]),
    ]
    for load in loads:
        load.start()
    for load in loads:
        load.wait()
    section, tile = lax.axis_index("depth"), lax.axis_index("tile")
    left, right = left_ref[...].astype(jnp.float32), right_ref[...].astype(jnp.float32)
    lanes = lax.broadcasted_iota(jnp.int32, left.shape, 1)
    tail = jnp.full((TAIL, columns), counts[0].astype(jnp.float32), jnp.float32)
    for q, message in enumerate(messages):
        offset = anchors[lax.rem(section, shots) ^ q] - (tile - 1) * columns
        merged = jnp.where(lanes >= offset, left, right)
        back = lax.rem(columns - lax.rem(offset, columns), columns)
        window = pltpu.roll(merged, back, 1).astype(message.dtype)
        for out in [message] + ([alone] if q == shots - 1 else []):
            spot = out.shape[0] - TAIL - slots * rows
            out[spot : spot + slots * rows, :] = window
            out[spot + slots * rows :, :] = tail.astype(out.dtype)


class Sweep:
    def __init__(self, shots, group, sizes, turned_y, turned_x, level_w, waves, stage_y, stage_x):
        self.sizes = sizes
        self.turned_y, self.turned_x, self.level_w = turned_y, turned_x, level_w
        self.waves, self.stage_y, self.stage_x = waves, stage_y, stage_x
        slots, rows, columns = sizes
        self.piece = rows // 2
        self.part = columns + self.piece
        self.first = (slots - 1) * self.part
        self.half_rows = self.first + self.part
        self.win_rows = slots * rows + TAIL
        self.here, tile = lax.axis_index("depth"), lax.axis_index("tile")
        self.shot = lax.rem(self.here, shots)
        self.is_worker = (self.here // shots == lax.rem(tile, group)).astype(jnp.int32)

    def window_start(self, window_ref):
        return window_ref.shape[0] - self.win_rows

    def fetch(self, r, slot, place, sources):
        slots, rows, columns = self.sizes
        for r_of, (early, late, window) in enumerate(sources):
            early_slots = slots if early.shape[0] == 2 * self.half_rows else slots - 1
            choices = [(early, early_slots * self.part, slot < early_slots, slot)]
            if late is not None:
                choices.append((late, self.part, slot == slots - 1, 0))
            for ref, stride, chosen, at in choices:

                @pl.when((r == r_of) & chosen)
                def _():
                    for half in range(2):
                        start = pl.multiple_of(half * stride + at * self.part, self.piece)
                        self.stage_y[half * columns : (half + 1) * columns, :] = ref[
                            pl.ds(start, columns), :
                        ]
                        tail = pl.multiple_of(start + columns, self.piece)
                        self.stage_x[half * self.piece : (half + 1) * self.piece, :] = ref[
                            pl.ds(tail, self.piece), :
                        ]
                    spot = self.window_start(window) + slot * rows
                    self.level_w[place] = window[pl.ds(pl.multiple_of(spot, TAIL), rows), :]

    def blocks(self, re, im):
        upper = jnp.concatenate([re, -im], axis=1)
        return jnp.concatenate([upper, jnp.concatenate([im, re], axis=1)], axis=0)

    def complex_sum(self, both):
        _, rows, columns = self.sizes
        with_re, with_im = both[:, :columns], both[:, columns:]
        return with_re[:rows] - with_im[rows:], with_im[:rows] + with_re[rows:]

    def dot(self, a, b, dims):
        return lax.dot_general(a, b, (dims, ((), ())), preferred_element_type=jnp.float32)

    def down(self, place):
        _, rows, columns = self.sizes
        x_re, x_im = self.stage_x[:, :rows], self.stage_x[:, rows:]
        wave = self.waves[place].astype(jnp.float32)
        gain = 1.0 + self.level_w[place].astype(jnp.float32)
        scaled = jnp.concatenate([gain * wave[:rows], gain * wave[rows:]], axis=0)
        self.turned_x[place] = self.blocks(x_re.T, x_im.T)
        middle = self.dot(self.blocks(x_re, x_im), scaled.astype(jnp.bfloat16), ((1,), (0,)))
        for i in range(2):
            lines = slice(i * columns, (i + 1) * columns)
            self.turned_y[place, lines, :] = self.stage_y[lines, :].T
        both = self.dot(middle.astype(jnp.bfloat16), self.stage_y[...], ((1,), (1,)))
        moved = jnp.concatenate(self.complex_sum(both), axis=0)
        self.waves[place + 1] = moved.astype(jnp.bfloat16)
        return place + 1

    def up(self, r, slot, place, wave_up, outs):
        _, rows, columns = self.sizes
        level = place - 1
        wave = self.waves[level].astype(jnp.float32)
        window = self.level_w[level].astype(jnp.float32)
        back = self.dot(self.turned_x[level], wave_up[...], ((1,), (0,)))
        both = self.dot(back.astype(jnp.bfloat16), self.turned_y[level], ((1,), (1,)))
        spread_re, spread_im = self.complex_sum(both)
        up_re = (window * wave[:rows] + spread_re).astype(jnp.bfloat16)
        up_im = (window * wave[rows:] + spread_im).astype(jnp.bfloat16)
        wave_up[:rows] = up_re
        wave_up[rows:] = up_im
        product = wave[:rows] * up_re.astype(jnp.float32)
        product += wave[rows:] * up_im.astype(jnp.float32)
        spot = pl.multiple_of(slot * rows, rows)
        for r_of, out in enumerate(outs):

            @pl.when(r == r_of)
            def _():
                out[pl.ds(spot, rows), :] = product.astype(out.dtype)

        return level


def down_kernel(sections, shots, group, sizes, source_ref, *refs):
    slots, rows, _ = sizes
    (own, near, far), (own_late, joined, far_window) = refs[:3], refs[3:6]
    *buffers, state, stage_y, stage_x = refs[6:]
    it = Sweep(shots, group, sizes, *buffers, stage_y, stage_x)
    waves = it.waves
    sources = [
        (own, own_late, own),
        (near, None, near),
        (far, None, far),
        (joined, None, far_window),
    ]

    @pl.when(it.is_worker == 0)
    def _():
        for i in range(3 + sections):
            state[i] = 0

    @pl.when(it.is_worker != 0)
    def _():
        waves[0] = source_ref[it.shot]
        for r, (_, _, window) in enumerate(sources):
            value = jnp.max(window[window.shape[0] - TAIL :, :].astype(jnp.float32))
            state[3 + r] = value.astype(jnp.int32)

        def section_down(section, carry):
            place, going, next_section, next_slot = carry
            r = section ^ it.here
            partial = (r != 0) & (r != sections - 1)
            count = state[3 + r]
            ready = jnp.where(partial, jnp.minimum(count, slots - 1), count)

            def level_down(slot, place):
                it.fetch(r, slot, place, sources)
                return it.down(place)

            place = lax.fori_loop(0, jnp.where(going, ready, 0), level_down, place)
            whole = ready == count
            next_section = jnp.where(going, jnp.where(whole, section + 1, section), next_section)
            next_slot = jnp.where(going, jnp.where(whole, 0, ready), next_slot)
            return place, going & whole, next_section, next_slot

        zero = jnp.int32(0)
        carry = (zero, jnp.bool_(True), zero, zero)
        place, _, next_section, next_slot = lax.fori_loop(0, sections, section_down, carry)
        state[0] = next_section
        state[1] = next_slot
        state[2] = place


def up_kernel(sections, shots, group, sizes, state, *refs):
    slots, rows, _ = sizes
    (own, near, far), (own_late, near_late, far_late, joined, far_window) = refs[:3], refs[3:8]
    outs, refs = refs[12 : 12 + sections], refs[12 + sections :]
    *buffers, stage_y, stage_x, wave_up = refs
    it = Sweep(shots, group, sizes, *buffers, stage_y, stage_x)
    sources = [
        (own, own_late, own),
        (near, near_late, near),
        (far, far_late, far),
        (joined, None, far_window),
    ]

    @pl.when(it.is_worker == 0)
    def _():
        outs[0][...] = jnp.zeros(outs[0].shape, outs[0].dtype)

    @pl.when(it.is_worker != 0)
    def _():
        for out in outs:
            out[...] = jnp.zeros(out.shape, out.dtype)
        wave_up[...] = jnp.zeros(wave_up.shape, wave_up.dtype)
        next_section, next_slot = state[0], state[1]

        def section_down(section, place):
            r = section ^ it.here
            begin = jnp.where(section == next_section, next_slot, 0)

            def level_down(slot, place):
                it.fetch(r, slot, place, sources)
                return it.down(place)

            return lax.fori_loop(begin, state[3 + r], level_down, place)

        last = lax.fori_loop(next_section, sections, section_down, state[2])

        def section_up(step, place):
            r = (sections - 1 - step) ^ it.here
            count = state[3 + r]
            return lax.fori_loop(
                0,
                count,
                lambda inner, place: it.up(r, count - 1 - inner, place, wave_up, outs),
                place,
            )

        lax.fori_loop(0, sections, section_up, last)


def join_kernel(group, first_ref, second_ref, out_ref):
    plane = lax.rem(lax.axis_index("tile") // group, 2)
    half_rows = first_ref.shape[0]
    for i, ref in enumerate((first_ref, second_ref)):
        start = pl.multiple_of((plane if i == 0 else 1 - plane) * half_rows, half_rows)
        out_ref[pl.ds(start, half_rows), :] = ref[...]


def hold_kernel(array_ref, after_ref, out_ref):
    pass


def place_kernel(shots, anchors, *refs):
    arrived, (left_out, own_out) = refs[:-2], refs[-2:]
    section, tile = lax.axis_index("depth"), lax.axis_index("tile")
    places, columns = left_out.shape
    left_sum, own_sum = None, None
    for q in range(shots):
        offset = anchors[lax.rem(section, shots) ^ q] - (tile - 1) * columns
        total = None
        for r in range(q, len(arrived), shots):
            value = arrived[r][:places, :].astype(jnp.float32)
            total = value if total is None else total + value
        turned = pltpu.roll(total, lax.rem(offset, columns), 1)
        lanes = lax.broadcasted_iota(jnp.int32, turned.shape, 1)
        left = jnp.where(lanes >= offset, turned, 0.0)
        own = jnp.where(lanes >= offset, 0.0, turned)
        left_sum = left if left_sum is None else left_sum + left
        own_sum = own if own_sum is None else own_sum + own
    left_out[...] = left_sum.astype(left_out.dtype)
    own_out[...] = own_sum


def kept(array):
    return pltpu.with_memory_space_constraint(array, pltpu.HBM)


def held(array):
    return pltpu.with_memory_space_constraint(array, pltpu.VMEM)


def on_device(source, anchors, counts, reflect, lateral_x, lateral_y):
    shots, _, rows, columns = source.shape
    slots = reflect.shape[1]
    sizes = (slots, rows, columns)
    plan = Plan(shots)
    sections, group = plan.sections, plan.group
    assert shots == 2
    bf16 = jnp.bfloat16
    smem = pl.BlockSpec(memory_space=pltpu.SMEM)
    vmem = pl.BlockSpec(memory_space=pltpu.VMEM)
    hbm = pl.BlockSpec(memory_space=pltpu.HBM)
    anywhere = pl.BlockSpec(memory_space=pl.ANY)

    def params(mib):
        return pltpu.CompilerParams(vmem_limit_bytes=mib * MIB)

    tile_reflect = reflect[0].reshape(slots * rows, columns)
    halo = lax.ppermute(tile_reflect, "tile", [(i, i + 1) for i in range(plan.tiles - 1)])
    part = columns + rows // 2
    half_rows, win_rows = slots * part, slots * rows + TAIL
    early_rows = 2 * (half_rows - part) + win_rows
    even = pltpu.VMEM((early_rows + 5 * TAIL, columns), bf16)
    odd = pltpu.VMEM((early_rows, columns), bf16)
    even_early, odd_early, late, far_half = pl.pallas_call(
        functools.partial(pack_kernel, group, sizes),
        out_shape=[
            even,
            odd,
            jax.ShapeDtypeStruct((2 * part, columns), bf16),
            jax.ShapeDtypeStruct((half_rows, columns), bf16),
        ],
        in_specs=[hbm, hbm],
        out_specs=[vmem] * 4,
        scratch_shapes=[
            pltpu.VMEM(lateral_x.shape[1:], bf16),
            pltpu.VMEM(lateral_y.shape[1:], bf16),
            pltpu.SemaphoreType.DMA((2,)),
        ],
        compiler_params=params(12),
        name="pack",
    )(kept(lateral_x[0]), kept(lateral_y[0]))
    last = sections - 1
    far_half = lax.ppermute(far_half, BOTH, plan.to_workers(last))
    even_early, odd_early, far_window = pl.pallas_call(
        functools.partial(window_kernel, shots, sizes),
        out_shape=[even, odd, jax.ShapeDtypeStruct((win_rows, columns), bf16)],
        in_specs=[hbm, smem, vmem, hbm, vmem, vmem],
        out_specs=[vmem] * 3,
        scratch_shapes=[
            pltpu.SMEM((shots,), jnp.int32),
            pltpu.VMEM((slots * rows, columns), bf16),
            pltpu.SemaphoreType.DMA((2,)),
        ],
        input_output_aliases={4: 0, 5: 1},
        compiler_params=params(12),
        cost_estimate=pl.CostEstimate(flops=3 * 10**9, bytes_accessed=4 * MIB, transcendentals=0),
        name="windows",
    )(kept(anchors), counts, halo, kept(tile_reflect), held(even_early), held(odd_early))
    messages = [
        even_early,
        lax.ppermute(odd_early, BOTH, plan.to_workers(1)),
        lax.ppermute(even_early, BOTH, plan.to_workers(2)),
    ]
    far_window = lax.ppermute(far_window, BOTH, plan.to_workers(last))
    other_half = lax.ppermute(far_half, BOTH, plan.swap_workers())
    late = pl.pallas_call(
        hold_kernel,
        out_shape=jax.ShapeDtypeStruct(late.shape, bf16),
        in_specs=[anywhere] * 2,
        out_specs=anywhere,
        input_output_aliases={0: 0},
        compiler_params=params(2),
        cost_estimate=pl.CostEstimate(flops=36 * 10**8, bytes_accessed=0, transcendentals=0),
        name="hold",
    )(late, far_window)
    lates = [lax.ppermute(late, BOTH, plan.ops_to_workers(r)) for r in (1, 2)]
    joined = pl.pallas_call(
        functools.partial(join_kernel, group),
        out_shape=pltpu.VMEM((2 * half_rows, columns), bf16),
        in_specs=[vmem] * 2,
        out_specs=vmem,
        compiler_params=params(8),
        name="join",
    )(held(far_half), held(other_half))

    levels = sections * slots
    buffers = [
        pltpu.VMEM((levels, 2 * columns, columns), bf16),
        pltpu.VMEM((levels, 2 * rows, 2 * rows), bf16),
        pltpu.VMEM((levels, rows, columns), bf16),
        pltpu.VMEM((levels + 1, 2 * rows, columns), bf16),
    ]
    stages = [pltpu.VMEM((2 * columns, columns), bf16), pltpu.VMEM((rows, 2 * rows), bf16)]
    messages = [held(message) for message in messages]
    late, joined, far_window = held(late), held(joined), held(far_window)
    *filled, state = pl.pallas_call(
        functools.partial(down_kernel, sections, shots, group, sizes),
        out_shape=buffers + [jax.ShapeDtypeStruct((3 + sections,), jnp.int32)],
        in_specs=[vmem] * 7,
        out_specs=[vmem] * 4 + [smem],
        scratch_shapes=stages,
        compiler_params=params(24),
        name="down",
    )(held(source.reshape(shots, 2 * rows, columns)), *messages, late, joined, far_window)
    correlations = pl.pallas_call(
        functools.partial(up_kernel, sections, shots, group, sizes),
        out_shape=[
            jax.ShapeDtypeStruct((slots * rows + TAIL * more, columns), bf16)
            for more in (0, 1, 0, 2)
        ]
        + buffers,
        in_specs=[smem] + [vmem] * 12,
        out_specs=[vmem] * (sections + 4),
        scratch_shapes=stages + [pltpu.VMEM((2 * rows, columns), bf16)],
        input_output_aliases={9 + i: sections + i for i in range(4)},
        compiler_params=params(24),
        name="up",
    )(
        state, *messages, late, *[held(part) for part in lates], joined, far_window,
        *[held(buffer) for buffer in filled],
    )

    corr_shape = jax.ShapeDtypeStruct((slots * rows, columns), bf16)
    arrived = [correlations[0]] + [
        lax.ppermute(correlations[r], BOTH, plan.from_workers(r)) for r in range(1, sections)
    ]
    left, own = pl.pallas_call(
        functools.partial(place_kernel, shots),
        out_shape=[corr_shape, jax.ShapeDtypeStruct((slots * rows, columns), jnp.float32)],
        in_specs=[smem] + [vmem] * sections,
        out_specs=[vmem, vmem],
        compiler_params=params(8),
        name="place",
    )(anchors, *arrived)
    from_right = lax.ppermute(left, "tile", [(i + 1, i) for i in range(plan.tiles - 1)])
    image = own + from_right.astype(jnp.float32)
    return image.reshape(1, slots, rows, columns)


def solution(mesh):
    return jax.shard_map(
        on_device,
        mesh=mesh,
        in_specs=(
            P("tile", None, None, None),
            P("tile"),
            P("depth"),
            P("depth", None, None, "tile"),
            P("depth", None, None, None, None),
            P("depth", None, None, None, None),
        ),
        out_specs=P("depth", None, None, "tile"),
        check_vma=False,
    )
```

```python
import functools

import jax
import jax.numpy as jnp
from jax import lax
from jax.experimental import pallas as pl
from jax.experimental.pallas import tpu as pltpu
from jax.sharding import PartitionSpec as P

BOTH = ("depth", "tile")
MIB = 1024 * 1024
TAIL = 16


class Plan:
    def __init__(self, shots):
        self.sections = lax.axis_size("depth")
        self.tiles = lax.axis_size("tile")
        self.shots = shots
        self.group = self.sections // shots
        assert self.sections == 4 and self.group * shots == self.sections
        assert self.tiles % (2 * self.group) == 0

    def device(self, depth, tile):
        return depth * self.tiles + tile

    def bases(self):
        return range(0, self.tiles, self.group)

    def worker(self, base, w):
        return self.device(w, base + w // self.shots)

    def other(self, w, base):
        return self.device(w, base + (w // self.shots + 1) % self.group)

    def ops_to_workers(self, r):
        return [
            (self.other(w ^ r, base), self.worker(base, w))
            for base in self.bases()
            for w in range(self.sections)
        ]

    def swap_workers(self):
        return [
            (self.worker(base, w), self.worker((base // self.group ^ 1) * self.group, w))
            for base in self.bases()
            for w in range(self.sections)
        ]

    def to_workers(self, r):
        return [
            (self.device(w ^ r, base + w // self.shots), self.worker(base, w))
            for base in self.bases()
            for w in range(self.sections)
        ]

    def from_workers(self, r):
        return [(b, a) for a, b in self.to_workers(r)]


def pack_kernel(group, sizes, x_hbm, y_hbm, reflect_hbm, anchors_hbm, *refs):
    slots, rows, columns = sizes
    even, odd, late, half_out, reflect, anchors, x_ref, y_ref, sem = refs
    loads = [
        pltpu.make_async_copy(x_hbm, x_ref, sem.at[0]),
        pltpu.make_async_copy(y_hbm, y_ref, sem.at[1]),
        pltpu.make_async_copy(reflect_hbm, reflect, sem.at[2]),
        pltpu.make_async_copy(anchors_hbm, anchors, sem.at[3]),
    ]
    for load in loads:
        load.start()
    for load in loads[:2]:
        load.wait()
    piece = rows // 2
    part = columns + piece
    first = (slots - 1) * part
    for half in range(2):
        for slot in range(slots):
            op_x = jnp.concatenate(
                [x_ref[slot, i, half * piece : (half + 1) * piece, :] for i in range(2)], axis=1
            )
            op_y = y_ref[slot, half]
            if slot < slots - 1:
                places = [(out, half * first + slot * part) for out in (even, odd)]
            else:
                places = [(late, half * part)]
            for out, spot in places:
                out[spot : spot + columns, :] = op_y
                out[spot + columns : spot + part, :] = op_x
    plane = lax.rem(lax.axis_index("tile") // group, 2)
    half_out[:first, :] = even[pl.ds(pl.multiple_of(plane * first, first), first), :]
    half_out[first:, :] = late[pl.ds(pl.multiple_of(plane * part, part), part), :]
    for load in loads[2:]:
        load.wait()


def window_kernel(shots, sizes, anchors, counts, left_ref, right_ref, *refs):
    slots, rows, columns = sizes
    messages, alone = refs[shots : 2 * shots], refs[2 * shots]
    section, tile = lax.axis_index("depth"), lax.axis_index("tile")
    left, right = left_ref[...].astype(jnp.float32), right_ref[...].astype(jnp.float32)
    lanes = lax.broadcasted_iota(jnp.int32, left.shape, 1)
    tail = jnp.full((TAIL, columns), counts[0].astype(jnp.float32), jnp.float32)
    for q, message in enumerate(messages):
        offset = anchors[lax.rem(section, shots) ^ q] - (tile - 1) * columns
        merged = jnp.where(lanes >= offset, left, right)
        back = lax.rem(columns - lax.rem(offset, columns), columns)
        window = pltpu.roll(merged, back, 1).astype(message.dtype)
        for out in [message] + ([alone] if q == shots - 1 else []):
            spot = out.shape[0] - TAIL - slots * rows
            out[spot : spot + slots * rows, :] = window
            out[spot + slots * rows :, :] = tail.astype(out.dtype)


class Sweep:
    def __init__(self, shots, group, sizes, turned_y, turned_x, level_w, waves, stage_y, stage_x):
        self.sizes = sizes
        self.turned_y, self.turned_x, self.level_w = turned_y, turned_x, level_w
        self.waves, self.stage_y, self.stage_x = waves, stage_y, stage_x
        slots, rows, columns = sizes
        self.piece = rows // 2
        self.part = columns + self.piece
        self.first = (slots - 1) * self.part
        self.half_rows = self.first + self.part
        self.win_rows = slots * rows + TAIL
        self.here, tile = lax.axis_index("depth"), lax.axis_index("tile")
        self.shot = lax.rem(self.here, shots)
        self.is_worker = (self.here // shots == lax.rem(tile, group)).astype(jnp.int32)

    def window_start(self, window_ref):
        return window_ref.shape[0] - self.win_rows

    def fetch(self, r, slot, place, sources):
        slots, rows, columns = self.sizes
        for r_of, (early, late, window) in enumerate(sources):
            early_slots = slots if early.shape[0] == 2 * self.half_rows else slots - 1
            choices = [(early, early_slots * self.part, slot < early_slots, slot)]
            if late is not None:
                choices.append((late, self.part, slot == slots - 1, 0))
            for ref, stride, chosen, at in choices:

                @pl.when((r == r_of) & chosen)
                def _():
                    for half in range(2):
                        start = pl.multiple_of(half * stride + at * self.part, self.piece)
                        self.stage_y[half * columns : (half + 1) * columns, :] = ref[
                            pl.ds(start, columns), :
                        ]
                        tail = pl.multiple_of(start + columns, self.piece)
                        self.stage_x[half * self.piece : (half + 1) * self.piece, :] = ref[
                            pl.ds(tail, self.piece), :
                        ]
                    spot = self.window_start(window) + slot * rows
                    self.level_w[place] = window[pl.ds(pl.multiple_of(spot, TAIL), rows), :]

    def blocks(self, re, im):
        upper = jnp.concatenate([re, -im], axis=1)
        return jnp.concatenate([upper, jnp.concatenate([im, re], axis=1)], axis=0)

    def complex_sum(self, both):
        _, rows, columns = self.sizes
        with_re, with_im = both[:, :columns], both[:, columns:]
        return with_re[:rows] - with_im[rows:], with_im[:rows] + with_re[rows:]

    def dot(self, a, b, dims):
        return lax.dot_general(a, b, (dims, ((), ())), preferred_element_type=jnp.float32)

    def down(self, place):
        _, rows, columns = self.sizes
        x_re, x_im = self.stage_x[:, :rows], self.stage_x[:, rows:]
        wave = self.waves[place].astype(jnp.float32)
        gain = 1.0 + self.level_w[place].astype(jnp.float32)
        scaled = jnp.concatenate([gain * wave[:rows], gain * wave[rows:]], axis=0)
        self.turned_x[place] = self.blocks(x_re.T, x_im.T)
        middle = self.dot(self.blocks(x_re, x_im), scaled.astype(jnp.bfloat16), ((1,), (0,)))
        for i in range(2):
            lines = slice(i * columns, (i + 1) * columns)
            self.turned_y[place, lines, :] = self.stage_y[lines, :].T
        both = self.dot(middle.astype(jnp.bfloat16), self.stage_y[...], ((1,), (1,)))
        moved = jnp.concatenate(self.complex_sum(both), axis=0)
        self.waves[place + 1] = moved.astype(jnp.bfloat16)
        return place + 1

    def up(self, r, slot, place, wave_up, outs):
        _, rows, columns = self.sizes
        level = place - 1
        wave = self.waves[level].astype(jnp.float32)
        window = self.level_w[level].astype(jnp.float32)
        back = self.dot(self.turned_x[level], wave_up[...], ((1,), (0,)))
        both = self.dot(back.astype(jnp.bfloat16), self.turned_y[level], ((1,), (1,)))
        spread_re, spread_im = self.complex_sum(both)
        up_re = (window * wave[:rows] + spread_re).astype(jnp.bfloat16)
        up_im = (window * wave[rows:] + spread_im).astype(jnp.bfloat16)
        wave_up[:rows] = up_re
        wave_up[rows:] = up_im
        product = wave[:rows] * up_re.astype(jnp.float32)
        product += wave[rows:] * up_im.astype(jnp.float32)
        spot = pl.multiple_of(slot * rows, rows)
        for r_of, out in enumerate(outs):

            @pl.when(r == r_of)
            def _():
                out[pl.ds(spot, rows), :] = product.astype(out.dtype)

        return level


def down_kernel(sections, shots, group, sizes, source_ref, *refs):
    slots, rows, _ = sizes
    (own, near, far), (own_late, joined, far_window) = refs[:3], refs[3:6]
    *buffers, state, stage_y, stage_x = refs[6:]
    it = Sweep(shots, group, sizes, *buffers, stage_y, stage_x)
    waves = it.waves
    sources = [
        (own, own_late, own),
        (near, None, near),
        (far, None, far),
        (joined, None, far_window),
    ]

    @pl.when(it.is_worker == 0)
    def _():
        for i in range(3 + sections):
            state[i] = 0

    @pl.when(it.is_worker != 0)
    def _():
        waves[0] = source_ref[it.shot]
        for r, (_, _, window) in enumerate(sources):
            value = jnp.max(window[window.shape[0] - TAIL :, :].astype(jnp.float32))
            state[3 + r] = value.astype(jnp.int32)

        def section_down(section, carry):
            place, going, next_section, next_slot = carry
            r = section ^ it.here
            partial = (r != 0) & (r != sections - 1)
            count = state[3 + r]
            ready = jnp.where(partial, jnp.minimum(count, slots - 1), count)

            def level_down(slot, place):
                it.fetch(r, slot, place, sources)
                return it.down(place)

            place = lax.fori_loop(0, jnp.where(going, ready, 0), level_down, place)
            whole = ready == count
            next_section = jnp.where(going, jnp.where(whole, section + 1, section), next_section)
            next_slot = jnp.where(going, jnp.where(whole, 0, ready), next_slot)
            return place, going & whole, next_section, next_slot

        zero = jnp.int32(0)
        carry = (zero, jnp.bool_(True), zero, zero)
        place, _, next_section, next_slot = lax.fori_loop(0, sections, section_down, carry)
        state[0] = next_section
        state[1] = next_slot
        state[2] = place


def up_kernel(sections, shots, group, sizes, state, *refs):
    slots, rows, _ = sizes
    (own, near, far), (own_late, near_late, far_late, joined, far_window) = refs[:3], refs[3:8]
    outs, refs = refs[12 : 12 + sections], refs[12 + sections :]
    *buffers, stage_y, stage_x, wave_up = refs
    it = Sweep(shots, group, sizes, *buffers, stage_y, stage_x)
    sources = [
        (own, own_late, own),
        (near, near_late, near),
        (far, far_late, far),
        (joined, None, far_window),
    ]

    @pl.when(it.is_worker == 0)
    def _():
        outs[0][...] = jnp.zeros(outs[0].shape, outs[0].dtype)

    @pl.when(it.is_worker != 0)
    def _():
        for out in outs:
            out[...] = jnp.zeros(out.shape, out.dtype)
        wave_up[...] = jnp.zeros(wave_up.shape, wave_up.dtype)
        next_section, next_slot = state[0], state[1]

        def section_down(section, place):
            r = section ^ it.here
            begin = jnp.where(section == next_section, next_slot, 0)

            def level_down(slot, place):
                it.fetch(r, slot, place, sources)
                return it.down(place)

            return lax.fori_loop(begin, state[3 + r], level_down, place)

        last = lax.fori_loop(next_section, sections, section_down, state[2])

        def section_up(step, place):
            r = (sections - 1 - step) ^ it.here
            count = state[3 + r]
            return lax.fori_loop(
                0,
                count,
                lambda inner, place: it.up(r, count - 1 - inner, place, wave_up, outs),
                place,
            )

        lax.fori_loop(0, sections, section_up, last)


def join_kernel(group, first_ref, second_ref, out_ref):
    plane = lax.rem(lax.axis_index("tile") // group, 2)
    half_rows = first_ref.shape[0]
    for i, ref in enumerate((first_ref, second_ref)):
        start = pl.multiple_of((plane if i == 0 else 1 - plane) * half_rows, half_rows)
        out_ref[pl.ds(start, half_rows), :] = ref[...]


def hold_kernel(array_ref, after_ref, out_ref):
    pass


def place_kernel(shots, to_left, anchors, *refs):
    arrived, out = refs[:-1], refs[-1]
    section, tile = lax.axis_index("depth"), lax.axis_index("tile")
    places, columns = out.shape
    lanes = lax.broadcasted_iota(jnp.int32, out.shape, 1)
    placed = None
    for q in range(shots):
        offset = anchors[lax.rem(section, shots) ^ q] - (tile - 1) * columns
        total = None
        for r in range(q, len(arrived), shots):
            value = arrived[r][:places, :].astype(jnp.float32)
            total = value if total is None else total + value
        turned = pltpu.roll(total, lax.rem(offset, columns), 1)
        chosen = lanes >= offset if to_left else lanes < offset
        part = jnp.where(chosen, turned, 0.0)
        placed = part if placed is None else placed + part
    out[...] = placed.astype(out.dtype)


def kept(array):
    return pltpu.with_memory_space_constraint(array, pltpu.HBM)


def held(array):
    return pltpu.with_memory_space_constraint(array, pltpu.VMEM)


def on_device(source, anchors, counts, reflect, lateral_x, lateral_y):
    shots, _, rows, columns = source.shape
    slots = reflect.shape[1]
    sizes = (slots, rows, columns)
    plan = Plan(shots)
    sections, group = plan.sections, plan.group
    assert shots == 2
    bf16 = jnp.bfloat16
    smem = pl.BlockSpec(memory_space=pltpu.SMEM)
    vmem = pl.BlockSpec(memory_space=pltpu.VMEM)
    hbm = pl.BlockSpec(memory_space=pltpu.HBM)
    anywhere = pl.BlockSpec(memory_space=pl.ANY)

    def params(mib):
        return pltpu.CompilerParams(vmem_limit_bytes=mib * MIB)

    tile_reflect = reflect[0].reshape(slots * rows, columns)
    halo = lax.ppermute(tile_reflect, "tile", [(i, i + 1) for i in range(plan.tiles - 1)])
    part = columns + rows // 2
    half_rows, win_rows = slots * part, slots * rows + TAIL
    early_rows = 2 * (half_rows - part) + win_rows
    even = pltpu.VMEM((early_rows + 5 * TAIL, columns), bf16)
    odd = pltpu.VMEM((early_rows, columns), bf16)
    even_early, odd_early, late, far_half, own_reflect, near_anchors = pl.pallas_call(
        functools.partial(pack_kernel, group, sizes),
        out_shape=[
            even,
            odd,
            jax.ShapeDtypeStruct((2 * part, columns), bf16),
            jax.ShapeDtypeStruct((half_rows, columns), bf16),
            pltpu.VMEM(tile_reflect.shape, bf16),
            jax.ShapeDtypeStruct(anchors.shape, jnp.int32),
        ],
        in_specs=[hbm] * 4,
        out_specs=[vmem] * 5 + [smem],
        scratch_shapes=[
            pltpu.VMEM(lateral_x.shape[1:], bf16),
            pltpu.VMEM(lateral_y.shape[1:], bf16),
            pltpu.SemaphoreType.DMA((4,)),
        ],
        compiler_params=params(12),
        name="pack",
    )(kept(lateral_x[0]), kept(lateral_y[0]), kept(tile_reflect), kept(anchors))
    last = sections - 1
    far_half = lax.ppermute(far_half, BOTH, plan.to_workers(last))
    even_early, odd_early, far_window = pl.pallas_call(
        functools.partial(window_kernel, shots, sizes),
        out_shape=[even, odd, jax.ShapeDtypeStruct((win_rows, columns), bf16)],
        in_specs=[smem, smem] + [vmem] * 4,
        out_specs=[vmem] * 3,
        input_output_aliases={4: 0, 5: 1},
        compiler_params=params(12),
        cost_estimate=pl.CostEstimate(flops=3 * 10**9, bytes_accessed=4 * MIB, transcendentals=0),
        name="windows",
    )(near_anchors, counts, halo, held(own_reflect), held(even_early), held(odd_early))
    messages = [
        even_early,
        lax.ppermute(odd_early, BOTH, plan.to_workers(1)),
        lax.ppermute(even_early, BOTH, plan.to_workers(2)),
    ]
    far_window = lax.ppermute(far_window, BOTH, plan.to_workers(last))
    other_half = lax.ppermute(far_half, BOTH, plan.swap_workers())
    late = pl.pallas_call(
        hold_kernel,
        out_shape=jax.ShapeDtypeStruct(late.shape, bf16),
        in_specs=[anywhere] * 2,
        out_specs=anywhere,
        input_output_aliases={0: 0},
        compiler_params=params(2),
        cost_estimate=pl.CostEstimate(flops=36 * 10**8, bytes_accessed=0, transcendentals=0),
        name="hold",
    )(late, far_window)
    lates = [lax.ppermute(late, BOTH, plan.ops_to_workers(r)) for r in (1, 2)]
    joined = pl.pallas_call(
        functools.partial(join_kernel, group),
        out_shape=pltpu.VMEM((2 * half_rows, columns), bf16),
        in_specs=[vmem] * 2,
        out_specs=vmem,
        compiler_params=params(8),
        name="join",
    )(held(far_half), held(other_half))

    levels = sections * slots
    buffers = [
        pltpu.VMEM((levels, 2 * columns, columns), bf16),
        pltpu.VMEM((levels, 2 * rows, 2 * rows), bf16),
        pltpu.VMEM((levels, rows, columns), bf16),
        pltpu.VMEM((levels + 1, 2 * rows, columns), bf16),
    ]
    stages = [pltpu.VMEM((2 * columns, columns), bf16), pltpu.VMEM((rows, 2 * rows), bf16)]
    messages = [held(message) for message in messages]
    late, joined, far_window = held(late), held(joined), held(far_window)
    *filled, state = pl.pallas_call(
        functools.partial(down_kernel, sections, shots, group, sizes),
        out_shape=buffers + [jax.ShapeDtypeStruct((3 + sections,), jnp.int32)],
        in_specs=[vmem] * 7,
        out_specs=[vmem] * 4 + [smem],
        scratch_shapes=stages,
        compiler_params=params(24),
        name="down",
    )(held(source.reshape(shots, 2 * rows, columns)), *messages, late, joined, far_window)
    correlations = pl.pallas_call(
        functools.partial(up_kernel, sections, shots, group, sizes),
        out_shape=[
            jax.ShapeDtypeStruct((slots * rows + TAIL * more, columns), bf16)
            for more in (0, 1, 0, 2)
        ]
        + buffers,
        in_specs=[smem] + [vmem] * 12,
        out_specs=[vmem] * (sections + 4),
        scratch_shapes=stages + [pltpu.VMEM((2 * rows, columns), bf16)],
        input_output_aliases={9 + i: sections + i for i in range(4)},
        compiler_params=params(24),
        name="up",
    )(
        state, *messages, late, *[held(part) for part in lates], joined, far_window,
        *[held(buffer) for buffer in filled],
    )

    arrived = [correlations[0]] + [
        lax.ppermute(correlations[r], BOTH, plan.from_workers(r)) for r in range(1, sections)
    ]
    left, own = [
        pl.pallas_call(
            functools.partial(place_kernel, shots, to_left),
            out_shape=jax.ShapeDtypeStruct((slots * rows, columns), kind),
            in_specs=[smem] + [vmem] * sections,
            out_specs=vmem,
            compiler_params=params(8),
            name=name,
        )(near_anchors, *arrived)
        for to_left, kind, name in ((True, bf16, "left"), (False, jnp.float32, "own"))
    ]
    from_right = lax.ppermute(left, "tile", [(i + 1, i) for i in range(plan.tiles - 1)])
    image = own + from_right.astype(jnp.float32)
    return image.reshape(1, slots, rows, columns)


def solution(mesh):
    return jax.shard_map(
        on_device,
        mesh=mesh,
        in_specs=(
            P("tile", None, None, None),
            P("tile"),
            P("depth"),
            P("depth", None, None, "tile"),
            P("depth", None, None, None, None),
            P("depth", None, None, None, None),
        ),
        out_specs=P("depth", None, None, "tile"),
        check_vma=False,
    )
```

```python
import functools

import jax
import jax.numpy as jnp
from jax import lax
from jax.experimental import pallas as pl
from jax.experimental.pallas import tpu as pltpu
from jax.sharding import PartitionSpec as P

BOTH = ("depth", "tile")
MIB = 1024 * 1024
TAIL = 16


class Plan:
    def __init__(self, shots):
        self.sections = lax.axis_size("depth")
        self.tiles = lax.axis_size("tile")
        self.shots = shots
        self.group = self.sections // shots
        assert self.sections == 4 and self.group * shots == self.sections
        assert self.tiles % (2 * self.group) == 0

    def device(self, depth, tile):
        return depth * self.tiles + tile

    def bases(self):
        return range(0, self.tiles, self.group)

    def worker(self, base, w):
        return self.device(w, base + w // self.shots)

    def other(self, w, base):
        return self.device(w, base + (w // self.shots + 1) % self.group)

    def ops_to_workers(self, r):
        return [
            (self.other(w ^ r, base), self.worker(base, w))
            for base in self.bases()
            for w in range(self.sections)
        ]

    def swap_workers(self):
        return [
            (self.worker(base, w), self.worker((base // self.group ^ 1) * self.group, w))
            for base in self.bases()
            for w in range(self.sections)
        ]

    def to_workers(self, r):
        return [
            (self.device(w ^ r, base + w // self.shots), self.worker(base, w))
            for base in self.bases()
            for w in range(self.sections)
        ]

    def from_workers(self, r):
        return [(b, a) for a, b in self.to_workers(r)]


def pack_kernel(group, sizes, x_hbm, y_hbm, even, odd, late, half_out, x_ref, y_ref, sem):
    slots, rows, columns = sizes
    loads = [
        pltpu.make_async_copy(x_hbm, x_ref, sem.at[0]),
        pltpu.make_async_copy(y_hbm, y_ref, sem.at[1]),
    ]
    for load in loads:
        load.start()
    for load in loads:
        load.wait()
    piece = rows // 2
    part = columns + piece
    first = (slots - 1) * part
    for half in range(2):
        for slot in range(slots):
            op_x = jnp.concatenate(
                [x_ref[slot, i, half * piece : (half + 1) * piece, :] for i in range(2)], axis=1
            )
            op_y = y_ref[slot, half]
            if slot < slots - 1:
                places = [(out, half * first + slot * part) for out in (even, odd)]
            else:
                places = [(late, half * part)]
            for out, spot in places:
                out[spot : spot + columns, :] = op_y
                out[spot + columns : spot + part, :] = op_x
    plane = lax.rem(lax.axis_index("tile") // group, 2)
    half_out[:first, :] = even[pl.ds(pl.multiple_of(plane * first, first), first), :]
    half_out[first:, :] = late[pl.ds(pl.multiple_of(plane * part, part), part), :]


def window_kernel(shots, sizes, anchors_hbm, counts, left_ref, right_hbm, *refs):
    slots, rows, columns = sizes
    messages, (alone, anchors, right_ref, sem) = refs[shots : 2 * shots], refs[2 * shots :]
    loads = [
        pltpu.make_async_copy(anchors_hbm, anchors, sem.at[0]),
        pltpu.make_async_copy(right_hbm, right_ref, sem.at[1]),
    ]
    for load in loads:
        load.start()
    for load in loads:
        load.wait()
    section, tile = lax.axis_index("depth"), lax.axis_index("tile")
    left, right = left_ref[...].astype(jnp.float32), right_ref[...].astype(jnp.float32)
    lanes = lax.broadcasted_iota(jnp.int32, left.shape, 1)
    tail = jnp.full((TAIL, columns), counts[0].astype(jnp.float32), jnp.float32)
    for q, message in enumerate(messages):
        offset = anchors[lax.rem(section, shots) ^ q] - (tile - 1) * columns
        merged = jnp.where(lanes >= offset, left, right)
        back = lax.rem(columns - lax.rem(offset, columns), columns)
        window = pltpu.roll(merged, back, 1).astype(message.dtype)
        for out in [message] + ([alone] if q == shots - 1 else []):
            spot = out.shape[0] - TAIL - slots * rows
            out[spot : spot + slots * rows, :] = window
            out[spot + slots * rows :, :] = tail.astype(out.dtype)


class Sweep:
    def __init__(self, shots, group, sizes, turned_y, turned_x, level_w, waves, stage_y, stage_x):
        self.sizes = sizes
        self.turned_y, self.turned_x, self.level_w = turned_y, turned_x, level_w
        self.waves, self.stage_y, self.stage_x = waves, stage_y, stage_x
        slots, rows, columns = sizes
        self.piece = rows // 2
        self.part = columns + self.piece
        self.first = (slots - 1) * self.part
        self.half_rows = self.first + self.part
        self.win_rows = slots * rows + TAIL
        self.here, tile = lax.axis_index("depth"), lax.axis_index("tile")
        self.shot = lax.rem(self.here, shots)
        self.is_worker = (self.here // shots == lax.rem(tile, group)).astype(jnp.int32)

    def window_start(self, window_ref):
        return window_ref.shape[0] - self.win_rows

    def fetch(self, r, slot, place, sources):
        slots, rows, columns = self.sizes
        for r_of, (early, late, window) in enumerate(sources):
            early_slots = slots if early.shape[0] == 2 * self.half_rows else slots - 1
            choices = [(early, early_slots * self.part, slot < early_slots, slot)]
            if late is not None:
                choices.append((late, self.part, slot == slots - 1, 0))
            for ref, stride, chosen, at in choices:

                @pl.when((r == r_of) & chosen)
                def _():
                    for half in range(2):
                        start = pl.multiple_of(half * stride + at * self.part, self.piece)
                        self.stage_y[half * columns : (half + 1) * columns, :] = ref[
                            pl.ds(start, columns), :
                        ]
                        tail = pl.multiple_of(start + columns, self.piece)
                        self.stage_x[half * self.piece : (half + 1) * self.piece, :] = ref[
                            pl.ds(tail, self.piece), :
                        ]
                    spot = self.window_start(window) + slot * rows
                    self.level_w[place] = window[pl.ds(pl.multiple_of(spot, TAIL), rows), :]

    def blocks(self, re, im):
        upper = jnp.concatenate([re, -im], axis=1)
        return jnp.concatenate([upper, jnp.concatenate([im, re], axis=1)], axis=0)

    def complex_sum(self, both):
        _, rows, columns = self.sizes
        with_re, with_im = both[:, :columns], both[:, columns:]
        return with_re[:rows] - with_im[rows:], with_im[:rows] + with_re[rows:]

    def dot(self, a, b, dims):
        return lax.dot_general(a, b, (dims, ((), ())), preferred_element_type=jnp.float32)

    def down(self, place):
        _, rows, columns = self.sizes
        x_re, x_im = self.stage_x[:, :rows], self.stage_x[:, rows:]
        wave = self.waves[place].astype(jnp.float32)
        gain = 1.0 + self.level_w[place].astype(jnp.float32)
        scaled = jnp.concatenate([gain * wave[:rows], gain * wave[rows:]], axis=0)
        self.turned_x[place] = self.blocks(x_re.T, x_im.T)
        middle = self.dot(self.blocks(x_re, x_im), scaled.astype(jnp.bfloat16), ((1,), (0,)))
        for i in range(2):
            lines = slice(i * columns, (i + 1) * columns)
            self.turned_y[place, lines, :] = self.stage_y[lines, :].T
        both = self.dot(middle.astype(jnp.bfloat16), self.stage_y[...], ((1,), (1,)))
        moved = jnp.concatenate(self.complex_sum(both), axis=0)
        self.waves[place + 1] = moved.astype(jnp.bfloat16)
        return place + 1

    def up(self, r, slot, place, wave_up, outs):
        _, rows, columns = self.sizes
        level = place - 1
        wave = self.waves[level].astype(jnp.float32)
        window = self.level_w[level].astype(jnp.float32)
        back = self.dot(self.turned_x[level], wave_up[...], ((1,), (0,)))
        both = self.dot(back.astype(jnp.bfloat16), self.turned_y[level], ((1,), (1,)))
        spread_re, spread_im = self.complex_sum(both)
        up_re = (window * wave[:rows] + spread_re).astype(jnp.bfloat16)
        up_im = (window * wave[rows:] + spread_im).astype(jnp.bfloat16)
        wave_up[:rows] = up_re
        wave_up[rows:] = up_im
        product = wave[:rows] * up_re.astype(jnp.float32)
        product += wave[rows:] * up_im.astype(jnp.float32)
        spot = pl.multiple_of(slot * rows, rows)
        for r_of, out in enumerate(outs):

            @pl.when(r == r_of)
            def _():
                out[pl.ds(spot, rows), :] = product.astype(out.dtype)

        return level


def sweep_kernel(sections, shots, group, sizes, source_ref, *refs):
    slots, rows, _ = sizes
    (own, near, far), (own_late, near_late, far_late, joined, far_window) = refs[:3], refs[3:8]
    outs, refs = refs[8 : 8 + sections], refs[8 + sections :]
    *buffers, stage_y, stage_x, wave_up, counts = refs
    it = Sweep(shots, group, sizes, *buffers, stage_y, stage_x)
    sources = [
        (own, own_late, own),
        (near, near_late, near),
        (far, far_late, far),
        (joined, None, far_window),
    ]

    @pl.when(it.is_worker == 0)
    def _():
        outs[0][...] = jnp.zeros(outs[0].shape, outs[0].dtype)

    @pl.when(it.is_worker != 0)
    def _():
        it.waves[0] = source_ref[it.shot]
        for r, (_, _, window) in enumerate(sources):
            value = jnp.max(window[window.shape[0] - TAIL :, :].astype(jnp.float32))
            counts[r] = value.astype(jnp.int32)
        for out in outs:
            out[...] = jnp.zeros(out.shape, out.dtype)
        wave_up[...] = jnp.zeros(wave_up.shape, wave_up.dtype)

        def section_down(section, place):
            r = section ^ it.here

            def level_down(slot, place):
                it.fetch(r, slot, place, sources)
                return it.down(place)

            return lax.fori_loop(0, counts[r], level_down, place)

        last = lax.fori_loop(0, sections, section_down, 0)

        def section_up(step, place):
            r = (sections - 1 - step) ^ it.here
            count = counts[r]
            return lax.fori_loop(
                0,
                count,
                lambda inner, place: it.up(r, count - 1 - inner, place, wave_up, outs),
                place,
            )

        lax.fori_loop(0, sections, section_up, last)


def join_kernel(group, first_ref, second_ref, out_ref):
    plane = lax.rem(lax.axis_index("tile") // group, 2)
    half_rows = first_ref.shape[0]
    for i, ref in enumerate((first_ref, second_ref)):
        start = pl.multiple_of((plane if i == 0 else 1 - plane) * half_rows, half_rows)
        out_ref[pl.ds(start, half_rows), :] = ref[...]


def hold_kernel(*refs):
    pass


def place_kernel(shots, anchors, *refs):
    arrived, (left_out, own_out) = refs[:-2], refs[-2:]
    section, tile = lax.axis_index("depth"), lax.axis_index("tile")
    places, columns = left_out.shape
    left_sum, own_sum = None, None
    for q in range(shots):
        offset = anchors[lax.rem(section, shots) ^ q] - (tile - 1) * columns
        total = None
        for r in range(q, len(arrived), shots):
            value = arrived[r][:places, :].astype(jnp.float32)
            total = value if total is None else total + value
        turned = pltpu.roll(total, lax.rem(offset, columns), 1)
        lanes = lax.broadcasted_iota(jnp.int32, turned.shape, 1)
        left = jnp.where(lanes >= offset, turned, 0.0)
        own = jnp.where(lanes >= offset, 0.0, turned)
        left_sum = left if left_sum is None else left_sum + left
        own_sum = own if own_sum is None else own_sum + own
    left_out[...] = left_sum.astype(left_out.dtype)
    own_out[...] = own_sum


def kept(array):
    return pltpu.with_memory_space_constraint(array, pltpu.HBM)


def held(array):
    return pltpu.with_memory_space_constraint(array, pltpu.VMEM)


def on_device(source, anchors, counts, reflect, lateral_x, lateral_y):
    shots, _, rows, columns = source.shape
    slots = reflect.shape[1]
    sizes = (slots, rows, columns)
    plan = Plan(shots)
    sections, group = plan.sections, plan.group
    assert shots == 2
    bf16 = jnp.bfloat16
    smem = pl.BlockSpec(memory_space=pltpu.SMEM)
    vmem = pl.BlockSpec(memory_space=pltpu.VMEM)
    hbm = pl.BlockSpec(memory_space=pltpu.HBM)
    anywhere = pl.BlockSpec(memory_space=pl.ANY)

    def params(mib):
        return pltpu.CompilerParams(vmem_limit_bytes=mib * MIB)

    tile_reflect = reflect[0].reshape(slots * rows, columns)
    halo = lax.ppermute(tile_reflect, "tile", [(i, i + 1) for i in range(plan.tiles - 1)])
    part = columns + rows // 2
    half_rows, win_rows = slots * part, slots * rows + TAIL
    early_rows = 2 * (half_rows - part) + win_rows
    even = pltpu.VMEM((early_rows + 5 * TAIL, columns), bf16)
    odd = pltpu.VMEM((early_rows, columns), bf16)
    even_early, odd_early, late, far_half = pl.pallas_call(
        functools.partial(pack_kernel, group, sizes),
        out_shape=[
            even,
            odd,
            jax.ShapeDtypeStruct((2 * part, columns), bf16),
            jax.ShapeDtypeStruct((half_rows, columns), bf16),
        ],
        in_specs=[hbm, hbm],
        out_specs=[vmem] * 4,
        scratch_shapes=[
            pltpu.VMEM(lateral_x.shape[1:], bf16),
            pltpu.VMEM(lateral_y.shape[1:], bf16),
            pltpu.SemaphoreType.DMA((2,)),
        ],
        compiler_params=params(12),
        name="pack",
    )(kept(lateral_x[0]), kept(lateral_y[0]))
    last = sections - 1
    far_half = lax.ppermute(far_half, BOTH, plan.to_workers(last))
    even_early, odd_early, far_window = pl.pallas_call(
        functools.partial(window_kernel, shots, sizes),
        out_shape=[even, odd, jax.ShapeDtypeStruct((win_rows, columns), bf16)],
        in_specs=[hbm, smem, vmem, hbm, vmem, vmem],
        out_specs=[vmem] * 3,
        scratch_shapes=[
            pltpu.SMEM((shots,), jnp.int32),
            pltpu.VMEM((slots * rows, columns), bf16),
            pltpu.SemaphoreType.DMA((2,)),
        ],
        input_output_aliases={4: 0, 5: 1},
        compiler_params=params(12),
        cost_estimate=pl.CostEstimate(flops=3 * 10**9, bytes_accessed=4 * MIB, transcendentals=0),
        name="windows",
    )(kept(anchors), counts, halo, kept(tile_reflect), held(even_early), held(odd_early))
    messages = [
        even_early,
        lax.ppermute(odd_early, BOTH, plan.to_workers(1)),
        lax.ppermute(even_early, BOTH, plan.to_workers(2)),
    ]
    far_window = lax.ppermute(far_window, BOTH, plan.to_workers(last))
    other_half = lax.ppermute(far_half, BOTH, plan.swap_workers())
    lates = pl.pallas_call(
        hold_kernel,
        out_shape=[jax.ShapeDtypeStruct(late.shape, bf16)] * 2,
        in_specs=[anywhere] * 2,
        out_specs=[anywhere] * 2,
        input_output_aliases={0: 0, 1: 1},
        compiler_params=params(2),
        cost_estimate=pl.CostEstimate(flops=9 * 10**9, bytes_accessed=0, transcendentals=0),
        name="hold",
    )(*[lax.ppermute(late, BOTH, plan.ops_to_workers(r)) for r in (1, 2)])
    joined = pl.pallas_call(
        functools.partial(join_kernel, group),
        out_shape=pltpu.VMEM((2 * half_rows, columns), bf16),
        in_specs=[vmem] * 2,
        out_specs=vmem,
        compiler_params=params(8),
        name="join",
    )(held(far_half), held(other_half))

    levels = sections * slots
    buffers = [
        pltpu.VMEM((levels, 2 * columns, columns), bf16),
        pltpu.VMEM((levels, 2 * rows, 2 * rows), bf16),
        pltpu.VMEM((levels, rows, columns), bf16),
        pltpu.VMEM((levels + 1, 2 * rows, columns), bf16),
    ]
    stages = [pltpu.VMEM((2 * columns, columns), bf16), pltpu.VMEM((rows, 2 * rows), bf16)]
    operands = [*messages, late, *lates, joined, far_window]
    correlations = pl.pallas_call(
        functools.partial(sweep_kernel, sections, shots, group, sizes),
        out_shape=[
            jax.ShapeDtypeStruct((slots * rows + TAIL * more, columns), bf16)
            for more in (0, 1, 0, 2)
        ],
        in_specs=[vmem] * 9,
        out_specs=[vmem] * sections,
        scratch_shapes=buffers
        + stages
        + [pltpu.VMEM((2 * rows, columns), bf16), pltpu.SMEM((sections,), jnp.int32)],
        compiler_params=params(24),
        name="sweep",
    )(held(source.reshape(shots, 2 * rows, columns)), *[held(operand) for operand in operands])

    corr_shape = jax.ShapeDtypeStruct((slots * rows, columns), bf16)
    arrived = [correlations[0]] + [
        lax.ppermute(correlations[r], BOTH, plan.from_workers(r)) for r in range(1, sections)
    ]
    left, own = pl.pallas_call(
        functools.partial(place_kernel, shots),
        out_shape=[corr_shape, jax.ShapeDtypeStruct((slots * rows, columns), jnp.float32)],
        in_specs=[smem] + [vmem] * sections,
        out_specs=[vmem, vmem],
        compiler_params=params(8),
        name="place",
    )(anchors, *arrived)
    from_right = lax.ppermute(left, "tile", [(i + 1, i) for i in range(plan.tiles - 1)])
    image = own + from_right.astype(jnp.float32)
    return image.reshape(1, slots, rows, columns)


def solution(mesh):
    return jax.shard_map(
        on_device,
        mesh=mesh,
        in_specs=(
            P("tile", None, None, None),
            P("tile"),
            P("depth"),
            P("depth", None, None, "tile"),
            P("depth", None, None, None, None),
            P("depth", None, None, None, None),
        ),
        out_specs=P("depth", None, None, "tile"),
        check_vma=False,
    )
```

```python
import functools

import jax
import jax.numpy as jnp
from jax import lax
from jax.experimental import pallas as pl
from jax.experimental.pallas import tpu as pltpu
from jax.sharding import PartitionSpec as P

BOTH = ("depth", "tile")
MIB = 1024 * 1024
TAIL = 16


class Plan:
    def __init__(self, shots):
        self.sections = lax.axis_size("depth")
        self.tiles = lax.axis_size("tile")
        self.shots = shots
        self.group = self.sections // shots
        assert self.sections == 4 and self.group * shots == self.sections
        assert self.tiles % (2 * self.group) == 0

    def device(self, depth, tile):
        return depth * self.tiles + tile

    def bases(self):
        return range(0, self.tiles, self.group)

    def worker(self, base, w):
        return self.device(w, base + w // self.shots)

    def other(self, w, base):
        return self.device(w, base + (w // self.shots + 1) % self.group)

    def ops_to_workers(self, r):
        return [
            (self.other(w ^ r, base), self.worker(base, w))
            for base in self.bases()
            for w in range(self.sections)
        ]

    def swap_workers(self):
        return [
            (self.worker(base, w), self.worker((base // self.group ^ 1) * self.group, w))
            for base in self.bases()
            for w in range(self.sections)
        ]

    def to_workers(self, r):
        return [
            (self.device(w ^ r, base + w // self.shots), self.worker(base, w))
            for base in self.bases()
            for w in range(self.sections)
        ]

    def from_workers(self, r):
        return [(b, a) for a, b in self.to_workers(r)]


def pack_kernel(group, sizes, x_hbm, y_hbm, even, odd, late, half_out, x_ref, y_ref, sem):
    slots, rows, columns = sizes
    loads = [
        pltpu.make_async_copy(x_hbm, x_ref, sem.at[0]),
        pltpu.make_async_copy(y_hbm, y_ref, sem.at[1]),
    ]
    for load in loads:
        load.start()
    for load in loads:
        load.wait()
    piece = rows // 2
    part = columns + piece
    first = (slots - 1) * part
    for half in range(2):
        for slot in range(slots):
            op_x = jnp.concatenate(
                [x_ref[slot, i, half * piece : (half + 1) * piece, :] for i in range(2)], axis=1
            )
            op_y = y_ref[slot, half]
            if slot < slots - 1:
                places = [(out, half * first + slot * part) for out in (even, odd)]
            else:
                places = [(late, half * part)]
            for out, spot in places:
                out[spot : spot + columns, :] = op_y
                out[spot + columns : spot + part, :] = op_x
    plane = lax.rem(lax.axis_index("tile") // group, 2)
    half_out[:first, :] = even[pl.ds(pl.multiple_of(plane * first, first), first), :]
    half_out[first:, :] = late[pl.ds(pl.multiple_of(plane * part, part), part), :]


def window_kernel(shots, sizes, anchors_hbm, counts, left_ref, right_hbm, *refs):
    slots, rows, columns = sizes
    messages, (alone, anchors, right_ref, sem) = refs[shots : 2 * shots], refs[2 * shots :]
    loads = [
        pltpu.make_async_copy(anchors_hbm, anchors, sem.at[0]),
        pltpu.make_async_copy(right_hbm, right_ref, sem.at[1]),
    ]
    for load in loads:
        load.start()
    for load in loads:
        load.wait()
    section, tile = lax.axis_index("depth"), lax.axis_index("tile")
    left, right = left_ref[...].astype(jnp.float32), right_ref[...].astype(jnp.float32)
    lanes = lax.broadcasted_iota(jnp.int32, left.shape, 1)
    tail = jnp.full((TAIL, columns), counts[0].astype(jnp.float32), jnp.float32)
    for q, message in enumerate(messages):
        offset = anchors[lax.rem(section, shots) ^ q] - (tile - 1) * columns
        merged = jnp.where(lanes >= offset, left, right)
        back = lax.rem(columns - lax.rem(offset, columns), columns)
        window = pltpu.roll(merged, back, 1).astype(message.dtype)
        for out in [message] + ([alone] if q == shots - 1 else []):
            spot = out.shape[0] - TAIL - slots * rows
            out[spot : spot + slots * rows, :] = window
            out[spot + slots * rows :, :] = tail.astype(out.dtype)


class Sweep:
    def __init__(self, shots, group, sizes, turned_y, turned_x, level_w, waves, stage_y, stage_x):
        self.sizes = sizes
        self.turned_y, self.turned_x, self.level_w = turned_y, turned_x, level_w
        self.waves, self.stage_y, self.stage_x = waves, stage_y, stage_x
        slots, rows, columns = sizes
        self.piece = rows // 2
        self.part = columns + self.piece
        self.first = (slots - 1) * self.part
        self.half_rows = self.first + self.part
        self.win_rows = slots * rows + TAIL
        self.here, tile = lax.axis_index("depth"), lax.axis_index("tile")
        self.shot = lax.rem(self.here, shots)
        self.is_worker = (self.here // shots == lax.rem(tile, group)).astype(jnp.int32)

    def window_start(self, window_ref):
        return window_ref.shape[0] - self.win_rows

    def fetch(self, r, slot, place, sources):
        slots, rows, columns = self.sizes
        for r_of, (early, late, window) in enumerate(sources):
            early_slots = slots if early.shape[0] == 2 * self.half_rows else slots - 1
            choices = [(early, early_slots * self.part, slot < early_slots, slot)]
            if late is not None:
                choices.append((late, self.part, slot == slots - 1, 0))
            for ref, stride, chosen, at in choices:

                @pl.when((r == r_of) & chosen)
                def _():
                    for half in range(2):
                        start = pl.multiple_of(half * stride + at * self.part, self.piece)
                        self.stage_y[half * columns : (half + 1) * columns, :] = ref[
                            pl.ds(start, columns), :
                        ]
                        tail = pl.multiple_of(start + columns, self.piece)
                        self.stage_x[half * self.piece : (half + 1) * self.piece, :] = ref[
                            pl.ds(tail, self.piece), :
                        ]
                    spot = self.window_start(window) + slot * rows
                    self.level_w[place] = window[pl.ds(pl.multiple_of(spot, TAIL), rows), :]

    def blocks(self, re, im):
        upper = jnp.concatenate([re, -im], axis=1)
        return jnp.concatenate([upper, jnp.concatenate([im, re], axis=1)], axis=0)

    def complex_sum(self, both):
        _, rows, columns = self.sizes
        with_re, with_im = both[:, :columns], both[:, columns:]
        return with_re[:rows] - with_im[rows:], with_im[:rows] + with_re[rows:]

    def dot(self, a, b, dims):
        return lax.dot_general(a, b, (dims, ((), ())), preferred_element_type=jnp.float32)

    def down(self, place):
        _, rows, columns = self.sizes
        x_re, x_im = self.stage_x[:, :rows], self.stage_x[:, rows:]
        wave = self.waves[place].astype(jnp.float32)
        gain = 1.0 + self.level_w[place].astype(jnp.float32)
        scaled = jnp.concatenate([gain * wave[:rows], gain * wave[rows:]], axis=0)
        self.turned_x[place] = self.blocks(x_re.T, x_im.T)
        middle = self.dot(self.blocks(x_re, x_im), scaled.astype(jnp.bfloat16), ((1,), (0,)))
        for i in range(2):
            lines = slice(i * columns, (i + 1) * columns)
            self.turned_y[place, lines, :] = self.stage_y[lines, :].T
        both = self.dot(middle.astype(jnp.bfloat16), self.stage_y[...], ((1,), (1,)))
        moved = jnp.concatenate(self.complex_sum(both), axis=0)
        self.waves[place + 1] = moved.astype(jnp.bfloat16)
        return place + 1

    def up(self, r, slot, place, wave_up, outs):
        _, rows, columns = self.sizes
        level = place - 1
        wave = self.waves[level].astype(jnp.float32)
        window = self.level_w[level].astype(jnp.float32)
        back = self.dot(self.turned_x[level], wave_up[...], ((1,), (0,)))
        both = self.dot(back.astype(jnp.bfloat16), self.turned_y[level], ((1,), (1,)))
        spread_re, spread_im = self.complex_sum(both)
        up_re = (window * wave[:rows] + spread_re).astype(jnp.bfloat16)
        up_im = (window * wave[rows:] + spread_im).astype(jnp.bfloat16)
        wave_up[:rows] = up_re
        wave_up[rows:] = up_im
        product = wave[:rows] * up_re.astype(jnp.float32)
        product += wave[rows:] * up_im.astype(jnp.float32)
        spot = pl.multiple_of(slot * rows, rows)
        for r_of, out in enumerate(outs):

            @pl.when(r == r_of)
            def _():
                out[pl.ds(spot, rows), :] = product.astype(out.dtype)

        return level


def sweep_kernel(sections, shots, group, sizes, source_ref, *refs):
    slots, rows, _ = sizes
    (own, near, far), (own_late, near_late, far_late, joined, far_window) = refs[:3], refs[3:8]
    outs, refs = refs[8 : 8 + sections], refs[8 + sections :]
    *buffers, stage_y, stage_x, wave_up, counts = refs
    it = Sweep(shots, group, sizes, *buffers, stage_y, stage_x)
    sources = [
        (own, own_late, own),
        (near, near_late, near),
        (far, far_late, far),
        (joined, None, far_window),
    ]

    @pl.when(it.is_worker == 0)
    def _():
        outs[0][...] = jnp.zeros(outs[0].shape, outs[0].dtype)

    @pl.when(it.is_worker != 0)
    def _():
        it.waves[0] = source_ref[it.shot]
        for r, (_, _, window) in enumerate(sources):
            value = jnp.max(window[window.shape[0] - TAIL :, :].astype(jnp.float32))
            counts[r] = value.astype(jnp.int32)
        for out in outs:
            out[...] = jnp.zeros(out.shape, out.dtype)
        wave_up[...] = jnp.zeros(wave_up.shape, wave_up.dtype)

        def section_down(section, place):
            r = section ^ it.here

            def level_down(slot, place):
                it.fetch(r, slot, place, sources)
                return it.down(place)

            return lax.fori_loop(0, counts[r], level_down, place)

        last = lax.fori_loop(0, sections, section_down, 0)

        def section_up(step, place):
            r = (sections - 1 - step) ^ it.here
            count = counts[r]
            return lax.fori_loop(
                0,
                count,
                lambda inner, place: it.up(r, count - 1 - inner, place, wave_up, outs),
                place,
            )

        lax.fori_loop(0, sections, section_up, last)


def join_kernel(group, first_ref, second_ref, out_ref):
    plane = lax.rem(lax.axis_index("tile") // group, 2)
    half_rows = first_ref.shape[0]
    for i, ref in enumerate((first_ref, second_ref)):
        start = pl.multiple_of((plane if i == 0 else 1 - plane) * half_rows, half_rows)
        out_ref[pl.ds(start, half_rows), :] = ref[...]


def follow_kernel(array_ref, after_ref, out_ref):
    pass


def hold_kernel(*refs):
    pass


def place_kernel(shots, anchors, *refs):
    arrived, (left_out, own_out) = refs[:-2], refs[-2:]
    section, tile = lax.axis_index("depth"), lax.axis_index("tile")
    places, columns = left_out.shape
    left_sum, own_sum = None, None
    for q in range(shots):
        offset = anchors[lax.rem(section, shots) ^ q] - (tile - 1) * columns
        total = None
        for r in range(q, len(arrived), shots):
            value = arrived[r][:places, :].astype(jnp.float32)
            total = value if total is None else total + value
        turned = pltpu.roll(total, lax.rem(offset, columns), 1)
        lanes = lax.broadcasted_iota(jnp.int32, turned.shape, 1)
        left = jnp.where(lanes >= offset, turned, 0.0)
        own = jnp.where(lanes >= offset, 0.0, turned)
        left_sum = left if left_sum is None else left_sum + left
        own_sum = own if own_sum is None else own_sum + own
    left_out[...] = left_sum.astype(left_out.dtype)
    own_out[...] = own_sum


def kept(array):
    return pltpu.with_memory_space_constraint(array, pltpu.HBM)


def held(array):
    return pltpu.with_memory_space_constraint(array, pltpu.VMEM)


def on_device(source, anchors, counts, reflect, lateral_x, lateral_y):
    shots, _, rows, columns = source.shape
    slots = reflect.shape[1]
    sizes = (slots, rows, columns)
    plan = Plan(shots)
    sections, group = plan.sections, plan.group
    assert shots == 2
    bf16 = jnp.bfloat16
    smem = pl.BlockSpec(memory_space=pltpu.SMEM)
    vmem = pl.BlockSpec(memory_space=pltpu.VMEM)
    hbm = pl.BlockSpec(memory_space=pltpu.HBM)
    anywhere = pl.BlockSpec(memory_space=pl.ANY)

    def params(mib):
        return pltpu.CompilerParams(vmem_limit_bytes=mib * MIB)

    tile_reflect = reflect[0].reshape(slots * rows, columns)
    halo = lax.ppermute(tile_reflect, "tile", [(i, i + 1) for i in range(plan.tiles - 1)])
    part = columns + rows // 2
    half_rows, win_rows = slots * part, slots * rows + TAIL
    early_rows = 2 * (half_rows - part) + win_rows
    even = pltpu.VMEM((early_rows + 5 * TAIL, columns), bf16)
    odd = pltpu.VMEM((early_rows, columns), bf16)
    even_early, odd_early, late, far_half = pl.pallas_call(
        functools.partial(pack_kernel, group, sizes),
        out_shape=[
            even,
            odd,
            jax.ShapeDtypeStruct((2 * part, columns), bf16),
            jax.ShapeDtypeStruct((half_rows, columns), bf16),
        ],
        in_specs=[hbm, hbm],
        out_specs=[vmem] * 4,
        scratch_shapes=[
            pltpu.VMEM(lateral_x.shape[1:], bf16),
            pltpu.VMEM(lateral_y.shape[1:], bf16),
            pltpu.SemaphoreType.DMA((2,)),
        ],
        compiler_params=params(12),
        name="pack",
    )(kept(lateral_x[0]), kept(lateral_y[0]))
    last = sections - 1
    far_half = lax.ppermute(far_half, BOTH, plan.to_workers(last))
    even_early, odd_early, far_window = pl.pallas_call(
        functools.partial(window_kernel, shots, sizes),
        out_shape=[even, odd, jax.ShapeDtypeStruct((win_rows, columns), bf16)],
        in_specs=[hbm, smem, vmem, hbm, vmem, vmem],
        out_specs=[vmem] * 3,
        scratch_shapes=[
            pltpu.SMEM((shots,), jnp.int32),
            pltpu.VMEM((slots * rows, columns), bf16),
            pltpu.SemaphoreType.DMA((2,)),
        ],
        input_output_aliases={4: 0, 5: 1},
        compiler_params=params(12),
        cost_estimate=pl.CostEstimate(flops=3 * 10**9, bytes_accessed=4 * MIB, transcendentals=0),
        name="windows",
    )(kept(anchors), counts, halo, kept(tile_reflect), held(even_early), held(odd_early))
    messages = [
        even_early,
        lax.ppermute(odd_early, BOTH, plan.to_workers(1)),
        lax.ppermute(even_early, BOTH, plan.to_workers(2)),
    ]
    other_half = lax.ppermute(far_half, BOTH, plan.swap_workers())
    lates = [lax.ppermute(late, BOTH, plan.ops_to_workers(r)) for r in (1, 2)]
    held_lates = pl.pallas_call(
        hold_kernel,
        out_shape=[jax.ShapeDtypeStruct(late.shape, bf16)] * 2,
        in_specs=[anywhere] * 2,
        out_specs=[anywhere] * 2,
        input_output_aliases={0: 0, 1: 1},
        compiler_params=params(2),
        cost_estimate=pl.CostEstimate(flops=6 * 10**9, bytes_accessed=0, transcendentals=0),
        name="hold",
    )(*lates)
    far_window = pl.pallas_call(
        follow_kernel,
        out_shape=jax.ShapeDtypeStruct(far_window.shape, bf16),
        in_specs=[anywhere] * 2,
        out_specs=anywhere,
        input_output_aliases={0: 0},
        compiler_params=params(2),
        cost_estimate=pl.CostEstimate(flops=0, bytes_accessed=0, transcendentals=0),
        name="follow",
    )(far_window, held_lates[0])
    far_window = lax.ppermute(far_window, BOTH, plan.to_workers(last))
    joined = pl.pallas_call(
        functools.partial(join_kernel, group),
        out_shape=pltpu.VMEM((2 * half_rows, columns), bf16),
        in_specs=[vmem] * 2,
        out_specs=vmem,
        compiler_params=params(8),
        name="join",
    )(held(far_half), held(other_half))

    levels = sections * slots
    buffers = [
        pltpu.VMEM((levels, 2 * columns, columns), bf16),
        pltpu.VMEM((levels, 2 * rows, 2 * rows), bf16),
        pltpu.VMEM((levels, rows, columns), bf16),
        pltpu.VMEM((levels + 1, 2 * rows, columns), bf16),
    ]
    stages = [pltpu.VMEM((2 * columns, columns), bf16), pltpu.VMEM((rows, 2 * rows), bf16)]
    operands = [*messages, late, *held_lates, joined, far_window]
    correlations = pl.pallas_call(
        functools.partial(sweep_kernel, sections, shots, group, sizes),
        out_shape=[
            jax.ShapeDtypeStruct((slots * rows + TAIL * more, columns), bf16)
            for more in (0, 1, 0, 2)
        ],
        in_specs=[vmem] * 9,
        out_specs=[vmem] * sections,
        scratch_shapes=buffers
        + stages
        + [pltpu.VMEM((2 * rows, columns), bf16), pltpu.SMEM((sections,), jnp.int32)],
        compiler_params=params(24),
        name="sweep",
    )(held(source.reshape(shots, 2 * rows, columns)), *[held(operand) for operand in operands])

    corr_shape = jax.ShapeDtypeStruct((slots * rows, columns), bf16)
    arrived = [correlations[0]] + [
        lax.ppermute(correlations[r], BOTH, plan.from_workers(r)) for r in range(1, sections)
    ]
    left, own = pl.pallas_call(
        functools.partial(place_kernel, shots),
        out_shape=[corr_shape, jax.ShapeDtypeStruct((slots * rows, columns), jnp.float32)],
        in_specs=[smem] + [vmem] * sections,
        out_specs=[vmem, vmem],
        compiler_params=params(8),
        name="place",
    )(anchors, *arrived)
    from_right = lax.ppermute(left, "tile", [(i + 1, i) for i in range(plan.tiles - 1)])
    image = own + from_right.astype(jnp.float32)
    return image.reshape(1, slots, rows, columns)


def solution(mesh):
    return jax.shard_map(
        on_device,
        mesh=mesh,
        in_specs=(
            P("tile", None, None, None),
            P("tile"),
            P("depth"),
            P("depth", None, None, "tile"),
            P("depth", None, None, None, None),
            P("depth", None, None, None, None),
        ),
        out_specs=P("depth", None, None, "tile"),
        check_vma=False,
    )
```

```python
import functools

import jax
import jax.numpy as jnp
from jax import lax
from jax.experimental import pallas as pl
from jax.experimental.pallas import tpu as pltpu
from jax.sharding import PartitionSpec as P

BOTH = ("depth", "tile")
MIB = 1024 * 1024
TAIL = 16


class Plan:
    def __init__(self, shots):
        self.sections = lax.axis_size("depth")
        self.tiles = lax.axis_size("tile")
        self.shots = shots
        self.group = self.sections // shots
        assert self.sections == 4 and self.group * shots == self.sections
        assert self.tiles % (2 * self.group) == 0

    def device(self, depth, tile):
        return depth * self.tiles + tile

    def bases(self):
        return range(0, self.tiles, self.group)

    def worker(self, base, w):
        return self.device(w, base + w // self.shots)

    def other(self, w, base):
        return self.device(w, base + (w // self.shots + 1) % self.group)

    def ops_to_workers(self, r):
        return [
            (self.other(w ^ r, base), self.worker(base, w))
            for base in self.bases()
            for w in range(self.sections)
        ]

    def swap_workers(self):
        return [
            (self.worker(base, w), self.worker((base // self.group ^ 1) * self.group, w))
            for base in self.bases()
            for w in range(self.sections)
        ]

    def to_workers(self, r):
        return [
            (self.device(w ^ r, base + w // self.shots), self.worker(base, w))
            for base in self.bases()
            for w in range(self.sections)
        ]

    def from_workers(self, r):
        return [(b, a) for a, b in self.to_workers(r)]


def pack_kernel(group, sizes, x_hbm, y_hbm, even, odd, late, half_out, x_ref, y_ref, sem):
    slots, rows, columns = sizes
    loads = [
        pltpu.make_async_copy(x_hbm, x_ref, sem.at[0]),
        pltpu.make_async_copy(y_hbm, y_ref, sem.at[1]),
    ]
    for load in loads:
        load.start()
    for load in loads:
        load.wait()
    piece = rows // 2
    part = columns + piece
    first = (slots - 1) * part
    for half in range(2):
        for slot in range(slots):
            op_x = jnp.concatenate(
                [x_ref[slot, i, half * piece : (half + 1) * piece, :] for i in range(2)], axis=1
            )
            op_y = y_ref[slot, half]
            if slot < slots - 1:
                places = [(out, half * first + slot * part) for out in (even, odd)]
            else:
                places = [(late, half * part)]
            for out, spot in places:
                out[spot : spot + columns, :] = op_y
                out[spot + columns : spot + part, :] = op_x
    plane = lax.rem(lax.axis_index("tile") // group, 2)
    half_out[:first, :] = even[pl.ds(pl.multiple_of(plane * first, first), first), :]
    half_out[first:, :] = late[pl.ds(pl.multiple_of(plane * part, part), part), :]


def window_kernel(shots, sizes, anchors_hbm, counts, left_ref, right_hbm, *refs):
    slots, rows, columns = sizes
    messages, (alone, anchors, right_ref, sem) = refs[shots : 2 * shots], refs[2 * shots :]
    loads = [
        pltpu.make_async_copy(anchors_hbm, anchors, sem.at[0]),
        pltpu.make_async_copy(right_hbm, right_ref, sem.at[1]),
    ]
    for load in loads:
        load.start()
    for load in loads:
        load.wait()
    section, tile = lax.axis_index("depth"), lax.axis_index("tile")
    left, right = left_ref[...].astype(jnp.float32), right_ref[...].astype(jnp.float32)
    lanes = lax.broadcasted_iota(jnp.int32, left.shape, 1)
    tail = jnp.full((TAIL, columns), counts[0].astype(jnp.float32), jnp.float32)
    for q, message in enumerate(messages):
        offset = anchors[lax.rem(section, shots) ^ q] - (tile - 1) * columns
        merged = jnp.where(lanes >= offset, left, right)
        back = lax.rem(columns - lax.rem(offset, columns), columns)
        window = pltpu.roll(merged, back, 1).astype(message.dtype)
        for out in [message] + ([alone] if q == shots - 1 else []):
            spot = out.shape[0] - TAIL - slots * rows
            out[spot : spot + slots * rows, :] = window
            out[spot + slots * rows :, :] = tail.astype(out.dtype)


class Sweep:
    def __init__(self, shots, group, sizes, turned_y, turned_x, level_w, waves, stage_y, stage_x):
        self.sizes = sizes
        self.turned_y, self.turned_x, self.level_w = turned_y, turned_x, level_w
        self.waves, self.stage_y, self.stage_x = waves, stage_y, stage_x
        slots, rows, columns = sizes
        self.piece = rows // 2
        self.part = columns + self.piece
        self.first = (slots - 1) * self.part
        self.half_rows = self.first + self.part
        self.win_rows = slots * rows + TAIL
        self.here, tile = lax.axis_index("depth"), lax.axis_index("tile")
        self.shot = lax.rem(self.here, shots)
        self.is_worker = (self.here // shots == lax.rem(tile, group)).astype(jnp.int32)

    def read_counts(self, sources, counts):
        for r, (_, _, window) in enumerate(sources):
            value = jnp.max(window[window.shape[0] - TAIL :, :].astype(jnp.float32))
            counts[r] = value.astype(jnp.int32)

    def early_slots(self, r, count, rounds):
        partial = (r != 0) & (r != rounds - 1)
        return jnp.where(partial, jnp.minimum(count, self.sizes[0] - 1), count)

    def window_start(self, window_ref):
        return window_ref.shape[0] - self.win_rows

    def fetch(self, r, slot, place, sources):
        slots, rows, columns = self.sizes
        for r_of, (early, late, window) in enumerate(sources):
            early_slots = slots if early.shape[0] == 2 * self.half_rows else slots - 1
            choices = [(early, early_slots * self.part, slot < early_slots, slot)]
            if late is not None:
                choices.append((late, self.part, slot == slots - 1, 0))
            for ref, stride, chosen, at in choices:

                @pl.when((r == r_of) & chosen)
                def _():
                    for half in range(2):
                        start = pl.multiple_of(half * stride + at * self.part, self.piece)
                        self.stage_y[half * columns : (half + 1) * columns, :] = ref[
                            pl.ds(start, columns), :
                        ]
                        tail = pl.multiple_of(start + columns, self.piece)
                        self.stage_x[half * self.piece : (half + 1) * self.piece, :] = ref[
                            pl.ds(tail, self.piece), :
                        ]
                    spot = self.window_start(window) + slot * rows
                    self.level_w[place] = window[pl.ds(pl.multiple_of(spot, TAIL), rows), :]

    def blocks(self, re, im):
        upper = jnp.concatenate([re, -im], axis=1)
        return jnp.concatenate([upper, jnp.concatenate([im, re], axis=1)], axis=0)

    def complex_sum(self, both):
        _, rows, columns = self.sizes
        with_re, with_im = both[:, :columns], both[:, columns:]
        return with_re[:rows] - with_im[rows:], with_im[:rows] + with_re[rows:]

    def dot(self, a, b, dims):
        return lax.dot_general(a, b, (dims, ((), ())), preferred_element_type=jnp.float32)

    def down(self, place):
        _, rows, columns = self.sizes
        x_re, x_im = self.stage_x[:, :rows], self.stage_x[:, rows:]
        wave = self.waves[place].astype(jnp.float32)
        gain = 1.0 + self.level_w[place].astype(jnp.float32)
        scaled = jnp.concatenate([gain * wave[:rows], gain * wave[rows:]], axis=0)
        self.turned_x[place] = self.blocks(x_re.T, x_im.T)
        middle = self.dot(self.blocks(x_re, x_im), scaled.astype(jnp.bfloat16), ((1,), (0,)))
        for i in range(2):
            lines = slice(i * columns, (i + 1) * columns)
            self.turned_y[place, lines, :] = self.stage_y[lines, :].T
        both = self.dot(middle.astype(jnp.bfloat16), self.stage_y[...], ((1,), (1,)))
        moved = jnp.concatenate(self.complex_sum(both), axis=0)
        self.waves[place + 1] = moved.astype(jnp.bfloat16)
        return place + 1

    def up(self, r, slot, place, wave_up, outs):
        _, rows, columns = self.sizes
        level = place - 1
        wave = self.waves[level].astype(jnp.float32)
        window = self.level_w[level].astype(jnp.float32)
        back = self.dot(self.turned_x[level], wave_up[...], ((1,), (0,)))
        both = self.dot(back.astype(jnp.bfloat16), self.turned_y[level], ((1,), (1,)))
        spread_re, spread_im = self.complex_sum(both)
        up_re = (window * wave[:rows] + spread_re).astype(jnp.bfloat16)
        up_im = (window * wave[rows:] + spread_im).astype(jnp.bfloat16)
        wave_up[:rows] = up_re
        wave_up[rows:] = up_im
        product = wave[:rows] * up_re.astype(jnp.float32)
        product += wave[rows:] * up_im.astype(jnp.float32)
        spot = pl.multiple_of(slot * rows, rows)
        for r_of, out in enumerate(outs):

            @pl.when(r == r_of)
            def _():
                out[pl.ds(spot, rows), :] = product.astype(out.dtype)

        return level


def down_kernel(sections, shots, group, sizes, source_ref, *refs):
    (own, near, far), (own_late, joined, far_window) = refs[:3], refs[3:6]
    *buffers, stage_y, stage_x, counts = refs[6:]
    it = Sweep(shots, group, sizes, *buffers, stage_y, stage_x)
    sources = [
        (own, own_late, own),
        (near, None, near),
        (far, None, far),
        (joined, None, far_window),
    ]

    @pl.when(it.is_worker != 0)
    def _():
        it.waves[0] = source_ref[it.shot]
        it.read_counts(sources, counts)

        def section_down(section, carry):
            place, going = carry
            r = section ^ it.here
            ready = it.early_slots(r, counts[r], sections)

            def level_down(slot, place):
                it.fetch(r, slot, place, sources)
                return it.down(place)

            place = lax.fori_loop(0, jnp.where(going, ready, 0), level_down, place)
            return place, going & (ready == counts[r])

        lax.fori_loop(0, sections, section_down, (jnp.int32(0), jnp.bool_(True)))


def up_kernel(sections, shots, group, sizes, *refs):
    (own, near, far), (own_late, near_late, far_late, joined, far_window) = refs[:3], refs[3:8]
    outs, refs = refs[12 : 12 + sections], refs[12 + sections :]
    *buffers, stage_y, stage_x, wave_up, counts = refs
    it = Sweep(shots, group, sizes, *buffers, stage_y, stage_x)
    sources = [
        (own, own_late, own),
        (near, near_late, near),
        (far, far_late, far),
        (joined, None, far_window),
    ]

    @pl.when(it.is_worker == 0)
    def _():
        outs[0][...] = jnp.zeros(outs[0].shape, outs[0].dtype)

    @pl.when(it.is_worker != 0)
    def _():
        it.read_counts(sources, counts)
        for out in outs:
            out[...] = jnp.zeros(out.shape, out.dtype)
        wave_up[...] = jnp.zeros(wave_up.shape, wave_up.dtype)

        def section_down(section, carry):
            place, going = carry
            r = section ^ it.here
            done = jnp.where(going, it.early_slots(r, counts[r], sections), 0)

            def level_down(slot, place):
                it.fetch(r, slot, place, sources)
                return it.down(place)

            place = lax.fori_loop(done, counts[r], level_down, place + done)
            return place, going & (done == counts[r])

        last, _ = lax.fori_loop(0, sections, section_down, (jnp.int32(0), jnp.bool_(True)))

        def section_up(step, place):
            r = (sections - 1 - step) ^ it.here
            count = counts[r]
            return lax.fori_loop(
                0,
                count,
                lambda inner, place: it.up(r, count - 1 - inner, place, wave_up, outs),
                place,
            )

        lax.fori_loop(0, sections, section_up, last)


def join_kernel(group, first_ref, second_ref, out_ref):
    plane = lax.rem(lax.axis_index("tile") // group, 2)
    half_rows = first_ref.shape[0]
    for i, ref in enumerate((first_ref, second_ref)):
        start = pl.multiple_of((plane if i == 0 else 1 - plane) * half_rows, half_rows)
        out_ref[pl.ds(start, half_rows), :] = ref[...]


def hold_kernel(array_ref, after_ref, out_ref):
    pass


def place_kernel(shots, anchors, *refs):
    arrived, (left_out, own_out) = refs[:-2], refs[-2:]
    section, tile = lax.axis_index("depth"), lax.axis_index("tile")
    places, columns = left_out.shape
    placed = None
    for q in range(shots):
        offset = anchors[lax.rem(section, shots) ^ q] - (tile - 1) * columns
        total = None
        for r in range(q, len(arrived), shots):
            value = arrived[r][:places, :]
            total = value if total is None else total + value
        to = lax.broadcasted_iota(jnp.int32, (columns, 2 * columns), 1)
        start = lax.broadcasted_iota(jnp.int32, (columns, 2 * columns), 0)
        shift = (to - start == offset).astype(jnp.float32).astype(total.dtype)
        part = jnp.dot(total, shift, preferred_element_type=jnp.float32)
        placed = part if placed is None else placed + part
    left_out[...] = placed[:, :columns].astype(left_out.dtype)
    own_out[...] = placed[:, columns:]


def kept(array):
    return pltpu.with_memory_space_constraint(array, pltpu.HBM)


def held(array):
    return pltpu.with_memory_space_constraint(array, pltpu.VMEM)


def on_device(source, anchors, counts, reflect, lateral_x, lateral_y):
    shots, _, rows, columns = source.shape
    slots = reflect.shape[1]
    sizes = (slots, rows, columns)
    plan = Plan(shots)
    sections, group = plan.sections, plan.group
    assert shots == 2
    bf16 = jnp.bfloat16
    smem = pl.BlockSpec(memory_space=pltpu.SMEM)
    vmem = pl.BlockSpec(memory_space=pltpu.VMEM)
    hbm = pl.BlockSpec(memory_space=pltpu.HBM)
    anywhere = pl.BlockSpec(memory_space=pl.ANY)

    def params(mib):
        return pltpu.CompilerParams(vmem_limit_bytes=mib * MIB)

    tile_reflect = reflect[0].reshape(slots * rows, columns)
    halo = lax.ppermute(tile_reflect, "tile", [(i, i + 1) for i in range(plan.tiles - 1)])
    part = columns + rows // 2
    half_rows, win_rows = slots * part, slots * rows + TAIL
    early_rows = 2 * (half_rows - part) + win_rows
    even = pltpu.VMEM((early_rows + 5 * TAIL, columns), bf16)
    odd = pltpu.VMEM((early_rows, columns), bf16)
    even_early, odd_early, late, far_half = pl.pallas_call(
        functools.partial(pack_kernel, group, sizes),
        out_shape=[
            even,
            odd,
            jax.ShapeDtypeStruct((2 * part, columns), bf16),
            jax.ShapeDtypeStruct((half_rows, columns), bf16),
        ],
        in_specs=[hbm, hbm],
        out_specs=[vmem] * 4,
        scratch_shapes=[
            pltpu.VMEM(lateral_x.shape[1:], bf16),
            pltpu.VMEM(lateral_y.shape[1:], bf16),
            pltpu.SemaphoreType.DMA((2,)),
        ],
        compiler_params=params(12),
        name="pack",
    )(kept(lateral_x[0]), kept(lateral_y[0]))
    last = sections - 1
    far_half = lax.ppermute(far_half, BOTH, plan.to_workers(last))
    even_early, odd_early, far_window = pl.pallas_call(
        functools.partial(window_kernel, shots, sizes),
        out_shape=[even, odd, jax.ShapeDtypeStruct((win_rows, columns), bf16)],
        in_specs=[hbm, smem, vmem, hbm, vmem, vmem],
        out_specs=[vmem] * 3,
        scratch_shapes=[
            pltpu.SMEM((shots,), jnp.int32),
            pltpu.VMEM((slots * rows, columns), bf16),
            pltpu.SemaphoreType.DMA((2,)),
        ],
        input_output_aliases={4: 0, 5: 1},
        compiler_params=params(12),
        cost_estimate=pl.CostEstimate(flops=3 * 10**9, bytes_accessed=4 * MIB, transcendentals=0),
        name="windows",
    )(kept(anchors), counts, halo, kept(tile_reflect), held(even_early), held(odd_early))
    messages = [
        even_early,
        lax.ppermute(odd_early, BOTH, plan.to_workers(1)),
        lax.ppermute(even_early, BOTH, plan.to_workers(2)),
    ]
    far_window = lax.ppermute(far_window, BOTH, plan.to_workers(last))
    other_half = lax.ppermute(far_half, BOTH, plan.swap_workers())
    late = pl.pallas_call(
        hold_kernel,
        out_shape=jax.ShapeDtypeStruct(late.shape, bf16),
        in_specs=[anywhere] * 2,
        out_specs=anywhere,
        input_output_aliases={0: 0},
        compiler_params=params(2),
        cost_estimate=pl.CostEstimate(flops=36 * 10**8, bytes_accessed=0, transcendentals=0),
        name="hold",
    )(late, far_window)
    lates = [lax.ppermute(late, BOTH, plan.ops_to_workers(r)) for r in (1, 2)]
    joined = pl.pallas_call(
        functools.partial(join_kernel, group),
        out_shape=pltpu.VMEM((2 * half_rows, columns), bf16),
        in_specs=[vmem] * 2,
        out_specs=vmem,
        compiler_params=params(8),
        name="join",
    )(held(far_half), held(other_half))

    levels = sections * slots
    buffers = [
        pltpu.VMEM((levels, 2 * columns, columns), bf16),
        pltpu.VMEM((levels, 2 * rows, 2 * rows), bf16),
        pltpu.VMEM((levels, rows, columns), bf16),
        pltpu.VMEM((levels + 1, 2 * rows, columns), bf16),
    ]
    stages = [pltpu.VMEM((2 * columns, columns), bf16), pltpu.VMEM((rows, 2 * rows), bf16)]
    messages = [held(message) for message in messages]
    late, joined, far_window = held(late), held(joined), held(far_window)
    filled = pl.pallas_call(
        functools.partial(down_kernel, sections, shots, group, sizes),
        out_shape=buffers,
        in_specs=[vmem] * 7,
        out_specs=[vmem] * 4,
        scratch_shapes=stages + [pltpu.SMEM((sections,), jnp.int32)],
        compiler_params=params(24),
        name="down",
    )(held(source.reshape(shots, 2 * rows, columns)), *messages, late, joined, far_window)
    correlations = pl.pallas_call(
        functools.partial(up_kernel, sections, shots, group, sizes),
        out_shape=[
            jax.ShapeDtypeStruct((slots * rows + TAIL * more, columns), bf16)
            for more in (0, 1, 0, 2)
        ]
        + buffers,
        in_specs=[vmem] * 12,
        out_specs=[vmem] * (sections + 4),
        scratch_shapes=stages
        + [pltpu.VMEM((2 * rows, columns), bf16), pltpu.SMEM((sections,), jnp.int32)],
        input_output_aliases={8 + i: sections + i for i in range(4)},
        compiler_params=params(24),
        name="up",
    )(
        *messages, late, *[held(part) for part in lates], joined, far_window,
        *[held(buffer) for buffer in filled],
    )

    corr_shape = jax.ShapeDtypeStruct((slots * rows, columns), bf16)
    arrived = [correlations[0]] + [
        lax.ppermute(correlations[r], BOTH, plan.from_workers(r)) for r in range(1, sections)
    ]
    left, own = pl.pallas_call(
        functools.partial(place_kernel, shots),
        out_shape=[corr_shape, jax.ShapeDtypeStruct((slots * rows, columns), jnp.float32)],
        in_specs=[smem] + [vmem] * sections,
        out_specs=[vmem, vmem],
        compiler_params=params(8),
        name="place",
    )(anchors, *arrived)
    from_right = lax.ppermute(left, "tile", [(i + 1, i) for i in range(plan.tiles - 1)])
    image = own + from_right.astype(jnp.float32)
    return image.reshape(1, slots, rows, columns)


def solution(mesh):
    return jax.shard_map(
        on_device,
        mesh=mesh,
        in_specs=(
            P("tile", None, None, None),
            P("tile"),
            P("depth"),
            P("depth", None, None, "tile"),
            P("depth", None, None, None, None),
            P("depth", None, None, None, None),
        ),
        out_specs=P("depth", None, None, "tile"),
        check_vma=False,
    )
```

```python
import functools

import jax
import jax.numpy as jnp
from jax import lax
from jax.experimental import pallas as pl
from jax.experimental.pallas import tpu as pltpu
from jax.sharding import PartitionSpec as P

BOTH = ("depth", "tile")
MIB = 1024 * 1024
TAIL = 16


class Plan:
    def __init__(self, shots):
        self.sections = lax.axis_size("depth")
        self.tiles = lax.axis_size("tile")
        self.shots = shots
        self.group = self.sections // shots
        assert self.sections == 4 and self.group * shots == self.sections
        assert self.tiles % (2 * self.group) == 0

    def device(self, depth, tile):
        return depth * self.tiles + tile

    def bases(self):
        return range(0, self.tiles, self.group)

    def worker(self, base, w):
        return self.device(w, base + w // self.shots)

    def other(self, w, base):
        return self.device(w, base + (w // self.shots + 1) % self.group)

    def ops_to_workers(self, r):
        return [
            (self.other(w ^ r, base), self.worker(base, w))
            for base in self.bases()
            for w in range(self.sections)
        ]

    def swap_workers(self):
        return [
            (self.worker(base, w), self.worker((base // self.group ^ 1) * self.group, w))
            for base in self.bases()
            for w in range(self.sections)
        ]

    def to_workers(self, r):
        return [
            (self.device(w ^ r, base + w // self.shots), self.worker(base, w))
            for base in self.bases()
            for w in range(self.sections)
        ]

    def from_workers(self, r):
        return [(b, a) for a, b in self.to_workers(r)]


def pack_kernel(shots, group, sizes, counts, x_hbm, y_hbm, reflect_hbm, anchors_hbm, *refs):
    slots, rows, columns = sizes
    even, odd, late, half_out, reflect, shifts, tail, *refs = refs
    x_ref, y_ref, anchors, sem = refs
    pairs = [
        (anchors_hbm, anchors),
        (y_hbm, y_ref),
        (x_hbm, x_ref),
        (reflect_hbm, reflect),
    ]
    loads = [pltpu.make_async_copy(a, b, sem.at[n]) for n, (a, b) in enumerate(pairs)]
    for load in loads:
        load.start()
    for load in loads[1:3]:
        load.wait()
    piece = rows // 2
    part = columns + piece
    first = (slots - 1) * part
    for half in range(2):
        for slot in range(slots):
            op_x = jnp.concatenate(
                [x_ref[slot, i, half * piece : (half + 1) * piece, :] for i in range(2)], axis=1
            )
            op_y = y_ref[slot, half]
            if slot < slots - 1:
                places = [(out, half * first + slot * part) for out in (even, odd)]
            else:
                places = [(late, half * part)]
            for out, spot in places:
                out[spot : spot + columns, :] = op_y
                out[spot + columns : spot + part, :] = op_x
    plane = lax.rem(lax.axis_index("tile") // group, 2)
    half_out[:first, :] = even[pl.ds(pl.multiple_of(plane * first, first), first), :]
    half_out[first:, :] = late[pl.ds(pl.multiple_of(plane * part, part), part), :]
    for load in loads[:1] + loads[3:]:
        load.wait()
    section, tile = lax.axis_index("depth"), lax.axis_index("tile")
    place = lax.broadcasted_iota(jnp.int32, shifts.shape[1:], 1)
    start = lax.broadcasted_iota(jnp.int32, shifts.shape[1:], 0)
    for q in range(shots):
        offset = anchors[lax.rem(section, shots) ^ q] - (tile - 1) * columns
        shifts[q] = (place - start == offset).astype(jnp.float32).astype(shifts.dtype)
    tail[...] = jnp.full(tail.shape, counts[0].astype(jnp.float32), jnp.float32).astype(tail.dtype)


def window_kernel(shots, sizes, left_ref, right_ref, shifts, tail, *refs):
    slots, rows, columns = sizes
    messages, alone = refs[shots : 2 * shots], refs[2 * shots]
    both = jnp.concatenate([left_ref[...], right_ref[...]], axis=1)
    for q, message in enumerate(messages):
        window = lax.dot_general(
            both, shifts[q], (((1,), (1,)), ((), ())), preferred_element_type=jnp.float32
        ).astype(message.dtype)
        for out in [message] + ([alone] if q == shots - 1 else []):
            spot = out.shape[0] - TAIL - slots * rows
            out[spot : spot + slots * rows, :] = window
            out[spot + slots * rows :, :] = tail[...]


class Sweep:
    def __init__(self, shots, group, sizes, turned_y, turned_x, level_w, waves, stage_y, stage_x):
        self.sizes = sizes
        self.turned_y, self.turned_x, self.level_w = turned_y, turned_x, level_w
        self.waves, self.stage_y, self.stage_x = waves, stage_y, stage_x
        slots, rows, columns = sizes
        self.piece = rows // 2
        self.part = columns + self.piece
        self.first = (slots - 1) * self.part
        self.half_rows = self.first + self.part
        self.win_rows = slots * rows + TAIL
        self.here, tile = lax.axis_index("depth"), lax.axis_index("tile")
        self.shot = lax.rem(self.here, shots)
        self.is_worker = (self.here // shots == lax.rem(tile, group)).astype(jnp.int32)

    def read_counts(self, sources, counts):
        for r, (_, _, window) in enumerate(sources):
            value = jnp.max(window[window.shape[0] - TAIL :, :].astype(jnp.float32))
            counts[r] = value.astype(jnp.int32)

    def early_slots(self, r, count, rounds):
        partial = (r != 0) & (r != rounds - 1)
        return jnp.where(partial, jnp.minimum(count, self.sizes[0] - 1), count)

    def window_start(self, window_ref):
        return window_ref.shape[0] - self.win_rows

    def fetch(self, r, slot, place, sources):
        slots, rows, columns = self.sizes
        for r_of, (early, late, window) in enumerate(sources):
            early_slots = slots if early.shape[0] == 2 * self.half_rows else slots - 1
            choices = [(early, early_slots * self.part, slot < early_slots, slot)]
            if late is not None:
                choices.append((late, self.part, slot == slots - 1, 0))
            for ref, stride, chosen, at in choices:

                @pl.when((r == r_of) & chosen)
                def _():
                    for half in range(2):
                        start = pl.multiple_of(half * stride + at * self.part, self.piece)
                        self.stage_y[half * columns : (half + 1) * columns, :] = ref[
                            pl.ds(start, columns), :
                        ]
                        tail = pl.multiple_of(start + columns, self.piece)
                        self.stage_x[half * self.piece : (half + 1) * self.piece, :] = ref[
                            pl.ds(tail, self.piece), :
                        ]
                    spot = self.window_start(window) + slot * rows
                    self.level_w[place] = window[pl.ds(pl.multiple_of(spot, TAIL), rows), :]

    def blocks(self, re, im):
        upper = jnp.concatenate([re, -im], axis=1)
        return jnp.concatenate([upper, jnp.concatenate([im, re], axis=1)], axis=0)

    def complex_sum(self, both):
        _, rows, columns = self.sizes
        with_re, with_im = both[:, :columns], both[:, columns:]
        return with_re[:rows] - with_im[rows:], with_im[:rows] + with_re[rows:]

    def dot(self, a, b, dims):
        return lax.dot_general(a, b, (dims, ((), ())), preferred_element_type=jnp.float32)

    def down(self, place):
        _, rows, columns = self.sizes
        x_re, x_im = self.stage_x[:, :rows], self.stage_x[:, rows:]
        wave = self.waves[place].astype(jnp.float32)
        gain = 1.0 + self.level_w[place].astype(jnp.float32)
        scaled = jnp.concatenate([gain * wave[:rows], gain * wave[rows:]], axis=0)
        self.turned_x[place] = self.blocks(x_re.T, x_im.T)
        middle = self.dot(self.blocks(x_re, x_im), scaled.astype(jnp.bfloat16), ((1,), (0,)))
        for i in range(2):
            lines = slice(i * columns, (i + 1) * columns)
            self.turned_y[place, lines, :] = self.stage_y[lines, :].T
        both = self.dot(middle.astype(jnp.bfloat16), self.stage_y[...], ((1,), (1,)))
        moved = jnp.concatenate(self.complex_sum(both), axis=0)
        self.waves[place + 1] = moved.astype(jnp.bfloat16)
        return place + 1

    def up(self, r, slot, place, wave_up, outs):
        _, rows, columns = self.sizes
        level = place - 1
        wave = self.waves[level].astype(jnp.float32)
        window = self.level_w[level].astype(jnp.float32)
        back = self.dot(self.turned_x[level], wave_up[...], ((1,), (0,)))
        both = self.dot(back.astype(jnp.bfloat16), self.turned_y[level], ((1,), (1,)))
        spread_re, spread_im = self.complex_sum(both)
        up_re = (window * wave[:rows] + spread_re).astype(jnp.bfloat16)
        up_im = (window * wave[rows:] + spread_im).astype(jnp.bfloat16)
        wave_up[:rows] = up_re
        wave_up[rows:] = up_im
        product = wave[:rows] * up_re.astype(jnp.float32)
        product += wave[rows:] * up_im.astype(jnp.float32)
        spot = pl.multiple_of(slot * rows, rows)
        for r_of, out in enumerate(outs):

            @pl.when(r == r_of)
            def _():
                out[pl.ds(spot, rows), :] = product.astype(out.dtype)

        return level


def down_kernel(sections, shots, group, sizes, source_ref, *refs):
    (own, near, far), (own_late, joined, far_window) = refs[:3], refs[3:6]
    *buffers, stage_y, stage_x, counts = refs[6:]
    it = Sweep(shots, group, sizes, *buffers, stage_y, stage_x)
    sources = [
        (own, own_late, own),
        (near, None, near),
        (far, None, far),
        (joined, None, far_window),
    ]

    @pl.when(it.is_worker != 0)
    def _():
        it.waves[0] = source_ref[it.shot]
        it.read_counts(sources, counts)

        def section_down(section, carry):
            place, going = carry
            r = section ^ it.here
            ready = it.early_slots(r, counts[r], sections)

            def level_down(slot, place):
                it.fetch(r, slot, place, sources)
                return it.down(place)

            place = lax.fori_loop(0, jnp.where(going, ready, 0), level_down, place)
            return place, going & (ready == counts[r])

        lax.fori_loop(0, sections, section_down, (jnp.int32(0), jnp.bool_(True)))


def up_kernel(sections, shots, group, sizes, *refs):
    (own, near, far), (own_late, near_late, far_late, joined, far_window) = refs[:3], refs[3:8]
    outs, refs = refs[12 : 12 + sections], refs[12 + sections :]
    *buffers, stage_y, stage_x, wave_up, counts = refs
    it = Sweep(shots, group, sizes, *buffers, stage_y, stage_x)
    sources = [
        (own, own_late, own),
        (near, near_late, near),
        (far, far_late, far),
        (joined, None, far_window),
    ]

    @pl.when(it.is_worker == 0)
    def _():
        outs[0][...] = jnp.zeros(outs[0].shape, outs[0].dtype)

    @pl.when(it.is_worker != 0)
    def _():
        it.read_counts(sources, counts)
        for out in outs:
            out[...] = jnp.zeros(out.shape, out.dtype)
        wave_up[...] = jnp.zeros(wave_up.shape, wave_up.dtype)

        def section_down(section, carry):
            place, going = carry
            r = section ^ it.here
            done = jnp.where(going, it.early_slots(r, counts[r], sections), 0)

            def level_down(slot, place):
                it.fetch(r, slot, place, sources)
                return it.down(place)

            place = lax.fori_loop(done, counts[r], level_down, place + done)
            return place, going & (done == counts[r])

        last, _ = lax.fori_loop(0, sections, section_down, (jnp.int32(0), jnp.bool_(True)))

        def section_up(step, place):
            r = (sections - 1 - step) ^ it.here
            count = counts[r]
            return lax.fori_loop(
                0,
                count,
                lambda inner, place: it.up(r, count - 1 - inner, place, wave_up, outs),
                place,
            )

        lax.fori_loop(0, sections, section_up, last)


def join_kernel(group, first_ref, second_ref, out_ref):
    plane = lax.rem(lax.axis_index("tile") // group, 2)
    half_rows = first_ref.shape[0]
    for i, ref in enumerate((first_ref, second_ref)):
        start = pl.multiple_of((plane if i == 0 else 1 - plane) * half_rows, half_rows)
        out_ref[pl.ds(start, half_rows), :] = ref[...]


def hold_kernel(array_ref, after_ref, out_ref):
    pass


def place_kernel(shots, shifts, *refs):
    arrived, (left_out, own_out) = refs[:-2], refs[-2:]
    places, columns = left_out.shape
    placed = None
    for q in range(shots):
        total = None
        for r in range(q, len(arrived), shots):
            value = arrived[r][:places, :]
            total = value if total is None else total + value
        part = jnp.dot(total, shifts[q], preferred_element_type=jnp.float32)
        placed = part if placed is None else placed + part
    left_out[...] = placed[:, :columns].astype(left_out.dtype)
    own_out[...] = placed[:, columns:]


def kept(array):
    return pltpu.with_memory_space_constraint(array, pltpu.HBM)


def held(array):
    return pltpu.with_memory_space_constraint(array, pltpu.VMEM)


def on_device(source, anchors, counts, reflect, lateral_x, lateral_y):
    shots, _, rows, columns = source.shape
    slots = reflect.shape[1]
    sizes = (slots, rows, columns)
    plan = Plan(shots)
    sections, group = plan.sections, plan.group
    assert shots == 2
    bf16 = jnp.bfloat16
    vmem = pl.BlockSpec(memory_space=pltpu.VMEM)
    smem = pl.BlockSpec(memory_space=pltpu.SMEM)
    hbm = pl.BlockSpec(memory_space=pltpu.HBM)
    anywhere = pl.BlockSpec(memory_space=pl.ANY)

    def params(mib):
        return pltpu.CompilerParams(vmem_limit_bytes=mib * MIB)

    tile_reflect = reflect[0].reshape(slots * rows, columns)
    halo = lax.ppermute(tile_reflect, "tile", [(i, i + 1) for i in range(plan.tiles - 1)])
    part = columns + rows // 2
    half_rows, win_rows = slots * part, slots * rows + TAIL
    early_rows = 2 * (half_rows - part) + win_rows
    even = pltpu.VMEM((early_rows + 5 * TAIL, columns), bf16)
    odd = pltpu.VMEM((early_rows, columns), bf16)
    even_early, odd_early, late, far_half, own_reflect, shifts, tail = pl.pallas_call(
        functools.partial(pack_kernel, shots, group, sizes),
        out_shape=[
            even,
            odd,
            jax.ShapeDtypeStruct((2 * part, columns), bf16),
            jax.ShapeDtypeStruct((half_rows, columns), bf16),
            pltpu.VMEM(tile_reflect.shape, bf16),
            pltpu.VMEM((shots, columns, 2 * columns), bf16),
            pltpu.VMEM((TAIL, columns), bf16),
        ],
        in_specs=[smem] + [hbm] * 4,
        out_specs=[vmem] * 7,
        scratch_shapes=[
            pltpu.VMEM(lateral_x.shape[1:], bf16),
            pltpu.VMEM(lateral_y.shape[1:], bf16),
            pltpu.SMEM(anchors.shape, jnp.int32),
            pltpu.SemaphoreType.DMA((4,)),
        ],
        compiler_params=params(12),
        name="pack",
    )(
        counts, kept(lateral_x[0]), kept(lateral_y[0]), kept(tile_reflect), kept(anchors)
    )
    shifts = held(shifts)
    last = sections - 1
    far_half = lax.ppermute(far_half, BOTH, plan.to_workers(last))
    even_early, odd_early, far_window = pl.pallas_call(
        functools.partial(window_kernel, shots, sizes),
        out_shape=[even, odd, jax.ShapeDtypeStruct((win_rows, columns), bf16)],
        in_specs=[vmem] * 6,
        out_specs=[vmem] * 3,
        input_output_aliases={4: 0, 5: 1},
        compiler_params=params(12),
        cost_estimate=pl.CostEstimate(flops=3 * 10**9, bytes_accessed=4 * MIB, transcendentals=0),
        name="windows",
    )(held(halo), held(own_reflect), shifts, held(tail), held(even_early), held(odd_early))
    messages = [
        even_early,
        lax.ppermute(odd_early, BOTH, plan.to_workers(1)),
        lax.ppermute(even_early, BOTH, plan.to_workers(2)),
    ]
    far_window = lax.ppermute(far_window, BOTH, plan.to_workers(last))
    other_half = lax.ppermute(far_half, BOTH, plan.swap_workers())
    late = pl.pallas_call(
        hold_kernel,
        out_shape=jax.ShapeDtypeStruct(late.shape, bf16),
        in_specs=[anywhere] * 2,
        out_specs=anywhere,
        input_output_aliases={0: 0},
        compiler_params=params(2),
        cost_estimate=pl.CostEstimate(flops=36 * 10**8, bytes_accessed=0, transcendentals=0),
        name="hold",
    )(late, far_window)
    lates = [lax.ppermute(late, BOTH, plan.ops_to_workers(r)) for r in (1, 2)]
    joined = pl.pallas_call(
        functools.partial(join_kernel, group),
        out_shape=pltpu.VMEM((2 * half_rows, columns), bf16),
        in_specs=[vmem] * 2,
        out_specs=vmem,
        compiler_params=params(8),
        name="join",
    )(held(far_half), held(other_half))

    levels = sections * slots
    buffers = [
        pltpu.VMEM((levels, 2 * columns, columns), bf16),
        pltpu.VMEM((levels, 2 * rows, 2 * rows), bf16),
        pltpu.VMEM((levels, rows, columns), bf16),
        pltpu.VMEM((levels + 1, 2 * rows, columns), bf16),
    ]
    stages = [pltpu.VMEM((2 * columns, columns), bf16), pltpu.VMEM((rows, 2 * rows), bf16)]
    messages = [held(message) for message in messages]
    late, joined, far_window = held(late), held(joined), held(far_window)
    filled = pl.pallas_call(
        functools.partial(down_kernel, sections, shots, group, sizes),
        out_shape=buffers,
        in_specs=[vmem] * 7,
        out_specs=[vmem] * 4,
        scratch_shapes=stages + [pltpu.SMEM((sections,), jnp.int32)],
        compiler_params=params(24),
        name="down",
    )(held(source.reshape(shots, 2 * rows, columns)), *messages, late, joined, far_window)
    correlations = pl.pallas_call(
        functools.partial(up_kernel, sections, shots, group, sizes),
        out_shape=[
            jax.ShapeDtypeStruct((slots * rows + TAIL * more, columns), bf16)
            for more in (0, 1, 0, 2)
        ]
        + buffers,
        in_specs=[vmem] * 12,
        out_specs=[vmem] * (sections + 4),
        scratch_shapes=stages
        + [pltpu.VMEM((2 * rows, columns), bf16), pltpu.SMEM((sections,), jnp.int32)],
        input_output_aliases={8 + i: sections + i for i in range(4)},
        compiler_params=params(24),
        name="up",
    )(
        *messages, late, *[held(part) for part in lates], joined, far_window,
        *[held(buffer) for buffer in filled],
    )

    corr_shape = jax.ShapeDtypeStruct((slots * rows, columns), bf16)
    arrived = [correlations[0]] + [
        lax.ppermute(correlations[r], BOTH, plan.from_workers(r)) for r in range(1, sections)
    ]
    left, own = pl.pallas_call(
        functools.partial(place_kernel, shots),
        out_shape=[corr_shape, jax.ShapeDtypeStruct((slots * rows, columns), jnp.float32)],
        in_specs=[vmem] * (1 + sections),
        out_specs=[vmem, vmem],
        compiler_params=params(8),
        name="place",
    )(shifts, *[held(part) for part in arrived])
    from_right = lax.ppermute(left, "tile", [(i + 1, i) for i in range(plan.tiles - 1)])
    image = own + from_right.astype(jnp.float32)
    return image.reshape(1, slots, rows, columns)


def solution(mesh):
    return jax.shard_map(
        on_device,
        mesh=mesh,
        in_specs=(
            P("tile", None, None, None),
            P("tile"),
            P("depth"),
            P("depth", None, None, "tile"),
            P("depth", None, None, None, None),
            P("depth", None, None, None, None),
        ),
        out_specs=P("depth", None, None, "tile"),
        check_vma=False,
    )
```

```python
import functools

import jax
import jax.numpy as jnp
from jax import lax
from jax.experimental import pallas as pl
from jax.experimental.pallas import tpu as pltpu
from jax.sharding import PartitionSpec as P

BOTH = ("depth", "tile")
MIB = 1024 * 1024
TAIL = 16


class Plan:
    def __init__(self, shots):
        self.sections = lax.axis_size("depth")
        self.tiles = lax.axis_size("tile")
        self.shots = shots
        self.group = self.sections // shots
        assert self.sections == 4 and self.group * shots == self.sections
        assert self.tiles % (2 * self.group) == 0

    def device(self, depth, tile):
        return depth * self.tiles + tile

    def bases(self):
        return range(0, self.tiles, self.group)

    def worker(self, base, w):
        return self.device(w, base + w // self.shots)

    def other(self, w, base):
        return self.device(w, base + (w // self.shots + 1) % self.group)

    def ops_to_workers(self, r):
        return [
            (self.other(w ^ r, base), self.worker(base, w))
            for base in self.bases()
            for w in range(self.sections)
        ]

    def swap_workers(self):
        return [
            (self.worker(base, w), self.worker((base // self.group ^ 1) * self.group, w))
            for base in self.bases()
            for w in range(self.sections)
        ]

    def to_workers(self, r):
        return [
            (self.device(w ^ r, base + w // self.shots), self.worker(base, w))
            for base in self.bases()
            for w in range(self.sections)
        ]

    def from_workers(self, r):
        return [(b, a) for a, b in self.to_workers(r)]


def pack_kernel(shots, group, sizes, x_hbm, y_hbm, reflect_hbm, anchors_hbm, *refs):
    slots, rows, columns = sizes
    even, odd, late, half_out, reflect, shifts, *refs = refs
    x_ref, y_ref, anchors, sem = refs
    pairs = [
        (anchors_hbm, anchors),
        (y_hbm, y_ref),
        (x_hbm, x_ref),
        (reflect_hbm, reflect),
    ]
    loads = [pltpu.make_async_copy(a, b, sem.at[n]) for n, (a, b) in enumerate(pairs)]
    for load in loads:
        load.start()
    for load in loads[1:3]:
        load.wait()
    piece = rows // 2
    part = columns + piece
    first = (slots - 1) * part
    for half in range(2):
        for slot in range(slots):
            op_x = jnp.concatenate(
                [x_ref[slot, i, half * piece : (half + 1) * piece, :] for i in range(2)], axis=1
            )
            op_y = y_ref[slot, half]
            if slot < slots - 1:
                places = [(out, half * first + slot * part) for out in (even, odd)]
            else:
                places = [(late, half * part)]
            for out, spot in places:
                out[spot : spot + columns, :] = op_y
                out[spot + columns : spot + part, :] = op_x
    plane = lax.rem(lax.axis_index("tile") // group, 2)
    half_out[:first, :] = even[pl.ds(pl.multiple_of(plane * first, first), first), :]
    half_out[first:, :] = late[pl.ds(pl.multiple_of(plane * part, part), part), :]
    for load in loads[:1] + loads[3:]:
        load.wait()
    section, tile = lax.axis_index("depth"), lax.axis_index("tile")
    place = lax.broadcasted_iota(jnp.int32, shifts.shape[1:], 1)
    start = lax.broadcasted_iota(jnp.int32, shifts.shape[1:], 0)
    for q in range(shots):
        offset = anchors[lax.rem(section, shots) ^ q] - (tile - 1) * columns
        shifts[q] = (place - start == offset).astype(jnp.float32).astype(shifts.dtype)


def window_kernel(shots, sizes, counts, left_ref, right_ref, shifts, *refs):
    slots, rows, columns = sizes
    messages, alone = refs[shots : 2 * shots], refs[2 * shots]
    both = jnp.concatenate([left_ref[...], right_ref[...]], axis=1)
    tail = jnp.full((TAIL, columns), counts[0].astype(jnp.float32), jnp.float32)
    for q, message in enumerate(messages):
        window = lax.dot_general(
            both, shifts[q], (((1,), (1,)), ((), ())), preferred_element_type=jnp.float32
        ).astype(message.dtype)
        for out in [message] + ([alone] if q == shots - 1 else []):
            spot = out.shape[0] - TAIL - slots * rows
            out[spot : spot + slots * rows, :] = window
            out[spot + slots * rows :, :] = tail.astype(out.dtype)


class Sweep:
    def __init__(self, shots, group, sizes, turned_y, turned_x, level_w, waves, stage_y, stage_x):
        self.sizes = sizes
        self.turned_y, self.turned_x, self.level_w = turned_y, turned_x, level_w
        self.waves, self.stage_y, self.stage_x = waves, stage_y, stage_x
        slots, rows, columns = sizes
        self.piece = rows // 2
        self.part = columns + self.piece
        self.first = (slots - 1) * self.part
        self.half_rows = self.first + self.part
        self.win_rows = slots * rows + TAIL
        self.here, tile = lax.axis_index("depth"), lax.axis_index("tile")
        self.shot = lax.rem(self.here, shots)
        self.is_worker = (self.here // shots == lax.rem(tile, group)).astype(jnp.int32)

    def read_counts(self, sources, counts):
        for r, (_, _, window) in enumerate(sources):
            value = jnp.max(window[window.shape[0] - TAIL :, :].astype(jnp.float32))
            counts[r] = value.astype(jnp.int32)

    def early_slots(self, r, count, rounds):
        partial = (r != 0) & (r != rounds - 1)
        return jnp.where(partial, jnp.minimum(count, self.sizes[0] - 1), count)

    def window_start(self, window_ref):
        return window_ref.shape[0] - self.win_rows

    def fetch(self, r, slot, place, sources):
        slots, rows, columns = self.sizes
        for r_of, (early, late, window) in enumerate(sources):
            early_slots = slots if early.shape[0] == 2 * self.half_rows else slots - 1
            choices = [(early, early_slots * self.part, slot < early_slots, slot)]
            if late is not None:
                choices.append((late, self.part, slot == slots - 1, 0))
            for ref, stride, chosen, at in choices:

                @pl.when((r == r_of) & chosen)
                def _():
                    for half in range(2):
                        start = pl.multiple_of(half * stride + at * self.part, self.piece)
                        self.stage_y[half * columns : (half + 1) * columns, :] = ref[
                            pl.ds(start, columns), :
                        ]
                        tail = pl.multiple_of(start + columns, self.piece)
                        self.stage_x[half * self.piece : (half + 1) * self.piece, :] = ref[
                            pl.ds(tail, self.piece), :
                        ]
                    spot = self.window_start(window) + slot * rows
                    self.level_w[place] = window[pl.ds(pl.multiple_of(spot, TAIL), rows), :]

    def blocks(self, re, im):
        upper = jnp.concatenate([re, -im], axis=1)
        return jnp.concatenate([upper, jnp.concatenate([im, re], axis=1)], axis=0)

    def complex_sum(self, both):
        _, rows, columns = self.sizes
        with_re, with_im = both[:, :columns], both[:, columns:]
        return with_re[:rows] - with_im[rows:], with_im[:rows] + with_re[rows:]

    def dot(self, a, b, dims):
        return lax.dot_general(a, b, (dims, ((), ())), preferred_element_type=jnp.float32)

    def down(self, place):
        _, rows, columns = self.sizes
        x_re, x_im = self.stage_x[:, :rows], self.stage_x[:, rows:]
        wave = self.waves[place].astype(jnp.float32)
        gain = 1.0 + self.level_w[place].astype(jnp.float32)
        scaled = jnp.concatenate([gain * wave[:rows], gain * wave[rows:]], axis=0)
        self.turned_x[place] = self.blocks(x_re.T, x_im.T)
        middle = self.dot(self.blocks(x_re, x_im), scaled.astype(jnp.bfloat16), ((1,), (0,)))
        for i in range(2):
            lines = slice(i * columns, (i + 1) * columns)
            self.turned_y[place, lines, :] = self.stage_y[lines, :].T
        both = self.dot(middle.astype(jnp.bfloat16), self.stage_y[...], ((1,), (1,)))
        moved = jnp.concatenate(self.complex_sum(both), axis=0)
        self.waves[place + 1] = moved.astype(jnp.bfloat16)
        return place + 1

    def up(self, r, slot, place, wave_up, outs):
        _, rows, columns = self.sizes
        level = place - 1
        wave = self.waves[level].astype(jnp.float32)
        window = self.level_w[level].astype(jnp.float32)
        back = self.dot(self.turned_x[level], wave_up[...], ((1,), (0,)))
        both = self.dot(back.astype(jnp.bfloat16), self.turned_y[level], ((1,), (1,)))
        spread_re, spread_im = self.complex_sum(both)
        up_re = (window * wave[:rows] + spread_re).astype(jnp.bfloat16)
        up_im = (window * wave[rows:] + spread_im).astype(jnp.bfloat16)
        wave_up[:rows] = up_re
        wave_up[rows:] = up_im
        product = wave[:rows] * up_re.astype(jnp.float32)
        product += wave[rows:] * up_im.astype(jnp.float32)
        spot = pl.multiple_of(slot * rows, rows)
        for r_of, out in enumerate(outs):

            @pl.when(r == r_of)
            def _():
                out[pl.ds(spot, rows), :] = product.astype(out.dtype)

        return level


def down_kernel(sections, shots, group, sizes, source_ref, *refs):
    (own, near, far), (own_late, joined, far_window) = refs[:3], refs[3:6]
    *buffers, stage_y, stage_x, counts = refs[6:]
    it = Sweep(shots, group, sizes, *buffers, stage_y, stage_x)
    sources = [
        (own, own_late, own),
        (near, None, near),
        (far, None, far),
        (joined, None, far_window),
    ]

    @pl.when(it.is_worker != 0)
    def _():
        it.waves[0] = source_ref[it.shot]
        it.read_counts(sources, counts)

        def section_down(section, carry):
            place, going = carry
            r = section ^ it.here
            ready = it.early_slots(r, counts[r], sections)

            def level_down(slot, place):
                it.fetch(r, slot, place, sources)
                return it.down(place)

            place = lax.fori_loop(0, jnp.where(going, ready, 0), level_down, place)
            return place, going & (ready == counts[r])

        lax.fori_loop(0, sections, section_down, (jnp.int32(0), jnp.bool_(True)))


def up_kernel(sections, shots, group, sizes, *refs):
    (own, near, far), (own_late, near_late, far_late, joined, far_window) = refs[:3], refs[3:8]
    outs, refs = refs[12 : 12 + sections], refs[12 + sections :]
    *buffers, stage_y, stage_x, wave_up, counts = refs
    it = Sweep(shots, group, sizes, *buffers, stage_y, stage_x)
    sources = [
        (own, own_late, own),
        (near, near_late, near),
        (far, far_late, far),
        (joined, None, far_window),
    ]

    @pl.when(it.is_worker == 0)
    def _():
        outs[0][...] = jnp.zeros(outs[0].shape, outs[0].dtype)

    @pl.when(it.is_worker != 0)
    def _():
        it.read_counts(sources, counts)
        for out in outs:
            out[...] = jnp.zeros(out.shape, out.dtype)
        wave_up[...] = jnp.zeros(wave_up.shape, wave_up.dtype)

        def section_down(section, carry):
            place, going = carry
            r = section ^ it.here
            done = jnp.where(going, it.early_slots(r, counts[r], sections), 0)

            def level_down(slot, place):
                it.fetch(r, slot, place, sources)
                return it.down(place)

            place = lax.fori_loop(done, counts[r], level_down, place + done)
            return place, going & (done == counts[r])

        last, _ = lax.fori_loop(0, sections, section_down, (jnp.int32(0), jnp.bool_(True)))

        def section_up(step, place):
            r = (sections - 1 - step) ^ it.here
            count = counts[r]
            return lax.fori_loop(
                0,
                count,
                lambda inner, place: it.up(r, count - 1 - inner, place, wave_up, outs),
                place,
            )

        lax.fori_loop(0, sections, section_up, last)


def join_kernel(group, first_ref, second_ref, out_ref):
    plane = lax.rem(lax.axis_index("tile") // group, 2)
    half_rows = first_ref.shape[0]
    for i, ref in enumerate((first_ref, second_ref)):
        start = pl.multiple_of((plane if i == 0 else 1 - plane) * half_rows, half_rows)
        out_ref[pl.ds(start, half_rows), :] = ref[...]


def hold_kernel(array_ref, after_ref, out_ref):
    pass


def place_kernel(shots, shifts, *refs):
    arrived, (left_out, own_out) = refs[:-2], refs[-2:]
    places, columns = left_out.shape
    placed = None
    for q in range(shots):
        total = None
        for r in range(q, len(arrived), shots):
            value = arrived[r][:places, :]
            total = value if total is None else total + value
        part = jnp.dot(total, shifts[q], preferred_element_type=jnp.float32)
        placed = part if placed is None else placed + part
    left_out[...] = placed[:, :columns].astype(left_out.dtype)
    own_out[...] = placed[:, columns:]


def kept(array):
    return pltpu.with_memory_space_constraint(array, pltpu.HBM)


def held(array):
    return pltpu.with_memory_space_constraint(array, pltpu.VMEM)


def on_device(source, anchors, counts, reflect, lateral_x, lateral_y):
    shots, _, rows, columns = source.shape
    slots = reflect.shape[1]
    sizes = (slots, rows, columns)
    plan = Plan(shots)
    sections, group = plan.sections, plan.group
    assert shots == 2
    bf16 = jnp.bfloat16
    vmem = pl.BlockSpec(memory_space=pltpu.VMEM)
    smem = pl.BlockSpec(memory_space=pltpu.SMEM)
    hbm = pl.BlockSpec(memory_space=pltpu.HBM)
    anywhere = pl.BlockSpec(memory_space=pl.ANY)

    def params(mib):
        return pltpu.CompilerParams(vmem_limit_bytes=mib * MIB)

    tile_reflect = reflect[0].reshape(slots * rows, columns)
    halo = lax.ppermute(tile_reflect, "tile", [(i, i + 1) for i in range(plan.tiles - 1)])
    part = columns + rows // 2
    half_rows, win_rows = slots * part, slots * rows + TAIL
    early_rows = 2 * (half_rows - part) + win_rows
    even = pltpu.VMEM((early_rows + 5 * TAIL, columns), bf16)
    odd = pltpu.VMEM((early_rows, columns), bf16)
    even_early, odd_early, late, far_half, own_reflect, shifts = pl.pallas_call(
        functools.partial(pack_kernel, shots, group, sizes),
        out_shape=[
            even,
            odd,
            jax.ShapeDtypeStruct((2 * part, columns), bf16),
            jax.ShapeDtypeStruct((half_rows, columns), bf16),
            pltpu.VMEM(tile_reflect.shape, bf16),
            pltpu.VMEM((shots, columns, 2 * columns), bf16),
        ],
        in_specs=[hbm] * 4,
        out_specs=[vmem] * 6,
        scratch_shapes=[
            pltpu.VMEM(lateral_x.shape[1:], bf16),
            pltpu.VMEM(lateral_y.shape[1:], bf16),
            pltpu.SMEM(anchors.shape, jnp.int32),
            pltpu.SemaphoreType.DMA((4,)),
        ],
        compiler_params=params(12),
        name="pack",
    )(
        kept(lateral_x[0]), kept(lateral_y[0]), kept(tile_reflect), kept(anchors)
    )
    shifts = held(shifts)
    last = sections - 1
    far_half = lax.ppermute(far_half, BOTH, plan.to_workers(last))
    even_early, odd_early, far_window = pl.pallas_call(
        functools.partial(window_kernel, shots, sizes),
        out_shape=[even, odd, jax.ShapeDtypeStruct((win_rows, columns), bf16)],
        in_specs=[smem] + [vmem] * 5,
        out_specs=[vmem] * 3,
        input_output_aliases={4: 0, 5: 1},
        compiler_params=params(12),
        cost_estimate=pl.CostEstimate(flops=3 * 10**9, bytes_accessed=4 * MIB, transcendentals=0),
        name="windows",
    )(counts, held(halo), held(own_reflect), shifts, held(even_early), held(odd_early))
    messages = [
        even_early,
        lax.ppermute(odd_early, BOTH, plan.to_workers(1)),
        lax.ppermute(even_early, BOTH, plan.to_workers(2)),
    ]
    far_window = lax.ppermute(far_window, BOTH, plan.to_workers(last))
    other_half = lax.ppermute(far_half, BOTH, plan.swap_workers())
    late = pl.pallas_call(
        hold_kernel,
        out_shape=jax.ShapeDtypeStruct(late.shape, bf16),
        in_specs=[anywhere] * 2,
        out_specs=anywhere,
        input_output_aliases={0: 0},
        compiler_params=params(2),
        cost_estimate=pl.CostEstimate(flops=36 * 10**8, bytes_accessed=0, transcendentals=0),
        name="hold",
    )(late, far_window)
    lates = [lax.ppermute(late, BOTH, plan.ops_to_workers(r)) for r in (1, 2)]
    joined = pl.pallas_call(
        functools.partial(join_kernel, group),
        out_shape=pltpu.VMEM((2 * half_rows, columns), bf16),
        in_specs=[vmem] * 2,
        out_specs=vmem,
        compiler_params=params(8),
        name="join",
    )(held(far_half), held(other_half))

    levels = sections * slots
    buffers = [
        pltpu.VMEM((levels, 2 * columns, columns), bf16),
        pltpu.VMEM((levels, 2 * rows, 2 * rows), bf16),
        pltpu.VMEM((levels, rows, columns), bf16),
        pltpu.VMEM((levels + 1, 2 * rows, columns), bf16),
    ]
    stages = [pltpu.VMEM((2 * columns, columns), bf16), pltpu.VMEM((rows, 2 * rows), bf16)]
    messages = [held(message) for message in messages]
    late, joined, far_window = held(late), held(joined), held(far_window)
    filled = pl.pallas_call(
        functools.partial(down_kernel, sections, shots, group, sizes),
        out_shape=buffers,
        in_specs=[vmem] * 7,
        out_specs=[vmem] * 4,
        scratch_shapes=stages + [pltpu.SMEM((sections,), jnp.int32)],
        compiler_params=params(24),
        name="down",
    )(held(source.reshape(shots, 2 * rows, columns)), *messages, late, joined, far_window)
    correlations = pl.pallas_call(
        functools.partial(up_kernel, sections, shots, group, sizes),
        out_shape=[
            jax.ShapeDtypeStruct((slots * rows + TAIL * more, columns), bf16)
            for more in (0, 1, 0, 2)
        ]
        + buffers,
        in_specs=[vmem] * 12,
        out_specs=[vmem] * (sections + 4),
        scratch_shapes=stages
        + [pltpu.VMEM((2 * rows, columns), bf16), pltpu.SMEM((sections,), jnp.int32)],
        input_output_aliases={8 + i: sections + i for i in range(4)},
        compiler_params=params(24),
        name="up",
    )(
        *messages, late, *[held(part) for part in lates], joined, far_window,
        *[held(buffer) for buffer in filled],
    )

    corr_shape = jax.ShapeDtypeStruct((slots * rows, columns), bf16)
    arrived = [correlations[0]] + [
        lax.ppermute(correlations[r], BOTH, plan.from_workers(r)) for r in range(1, sections)
    ]
    left, own = pl.pallas_call(
        functools.partial(place_kernel, shots),
        out_shape=[corr_shape, jax.ShapeDtypeStruct((slots * rows, columns), jnp.float32)],
        in_specs=[vmem] * (1 + sections),
        out_specs=[vmem, vmem],
        compiler_params=params(8),
        name="place",
    )(shifts, *[held(part) for part in arrived])
    from_right = lax.ppermute(left, "tile", [(i + 1, i) for i in range(plan.tiles - 1)])
    image = own + from_right.astype(jnp.float32)
    return image.reshape(1, slots, rows, columns)


def solution(mesh):
    return jax.shard_map(
        on_device,
        mesh=mesh,
        in_specs=(
            P("tile", None, None, None),
            P("tile"),
            P("depth"),
            P("depth", None, None, "tile"),
            P("depth", None, None, None, None),
            P("depth", None, None, None, None),
        ),
        out_specs=P("depth", None, None, "tile"),
        check_vma=False,
    )
```

```python
import functools

import jax
import jax.numpy as jnp
from jax import lax
from jax.experimental import pallas as pl
from jax.experimental.pallas import tpu as pltpu
from jax.sharding import PartitionSpec as P

BOTH = ("depth", "tile")
MIB = 1024 * 1024
TAIL = 16


class Plan:
    def __init__(self, shots):
        self.sections = lax.axis_size("depth")
        self.tiles = lax.axis_size("tile")
        self.shots = shots
        self.group = self.sections // shots
        assert self.sections == 4 and self.group * shots == self.sections
        assert self.tiles % (2 * self.group) == 0

    def device(self, depth, tile):
        return depth * self.tiles + tile

    def bases(self):
        return range(0, self.tiles, self.group)

    def worker(self, base, w):
        return self.device(w, base + w // self.shots)

    def other(self, w, base):
        return self.device(w, base + (w // self.shots + 1) % self.group)

    def ops_to_workers(self, r):
        return [
            (self.other(w ^ r, base), self.worker(base, w))
            for base in self.bases()
            for w in range(self.sections)
        ]

    def swap_workers(self):
        return [
            (self.worker(base, w), self.worker((base // self.group ^ 1) * self.group, w))
            for base in self.bases()
            for w in range(self.sections)
        ]

    def to_workers(self, r):
        return [
            (self.device(w ^ r, base + w // self.shots), self.worker(base, w))
            for base in self.bases()
            for w in range(self.sections)
        ]

    def from_workers(self, r):
        return [(b, a) for a, b in self.to_workers(r)]


def pack_kernel(group, sizes, x_hbm, y_hbm, even, odd, late, half_out, x_ref, y_ref, sem):
    slots, rows, columns = sizes
    loads = [
        pltpu.make_async_copy(x_hbm, x_ref, sem.at[0]),
        pltpu.make_async_copy(y_hbm, y_ref, sem.at[1]),
    ]
    for load in loads:
        load.start()
    for load in loads:
        load.wait()
    piece = rows // 2
    part = columns + piece
    first = (slots - 1) * part
    for half in range(2):
        for slot in range(slots):
            op_x = jnp.concatenate(
                [x_ref[slot, i, half * piece : (half + 1) * piece, :] for i in range(2)], axis=1
            )
            op_y = y_ref[slot, half]
            if slot < slots - 1:
                places = [(out, half * first + slot * part) for out in (even, odd)]
            else:
                places = [(late, half * part)]
            for out, spot in places:
                out[spot : spot + columns, :] = op_y
                out[spot + columns : spot + part, :] = op_x
    plane = lax.rem(lax.axis_index("tile") // group, 2)
    half_out[:first, :] = even[pl.ds(pl.multiple_of(plane * first, first), first), :]
    half_out[first:, :] = late[pl.ds(pl.multiple_of(plane * part, part), part), :]


def window_kernel(shots, sizes, anchors_hbm, counts, left_ref, right_hbm, *refs):
    slots, rows, columns = sizes
    messages, (alone, anchors, right_ref, sem) = refs[shots : 2 * shots], refs[2 * shots :]
    loads = [
        pltpu.make_async_copy(anchors_hbm, anchors, sem.at[0]),
        pltpu.make_async_copy(right_hbm, right_ref, sem.at[1]),
    ]
    for load in loads:
        load.start()
    for load in loads:
        load.wait()
    section, tile = lax.axis_index("depth"), lax.axis_index("tile")
    left, right = left_ref[...].astype(jnp.float32), right_ref[...].astype(jnp.float32)
    lanes = lax.broadcasted_iota(jnp.int32, left.shape, 1)
    tail = jnp.full((TAIL, columns), counts[0].astype(jnp.float32), jnp.float32)
    for q, message in enumerate(messages):
        offset = anchors[lax.rem(section, shots) ^ q] - (tile - 1) * columns
        merged = jnp.where(lanes >= offset, left, right)
        back = lax.rem(columns - lax.rem(offset, columns), columns)
        window = pltpu.roll(merged, back, 1).astype(message.dtype)
        for out in [message] + ([alone] if q == shots - 1 else []):
            spot = out.shape[0] - TAIL - slots * rows
            out[spot : spot + slots * rows, :] = window
            out[spot + slots * rows :, :] = tail.astype(out.dtype)


class Sweep:
    def __init__(self, shots, group, sizes, turned_y, turned_x, level_w, waves, stage_y, stage_x):
        self.sizes = sizes
        self.turned_y, self.turned_x, self.level_w = turned_y, turned_x, level_w
        self.waves, self.stage_y, self.stage_x = waves, stage_y, stage_x
        slots, rows, columns = sizes
        self.piece = rows // 2
        self.part = columns + self.piece
        self.first = (slots - 1) * self.part
        self.half_rows = self.first + self.part
        self.win_rows = slots * rows + TAIL
        self.here, tile = lax.axis_index("depth"), lax.axis_index("tile")
        self.shot = lax.rem(self.here, shots)
        self.is_worker = (self.here // shots == lax.rem(tile, group)).astype(jnp.int32)

    def read_counts(self, sources, counts):
        for r, (_, _, window) in enumerate(sources):
            value = jnp.max(window[window.shape[0] - TAIL :, :].astype(jnp.float32))
            counts[r] = value.astype(jnp.int32)

    def early_slots(self, r, count, rounds):
        partial = (r != 0) & (r != rounds - 1)
        return jnp.where(partial, jnp.minimum(count, self.sizes[0] - 1), count)

    def window_start(self, window_ref):
        return window_ref.shape[0] - self.win_rows

    def fetch(self, r, slot, place, sources):
        slots, rows, columns = self.sizes
        for r_of, (early, late, window) in enumerate(sources):
            early_slots = slots if early.shape[0] == 2 * self.half_rows else slots - 1
            choices = [(early, early_slots * self.part, slot < early_slots, slot)]
            if late is not None:
                choices.append((late, self.part, slot == slots - 1, 0))
            for ref, stride, chosen, at in choices:

                @pl.when((r == r_of) & chosen)
                def _():
                    for half in range(2):
                        start = pl.multiple_of(half * stride + at * self.part, self.piece)
                        self.stage_y[half * columns : (half + 1) * columns, :] = ref[
                            pl.ds(start, columns), :
                        ]
                        tail = pl.multiple_of(start + columns, self.piece)
                        self.stage_x[half * self.piece : (half + 1) * self.piece, :] = ref[
                            pl.ds(tail, self.piece), :
                        ]
                    spot = self.window_start(window) + slot * rows
                    self.level_w[place] = window[pl.ds(pl.multiple_of(spot, TAIL), rows), :]

    def blocks(self, re, im):
        upper = jnp.concatenate([re, -im], axis=1)
        return jnp.concatenate([upper, jnp.concatenate([im, re], axis=1)], axis=0)

    def complex_sum(self, both):
        _, rows, columns = self.sizes
        with_re, with_im = both[:, :columns], both[:, columns:]
        return with_re[:rows] - with_im[rows:], with_im[:rows] + with_re[rows:]

    def dot(self, a, b, dims):
        return lax.dot_general(a, b, (dims, ((), ())), preferred_element_type=jnp.float32)

    def down(self, place):
        _, rows, columns = self.sizes
        x_re, x_im = self.stage_x[:, :rows], self.stage_x[:, rows:]
        wave = self.waves[place].astype(jnp.float32)
        gain = 1.0 + self.level_w[place].astype(jnp.float32)
        scaled = jnp.concatenate([gain * wave[:rows], gain * wave[rows:]], axis=0)
        self.turned_x[place] = self.blocks(x_re.T, x_im.T)
        middle = self.dot(self.blocks(x_re, x_im), scaled.astype(jnp.bfloat16), ((1,), (0,)))
        for i in range(2):
            lines = slice(i * columns, (i + 1) * columns)
            self.turned_y[place, lines, :] = self.stage_y[lines, :].T
        both = self.dot(middle.astype(jnp.bfloat16), self.stage_y[...], ((1,), (1,)))
        moved = jnp.concatenate(self.complex_sum(both), axis=0)
        self.waves[place + 1] = moved.astype(jnp.bfloat16)
        return place + 1

    def up(self, r, slot, place, wave_up, outs):
        _, rows, columns = self.sizes
        level = place - 1
        wave = self.waves[level].astype(jnp.float32)
        window = self.level_w[level].astype(jnp.float32)
        back = self.dot(self.turned_x[level], wave_up[...], ((1,), (0,)))
        both = self.dot(back.astype(jnp.bfloat16), self.turned_y[level], ((1,), (1,)))
        spread_re, spread_im = self.complex_sum(both)
        up_re = (window * wave[:rows] + spread_re).astype(jnp.bfloat16)
        up_im = (window * wave[rows:] + spread_im).astype(jnp.bfloat16)
        wave_up[:rows] = up_re
        wave_up[rows:] = up_im
        product = wave[:rows] * up_re.astype(jnp.float32)
        product += wave[rows:] * up_im.astype(jnp.float32)
        spot = pl.multiple_of(slot * rows, rows)
        for r_of, out in enumerate(outs):

            @pl.when(r == r_of)
            def _():
                out[pl.ds(spot, rows), :] = product.astype(out.dtype)

        return level


def down_kernel(sections, shots, group, sizes, source_ref, *refs):
    (own, near, far), (own_late, joined, far_window) = refs[:3], refs[3:6]
    *buffers, stage_y, stage_x, counts = refs[6:]
    it = Sweep(shots, group, sizes, *buffers, stage_y, stage_x)
    sources = [
        (own, own_late, own),
        (near, None, near),
        (far, None, far),
        (joined, None, far_window),
    ]

    @pl.when(it.is_worker != 0)
    def _():
        it.waves[0] = source_ref[it.shot]
        it.read_counts(sources, counts)

        def section_down(section, carry):
            place, going = carry
            r = section ^ it.here
            ready = it.early_slots(r, counts[r], sections)

            def level_down(slot, place):
                it.fetch(r, slot, place, sources)
                return it.down(place)

            place = lax.fori_loop(0, jnp.where(going, ready, 0), level_down, place)
            return place, going & (ready == counts[r])

        lax.fori_loop(0, sections, section_down, (jnp.int32(0), jnp.bool_(True)))


def up_kernel(sections, shots, group, sizes, *refs):
    (own, near, far), (own_late, near_late, far_late, joined, far_window) = refs[:3], refs[3:8]
    outs, refs = refs[12 : 12 + sections], refs[12 + sections :]
    *buffers, stage_y, stage_x, wave_up, counts = refs
    it = Sweep(shots, group, sizes, *buffers, stage_y, stage_x)
    sources = [
        (own, own_late, own),
        (near, near_late, near),
        (far, far_late, far),
        (joined, None, far_window),
    ]

    @pl.when(it.is_worker == 0)
    def _():
        outs[0][...] = jnp.zeros(outs[0].shape, outs[0].dtype)

    @pl.when(it.is_worker != 0)
    def _():
        it.read_counts(sources, counts)
        for out in outs:
            out[...] = jnp.zeros(out.shape, out.dtype)
        wave_up[...] = jnp.zeros(wave_up.shape, wave_up.dtype)

        def section_down(section, carry):
            place, going = carry
            r = section ^ it.here
            done = jnp.where(going, it.early_slots(r, counts[r], sections), 0)

            def level_down(slot, place):
                it.fetch(r, slot, place, sources)
                return it.down(place)

            place = lax.fori_loop(done, counts[r], level_down, place + done)
            return place, going & (done == counts[r])

        last, _ = lax.fori_loop(0, sections, section_down, (jnp.int32(0), jnp.bool_(True)))

        def section_up(step, place):
            r = (sections - 1 - step) ^ it.here
            count = counts[r]
            return lax.fori_loop(
                0,
                count,
                lambda inner, place: it.up(r, count - 1 - inner, place, wave_up, outs),
                place,
            )

        lax.fori_loop(0, sections, section_up, last)


def join_kernel(shots, group, anchors, first_ref, second_ref, out_ref, shifts):
    section, tile = lax.axis_index("depth"), lax.axis_index("tile")
    plane = lax.rem(tile // group, 2)
    half_rows = first_ref.shape[0]
    for i, ref in enumerate((first_ref, second_ref)):
        start = pl.multiple_of((plane if i == 0 else 1 - plane) * half_rows, half_rows)
        out_ref[pl.ds(start, half_rows), :] = ref[...]
    columns = shifts.shape[1]
    place = lax.broadcasted_iota(jnp.int32, shifts.shape[1:], 1)
    start = lax.broadcasted_iota(jnp.int32, shifts.shape[1:], 0)
    for q in range(shots):
        offset = anchors[lax.rem(section, shots) ^ q] - (tile - 1) * columns
        shifts[q] = (place - start == offset).astype(jnp.float32).astype(shifts.dtype)


def hold_kernel(array_ref, after_ref, out_ref):
    pass


def place_kernel(shots, shifts, *refs):
    arrived, (left_out, own_out) = refs[:-2], refs[-2:]
    places, columns = left_out.shape
    placed = None
    for q in range(shots):
        total = None
        for r in range(q, len(arrived), shots):
            value = arrived[r][:places, :]
            total = value if total is None else total + value
        part = jnp.dot(total, shifts[q], preferred_element_type=jnp.float32)
        placed = part if placed is None else placed + part
    left_out[...] = placed[:, :columns].astype(left_out.dtype)
    own_out[...] = placed[:, columns:]


def kept(array):
    return pltpu.with_memory_space_constraint(array, pltpu.HBM)


def held(array):
    return pltpu.with_memory_space_constraint(array, pltpu.VMEM)


def on_device(source, anchors, counts, reflect, lateral_x, lateral_y):
    shots, _, rows, columns = source.shape
    slots = reflect.shape[1]
    sizes = (slots, rows, columns)
    plan = Plan(shots)
    sections, group = plan.sections, plan.group
    assert shots == 2
    bf16 = jnp.bfloat16
    smem = pl.BlockSpec(memory_space=pltpu.SMEM)
    vmem = pl.BlockSpec(memory_space=pltpu.VMEM)
    hbm = pl.BlockSpec(memory_space=pltpu.HBM)
    anywhere = pl.BlockSpec(memory_space=pl.ANY)

    def params(mib):
        return pltpu.CompilerParams(vmem_limit_bytes=mib * MIB)

    tile_reflect = reflect[0].reshape(slots * rows, columns)
    halo = lax.ppermute(tile_reflect, "tile", [(i, i + 1) for i in range(plan.tiles - 1)])
    part = columns + rows // 2
    half_rows, win_rows = slots * part, slots * rows + TAIL
    early_rows = 2 * (half_rows - part) + win_rows
    even = pltpu.VMEM((early_rows + 5 * TAIL, columns), bf16)
    odd = pltpu.VMEM((early_rows, columns), bf16)
    even_early, odd_early, late, far_half = pl.pallas_call(
        functools.partial(pack_kernel, group, sizes),
        out_shape=[
            even,
            odd,
            jax.ShapeDtypeStruct((2 * part, columns), bf16),
            jax.ShapeDtypeStruct((half_rows, columns), bf16),
        ],
        in_specs=[hbm, hbm],
        out_specs=[vmem] * 4,
        scratch_shapes=[
            pltpu.VMEM(lateral_x.shape[1:], bf16),
            pltpu.VMEM(lateral_y.shape[1:], bf16),
            pltpu.SemaphoreType.DMA((2,)),
        ],
        compiler_params=params(12),
        name="pack",
    )(kept(lateral_x[0]), kept(lateral_y[0]))
    last = sections - 1
    far_half = lax.ppermute(far_half, BOTH, plan.to_workers(last))
    even_early, odd_early, far_window = pl.pallas_call(
        functools.partial(window_kernel, shots, sizes),
        out_shape=[even, odd, jax.ShapeDtypeStruct((win_rows, columns), bf16)],
        in_specs=[hbm, smem, vmem, hbm, vmem, vmem],
        out_specs=[vmem] * 3,
        scratch_shapes=[
            pltpu.SMEM((shots,), jnp.int32),
            pltpu.VMEM((slots * rows, columns), bf16),
            pltpu.SemaphoreType.DMA((2,)),
        ],
        input_output_aliases={4: 0, 5: 1},
        compiler_params=params(12),
        cost_estimate=pl.CostEstimate(flops=3 * 10**9, bytes_accessed=4 * MIB, transcendentals=0),
        name="windows",
    )(kept(anchors), counts, halo, kept(tile_reflect), held(even_early), held(odd_early))
    messages = [
        even_early,
        lax.ppermute(odd_early, BOTH, plan.to_workers(1)),
        lax.ppermute(even_early, BOTH, plan.to_workers(2)),
    ]
    far_window = lax.ppermute(far_window, BOTH, plan.to_workers(last))
    other_half = lax.ppermute(far_half, BOTH, plan.swap_workers())
    late = pl.pallas_call(
        hold_kernel,
        out_shape=jax.ShapeDtypeStruct(late.shape, bf16),
        in_specs=[anywhere] * 2,
        out_specs=anywhere,
        input_output_aliases={0: 0},
        compiler_params=params(2),
        cost_estimate=pl.CostEstimate(flops=36 * 10**8, bytes_accessed=0, transcendentals=0),
        name="hold",
    )(late, far_window)
    lates = [lax.ppermute(late, BOTH, plan.ops_to_workers(r)) for r in (1, 2)]
    joined, shifts = pl.pallas_call(
        functools.partial(join_kernel, shots, group),
        out_shape=[
            pltpu.VMEM((2 * half_rows, columns), bf16),
            pltpu.VMEM((shots, columns, 2 * columns), bf16),
        ],
        in_specs=[smem] + [vmem] * 2,
        out_specs=[vmem] * 2,
        compiler_params=params(8),
        name="join",
    )(anchors, held(far_half), held(other_half))

    levels = sections * slots
    buffers = [
        pltpu.VMEM((levels, 2 * columns, columns), bf16),
        pltpu.VMEM((levels, 2 * rows, 2 * rows), bf16),
        pltpu.VMEM((levels, rows, columns), bf16),
        pltpu.VMEM((levels + 1, 2 * rows, columns), bf16),
    ]
    stages = [pltpu.VMEM((2 * columns, columns), bf16), pltpu.VMEM((rows, 2 * rows), bf16)]
    messages = [held(message) for message in messages]
    late, joined, far_window = held(late), held(joined), held(far_window)
    filled = pl.pallas_call(
        functools.partial(down_kernel, sections, shots, group, sizes),
        out_shape=buffers,
        in_specs=[vmem] * 7,
        out_specs=[vmem] * 4,
        scratch_shapes=stages + [pltpu.SMEM((sections,), jnp.int32)],
        compiler_params=params(24),
        name="down",
    )(held(source.reshape(shots, 2 * rows, columns)), *messages, late, joined, far_window)
    correlations = pl.pallas_call(
        functools.partial(up_kernel, sections, shots, group, sizes),
        out_shape=[
            jax.ShapeDtypeStruct((slots * rows + TAIL * more, columns), bf16)
            for more in (0, 1, 0, 2)
        ]
        + buffers,
        in_specs=[vmem] * 12,
        out_specs=[vmem] * (sections + 4),
        scratch_shapes=stages
        + [pltpu.VMEM((2 * rows, columns), bf16), pltpu.SMEM((sections,), jnp.int32)],
        input_output_aliases={8 + i: sections + i for i in range(4)},
        compiler_params=params(24),
        name="up",
    )(
        *messages, late, *[held(part) for part in lates], joined, far_window,
        *[held(buffer) for buffer in filled],
    )

    corr_shape = jax.ShapeDtypeStruct((slots * rows, columns), bf16)
    arrived = [correlations[0]] + [
        lax.ppermute(correlations[r], BOTH, plan.from_workers(r)) for r in range(1, sections)
    ]
    left, own = pl.pallas_call(
        functools.partial(place_kernel, shots),
        out_shape=[corr_shape, jax.ShapeDtypeStruct((slots * rows, columns), jnp.float32)],
        in_specs=[vmem] * (1 + sections),
        out_specs=[vmem, vmem],
        compiler_params=params(8),
        name="place",
    )(held(shifts), *[held(part) for part in arrived])
    from_right = lax.ppermute(left, "tile", [(i + 1, i) for i in range(plan.tiles - 1)])
    image = own + from_right.astype(jnp.float32)
    return image.reshape(1, slots, rows, columns)


def solution(mesh):
    return jax.shard_map(
        on_device,
        mesh=mesh,
        in_specs=(
            P("tile", None, None, None),
            P("tile"),
            P("depth"),
            P("depth", None, None, "tile"),
            P("depth", None, None, None, None),
            P("depth", None, None, None, None),
        ),
        out_specs=P("depth", None, None, "tile"),
        check_vma=False,
    )
```

```python
import functools

import jax
import jax.numpy as jnp
from jax import lax
from jax.experimental import pallas as pl
from jax.experimental.pallas import tpu as pltpu
from jax.sharding import PartitionSpec as P

BOTH = ("depth", "tile")
MIB = 1024 * 1024
TAIL = 16


class Plan:
    def __init__(self, shots):
        self.sections = lax.axis_size("depth")
        self.tiles = lax.axis_size("tile")
        self.shots = shots
        self.group = self.sections // shots
        assert self.sections == 4 and self.group * shots == self.sections
        assert self.tiles % (2 * self.group) == 0

    def device(self, depth, tile):
        return depth * self.tiles + tile

    def bases(self):
        return range(0, self.tiles, self.group)

    def worker(self, base, w):
        return self.device(w, base + w // self.shots)

    def other(self, w, base):
        return self.device(w, base + (w // self.shots + 1) % self.group)

    def ops_to_workers(self, r):
        return [
            (self.other(w ^ r, base), self.worker(base, w))
            for base in self.bases()
            for w in range(self.sections)
        ]

    def swap_workers(self):
        return [
            (self.worker(base, w), self.worker((base // self.group ^ 1) * self.group, w))
            for base in self.bases()
            for w in range(self.sections)
        ]

    def to_workers(self, r):
        return [
            (self.device(w ^ r, base + w // self.shots), self.worker(base, w))
            for base in self.bases()
            for w in range(self.sections)
        ]

    def from_workers(self, r):
        return [(b, a) for a, b in self.to_workers(r)]


def pack_kernel(group, sizes, x_hbm, y_hbm, even, odd, late, half_out, x_ref, y_ref, sem):
    slots, rows, columns = sizes
    loads = [
        pltpu.make_async_copy(x_hbm, x_ref, sem.at[0]),
        pltpu.make_async_copy(y_hbm, y_ref, sem.at[1]),
    ]
    for load in loads:
        load.start()
    for load in loads:
        load.wait()
    piece = rows // 2
    part = columns + piece
    first = (slots - 1) * part
    for half in range(2):
        for slot in range(slots):
            op_x = jnp.concatenate(
                [x_ref[slot, i, half * piece : (half + 1) * piece, :] for i in range(2)], axis=1
            )
            op_y = y_ref[slot, half]
            if slot < slots - 1:
                places = [(out, half * first + slot * part) for out in (even, odd)]
            else:
                places = [(late, half * part)]
            for out, spot in places:
                out[spot : spot + columns, :] = op_y
                out[spot + columns : spot + part, :] = op_x
    plane = lax.rem(lax.axis_index("tile") // group, 2)
    half_out[:first, :] = even[pl.ds(pl.multiple_of(plane * first, first), first), :]
    half_out[first:, :] = late[pl.ds(pl.multiple_of(plane * part, part), part), :]


def window_kernel(shots, sizes, anchors_hbm, counts, left_ref, right_hbm, *refs):
    slots, rows, columns = sizes
    messages, (alone, anchors, right_ref, sem) = refs[shots : 2 * shots], refs[2 * shots :]
    loads = [
        pltpu.make_async_copy(anchors_hbm, anchors, sem.at[0]),
        pltpu.make_async_copy(right_hbm, right_ref, sem.at[1]),
    ]
    for load in loads:
        load.start()
    for load in loads:
        load.wait()
    section, tile = lax.axis_index("depth"), lax.axis_index("tile")
    left, right = left_ref[...].astype(jnp.float32), right_ref[...].astype(jnp.float32)
    lanes = lax.broadcasted_iota(jnp.int32, left.shape, 1)
    tail = jnp.full((TAIL, columns), counts[0].astype(jnp.float32), jnp.float32)
    for q, message in enumerate(messages):
        offset = anchors[lax.rem(section, shots) ^ q] - (tile - 1) * columns
        merged = jnp.where(lanes >= offset, left, right)
        back = lax.rem(columns - lax.rem(offset, columns), columns)
        window = pltpu.roll(merged, back, 1).astype(message.dtype)
        for out in [message] + ([alone] if q == shots - 1 else []):
            spot = out.shape[0] - TAIL - slots * rows
            out[spot : spot + slots * rows, :] = window
            out[spot + slots * rows :, :] = tail.astype(out.dtype)


class Sweep:
    def __init__(self, shots, group, sizes, turned_y, turned_x, level_w, waves, stage_y, stage_x):
        self.sizes = sizes
        self.turned_y, self.turned_x, self.level_w = turned_y, turned_x, level_w
        self.waves, self.stage_y, self.stage_x = waves, stage_y, stage_x
        slots, rows, columns = sizes
        self.piece = rows // 2
        self.part = columns + self.piece
        self.first = (slots - 1) * self.part
        self.half_rows = self.first + self.part
        self.win_rows = slots * rows + TAIL
        self.here, tile = lax.axis_index("depth"), lax.axis_index("tile")
        self.shot = lax.rem(self.here, shots)
        self.is_worker = (self.here // shots == lax.rem(tile, group)).astype(jnp.int32)

    def read_counts(self, sources, counts):
        for r, (_, _, window) in enumerate(sources):
            value = jnp.max(window[window.shape[0] - TAIL :, :].astype(jnp.float32))
            counts[r] = value.astype(jnp.int32)

    def early_slots(self, r, count, rounds):
        partial = (r != 0) & (r != rounds - 1)
        return jnp.where(partial, jnp.minimum(count, self.sizes[0] - 1), count)

    def window_start(self, window_ref):
        return window_ref.shape[0] - self.win_rows

    def fetch(self, r, slot, place, sources):
        slots, rows, columns = self.sizes
        for r_of, (early, late, window) in enumerate(sources):
            early_slots = slots if early.shape[0] == 2 * self.half_rows else slots - 1
            choices = [(early, early_slots * self.part, slot < early_slots, slot)]
            if late is not None:
                choices.append((late, self.part, slot == slots - 1, 0))
            for ref, stride, chosen, at in choices:

                @pl.when((r == r_of) & chosen)
                def _():
                    for half in range(2):
                        start = pl.multiple_of(half * stride + at * self.part, self.piece)
                        self.stage_y[half * columns : (half + 1) * columns, :] = ref[
                            pl.ds(start, columns), :
                        ]
                        tail = pl.multiple_of(start + columns, self.piece)
                        self.stage_x[half * self.piece : (half + 1) * self.piece, :] = ref[
                            pl.ds(tail, self.piece), :
                        ]
                    spot = self.window_start(window) + slot * rows
                    self.level_w[place] = window[pl.ds(pl.multiple_of(spot, TAIL), rows), :]

    def blocks(self, re, im):
        upper = jnp.concatenate([re, -im], axis=1)
        return jnp.concatenate([upper, jnp.concatenate([im, re], axis=1)], axis=0)

    def complex_sum(self, both):
        _, rows, columns = self.sizes
        with_re, with_im = both[:, :columns], both[:, columns:]
        return with_re[:rows] - with_im[rows:], with_im[:rows] + with_re[rows:]

    def dot(self, a, b, dims):
        return lax.dot_general(a, b, (dims, ((), ())), preferred_element_type=jnp.float32)

    def down(self, place):
        _, rows, columns = self.sizes
        x_re, x_im = self.stage_x[:, :rows], self.stage_x[:, rows:]
        wave = self.waves[place].astype(jnp.float32)
        gain = 1.0 + self.level_w[place].astype(jnp.float32)
        scaled = jnp.concatenate([gain * wave[:rows], gain * wave[rows:]], axis=0)
        self.turned_x[place] = self.blocks(x_re.T, x_im.T)
        middle = self.dot(self.blocks(x_re, x_im), scaled.astype(jnp.bfloat16), ((1,), (0,)))
        for i in range(2):
            lines = slice(i * columns, (i + 1) * columns)
            self.turned_y[place, lines, :] = self.stage_y[lines, :].T
        both = self.dot(middle.astype(jnp.bfloat16), self.stage_y[...], ((1,), (1,)))
        moved = jnp.concatenate(self.complex_sum(both), axis=0)
        self.waves[place + 1] = moved.astype(jnp.bfloat16)
        return place + 1

    def up(self, r, slot, place, wave_up, outs):
        _, rows, columns = self.sizes
        level = place - 1
        wave = self.waves[level].astype(jnp.float32)
        window = self.level_w[level].astype(jnp.float32)
        back = self.dot(self.turned_x[level], wave_up[...], ((1,), (0,)))
        both = self.dot(back.astype(jnp.bfloat16), self.turned_y[level], ((1,), (1,)))
        spread_re, spread_im = self.complex_sum(both)
        up_re = (window * wave[:rows] + spread_re).astype(jnp.bfloat16)
        up_im = (window * wave[rows:] + spread_im).astype(jnp.bfloat16)
        wave_up[:rows] = up_re
        wave_up[rows:] = up_im
        product = wave[:rows] * up_re.astype(jnp.float32)
        product += wave[rows:] * up_im.astype(jnp.float32)
        spot = pl.multiple_of(slot * rows, rows)
        for r_of, out in enumerate(outs):

            @pl.when(r == r_of)
            def _():
                out[pl.ds(spot, rows), :] = product.astype(out.dtype)

        return level


def down_kernel(sections, shots, group, sizes, source_ref, *refs):
    (own, near, far), (own_late, joined, far_window) = refs[:3], refs[3:6]
    *buffers, stage_y, stage_x, counts = refs[6:]
    it = Sweep(shots, group, sizes, *buffers, stage_y, stage_x)
    sources = [
        (own, own_late, own),
        (near, None, near),
        (far, None, far),
        (joined, None, far_window),
    ]

    @pl.when(it.is_worker != 0)
    def _():
        it.waves[0] = source_ref[it.shot]
        it.read_counts(sources, counts)

        def section_down(section, carry):
            place, going = carry
            r = section ^ it.here
            ready = it.early_slots(r, counts[r], sections)

            def level_down(slot, place):
                it.fetch(r, slot, place, sources)
                return it.down(place)

            place = lax.fori_loop(0, jnp.where(going, ready, 0), level_down, place)
            return place, going & (ready == counts[r])

        lax.fori_loop(0, sections, section_down, (jnp.int32(0), jnp.bool_(True)))


def up_kernel(sections, shots, group, sizes, *refs):
    (own, near, far), (own_late, near_late, far_late, joined, far_window) = refs[:3], refs[3:8]
    outs, refs = refs[12 : 12 + sections], refs[12 + sections :]
    *buffers, stage_y, stage_x, wave_up, counts = refs
    it = Sweep(shots, group, sizes, *buffers, stage_y, stage_x)
    sources = [
        (own, own_late, own),
        (near, near_late, near),
        (far, far_late, far),
        (joined, None, far_window),
    ]

    @pl.when(it.is_worker == 0)
    def _():
        outs[0][...] = jnp.zeros(outs[0].shape, outs[0].dtype)

    @pl.when(it.is_worker != 0)
    def _():
        it.read_counts(sources, counts)
        for out in outs:
            out[...] = jnp.zeros(out.shape, out.dtype)
        wave_up[...] = jnp.zeros(wave_up.shape, wave_up.dtype)

        def section_down(section, carry):
            place, going = carry
            r = section ^ it.here
            done = jnp.where(going, it.early_slots(r, counts[r], sections), 0)

            def level_down(slot, place):
                it.fetch(r, slot, place, sources)
                return it.down(place)

            place = lax.fori_loop(done, counts[r], level_down, place + done)
            return place, going & (done == counts[r])

        last, _ = lax.fori_loop(0, sections, section_down, (jnp.int32(0), jnp.bool_(True)))

        def section_up(step, place):
            r = (sections - 1 - step) ^ it.here
            count = counts[r]
            return lax.fori_loop(
                0,
                count,
                lambda inner, place: it.up(r, count - 1 - inner, place, wave_up, outs),
                place,
            )

        lax.fori_loop(0, sections, section_up, last)


def join_kernel(shots, group, anchors, first_ref, second_ref, out_ref, shifts):
    section, tile = lax.axis_index("depth"), lax.axis_index("tile")
    plane = lax.rem(tile // group, 2)
    half_rows = first_ref.shape[0]
    for i, ref in enumerate((first_ref, second_ref)):
        start = pl.multiple_of((plane if i == 0 else 1 - plane) * half_rows, half_rows)
        out_ref[pl.ds(start, half_rows), :] = ref[...]
    columns = shifts.shape[1]
    place = lax.broadcasted_iota(jnp.int32, shifts.shape[1:], 1)
    start = lax.broadcasted_iota(jnp.int32, shifts.shape[1:], 0)
    for q in range(shots):
        offset = anchors[lax.rem(section, shots) ^ q] - (tile - 1) * columns
        shifts[q] = (place - start == offset).astype(jnp.float32).astype(shifts.dtype)


def hold_kernel(array_ref, after_ref, out_ref):
    pass


def place_kernel(shots, shifts, *refs):
    arrived, (left_out, own_out) = refs[:-2], refs[-2:]
    places, columns = left_out.shape
    placed = None
    for q in range(shots):
        total = None
        for r in range(q, len(arrived), shots):
            value = arrived[r][:places, :]
            total = value if total is None else total + value
        part = jnp.dot(total, shifts[q], preferred_element_type=jnp.float32)
        placed = part if placed is None else placed + part
    left_out[...] = placed[:, :columns].astype(left_out.dtype)
    own_out[...] = placed[:, columns:]


def kept(array):
    return pltpu.with_memory_space_constraint(array, pltpu.HBM)


def held(array):
    return pltpu.with_memory_space_constraint(array, pltpu.VMEM)


def on_device(source, anchors, counts, reflect, lateral_x, lateral_y):
    shots, _, rows, columns = source.shape
    slots = reflect.shape[1]
    sizes = (slots, rows, columns)
    plan = Plan(shots)
    sections, group = plan.sections, plan.group
    assert shots == 2
    bf16 = jnp.bfloat16
    smem = pl.BlockSpec(memory_space=pltpu.SMEM)
    vmem = pl.BlockSpec(memory_space=pltpu.VMEM)
    hbm = pl.BlockSpec(memory_space=pltpu.HBM)
    anywhere = pl.BlockSpec(memory_space=pl.ANY)

    def params(mib):
        return pltpu.CompilerParams(vmem_limit_bytes=mib * MIB)

    tile_reflect = reflect[0].reshape(slots * rows, columns)
    halo = lax.ppermute(tile_reflect, "tile", [(i, i + 1) for i in range(plan.tiles - 1)])
    part = columns + rows // 2
    half_rows, win_rows = slots * part, slots * rows + TAIL
    early_rows = 2 * (half_rows - part) + win_rows
    even = pltpu.VMEM((early_rows + 5 * TAIL, columns), bf16)
    odd = pltpu.VMEM((early_rows, columns), bf16)
    even_early, odd_early, late, far_half = pl.pallas_call(
        functools.partial(pack_kernel, group, sizes),
        out_shape=[
            even,
            odd,
            jax.ShapeDtypeStruct((2 * part, columns), bf16),
            jax.ShapeDtypeStruct((half_rows, columns), bf16),
        ],
        in_specs=[hbm, hbm],
        out_specs=[vmem] * 4,
        scratch_shapes=[
            pltpu.VMEM(lateral_x.shape[1:], bf16),
            pltpu.VMEM(lateral_y.shape[1:], bf16),
            pltpu.SemaphoreType.DMA((2,)),
        ],
        compiler_params=params(12),
        name="pack",
    )(kept(lateral_x[0]), kept(lateral_y[0]))
    last = sections - 1
    far_half = lax.ppermute(far_half, BOTH, plan.to_workers(last))
    even_early, odd_early, far_window = pl.pallas_call(
        functools.partial(window_kernel, shots, sizes),
        out_shape=[even, odd, jax.ShapeDtypeStruct((win_rows, columns), bf16)],
        in_specs=[hbm, smem, vmem, hbm, vmem, vmem],
        out_specs=[vmem] * 3,
        scratch_shapes=[
            pltpu.SMEM((shots,), jnp.int32),
            pltpu.VMEM((slots * rows, columns), bf16),
            pltpu.SemaphoreType.DMA((2,)),
        ],
        input_output_aliases={4: 0, 5: 1},
        compiler_params=params(12),
        cost_estimate=pl.CostEstimate(flops=3 * 10**9, bytes_accessed=4 * MIB, transcendentals=0),
        name="windows",
    )(kept(anchors), counts, halo, kept(tile_reflect), held(even_early), held(odd_early))
    messages = [
        even_early,
        lax.ppermute(odd_early, BOTH, plan.to_workers(1)),
        lax.ppermute(even_early, BOTH, plan.to_workers(2)),
    ]
    far_window = lax.ppermute(far_window, BOTH, plan.to_workers(last))
    other_half = lax.ppermute(far_half, BOTH, plan.swap_workers())
    late = pl.pallas_call(
        hold_kernel,
        out_shape=jax.ShapeDtypeStruct(late.shape, bf16),
        in_specs=[anywhere] * 2,
        out_specs=anywhere,
        input_output_aliases={0: 0},
        compiler_params=params(2),
        cost_estimate=pl.CostEstimate(flops=36 * 10**8, bytes_accessed=0, transcendentals=0),
        name="hold",
    )(late, far_window)
    lates = [lax.ppermute(late, BOTH, plan.ops_to_workers(r)) for r in (1, 2)]
    joined, shifts = pl.pallas_call(
        functools.partial(join_kernel, shots, group),
        out_shape=[
            pltpu.VMEM((2 * half_rows, columns), bf16),
            pltpu.VMEM((shots, columns, 2 * columns), bf16),
        ],
        in_specs=[smem] + [vmem] * 2,
        out_specs=[vmem] * 2,
        compiler_params=params(8),
        name="join",
    )(anchors, held(far_half), held(other_half))

    levels = sections * slots
    buffers = [
        pltpu.VMEM((levels, 2 * columns, columns), bf16),
        pltpu.VMEM((levels, 2 * rows, 2 * rows), bf16),
        pltpu.VMEM((levels, rows, columns), bf16),
        pltpu.VMEM((levels + 1, 2 * rows, columns), bf16),
    ]
    stages = [pltpu.VMEM((2 * columns, columns), bf16), pltpu.VMEM((rows, 2 * rows), bf16)]
    messages = [held(message) for message in messages]
    late, joined, far_window = held(late), held(joined), held(far_window)
    filled = pl.pallas_call(
        functools.partial(down_kernel, sections, shots, group, sizes),
        out_shape=buffers,
        in_specs=[vmem] * 7,
        out_specs=[vmem] * 4,
        scratch_shapes=stages + [pltpu.SMEM((sections,), jnp.int32)],
        compiler_params=params(24),
        name="down",
    )(held(source.reshape(shots, 2 * rows, columns)), *messages, late, joined, far_window)
    correlations = pl.pallas_call(
        functools.partial(up_kernel, sections, shots, group, sizes),
        out_shape=[
            jax.ShapeDtypeStruct((slots * rows + TAIL * more, columns), bf16)
            for more in (0, 0, 1, 2)
        ]
        + buffers,
        in_specs=[vmem] * 12,
        out_specs=[vmem] * (sections + 4),
        scratch_shapes=stages
        + [pltpu.VMEM((2 * rows, columns), bf16), pltpu.SMEM((sections,), jnp.int32)],
        input_output_aliases={8 + i: sections + i for i in range(4)},
        compiler_params=params(24),
        name="up",
    )(
        *messages, late, *[held(part) for part in lates], joined, far_window,
        *[held(buffer) for buffer in filled],
    )

    corr_shape = jax.ShapeDtypeStruct((slots * rows, columns), bf16)
    arrived = [correlations[0]] + [
        lax.ppermute(correlations[r], BOTH, plan.from_workers(r)) for r in range(1, sections)
    ]
    left, own = pl.pallas_call(
        functools.partial(place_kernel, shots),
        out_shape=[corr_shape, jax.ShapeDtypeStruct((slots * rows, columns), jnp.float32)],
        in_specs=[vmem] * (1 + sections),
        out_specs=[vmem, vmem],
        compiler_params=params(8),
        name="place",
    )(held(shifts), *[held(part) for part in arrived])
    from_right = lax.ppermute(left, "tile", [(i + 1, i) for i in range(plan.tiles - 1)])
    image = own + from_right.astype(jnp.float32)
    return image.reshape(1, slots, rows, columns)


def solution(mesh):
    return jax.shard_map(
        on_device,
        mesh=mesh,
        in_specs=(
            P("tile", None, None, None),
            P("tile"),
            P("depth"),
            P("depth", None, None, "tile"),
            P("depth", None, None, None, None),
            P("depth", None, None, None, None),
        ),
        out_specs=P("depth", None, None, "tile"),
        check_vma=False,
    )
```

```python
import functools

import jax
import jax.numpy as jnp
from jax import lax
from jax.experimental import pallas as pl
from jax.experimental.pallas import tpu as pltpu
from jax.sharding import PartitionSpec as P

BOTH = ("depth", "tile")
MIB = 1024 * 1024
TAIL = 16


class Plan:
    def __init__(self, shots):
        self.sections = lax.axis_size("depth")
        self.tiles = lax.axis_size("tile")
        self.shots = shots
        self.group = self.sections // shots
        assert self.sections == 4 and self.group * shots == self.sections
        assert self.tiles % (2 * self.group) == 0

    def device(self, depth, tile):
        return depth * self.tiles + tile

    def bases(self):
        return range(0, self.tiles, self.group)

    def worker(self, base, w):
        return self.device(w, base + w // self.shots)

    def other(self, w, base):
        return self.device(w, base + (w // self.shots + 1) % self.group)

    def ops_to_workers(self, r):
        return [
            (self.other(w ^ r, base), self.worker(base, w))
            for base in self.bases()
            for w in range(self.sections)
        ]

    def swap_workers(self):
        return [
            (self.worker(base, w), self.worker((base // self.group ^ 1) * self.group, w))
            for base in self.bases()
            for w in range(self.sections)
        ]

    def to_workers(self, r):
        return [
            (self.device(w ^ r, base + w // self.shots), self.worker(base, w))
            for base in self.bases()
            for w in range(self.sections)
        ]

    def from_workers(self, r):
        return [(b, a) for a, b in self.to_workers(r)]


def pack_kernel(group, sizes, x_hbm, y_hbm, even, odd, late, half_out, x_ref, y_ref, sem):
    slots, rows, columns = sizes
    loads = [
        pltpu.make_async_copy(x_hbm, x_ref, sem.at[0]),
        pltpu.make_async_copy(y_hbm, y_ref, sem.at[1]),
    ]
    for load in loads:
        load.start()
    for load in loads:
        load.wait()
    piece = rows // 2
    part = columns + piece
    first = (slots - 1) * part
    for half in range(2):
        for slot in range(slots):
            op_x = jnp.concatenate(
                [x_ref[slot, i, half * piece : (half + 1) * piece, :] for i in range(2)], axis=1
            )
            op_y = y_ref[slot, half]
            if slot < slots - 1:
                places = [(out, half * first + slot * part) for out in (even, odd)]
            else:
                places = [(late, half * part)]
            for out, spot in places:
                out[spot : spot + columns, :] = op_y
                out[spot + columns : spot + part, :] = op_x
    plane = lax.rem(lax.axis_index("tile") // group, 2)
    half_out[:first, :] = even[pl.ds(pl.multiple_of(plane * first, first), first), :]
    half_out[first:, :] = late[pl.ds(pl.multiple_of(plane * part, part), part), :]


def window_kernel(shots, sizes, anchors_hbm, counts, left_ref, right_hbm, *refs):
    slots, rows, columns = sizes
    messages, (alone, anchors, right_ref, sem) = refs[shots : 2 * shots], refs[2 * shots :]
    loads = [
        pltpu.make_async_copy(anchors_hbm, anchors, sem.at[0]),
        pltpu.make_async_copy(right_hbm, right_ref, sem.at[1]),
    ]
    for load in loads:
        load.start()
    for load in loads:
        load.wait()
    section, tile = lax.axis_index("depth"), lax.axis_index("tile")
    left, right = left_ref[...].astype(jnp.float32), right_ref[...].astype(jnp.float32)
    lanes = lax.broadcasted_iota(jnp.int32, left.shape, 1)
    tail = jnp.full((TAIL, columns), counts[0].astype(jnp.float32), jnp.float32)
    for q, message in enumerate(messages):
        offset = anchors[lax.rem(section, shots) ^ q] - (tile - 1) * columns
        merged = jnp.where(lanes >= offset, left, right)
        back = lax.rem(columns - lax.rem(offset, columns), columns)
        window = pltpu.roll(merged, back, 1).astype(message.dtype)
        for out in [message] + ([alone] if q == shots - 1 else []):
            spot = out.shape[0] - TAIL - slots * rows
            out[spot : spot + slots * rows, :] = window
            out[spot + slots * rows :, :] = tail.astype(out.dtype)


class Sweep:
    def __init__(self, shots, group, sizes, turned_y, turned_x, level_w, waves, stage_y, stage_x):
        self.sizes = sizes
        self.turned_y, self.turned_x, self.level_w = turned_y, turned_x, level_w
        self.waves, self.stage_y, self.stage_x = waves, stage_y, stage_x
        slots, rows, columns = sizes
        self.piece = rows // 2
        self.part = columns + self.piece
        self.first = (slots - 1) * self.part
        self.half_rows = self.first + self.part
        self.win_rows = slots * rows + TAIL
        self.here, tile = lax.axis_index("depth"), lax.axis_index("tile")
        self.shot = lax.rem(self.here, shots)
        self.is_worker = (self.here // shots == lax.rem(tile, group)).astype(jnp.int32)

    def read_counts(self, sources, counts):
        for r, (_, _, window) in enumerate(sources):
            value = jnp.max(window[window.shape[0] - TAIL :, :].astype(jnp.float32))
            counts[r] = value.astype(jnp.int32)

    def early_slots(self, r, count, rounds):
        partial = (r != 0) & (r != rounds - 1)
        return jnp.where(partial, jnp.minimum(count, self.sizes[0] - 1), count)

    def window_start(self, window_ref):
        return window_ref.shape[0] - self.win_rows

    def fetch(self, r, slot, place, sources):
        slots, rows, columns = self.sizes
        for r_of, (early, late, window) in enumerate(sources):
            early_slots = slots if early.shape[0] == 2 * self.half_rows else slots - 1
            choices = [(early, early_slots * self.part, slot < early_slots, slot)]
            if late is not None:
                choices.append((late, self.part, slot == slots - 1, 0))
            for ref, stride, chosen, at in choices:

                @pl.when((r == r_of) & chosen)
                def _():
                    for half in range(2):
                        start = pl.multiple_of(half * stride + at * self.part, self.piece)
                        self.stage_y[half * columns : (half + 1) * columns, :] = ref[
                            pl.ds(start, columns), :
                        ]
                        tail = pl.multiple_of(start + columns, self.piece)
                        self.stage_x[half * self.piece : (half + 1) * self.piece, :] = ref[
                            pl.ds(tail, self.piece), :
                        ]
                    spot = self.window_start(window) + slot * rows
                    self.level_w[place] = window[pl.ds(pl.multiple_of(spot, TAIL), rows), :]

    def blocks(self, re, im):
        upper = jnp.concatenate([re, -im], axis=1)
        return jnp.concatenate([upper, jnp.concatenate([im, re], axis=1)], axis=0)

    def complex_sum(self, both):
        _, rows, columns = self.sizes
        with_re, with_im = both[:, :columns], both[:, columns:]
        return with_re[:rows] - with_im[rows:], with_im[:rows] + with_re[rows:]

    def dot(self, a, b, dims):
        return lax.dot_general(a, b, (dims, ((), ())), preferred_element_type=jnp.float32)

    def down(self, place):
        _, rows, columns = self.sizes
        x_re, x_im = self.stage_x[:, :rows], self.stage_x[:, rows:]
        wave = self.waves[place].astype(jnp.float32)
        gain = 1.0 + self.level_w[place].astype(jnp.float32)
        scaled = jnp.concatenate([gain * wave[:rows], gain * wave[rows:]], axis=0)
        self.turned_x[place] = self.blocks(x_re.T, x_im.T)
        middle = self.dot(self.blocks(x_re, x_im), scaled.astype(jnp.bfloat16), ((1,), (0,)))
        for i in range(2):
            lines = slice(i * columns, (i + 1) * columns)
            self.turned_y[place, lines, :] = self.stage_y[lines, :].T
        both = self.dot(middle.astype(jnp.bfloat16), self.stage_y[...], ((1,), (1,)))
        moved = jnp.concatenate(self.complex_sum(both), axis=0)
        self.waves[place + 1] = moved.astype(jnp.bfloat16)
        return place + 1

    def up(self, r, slot, place, wave_up, outs):
        _, rows, columns = self.sizes
        level = place - 1
        wave = self.waves[level].astype(jnp.float32)
        window = self.level_w[level].astype(jnp.float32)
        back = self.dot(self.turned_x[level], wave_up[...], ((1,), (0,)))
        both = self.dot(back.astype(jnp.bfloat16), self.turned_y[level], ((1,), (1,)))
        spread_re, spread_im = self.complex_sum(both)
        up_re = (window * wave[:rows] + spread_re).astype(jnp.bfloat16)
        up_im = (window * wave[rows:] + spread_im).astype(jnp.bfloat16)
        wave_up[:rows] = up_re
        wave_up[rows:] = up_im
        product = wave[:rows] * up_re.astype(jnp.float32)
        product += wave[rows:] * up_im.astype(jnp.float32)
        spot = pl.multiple_of(slot * rows, rows)
        for r_of, out in enumerate(outs):

            @pl.when(r == r_of)
            def _():
                out[pl.ds(spot, rows), :] = product.astype(out.dtype)

        return level


def down_kernel(sections, shots, group, sizes, source_ref, *refs):
    (own, near, far), (own_late, joined, far_window) = refs[:3], refs[3:6]
    *buffers, stage_y, stage_x, counts = refs[6:]
    it = Sweep(shots, group, sizes, *buffers, stage_y, stage_x)
    sources = [
        (own, own_late, own),
        (near, None, near),
        (far, None, far),
        (joined, None, far_window),
    ]

    @pl.when(it.is_worker != 0)
    def _():
        it.waves[0] = source_ref[it.shot]
        it.read_counts(sources, counts)

        def section_down(section, carry):
            place, going = carry
            r = section ^ it.here
            ready = it.early_slots(r, counts[r], sections)

            def level_down(slot, place):
                it.fetch(r, slot, place, sources)
                return it.down(place)

            place = lax.fori_loop(0, jnp.where(going, ready, 0), level_down, place)
            return place, going & (ready == counts[r])

        lax.fori_loop(0, sections, section_down, (jnp.int32(0), jnp.bool_(True)))


def up_kernel(sections, shots, group, sizes, *refs):
    (own, near, far), (own_late, near_late, far_late, joined, far_window) = refs[:3], refs[3:8]
    outs, refs = refs[12 : 12 + sections], refs[12 + sections :]
    *buffers, stage_y, stage_x, wave_up, counts = refs
    it = Sweep(shots, group, sizes, *buffers, stage_y, stage_x)
    sources = [
        (own, own_late, own),
        (near, near_late, near),
        (far, far_late, far),
        (joined, None, far_window),
    ]

    @pl.when(it.is_worker == 0)
    def _():
        outs[0][...] = jnp.zeros(outs[0].shape, outs[0].dtype)

    @pl.when(it.is_worker != 0)
    def _():
        it.read_counts(sources, counts)
        for out in outs:
            out[...] = jnp.zeros(out.shape, out.dtype)
        wave_up[...] = jnp.zeros(wave_up.shape, wave_up.dtype)

        def section_down(section, carry):
            place, going = carry
            r = section ^ it.here
            done = jnp.where(going, it.early_slots(r, counts[r], sections), 0)

            def level_down(slot, place):
                it.fetch(r, slot, place, sources)
                return it.down(place)

            place = lax.fori_loop(done, counts[r], level_down, place + done)
            return place, going & (done == counts[r])

        last, _ = lax.fori_loop(0, sections, section_down, (jnp.int32(0), jnp.bool_(True)))

        def section_up(step, place):
            r = (sections - 1 - step) ^ it.here
            count = counts[r]
            return lax.fori_loop(
                0,
                count,
                lambda inner, place: it.up(r, count - 1 - inner, place, wave_up, outs),
                place,
            )

        lax.fori_loop(0, sections, section_up, last)


def join_kernel(shots, group, anchors, first_ref, second_ref, out_ref, shifts):
    section, tile = lax.axis_index("depth"), lax.axis_index("tile")
    plane = lax.rem(tile // group, 2)
    half_rows = first_ref.shape[0]
    for i, ref in enumerate((first_ref, second_ref)):
        start = pl.multiple_of((plane if i == 0 else 1 - plane) * half_rows, half_rows)
        out_ref[pl.ds(start, half_rows), :] = ref[...]
    columns = shifts.shape[1]
    place = lax.broadcasted_iota(jnp.int32, shifts.shape[1:], 1)
    start = lax.broadcasted_iota(jnp.int32, shifts.shape[1:], 0)
    for q in range(shots):
        offset = anchors[lax.rem(section, shots) ^ q] - (tile - 1) * columns
        shifts[q] = (place - start == offset).astype(jnp.float32).astype(shifts.dtype)


def hold_kernel(array_ref, after_ref, out_ref):
    pass


def place_kernel(shots, shifts, *refs):
    arrived, (left_out, own_out) = refs[:-2], refs[-2:]
    places, columns = left_out.shape
    placed = None
    for q in range(shots):
        total = None
        for r in range(q, len(arrived), shots):
            value = arrived[r][:places, :]
            total = value if total is None else total + value
        part = jnp.dot(total, shifts[q], preferred_element_type=jnp.float32)
        placed = part if placed is None else placed + part
    left_out[...] = placed[:, :columns].astype(left_out.dtype)
    own_out[...] = placed[:, columns:]


def kept(array):
    return pltpu.with_memory_space_constraint(array, pltpu.HBM)


def held(array):
    return pltpu.with_memory_space_constraint(array, pltpu.VMEM)


def on_device(source, anchors, counts, reflect, lateral_x, lateral_y):
    shots, _, rows, columns = source.shape
    slots = reflect.shape[1]
    sizes = (slots, rows, columns)
    plan = Plan(shots)
    sections, group = plan.sections, plan.group
    assert shots == 2
    bf16 = jnp.bfloat16
    smem = pl.BlockSpec(memory_space=pltpu.SMEM)
    vmem = pl.BlockSpec(memory_space=pltpu.VMEM)
    hbm = pl.BlockSpec(memory_space=pltpu.HBM)
    anywhere = pl.BlockSpec(memory_space=pl.ANY)

    def params(mib):
        return pltpu.CompilerParams(vmem_limit_bytes=mib * MIB)

    tile_reflect = reflect[0].reshape(slots * rows, columns)
    halo = lax.ppermute(tile_reflect, "tile", [(i, i + 1) for i in range(plan.tiles - 1)])
    part = columns + rows // 2
    half_rows, win_rows = slots * part, slots * rows + TAIL
    early_rows = 2 * (half_rows - part) + win_rows
    even = pltpu.VMEM((early_rows + 2 * TAIL, columns), bf16)
    odd = pltpu.VMEM((early_rows, columns), bf16)
    even_early, odd_early, late, far_half = pl.pallas_call(
        functools.partial(pack_kernel, group, sizes),
        out_shape=[
            even,
            odd,
            jax.ShapeDtypeStruct((2 * part, columns), bf16),
            jax.ShapeDtypeStruct((half_rows, columns), bf16),
        ],
        in_specs=[hbm, hbm],
        out_specs=[vmem] * 4,
        scratch_shapes=[
            pltpu.VMEM(lateral_x.shape[1:], bf16),
            pltpu.VMEM(lateral_y.shape[1:], bf16),
            pltpu.SemaphoreType.DMA((2,)),
        ],
        compiler_params=params(12),
        name="pack",
    )(kept(lateral_x[0]), kept(lateral_y[0]))
    last = sections - 1
    far_half = lax.ppermute(far_half, BOTH, plan.to_workers(last))
    even_early, odd_early, far_window = pl.pallas_call(
        functools.partial(window_kernel, shots, sizes),
        out_shape=[even, odd, jax.ShapeDtypeStruct((win_rows, columns), bf16)],
        in_specs=[hbm, smem, vmem, hbm, vmem, vmem],
        out_specs=[vmem] * 3,
        scratch_shapes=[
            pltpu.SMEM((shots,), jnp.int32),
            pltpu.VMEM((slots * rows, columns), bf16),
            pltpu.SemaphoreType.DMA((2,)),
        ],
        input_output_aliases={4: 0, 5: 1},
        compiler_params=params(12),
        cost_estimate=pl.CostEstimate(flops=3 * 10**9, bytes_accessed=4 * MIB, transcendentals=0),
        name="windows",
    )(kept(anchors), counts, halo, kept(tile_reflect), held(even_early), held(odd_early))
    messages = [
        even_early,
        lax.ppermute(odd_early, BOTH, plan.to_workers(1)),
        lax.ppermute(even_early, BOTH, plan.to_workers(2)),
    ]
    far_window = lax.ppermute(far_window, BOTH, plan.to_workers(last))
    other_half = lax.ppermute(far_half, BOTH, plan.swap_workers())
    late = pl.pallas_call(
        hold_kernel,
        out_shape=jax.ShapeDtypeStruct(late.shape, bf16),
        in_specs=[anywhere] * 2,
        out_specs=anywhere,
        input_output_aliases={0: 0},
        compiler_params=params(2),
        cost_estimate=pl.CostEstimate(flops=352 * 10**7, bytes_accessed=0, transcendentals=0),
        name="hold",
    )(late, far_window)
    lates = [lax.ppermute(late, BOTH, plan.ops_to_workers(r)) for r in (1, 2)]
    joined, shifts = pl.pallas_call(
        functools.partial(join_kernel, shots, group),
        out_shape=[
            pltpu.VMEM((2 * half_rows, columns), bf16),
            pltpu.VMEM((shots, columns, 2 * columns), bf16),
        ],
        in_specs=[smem] + [vmem] * 2,
        out_specs=[vmem] * 2,
        compiler_params=params(8),
        name="join",
    )(anchors, held(far_half), held(other_half))

    levels = sections * slots
    buffers = [
        pltpu.VMEM((levels, 2 * columns, columns), bf16),
        pltpu.VMEM((levels, 2 * rows, 2 * rows), bf16),
        pltpu.VMEM((levels, rows, columns), bf16),
        pltpu.VMEM((levels + 1, 2 * rows, columns), bf16),
    ]
    stages = [pltpu.VMEM((2 * columns, columns), bf16), pltpu.VMEM((rows, 2 * rows), bf16)]
    messages = [held(message) for message in messages]
    late, joined, far_window = held(late), held(joined), held(far_window)
    filled = pl.pallas_call(
        functools.partial(down_kernel, sections, shots, group, sizes),
        out_shape=buffers,
        in_specs=[vmem] * 7,
        out_specs=[vmem] * 4,
        scratch_shapes=stages + [pltpu.SMEM((sections,), jnp.int32)],
        compiler_params=params(24),
        name="down",
    )(held(source.reshape(shots, 2 * rows, columns)), *messages, late, joined, far_window)
    correlations = pl.pallas_call(
        functools.partial(up_kernel, sections, shots, group, sizes),
        out_shape=[
            jax.ShapeDtypeStruct((slots * rows + TAIL * more, columns), bf16)
            for more in (0, 0, 1, 2)
        ]
        + buffers,
        in_specs=[vmem] * 12,
        out_specs=[vmem] * (sections + 4),
        scratch_shapes=stages
        + [pltpu.VMEM((2 * rows, columns), bf16), pltpu.SMEM((sections,), jnp.int32)],
        input_output_aliases={8 + i: sections + i for i in range(4)},
        compiler_params=params(24),
        name="up",
    )(
        *messages, late, *[held(part) for part in lates], joined, far_window,
        *[held(buffer) for buffer in filled],
    )

    corr_shape = jax.ShapeDtypeStruct((slots * rows, columns), bf16)
    arrived = [correlations[0]] + [
        lax.ppermute(correlations[r], BOTH, plan.from_workers(r)) for r in range(1, sections)
    ]
    left, own = pl.pallas_call(
        functools.partial(place_kernel, shots),
        out_shape=[corr_shape, jax.ShapeDtypeStruct((slots * rows, columns), jnp.float32)],
        in_specs=[vmem] * (1 + sections),
        out_specs=[vmem, vmem],
        compiler_params=params(8),
        name="place",
    )(held(shifts), *[held(part) for part in arrived])
    from_right = lax.ppermute(left, "tile", [(i + 1, i) for i in range(plan.tiles - 1)])
    image = own + from_right.astype(jnp.float32)
    return image.reshape(1, slots, rows, columns)


def solution(mesh):
    return jax.shard_map(
        on_device,
        mesh=mesh,
        in_specs=(
            P("tile", None, None, None),
            P("tile"),
            P("depth"),
            P("depth", None, None, "tile"),
            P("depth", None, None, None, None),
            P("depth", None, None, None, None),
        ),
        out_specs=P("depth", None, None, "tile"),
        check_vma=False,
    )
```

```python
import functools

import jax
import jax.numpy as jnp
from jax import lax
from jax.experimental import pallas as pl
from jax.experimental.pallas import tpu as pltpu
from jax.sharding import PartitionSpec as P

BOTH = ("depth", "tile")
MIB = 1024 * 1024
TAIL = 16


class Plan:
    def __init__(self, shots):
        self.sections = lax.axis_size("depth")
        self.tiles = lax.axis_size("tile")
        self.shots = shots
        self.group = self.sections // shots
        assert self.sections == 4 and self.group * shots == self.sections
        assert self.tiles % (2 * self.group) == 0

    def device(self, depth, tile):
        return depth * self.tiles + tile

    def bases(self):
        return range(0, self.tiles, self.group)

    def worker(self, base, w):
        return self.device(w, base + w // self.shots)

    def other(self, w, base):
        return self.device(w, base + (w // self.shots + 1) % self.group)

    def ops_to_workers(self, r):
        return [
            (self.other(w ^ r, base), self.worker(base, w))
            for base in self.bases()
            for w in range(self.sections)
        ]

    def swap_workers(self):
        return [
            (self.worker(base, w), self.worker((base // self.group ^ 1) * self.group, w))
            for base in self.bases()
            for w in range(self.sections)
        ]

    def to_workers(self, r):
        return [
            (self.device(w ^ r, base + w // self.shots), self.worker(base, w))
            for base in self.bases()
            for w in range(self.sections)
        ]

    def from_workers(self, r):
        return [(b, a) for a, b in self.to_workers(r)]


def pack_kernel(group, sizes, x_hbm, y_hbm, even, odd, late, half_out, x_ref, y_ref, sem):
    slots, rows, columns = sizes
    loads = [
        pltpu.make_async_copy(x_hbm, x_ref, sem.at[0]),
        pltpu.make_async_copy(y_hbm, y_ref, sem.at[1]),
    ]
    for load in loads:
        load.start()
    for load in loads:
        load.wait()
    piece = rows // 2
    part = columns + piece
    first = (slots - 1) * part
    for half in range(2):
        for slot in range(slots):
            op_x = jnp.concatenate(
                [x_ref[slot, i, half * piece : (half + 1) * piece, :] for i in range(2)], axis=1
            )
            op_y = y_ref[slot, half]
            if slot < slots - 1:
                places = [(out, half * first + slot * part) for out in (even, odd)]
            else:
                places = [(late, half * part)]
            for out, spot in places:
                out[spot : spot + columns, :] = op_y
                out[spot + columns : spot + part, :] = op_x
    plane = lax.rem(lax.axis_index("tile") // group, 2)
    half_out[:first, :] = even[pl.ds(pl.multiple_of(plane * first, first), first), :]
    half_out[first:, :] = late[pl.ds(pl.multiple_of(plane * part, part), part), :]


def window_kernel(shots, sizes, anchors_hbm, counts, left_ref, right_hbm, *refs):
    slots, rows, columns = sizes
    messages, (alone, anchors, right_ref, sem) = refs[shots : 2 * shots], refs[2 * shots :]
    loads = [
        pltpu.make_async_copy(anchors_hbm, anchors, sem.at[0]),
        pltpu.make_async_copy(right_hbm, right_ref, sem.at[1]),
    ]
    for load in loads:
        load.start()
    for load in loads:
        load.wait()
    section, tile = lax.axis_index("depth"), lax.axis_index("tile")
    left, right = left_ref[...].astype(jnp.float32), right_ref[...].astype(jnp.float32)
    lanes = lax.broadcasted_iota(jnp.int32, left.shape, 1)
    tail = jnp.full((TAIL, columns), counts[0].astype(jnp.float32), jnp.float32)
    for q, message in enumerate(messages):
        offset = anchors[lax.rem(section, shots) ^ q] - (tile - 1) * columns
        merged = jnp.where(lanes >= offset, left, right)
        back = lax.rem(columns - lax.rem(offset, columns), columns)
        window = pltpu.roll(merged, back, 1).astype(message.dtype)
        for out in [message] + ([alone] if q == shots - 1 else []):
            spot = out.shape[0] - TAIL - slots * rows
            out[spot : spot + slots * rows, :] = window
            out[spot + slots * rows :, :] = tail.astype(out.dtype)


class Sweep:
    def __init__(self, shots, group, sizes, turned_y, turned_x, level_w, waves, stage_y, stage_x):
        self.sizes = sizes
        self.turned_y, self.turned_x, self.level_w = turned_y, turned_x, level_w
        self.waves, self.stage_y, self.stage_x = waves, stage_y, stage_x
        slots, rows, columns = sizes
        self.piece = rows // 2
        self.part = columns + self.piece
        self.first = (slots - 1) * self.part
        self.half_rows = self.first + self.part
        self.win_rows = slots * rows + TAIL
        self.here, tile = lax.axis_index("depth"), lax.axis_index("tile")
        self.shot = lax.rem(self.here, shots)
        self.is_worker = (self.here // shots == lax.rem(tile, group)).astype(jnp.int32)

    def read_counts(self, sources, counts):
        for r, (_, _, window) in enumerate(sources):
            value = jnp.max(window[window.shape[0] - TAIL :, :].astype(jnp.float32))
            counts[r] = value.astype(jnp.int32)

    def early_slots(self, r, count, rounds):
        partial = (r != 0) & (r != rounds - 1)
        return jnp.where(partial, jnp.minimum(count, self.sizes[0] - 1), count)

    def window_start(self, window_ref):
        return window_ref.shape[0] - self.win_rows

    def fetch(self, r, slot, place, sources):
        slots, rows, columns = self.sizes
        for r_of, (early, late, window) in enumerate(sources):
            early_slots = slots if early.shape[0] == 2 * self.half_rows else slots - 1
            choices = [(early, early_slots * self.part, slot < early_slots, slot)]
            if late is not None:
                choices.append((late, self.part, slot == slots - 1, 0))
            for ref, stride, chosen, at in choices:

                @pl.when((r == r_of) & chosen)
                def _():
                    for half in range(2):
                        start = pl.multiple_of(half * stride + at * self.part, self.piece)
                        self.stage_y[half * columns : (half + 1) * columns, :] = ref[
                            pl.ds(start, columns), :
                        ]
                        tail = pl.multiple_of(start + columns, self.piece)
                        self.stage_x[half * self.piece : (half + 1) * self.piece, :] = ref[
                            pl.ds(tail, self.piece), :
                        ]
                    spot = self.window_start(window) + slot * rows
                    self.level_w[place] = window[pl.ds(pl.multiple_of(spot, TAIL), rows), :]

    def blocks(self, re, im):
        upper = jnp.concatenate([re, -im], axis=1)
        return jnp.concatenate([upper, jnp.concatenate([im, re], axis=1)], axis=0)

    def complex_sum(self, both):
        _, rows, columns = self.sizes
        with_re, with_im = both[:, :columns], both[:, columns:]
        return with_re[:rows] - with_im[rows:], with_im[:rows] + with_re[rows:]

    def dot(self, a, b, dims):
        return lax.dot_general(a, b, (dims, ((), ())), preferred_element_type=jnp.float32)

    def down(self, place):
        _, rows, columns = self.sizes
        x_re, x_im = self.stage_x[:, :rows], self.stage_x[:, rows:]
        wave = self.waves[place].astype(jnp.float32)
        gain = 1.0 + self.level_w[place].astype(jnp.float32)
        scaled = jnp.concatenate([gain * wave[:rows], gain * wave[rows:]], axis=0)
        self.turned_x[place] = self.blocks(x_re.T, x_im.T)
        middle = self.dot(self.blocks(x_re, x_im), scaled.astype(jnp.bfloat16), ((1,), (0,)))
        for i in range(2):
            lines = slice(i * columns, (i + 1) * columns)
            self.turned_y[place, lines, :] = self.stage_y[lines, :].T
        both = self.dot(middle.astype(jnp.bfloat16), self.stage_y[...], ((1,), (1,)))
        moved = jnp.concatenate(self.complex_sum(both), axis=0)
        self.waves[place + 1] = moved.astype(jnp.bfloat16)
        return place + 1

    def up(self, r, slot, place, wave_up, outs):
        _, rows, columns = self.sizes
        level = place - 1
        wave = self.waves[level].astype(jnp.float32)
        window = self.level_w[level].astype(jnp.float32)
        back = self.dot(self.turned_x[level], wave_up[...], ((1,), (0,)))
        both = self.dot(back.astype(jnp.bfloat16), self.turned_y[level], ((1,), (1,)))
        spread_re, spread_im = self.complex_sum(both)
        up_re = (window * wave[:rows] + spread_re).astype(jnp.bfloat16)
        up_im = (window * wave[rows:] + spread_im).astype(jnp.bfloat16)
        wave_up[:rows] = up_re
        wave_up[rows:] = up_im
        product = wave[:rows] * up_re.astype(jnp.float32)
        product += wave[rows:] * up_im.astype(jnp.float32)
        spot = pl.multiple_of(slot * rows, rows)
        for r_of, out in enumerate(outs):

            @pl.when(r == r_of)
            def _():
                out[pl.ds(spot, rows), :] = product.astype(out.dtype)

        return level


def down_kernel(sections, shots, group, sizes, source_ref, *refs):
    (own, near, far), (own_late, joined, far_window) = refs[:3], refs[3:6]
    *buffers, stage_y, stage_x, counts = refs[6:]
    it = Sweep(shots, group, sizes, *buffers, stage_y, stage_x)
    sources = [
        (own, own_late, own),
        (near, None, near),
        (far, None, far),
        (joined, None, far_window),
    ]

    @pl.when(it.is_worker != 0)
    def _():
        it.waves[0] = source_ref[it.shot]
        it.read_counts(sources, counts)

        def section_down(section, carry):
            place, going = carry
            r = section ^ it.here
            ready = it.early_slots(r, counts[r], sections)

            def level_down(slot, place):
                it.fetch(r, slot, place, sources)
                return it.down(place)

            place = lax.fori_loop(0, jnp.where(going, ready, 0), level_down, place)
            return place, going & (ready == counts[r])

        lax.fori_loop(0, sections, section_down, (jnp.int32(0), jnp.bool_(True)))


def up_kernel(sections, shots, group, sizes, *refs):
    (own, near, far), (own_late, near_late, far_late, joined, far_window) = refs[:3], refs[3:8]
    outs, refs = refs[12 : 12 + sections], refs[12 + sections :]
    *buffers, stage_y, stage_x, wave_up, counts = refs
    it = Sweep(shots, group, sizes, *buffers, stage_y, stage_x)
    sources = [
        (own, own_late, own),
        (near, near_late, near),
        (far, far_late, far),
        (joined, None, far_window),
    ]

    @pl.when(it.is_worker == 0)
    def _():
        outs[0][...] = jnp.zeros(outs[0].shape, outs[0].dtype)

    @pl.when(it.is_worker != 0)
    def _():
        it.read_counts(sources, counts)
        for out in outs:
            out[...] = jnp.zeros(out.shape, out.dtype)
        wave_up[...] = jnp.zeros(wave_up.shape, wave_up.dtype)

        def section_down(section, carry):
            place, going = carry
            r = section ^ it.here
            done = jnp.where(going, it.early_slots(r, counts[r], sections), 0)

            def level_down(slot, place):
                it.fetch(r, slot, place, sources)
                return it.down(place)

            place = lax.fori_loop(done, counts[r], level_down, place + done)
            return place, going & (done == counts[r])

        last, _ = lax.fori_loop(0, sections, section_down, (jnp.int32(0), jnp.bool_(True)))

        def section_up(step, place):
            r = (sections - 1 - step) ^ it.here
            count = counts[r]
            return lax.fori_loop(
                0,
                count,
                lambda inner, place: it.up(r, count - 1 - inner, place, wave_up, outs),
                place,
            )

        lax.fori_loop(0, sections, section_up, last)


def join_kernel(shots, group, anchors, first_ref, second_ref, out_ref, shifts):
    section, tile = lax.axis_index("depth"), lax.axis_index("tile")
    plane = lax.rem(tile // group, 2)
    half_rows = first_ref.shape[0]
    for i, ref in enumerate((first_ref, second_ref)):
        start = pl.multiple_of((plane if i == 0 else 1 - plane) * half_rows, half_rows)
        out_ref[pl.ds(start, half_rows), :] = ref[...]
    columns = shifts.shape[1]
    place = lax.broadcasted_iota(jnp.int32, shifts.shape[1:], 1)
    start = lax.broadcasted_iota(jnp.int32, shifts.shape[1:], 0)
    for q in range(shots):
        offset = anchors[lax.rem(section, shots) ^ q] - (tile - 1) * columns
        shifts[q] = (place - start == offset).astype(jnp.float32).astype(shifts.dtype)


def hold_kernel(array_ref, after_ref, out_ref):
    pass


def place_kernel(shots, shifts, *refs):
    arrived, (left_out, own_out) = refs[:-2], refs[-2:]
    places, columns = left_out.shape
    placed = None
    for q in range(shots):
        total = None
        for r in range(q, len(arrived), shots):
            value = arrived[r][:places, :]
            total = value if total is None else total + value
        part = jnp.dot(total, shifts[q], preferred_element_type=jnp.float32)
        placed = part if placed is None else placed + part
    left_out[...] = placed[:, :columns].astype(left_out.dtype)
    own_out[...] = placed[:, columns:]


def sum_kernel(slots, own, other, out_hbm, held_sum, sem):
    rows = own.shape[0] // slots
    copies = []
    for slot in range(slots):
        lines = pl.ds(slot * rows, rows)
        held_sum[lines, :] = own[lines, :] + other[lines, :].astype(jnp.float32)
        copy = pltpu.make_async_copy(held_sum.at[lines, :], out_hbm.at[lines, :], sem.at[slot])
        copy.start()
        copies.append(copy)
    for copy in copies:
        copy.wait()


def kept(array):
    return pltpu.with_memory_space_constraint(array, pltpu.HBM)


def held(array):
    return pltpu.with_memory_space_constraint(array, pltpu.VMEM)


def on_device(source, anchors, counts, reflect, lateral_x, lateral_y):
    shots, _, rows, columns = source.shape
    slots = reflect.shape[1]
    sizes = (slots, rows, columns)
    plan = Plan(shots)
    sections, group = plan.sections, plan.group
    assert shots == 2
    bf16 = jnp.bfloat16
    smem = pl.BlockSpec(memory_space=pltpu.SMEM)
    vmem = pl.BlockSpec(memory_space=pltpu.VMEM)
    hbm = pl.BlockSpec(memory_space=pltpu.HBM)
    anywhere = pl.BlockSpec(memory_space=pl.ANY)

    def params(mib):
        return pltpu.CompilerParams(vmem_limit_bytes=mib * MIB)

    tile_reflect = reflect[0].reshape(slots * rows, columns)
    halo = lax.ppermute(tile_reflect, "tile", [(i, i + 1) for i in range(plan.tiles - 1)])
    part = columns + rows // 2
    half_rows, win_rows = slots * part, slots * rows + TAIL
    early_rows = 2 * (half_rows - part) + win_rows
    even = pltpu.VMEM((early_rows + 2 * TAIL, columns), bf16)
    odd = pltpu.VMEM((early_rows, columns), bf16)
    even_early, odd_early, late, far_half = pl.pallas_call(
        functools.partial(pack_kernel, group, sizes),
        out_shape=[
            even,
            odd,
            jax.ShapeDtypeStruct((2 * part, columns), bf16),
            jax.ShapeDtypeStruct((half_rows, columns), bf16),
        ],
        in_specs=[hbm, hbm],
        out_specs=[vmem] * 4,
        scratch_shapes=[
            pltpu.VMEM(lateral_x.shape[1:], bf16),
            pltpu.VMEM(lateral_y.shape[1:], bf16),
            pltpu.SemaphoreType.DMA((2,)),
        ],
        compiler_params=params(12),
        name="pack",
    )(kept(lateral_x[0]), kept(lateral_y[0]))
    last = sections - 1
    far_half = lax.ppermute(far_half, BOTH, plan.to_workers(last))
    even_early, odd_early, far_window = pl.pallas_call(
        functools.partial(window_kernel, shots, sizes),
        out_shape=[even, odd, jax.ShapeDtypeStruct((win_rows, columns), bf16)],
        in_specs=[hbm, smem, vmem, hbm, vmem, vmem],
        out_specs=[vmem] * 3,
        scratch_shapes=[
            pltpu.SMEM((shots,), jnp.int32),
            pltpu.VMEM((slots * rows, columns), bf16),
            pltpu.SemaphoreType.DMA((2,)),
        ],
        input_output_aliases={4: 0, 5: 1},
        compiler_params=params(12),
        cost_estimate=pl.CostEstimate(flops=3 * 10**9, bytes_accessed=4 * MIB, transcendentals=0),
        name="windows",
    )(kept(anchors), counts, halo, kept(tile_reflect), held(even_early), held(odd_early))
    messages = [
        even_early,
        lax.ppermute(odd_early, BOTH, plan.to_workers(1)),
        lax.ppermute(even_early, BOTH, plan.to_workers(2)),
    ]
    far_window = lax.ppermute(far_window, BOTH, plan.to_workers(last))
    other_half = lax.ppermute(far_half, BOTH, plan.swap_workers())
    late = pl.pallas_call(
        hold_kernel,
        out_shape=jax.ShapeDtypeStruct(late.shape, bf16),
        in_specs=[anywhere] * 2,
        out_specs=anywhere,
        input_output_aliases={0: 0},
        compiler_params=params(2),
        cost_estimate=pl.CostEstimate(flops=352 * 10**7, bytes_accessed=0, transcendentals=0),
        name="hold",
    )(late, far_window)
    lates = [lax.ppermute(late, BOTH, plan.ops_to_workers(r)) for r in (1, 2)]
    joined, shifts = pl.pallas_call(
        functools.partial(join_kernel, shots, group),
        out_shape=[
            pltpu.VMEM((2 * half_rows, columns), bf16),
            pltpu.VMEM((shots, columns, 2 * columns), bf16),
        ],
        in_specs=[smem] + [vmem] * 2,
        out_specs=[vmem] * 2,
        compiler_params=params(8),
        name="join",
    )(anchors, held(far_half), held(other_half))

    levels = sections * slots
    buffers = [
        pltpu.VMEM((levels, 2 * columns, columns), bf16),
        pltpu.VMEM((levels, 2 * rows, 2 * rows), bf16),
        pltpu.VMEM((levels, rows, columns), bf16),
        pltpu.VMEM((levels + 1, 2 * rows, columns), bf16),
    ]
    stages = [pltpu.VMEM((2 * columns, columns), bf16), pltpu.VMEM((rows, 2 * rows), bf16)]
    messages = [held(message) for message in messages]
    late, joined, far_window = held(late), held(joined), held(far_window)
    filled = pl.pallas_call(
        functools.partial(down_kernel, sections, shots, group, sizes),
        out_shape=buffers,
        in_specs=[vmem] * 7,
        out_specs=[vmem] * 4,
        scratch_shapes=stages + [pltpu.SMEM((sections,), jnp.int32)],
        compiler_params=params(24),
        name="down",
    )(held(source.reshape(shots, 2 * rows, columns)), *messages, late, joined, far_window)
    correlations = pl.pallas_call(
        functools.partial(up_kernel, sections, shots, group, sizes),
        out_shape=[
            jax.ShapeDtypeStruct((slots * rows + TAIL * more, columns), bf16)
            for more in (0, 0, 1, 2)
        ]
        + buffers,
        in_specs=[vmem] * 12,
        out_specs=[vmem] * (sections + 4),
        scratch_shapes=stages
        + [pltpu.VMEM((2 * rows, columns), bf16), pltpu.SMEM((sections,), jnp.int32)],
        input_output_aliases={8 + i: sections + i for i in range(4)},
        compiler_params=params(24),
        name="up",
    )(
        *messages, late, *[held(part) for part in lates], joined, far_window,
        *[held(buffer) for buffer in filled],
    )

    corr_shape = jax.ShapeDtypeStruct((slots * rows, columns), bf16)
    arrived = [correlations[0]] + [
        lax.ppermute(correlations[r], BOTH, plan.from_workers(r)) for r in range(1, sections)
    ]
    left, own = pl.pallas_call(
        functools.partial(place_kernel, shots),
        out_shape=[corr_shape, jax.ShapeDtypeStruct((slots * rows, columns), jnp.float32)],
        in_specs=[vmem] * (1 + sections),
        out_specs=[vmem, vmem],
        compiler_params=params(8),
        name="place",
    )(held(shifts), *[held(part) for part in arrived])
    from_right = lax.ppermute(left, "tile", [(i + 1, i) for i in range(plan.tiles - 1)])
    image = pl.pallas_call(
        functools.partial(sum_kernel, slots),
        out_shape=jax.ShapeDtypeStruct(own.shape, jnp.float32),
        in_specs=[vmem, vmem],
        out_specs=anywhere,
        scratch_shapes=[pltpu.VMEM(own.shape, jnp.float32), pltpu.SemaphoreType.DMA((slots,))],
        compiler_params=params(8),
        name="sum",
    )(held(own), held(from_right))
    return image.reshape(1, slots, rows, columns)


def solution(mesh):
    return jax.shard_map(
        on_device,
        mesh=mesh,
        in_specs=(
            P("tile", None, None, None),
            P("tile"),
            P("depth"),
            P("depth", None, None, "tile"),
            P("depth", None, None, None, None),
            P("depth", None, None, None, None),
        ),
        out_specs=P("depth", None, None, "tile"),
        check_vma=False,
    )
```

```python
import functools

import jax
import jax.numpy as jnp
from jax import lax
from jax.experimental import pallas as pl
from jax.experimental.pallas import tpu as pltpu
from jax.sharding import PartitionSpec as P

BOTH = ("depth", "tile")
MIB = 1024 * 1024
TAIL = 16


class Plan:
    def __init__(self, shots):
        self.sections = lax.axis_size("depth")
        self.tiles = lax.axis_size("tile")
        self.shots = shots
        self.group = self.sections // shots
        assert self.sections == 4 and self.group * shots == self.sections
        assert self.tiles % (2 * self.group) == 0

    def device(self, depth, tile):
        return depth * self.tiles + tile

    def bases(self):
        return range(0, self.tiles, self.group)

    def worker(self, base, w):
        return self.device(w, base + w // self.shots)

    def other(self, w, base):
        return self.device(w, base + (w // self.shots + 1) % self.group)

    def ops_to_workers(self, r):
        return [
            (self.other(w ^ r, base), self.worker(base, w))
            for base in self.bases()
            for w in range(self.sections)
        ]

    def swap_workers(self):
        return [
            (self.worker(base, w), self.worker((base // self.group ^ 1) * self.group, w))
            for base in self.bases()
            for w in range(self.sections)
        ]

    def to_workers(self, r):
        return [
            (self.device(w ^ r, base + w // self.shots), self.worker(base, w))
            for base in self.bases()
            for w in range(self.sections)
        ]

    def from_workers(self, r):
        return [(b, a) for a, b in self.to_workers(r)]


def pack_kernel(group, sizes, x_hbm, y_hbm, even, odd, late, half_out, x_ref, y_ref, sem):
    slots, rows, columns = sizes
    loads = [
        pltpu.make_async_copy(x_hbm, x_ref, sem.at[0]),
        pltpu.make_async_copy(y_hbm, y_ref, sem.at[1]),
    ]
    for load in loads:
        load.start()
    for load in loads:
        load.wait()
    piece = rows // 2
    part = columns + piece
    first = (slots - 1) * part
    for half in range(2):
        for slot in range(slots):
            op_x = jnp.concatenate(
                [x_ref[slot, i, half * piece : (half + 1) * piece, :] for i in range(2)], axis=1
            )
            op_y = y_ref[slot, half]
            if slot < slots - 1:
                places = [(out, half * first + slot * part) for out in (even, odd)]
            else:
                places = [(late, half * part)]
            for out, spot in places:
                out[spot : spot + columns, :] = op_y
                out[spot + columns : spot + part, :] = op_x
    plane = lax.rem(lax.axis_index("tile") // group, 2)
    half_out[:first, :] = even[pl.ds(pl.multiple_of(plane * first, first), first), :]
    half_out[first:, :] = late[pl.ds(pl.multiple_of(plane * part, part), part), :]


def window_kernel(shots, sizes, anchors_hbm, counts, left_ref, right_hbm, *refs):
    slots, rows, columns = sizes
    messages, (alone, anchors, right_ref, sem) = refs[shots : 2 * shots], refs[2 * shots :]
    loads = [
        pltpu.make_async_copy(anchors_hbm, anchors, sem.at[0]),
        pltpu.make_async_copy(right_hbm, right_ref, sem.at[1]),
    ]
    for load in loads:
        load.start()
    for load in loads:
        load.wait()
    section, tile = lax.axis_index("depth"), lax.axis_index("tile")
    left, right = left_ref[...].astype(jnp.float32), right_ref[...].astype(jnp.float32)
    lanes = lax.broadcasted_iota(jnp.int32, left.shape, 1)
    tail = jnp.full((TAIL, columns), counts[0].astype(jnp.float32), jnp.float32)
    for q, message in enumerate(messages):
        offset = anchors[lax.rem(section, shots) ^ q] - (tile - 1) * columns
        merged = jnp.where(lanes >= offset, left, right)
        back = lax.rem(columns - lax.rem(offset, columns), columns)
        window = pltpu.roll(merged, back, 1).astype(message.dtype)
        for out in [message] + ([alone] if q == shots - 1 else []):
            spot = out.shape[0] - TAIL - slots * rows
            out[spot : spot + slots * rows, :] = window
            out[spot + slots * rows :, :] = tail.astype(out.dtype)


class Sweep:
    def __init__(self, shots, group, sizes, turned_y, turned_x, level_w, waves, stage_y, stage_x):
        self.sizes = sizes
        self.turned_y, self.turned_x, self.level_w = turned_y, turned_x, level_w
        self.waves, self.stage_y, self.stage_x = waves, stage_y, stage_x
        slots, rows, columns = sizes
        self.piece = rows // 2
        self.part = columns + self.piece
        self.first = (slots - 1) * self.part
        self.half_rows = self.first + self.part
        self.win_rows = slots * rows + TAIL
        self.here, tile = lax.axis_index("depth"), lax.axis_index("tile")
        self.shot = lax.rem(self.here, shots)
        self.is_worker = (self.here // shots == lax.rem(tile, group)).astype(jnp.int32)

    def read_counts(self, sources, counts):
        for r, (_, _, window) in enumerate(sources):
            value = jnp.max(window[window.shape[0] - TAIL :, :].astype(jnp.float32))
            counts[r] = value.astype(jnp.int32)

    def early_slots(self, r, count, rounds):
        partial = (r != 0) & (r != rounds - 1)
        return jnp.where(partial, jnp.minimum(count, self.sizes[0] - 1), count)

    def window_start(self, window_ref):
        return window_ref.shape[0] - self.win_rows

    def fetch(self, r, slot, place, sources):
        slots, rows, columns = self.sizes
        for r_of, (early, late, window) in enumerate(sources):
            early_slots = slots if early.shape[0] == 2 * self.half_rows else slots - 1
            choices = [(early, early_slots * self.part, slot < early_slots, slot)]
            if late is not None:
                choices.append((late, self.part, slot == slots - 1, 0))
            for ref, stride, chosen, at in choices:

                @pl.when((r == r_of) & chosen)
                def _():
                    for half in range(2):
                        start = pl.multiple_of(half * stride + at * self.part, self.piece)
                        self.stage_y[half * columns : (half + 1) * columns, :] = ref[
                            pl.ds(start, columns), :
                        ]
                        tail = pl.multiple_of(start + columns, self.piece)
                        self.stage_x[half * self.piece : (half + 1) * self.piece, :] = ref[
                            pl.ds(tail, self.piece), :
                        ]
                    spot = self.window_start(window) + slot * rows
                    self.level_w[place] = window[pl.ds(pl.multiple_of(spot, TAIL), rows), :]

    def blocks(self, re, im):
        upper = jnp.concatenate([re, -im], axis=1)
        return jnp.concatenate([upper, jnp.concatenate([im, re], axis=1)], axis=0)

    def complex_sum(self, both):
        _, rows, columns = self.sizes
        with_re, with_im = both[:, :columns], both[:, columns:]
        return with_re[:rows] - with_im[rows:], with_im[:rows] + with_re[rows:]

    def dot(self, a, b, dims):
        return lax.dot_general(a, b, (dims, ((), ())), preferred_element_type=jnp.float32)

    def down(self, place):
        _, rows, columns = self.sizes
        x_re, x_im = self.stage_x[:, :rows], self.stage_x[:, rows:]
        wave = self.waves[place].astype(jnp.float32)
        gain = 1.0 + self.level_w[place].astype(jnp.float32)
        scaled = jnp.concatenate([gain * wave[:rows], gain * wave[rows:]], axis=0)
        self.turned_x[place] = self.blocks(x_re.T, x_im.T)
        middle = self.dot(self.blocks(x_re, x_im), scaled.astype(jnp.bfloat16), ((1,), (0,)))
        for i in range(2):
            lines = slice(i * columns, (i + 1) * columns)
            self.turned_y[place, lines, :] = self.stage_y[lines, :].T
        both = self.dot(middle.astype(jnp.bfloat16), self.stage_y[...], ((1,), (1,)))
        moved = jnp.concatenate(self.complex_sum(both), axis=0)
        self.waves[place + 1] = moved.astype(jnp.bfloat16)
        return place + 1

    def up(self, r, slot, place, wave_up, outs):
        _, rows, columns = self.sizes
        level = place - 1
        wave = self.waves[level].astype(jnp.float32)
        window = self.level_w[level].astype(jnp.float32)
        back = self.dot(self.turned_x[level], wave_up[...], ((1,), (0,)))
        both = self.dot(back.astype(jnp.bfloat16), self.turned_y[level], ((1,), (1,)))
        spread_re, spread_im = self.complex_sum(both)
        up_re = (window * wave[:rows] + spread_re).astype(jnp.bfloat16)
        up_im = (window * wave[rows:] + spread_im).astype(jnp.bfloat16)
        wave_up[:rows] = up_re
        wave_up[rows:] = up_im
        product = wave[:rows] * up_re.astype(jnp.float32)
        product += wave[rows:] * up_im.astype(jnp.float32)
        spot = pl.multiple_of(slot * rows, rows)
        for r_of, out in enumerate(outs):

            @pl.when(r == r_of)
            def _():
                out[pl.ds(spot, rows), :] = product.astype(out.dtype)

        return level


def down_kernel(sections, shots, group, sizes, source_ref, *refs):
    (own, near, far), (own_late, joined, far_window) = refs[:3], refs[3:6]
    *buffers, stage_y, stage_x, counts = refs[6:]
    it = Sweep(shots, group, sizes, *buffers, stage_y, stage_x)
    sources = [
        (own, own_late, own),
        (near, None, near),
        (far, None, far),
        (joined, None, far_window),
    ]

    @pl.when(it.is_worker != 0)
    def _():
        it.waves[0] = source_ref[it.shot]
        it.read_counts(sources, counts)

        def section_down(section, carry):
            place, going = carry
            r = section ^ it.here
            ready = it.early_slots(r, counts[r], sections)

            def level_down(slot, place):
                it.fetch(r, slot, place, sources)
                return it.down(place)

            place = lax.fori_loop(0, jnp.where(going, ready, 0), level_down, place)
            return place, going & (ready == counts[r])

        lax.fori_loop(0, sections, section_down, (jnp.int32(0), jnp.bool_(True)))


def up_kernel(sections, shots, group, sizes, *refs):
    (own, near, far), (own_late, near_late, far_late, joined, far_window) = refs[:3], refs[3:8]
    outs, refs = refs[12 : 12 + sections], refs[12 + sections :]
    *buffers, stage_y, stage_x, wave_up, counts = refs
    it = Sweep(shots, group, sizes, *buffers, stage_y, stage_x)
    sources = [
        (own, own_late, own),
        (near, near_late, near),
        (far, far_late, far),
        (joined, None, far_window),
    ]

    @pl.when(it.is_worker == 0)
    def _():
        outs[0][...] = jnp.zeros(outs[0].shape, outs[0].dtype)

    @pl.when(it.is_worker != 0)
    def _():
        it.read_counts(sources, counts)
        for out in outs:
            out[...] = jnp.zeros(out.shape, out.dtype)
        wave_up[...] = jnp.zeros(wave_up.shape, wave_up.dtype)

        def section_down(section, carry):
            place, going = carry
            r = section ^ it.here
            done = jnp.where(going, it.early_slots(r, counts[r], sections), 0)

            def level_down(slot, place):
                it.fetch(r, slot, place, sources)
                return it.down(place)

            place = lax.fori_loop(done, counts[r], level_down, place + done)
            return place, going & (done == counts[r])

        last, _ = lax.fori_loop(0, sections, section_down, (jnp.int32(0), jnp.bool_(True)))

        def section_up(step, place):
            r = (sections - 1 - step) ^ it.here
            count = counts[r]
            return lax.fori_loop(
                0,
                count,
                lambda inner, place: it.up(r, count - 1 - inner, place, wave_up, outs),
                place,
            )

        lax.fori_loop(0, sections, section_up, last)


def join_kernel(shots, group, anchors, first_ref, second_ref, out_ref, shifts):
    section, tile = lax.axis_index("depth"), lax.axis_index("tile")
    plane = lax.rem(tile // group, 2)
    half_rows = first_ref.shape[0]
    for i, ref in enumerate((first_ref, second_ref)):
        start = pl.multiple_of((plane if i == 0 else 1 - plane) * half_rows, half_rows)
        out_ref[pl.ds(start, half_rows), :] = ref[...]
    columns = shifts.shape[1]
    place = lax.broadcasted_iota(jnp.int32, shifts.shape[1:], 1)
    start = lax.broadcasted_iota(jnp.int32, shifts.shape[1:], 0)
    for q in range(shots):
        offset = anchors[lax.rem(section, shots) ^ q] - (tile - 1) * columns
        shifts[q] = (place - start == offset).astype(jnp.float32).astype(shifts.dtype)


def hold_kernel(array_ref, after_ref, out_ref):
    pass


def place_kernel(shots, shifts, *refs):
    arrived, (left_out, own_out) = refs[:-2], refs[-2:]
    places, columns = left_out.shape
    placed = None
    for q in range(shots):
        total = None
        for r in range(q, len(arrived), shots):
            value = arrived[r][:places, :]
            total = value if total is None else total + value
        part = jnp.dot(total, shifts[q], preferred_element_type=jnp.float32)
        placed = part if placed is None else placed + part
    left_out[...] = placed[:, :columns].astype(left_out.dtype)
    own_out[...] = placed[:, columns:]


def kept(array):
    return pltpu.with_memory_space_constraint(array, pltpu.HBM)


def held(array):
    return pltpu.with_memory_space_constraint(array, pltpu.VMEM)


def on_device(source, anchors, counts, reflect, lateral_x, lateral_y):
    shots, _, rows, columns = source.shape
    slots = reflect.shape[1]
    sizes = (slots, rows, columns)
    plan = Plan(shots)
    sections, group = plan.sections, plan.group
    assert shots == 2
    bf16 = jnp.bfloat16
    smem = pl.BlockSpec(memory_space=pltpu.SMEM)
    vmem = pl.BlockSpec(memory_space=pltpu.VMEM)
    hbm = pl.BlockSpec(memory_space=pltpu.HBM)
    anywhere = pl.BlockSpec(memory_space=pl.ANY)

    def params(mib):
        return pltpu.CompilerParams(vmem_limit_bytes=mib * MIB)

    tile_reflect = reflect[0].reshape(slots * rows, columns)
    halo = lax.ppermute(tile_reflect, "tile", [(i, i + 1) for i in range(plan.tiles - 1)])
    part = columns + rows // 2
    half_rows, win_rows = slots * part, slots * rows + TAIL
    early_rows = 2 * (half_rows - part) + win_rows
    even = pltpu.VMEM((early_rows + 2 * TAIL, columns), bf16)
    odd = pltpu.VMEM((early_rows, columns), bf16)
    even_early, odd_early, late, far_half = pl.pallas_call(
        functools.partial(pack_kernel, group, sizes),
        out_shape=[
            even,
            odd,
            jax.ShapeDtypeStruct((2 * part, columns), bf16),
            jax.ShapeDtypeStruct((half_rows, columns), bf16),
        ],
        in_specs=[hbm, hbm],
        out_specs=[vmem] * 4,
        scratch_shapes=[
            pltpu.VMEM(lateral_x.shape[1:], bf16),
            pltpu.VMEM(lateral_y.shape[1:], bf16),
            pltpu.SemaphoreType.DMA((2,)),
        ],
        compiler_params=params(12),
        name="pack",
    )(kept(lateral_x[0]), kept(lateral_y[0]))
    last = sections - 1
    far_half = lax.ppermute(far_half, BOTH, plan.to_workers(last))
    even_early, odd_early, far_window = pl.pallas_call(
        functools.partial(window_kernel, shots, sizes),
        out_shape=[even, odd, jax.ShapeDtypeStruct((win_rows, columns), bf16)],
        in_specs=[hbm, smem, vmem, hbm, vmem, vmem],
        out_specs=[vmem] * 3,
        scratch_shapes=[
            pltpu.SMEM((shots,), jnp.int32),
            pltpu.VMEM((slots * rows, columns), bf16),
            pltpu.SemaphoreType.DMA((2,)),
        ],
        input_output_aliases={4: 0, 5: 1},
        compiler_params=params(12),
        cost_estimate=pl.CostEstimate(flops=3 * 10**9, bytes_accessed=4 * MIB, transcendentals=0),
        name="windows",
    )(kept(anchors), counts, halo, kept(tile_reflect), held(even_early), held(odd_early))
    messages = [
        even_early,
        lax.ppermute(odd_early, BOTH, plan.to_workers(1)),
        lax.ppermute(even_early, BOTH, plan.to_workers(2)),
    ]
    far_window = lax.ppermute(far_window, BOTH, plan.to_workers(last))
    other_half = lax.ppermute(far_half, BOTH, plan.swap_workers())
    late = pl.pallas_call(
        hold_kernel,
        out_shape=jax.ShapeDtypeStruct(late.shape, bf16),
        in_specs=[anywhere] * 2,
        out_specs=anywhere,
        input_output_aliases={0: 0},
        compiler_params=params(2),
        cost_estimate=pl.CostEstimate(flops=352 * 10**7, bytes_accessed=0, transcendentals=0),
        name="hold",
    )(late, far_window)
    lates = [lax.ppermute(late, BOTH, plan.ops_to_workers(r)) for r in (1, 2)]
    joined, shifts = pl.pallas_call(
        functools.partial(join_kernel, shots, group),
        out_shape=[
            pltpu.VMEM((2 * half_rows, columns), bf16),
            pltpu.VMEM((shots, columns, 2 * columns), bf16),
        ],
        in_specs=[smem] + [vmem] * 2,
        out_specs=[vmem] * 2,
        compiler_params=params(8),
        name="join",
    )(anchors, held(far_half), held(other_half))

    levels = sections * slots
    buffers = [
        pltpu.VMEM((levels, 2 * columns, columns), bf16),
        pltpu.VMEM((levels, 2 * rows, 2 * rows), bf16),
        pltpu.VMEM((levels, rows, columns), bf16),
        pltpu.VMEM((levels + 1, 2 * rows, columns), bf16),
    ]
    stages = [pltpu.VMEM((2 * columns, columns), bf16), pltpu.VMEM((rows, 2 * rows), bf16)]
    messages = [held(message) for message in messages]
    late, joined, far_window = held(late), held(joined), held(far_window)
    filled = pl.pallas_call(
        functools.partial(down_kernel, sections, shots, group, sizes),
        out_shape=buffers,
        in_specs=[vmem] * 7,
        out_specs=[vmem] * 4,
        scratch_shapes=stages + [pltpu.SMEM((sections,), jnp.int32)],
        compiler_params=params(24),
        name="down",
    )(held(source.reshape(shots, 2 * rows, columns)), *messages, late, joined, far_window)
    correlations = pl.pallas_call(
        functools.partial(up_kernel, sections, shots, group, sizes),
        out_shape=[
            jax.ShapeDtypeStruct((slots * rows + TAIL * more, columns), bf16)
            for more in (0, 0, 2, 1)
        ]
        + buffers,
        in_specs=[vmem] * 12,
        out_specs=[vmem] * (sections + 4),
        scratch_shapes=stages
        + [pltpu.VMEM((2 * rows, columns), bf16), pltpu.SMEM((sections,), jnp.int32)],
        input_output_aliases={8 + i: sections + i for i in range(4)},
        compiler_params=params(24),
        name="up",
    )(
        *messages, late, *[held(part) for part in lates], joined, far_window,
        *[held(buffer) for buffer in filled],
    )

    corr_shape = jax.ShapeDtypeStruct((slots * rows, columns), bf16)
    arrived = [correlations[0]] + [
        lax.ppermute(correlations[r], BOTH, plan.from_workers(r)) for r in range(1, sections)
    ]
    left, own = pl.pallas_call(
        functools.partial(place_kernel, shots),
        out_shape=[corr_shape, jax.ShapeDtypeStruct((slots * rows, columns), jnp.float32)],
        in_specs=[vmem] * (1 + sections),
        out_specs=[vmem, vmem],
        compiler_params=params(8),
        name="place",
    )(held(shifts), *[held(part) for part in arrived])
    from_right = lax.ppermute(left, "tile", [(i + 1, i) for i in range(plan.tiles - 1)])
    image = own + from_right.astype(jnp.float32)
    return image.reshape(1, slots, rows, columns)


def solution(mesh):
    return jax.shard_map(
        on_device,
        mesh=mesh,
        in_specs=(
            P("tile", None, None, None),
            P("tile"),
            P("depth"),
            P("depth", None, None, "tile"),
            P("depth", None, None, None, None),
            P("depth", None, None, None, None),
        ),
        out_specs=P("depth", None, None, "tile"),
        check_vma=False,
    )
```
